32 devices in a mesh: gx: 8 (over z, y), gy: 4 (over x, core).
Axes of the slice: x: 2, y: 2, z: 4, core: 2. Of those that a mesh axis runs over, the one named last changes fastest.
Arguments:
- signal: bfloat16 [16384, 384], P(('gx', 'gy')), may hold values from -6 to 6
- w_up: bfloat16 [768, 1536], replicated, may hold values from -0.21875 to 0.21875
- w_down: bfloat16 [768, 1536], replicated, may hold values from -0.15625 to 0.15625
- cotangent: bfloat16 [16384, 384], P(('gx', 'gy')), may hold values from -0.046875 to 0.046875
Outputs:
- mixed_out: bfloat16 [16384, 384], P(('gx', 'gy'))
- grad_up: float32 [768, 1536], P('gx', 'gy')
- grad_down: float32 [768, 1536], P('gx', 'gy')
The draws below stay inside these ranges and needn't reach their ends.
All inputs are finite; a program needn't handle non-finite values.
Results may differ from the reference program's by a relative error of at most 0.023.
Values may be sent and summed in bfloat16 or wider, within the bound.
No kernel may reach another device: no remote copies, remote signals or barrier semaphores. Data moves between devices by JAX's collectives and lax.ppermute only.
A program may use at most 128 MiB of HBM per device.

```python
import math
import jax
import jax.numpy as jnp
from jax import lax

D = 384
FF = 1536
POS_DEV = 512
D2 = 768
POSITIONS = 16384
N_GY = 4


def block_levels(own_key, extent, pieces, least, largest):
    level = 1.0
    for axis_at, parts in pieces:
        heights = jax.random.uniform(jax.random.fold_in(jax.random.fold_in(own_key, 6), axis_at), (parts,), jnp.float32, least / len(pieces), largest / len(pieces))
        level = level * jnp.repeat(jnp.exp(heights), extent[axis_at] // parts).reshape((-1,) + (1,) * (len(extent) - 1 - axis_at))
    return level


def normal_values(own_key, shape, scale, bound, shards=(), dtype=jnp.bfloat16):
    values = scale * jax.random.normal(own_key, shape, jnp.float32)
    if shards:
        values = values * block_levels(own_key, shape, shards, -0.22, 0.18)
    return jnp.clip(values, -bound, bound).astype(dtype)


def setup_inputs(seed: int = 0) -> dict:
    arg_keys = jax.random.split(jax.random.key(seed), 5)
    return {
        "signal": normal_values(arg_keys[0], (POSITIONS, D), 1.0, 6.0, ((0, 32),)),
        "w_up": normal_values(arg_keys[1], (D2, FF), D2 ** -0.5, 0.21875),
        "w_down": normal_values(arg_keys[2], (D2, FF), FF ** -0.5, 0.15625),
        "cotangent": normal_values(arg_keys[3], (POSITIONS, D), (2 * POSITIONS ** -0.5), 0.046875, ((0, 32),)),
    }


def normalize(pair):
    values = pair.astype(jnp.float32)
    centre = lax.optimization_barrier(jnp.mean(values, axis=-1, keepdims=True))
    shifted = values - centre
    spread = lax.optimization_barrier(jnp.mean(shifted * shifted, axis=-1, keepdims=True))
    factor = lax.rsqrt(spread + 1e-05)
    return (shifted * factor, factor)

def gelu_value(pre):
    return 0.5 * pre * (1.0 + lax.erf(pre * (1.0 / math.sqrt(2.0))))

def gelu_slope(pre):
    return 0.5 * (1.0 + lax.erf(pre * (1.0 / math.sqrt(2.0)))) + pre * jnp.exp(-0.5 * pre * pre) * (1.0 / math.sqrt(2.0 * math.pi))

def switch_forward(pair, w_up, w_down):
    normed, factor = normalize(pair)
    normed_bf = normed.astype(jnp.bfloat16)
    pre = jnp.dot(normed_bf, w_up, preferred_element_type=jnp.float32)
    hidden = gelu_value(pre).astype(jnp.bfloat16)
    mixed = pair.astype(jnp.float32) + jnp.dot(hidden, w_down.T, preferred_element_type=jnp.float32)
    return (mixed.astype(jnp.bfloat16), pre)

def switch_backward(pair, pre, pair_grad, w_up, w_down, need_input):
    normed, factor = normalize(pair)
    normed_bf = normed.astype(jnp.bfloat16)
    hidden = gelu_value(pre).astype(jnp.bfloat16)
    d_hidden = jnp.dot(pair_grad, w_down, preferred_element_type=jnp.float32)
    grad_down = jnp.dot(pair_grad.T, hidden, preferred_element_type=jnp.float32)
    d_pre = (d_hidden * gelu_slope(pre)).astype(jnp.bfloat16)
    grad_up = jnp.dot(normed_bf.T, d_pre, preferred_element_type=jnp.float32)
    d_input = None
    if need_input:
        d_norm = jnp.dot(d_pre, w_up.T, preferred_element_type=jnp.float32)
        d_pair = factor * (d_norm - lax.optimization_barrier(jnp.mean(d_norm, axis=-1, keepdims=True)) - normed * lax.optimization_barrier(jnp.mean(d_norm * normed, axis=-1, keepdims=True)))
        d_input = (pair_grad.astype(jnp.float32) + d_pair).astype(jnp.bfloat16)
    return (grad_up, grad_down, d_input)

def to_pairs(state, dist):
    width = state.shape[1]
    blocks = state.reshape(-1, 2, dist, width)
    return jnp.concatenate([blocks[:, 0], blocks[:, 1]], axis=-1).reshape(-1, 2 * width)

def from_pairs(pairs, dist, width):
    blocks = pairs.reshape(-1, dist, 2 * width)
    return jnp.stack([blocks[..., :width], blocks[..., width:]], axis=1).reshape(-1, width)

def reference(signal, w_up, w_down, cotangent):
    width = signal.shape[1]
    dists = [POSITIONS // 2, POS_DEV * N_GY, POS_DEV * N_GY // 2, POS_DEV]
    state = signal
    stored = []
    for dist in dists:
        pair = to_pairs(state, dist)
        mixed, pre = switch_forward(pair, w_up, w_down)
        stored.append((pair, pre))
        state = from_pairs(mixed, dist, width)
    mixed_out = state
    grad = cotangent
    total_up = jnp.zeros(w_up.shape, jnp.float32)
    total_down = jnp.zeros(w_down.shape, jnp.float32)
    for section in range(3, -1, -1):
        pair, pre = stored[section]
        pair_grad = to_pairs(grad, dists[section])
        part_up, part_down, d_input = switch_backward(pair, pre, pair_grad, w_up, w_down, section > 0)
        total_up = total_up + part_up
        total_down = total_down + part_down
        if section > 0:
            grad = from_pairs(d_input, dists[section], width)
    return (mixed_out, total_up, total_down)
```

```python
import math

import jax
import jax.numpy as jnp
from jax import lax
from jax.sharding import PartitionSpec as P


def normalize(pair):
    values = pair.astype(jnp.float32)
    centre = jnp.mean(values, axis=-1, keepdims=True)
    shifted = values - centre
    spread = jnp.mean(shifted * shifted, axis=-1, keepdims=True)
    factor = lax.rsqrt(spread + 1e-05)
    return (shifted * factor, factor)


def gelu_value(pre):
    return 0.5 * pre * (1.0 + lax.erf(pre * (1.0 / math.sqrt(2.0))))


def gelu_slope(pre):
    return 0.5 * (1.0 + lax.erf(pre * (1.0 / math.sqrt(2.0)))) + pre * jnp.exp(-0.5 * pre * pre) * (
        1.0 / math.sqrt(2.0 * math.pi)
    )


def contract_last(left, right):
    return lax.dot_general(
        left, right, (((1,), (1,)), ((), ())), preferred_element_type=jnp.float32
    )


def contract_first(left, right):
    return lax.dot_general(
        left, right, (((0,), (0,)), ((), ())), preferred_element_type=jnp.float32
    )


def section_groups(span_x, span_y):
    bits_x = [span_x.bit_length() - 2, 0]
    bits_y = [span_y.bit_length() - 2, 0]
    mask_x = sum(1 << bit for bit in bits_x)
    mask_y = sum(1 << bit for bit in bits_y)
    groups = []
    for base_x in range(span_x):
        for base_y in range(span_y):
            if base_x & mask_x or base_y & mask_y:
                continue
            group = []
            for member in range(16):
                at_x, at_y = base_x, base_y
                at_x |= (member >> 3 & 1) << bits_x[0] | (member >> 2 & 1) << bits_x[1]
                at_y |= (member >> 1 & 1) << bits_y[0] | (member & 1) << bits_y[1]
                group.append(at_x * span_y + at_y)
            groups.append(group)
    return groups


def exchange(block, groups):
    return lax.all_to_all(
        block, ("gx", "gy"), split_axis=0, concat_axis=0, axis_index_groups=groups, tiled=True
    )


def to_pairs(state, mask):
    members, rows, width = state.shape
    blocks = state.reshape(members // (2 * mask), 2, mask * rows, width)
    return jnp.concatenate([blocks[:, 0], blocks[:, 1]], axis=-1).reshape(-1, 2 * width)


def from_pairs(pairs, mask, members):
    width = pairs.shape[1] // 2
    blocks = pairs.reshape(members // (2 * mask), -1, 2 * width)
    return jnp.stack([blocks[..., :width], blocks[..., width:]], axis=1).reshape(members, -1, width)


def halve(total, axis, bit, dim):
    mine = lax.axis_index(axis) // (1 << bit) % 2
    give = lax.dynamic_index_in_dim(total, 1 - mine, dim, keepdims=False).astype(jnp.bfloat16)
    keep = lax.dynamic_index_in_dim(total, mine, dim, keepdims=False)
    pairs = [(source, source ^ (1 << bit)) for source in range(lax.axis_size(axis))]
    taken = lax.ppermute(give, axis, pairs)
    return (keep.astype(jnp.float32) + taken.astype(jnp.float32)).astype(jnp.bfloat16)


def scatter_sum(total, order):
    span_x = lax.axis_size("gx")
    span_y = lax.axis_size("gy")
    count_x = span_x.bit_length() - 1
    count_y = span_y.bit_length() - 1
    rows = total.shape[0] // span_x
    columns = total.shape[1] // span_y
    left = [("gy", bit) for bit in range(count_y)][::-1] + [("gx", bit) for bit in range(count_x)][::-1]
    blocks = total.reshape(span_x, rows, span_y, columns).transpose(2, 0, 1, 3)
    blocks = blocks.reshape((2,) * len(left) + (rows, columns)).astype(jnp.bfloat16)
    for step in order:
        dim = left.index(step)
        blocks = halve(blocks, step[0], step[1], dim)
        left.pop(dim)
    return blocks.astype(jnp.float32)


def local(signal, w_up, w_down, cotangent):
    span_x = lax.axis_size("gx")
    span_y = lax.axis_size("gy")
    groups = section_groups(span_x, span_y)
    rows, width = signal.shape
    state = exchange(signal.reshape(16, rows // 16, width), groups)
    grad = exchange(cotangent.reshape(16, rows // 16, width), groups)
    masks = [8, 4, 2, 1]
    saved = []
    for mask in masks:
        pair = to_pairs(state, mask)
        normed, factor = normalize(pair)
        normed_bf = normed.astype(jnp.bfloat16)
        pre = jnp.dot(normed_bf, w_up, preferred_element_type=jnp.float32)
        hidden = gelu_value(pre).astype(jnp.bfloat16)
        mixed = (pair.astype(jnp.float32) + contract_last(hidden, w_down)).astype(jnp.bfloat16)
        state = from_pairs(mixed, mask, 16)
        saved.append((normed, normed_bf, factor, pre, hidden))
    mixed_out = exchange(state, groups).reshape(rows, width)
    grads, slopes = [], []
    for section in [3, 2, 1, 0]:
        normed, normed_bf, factor, pre, hidden = saved[section]
        pair_grad = to_pairs(grad, masks[section])
        d_hidden = jnp.dot(pair_grad, w_down, preferred_element_type=jnp.float32)
        d_pre = (d_hidden * gelu_slope(pre)).astype(jnp.bfloat16)
        grads.append(pair_grad)
        slopes.append(d_pre)
        if section > 0:
            d_norm = contract_last(d_pre, w_up)
            d_pair = factor * (
                d_norm
                - jnp.mean(d_norm, axis=-1, keepdims=True)
                - normed * jnp.mean(d_norm * normed, axis=-1, keepdims=True)
            )
            d_input = (pair_grad.astype(jnp.float32) + d_pair).astype(jnp.bfloat16)
            grad = from_pairs(d_input, masks[section], 16)
    order = [3, 2, 1, 0]
    total_down = contract_first(
        jnp.concatenate(grads, 0), jnp.concatenate([saved[k][4] for k in order], 0)
    )
    total_up = contract_first(
        jnp.concatenate([saved[k][1] for k in order], 0), jnp.concatenate(slopes, 0)
    )
    rest_y = [("gy", bit) for bit in range(1, span_y.bit_length() - 1)]
    rest_x = [("gx", bit) for bit in range(1, span_x.bit_length() - 1)]
    core, across = ("gy", 0), ("gx", 0)
    grad_up = scatter_sum(total_up, [core] + rest_y + [across] + rest_x)
    grad_down = scatter_sum(total_down, [core, across] + rest_y + rest_x)
    return (mixed_out, grad_up, grad_down)


def solution(mesh):
    return jax.shard_map(
        local,
        mesh=mesh,
        in_specs=(P(("gx", "gy"), None), P(), P(), P(("gx", "gy"), None)),
        out_specs=(P(("gx", "gy"), None), P("gx", "gy"), P("gx", "gy")),
        check_vma=False,
    )
```

```python
import functools
import math

import jax
import jax.numpy as jnp
from jax import lax
from jax.experimental import pallas as pl
from jax.experimental.pallas import tpu as pltpu
from jax.sharding import PartitionSpec as P

MEMBERS = 16
MASKS = (8, 4, 2, 1)
LANES = 128
CHUNK = 256
VMEM_BYTES = 40 * 1024 * 1024


def section_groups(span_x, span_y):
    bits_x = [span_x.bit_length() - 2, 0]
    bits_y = [span_y.bit_length() - 2, 0]
    mask_x = sum(1 << bit for bit in bits_x)
    mask_y = sum(1 << bit for bit in bits_y)
    groups = []
    for base_x in range(span_x):
        for base_y in range(span_y):
            if base_x & mask_x or base_y & mask_y:
                continue
            group = []
            for member in range(MEMBERS):
                at_x, at_y = base_x, base_y
                at_x |= (member >> 3 & 1) << bits_x[0] | (member >> 2 & 1) << bits_x[1]
                at_y |= (member >> 1 & 1) << bits_y[0] | (member & 1) << bits_y[1]
                group.append(at_x * span_y + at_y)
            groups.append(group)
    return groups


def exchange(block, groups):
    return lax.all_to_all(
        block, ("gx", "gy"), split_axis=0, concat_axis=0, axis_index_groups=groups, tiled=True
    )


def low_members(mask):
    return [member for member in range(MEMBERS) if not member & mask]


def read_pair(ref, mask):
    low = jnp.concatenate([ref[member] for member in low_members(mask)], 0)
    high = jnp.concatenate([ref[member | mask] for member in low_members(mask)], 0)
    return jnp.concatenate([low, high], 1).astype(jnp.float32)


def write_pair(ref, mask, pair):
    rows, width = ref.shape[1:]
    for place, member in enumerate(low_members(mask)):
        part = pair[place * rows : (place + 1) * rows]
        ref[member] = part[:, :width]
        ref[member | mask] = part[:, width:]


def forward_kernel(
    state_ref, up_ref, down_t_ref, out_ref, normed_ref, normed_t_ref, factor_ref, hidden_ref, slope_ref
):
    pairs = MEMBERS // 2 * state_ref.shape[1]
    hidden_units = up_ref.shape[1]
    for section, mask in enumerate(MASKS):
        at = pl.ds(section * pairs, pairs)
        pair = read_pair(state_ref if section == 0 else out_ref, mask)
        centre = jnp.mean(pair, axis=-1, keepdims=True)
        shifted = pair - centre
        spread = jnp.mean(shifted * shifted, axis=-1, keepdims=True)
        factor = lax.rsqrt(spread + 1e-05)
        normed = (shifted * factor).astype(jnp.bfloat16)
        normed_ref[at, :] = normed
        factor_ref[at, :] = jnp.broadcast_to(factor, (pairs, LANES))
        total = pair
        for start in range(0, hidden_units, CHUNK):
            units = pl.ds(start, CHUNK)
            pre = jnp.dot(normed, up_ref[:, units], preferred_element_type=jnp.float32)
            share = 0.5 * (1.0 + lax.erf(pre * (1.0 / math.sqrt(2.0))))
            hidden = (pre * share).astype(jnp.bfloat16)
            hidden_ref[at, units] = hidden
            bell = jnp.exp(-0.5 * pre * pre) * (1.0 / math.sqrt(2.0 * math.pi))
            slope_ref[at, units] = (share + pre * bell).astype(jnp.bfloat16)
            total = total + jnp.dot(hidden, down_t_ref[units, :], preferred_element_type=jnp.float32)
        write_pair(out_ref, mask, total.astype(jnp.bfloat16))
        normed_t_ref[:, at] = normed.T


def backward_kernel(
    grad_ref, normed_ref, factor_ref, slope_ref, down_ref, up_t_ref, grad_t_ref, d_pre_ref, work_ref
):
    pairs = MEMBERS // 2 * grad_ref.shape[1]
    hidden_units = down_ref.shape[1]
    last = len(MASKS) - 1
    for section in range(last, -1, -1):
        mask = MASKS[section]
        at = pl.ds(section * pairs, pairs)
        pair_grad = read_pair(grad_ref if section == last else work_ref, mask)
        pair_bf = pair_grad.astype(jnp.bfloat16)
        d_norm = jnp.zeros(pair_grad.shape, jnp.float32)
        for start in range(0, hidden_units, CHUNK):
            units = pl.ds(start, CHUNK)
            d_hidden = jnp.dot(pair_bf, down_ref[:, units], preferred_element_type=jnp.float32)
            d_pre = (d_hidden * slope_ref[at, units].astype(jnp.float32)).astype(jnp.bfloat16)
            d_pre_ref[at, units] = d_pre
            if section > 0:
                d_norm = d_norm + jnp.dot(d_pre, up_t_ref[units, :], preferred_element_type=jnp.float32)
        if section > 0:
            normed = normed_ref[at, :].astype(jnp.float32)
            d_pair = factor_ref[at, :][:, :1] * (
                d_norm
                - jnp.mean(d_norm, axis=-1, keepdims=True)
                - normed * jnp.mean(d_norm * normed, axis=-1, keepdims=True)
            )
            write_pair(work_ref, mask, (pair_grad + d_pair).astype(jnp.bfloat16))
        grad_t_ref[:, at] = pair_bf.T


def blocks_kernel(places, bit_ref, left_ref, right_ref, out_ref):
    rows, columns = out_ref.shape[1:]
    pieces = []
    for group in range(len(places[0])):
        base = (2 * group + bit_ref[0]) * columns
        for inner in range(0, columns, LANES):
            pieces.append((group, inner, pl.multiple_of(base + inner, LANES)))
    for first in range(0, len(pieces), 2):
        some = pieces[first : first + 2]
        right = jnp.concatenate([right_ref[:, pl.ds(start, LANES)] for _, _, start in some], 1)
        total = jnp.dot(left_ref[...], right, preferred_element_type=jnp.float32)
        total = total.astype(jnp.bfloat16)
        for which, (group, inner, _) in enumerate(some):
            for block in range(len(places)):
                out_ref[places[block][group], :, inner : inner + LANES] = total[
                    block * rows : (block + 1) * rows, which * LANES : (which + 1) * LANES
                ]


def call(kernel, outs, flops, *args, scalars=0, scratch=()):
    size = sum(math.prod(item.shape) * item.dtype.itemsize for item in list(args) + list(outs))
    whole = pl.BlockSpec(memory_space=pltpu.VMEM)
    return pl.pallas_call(
        kernel,
        out_shape=list(outs),
        in_specs=[pl.BlockSpec(memory_space=pltpu.SMEM)] * scalars + [whole] * (len(args) - scalars),
        out_specs=[whole] * len(outs),
        scratch_shapes=list(scratch),
        compiler_params=pltpu.CompilerParams(vmem_limit_bytes=VMEM_BYTES),
        cost_estimate=pl.CostEstimate(flops=flops, bytes_accessed=size, transcendentals=0),
    )(*args)


def forward(state, w_up, down_t):
    _, rows, width = state.shape
    total = len(MASKS) * (MEMBERS // 2) * rows
    depth, units = w_up.shape
    bf16, f32 = jnp.bfloat16, jnp.float32
    outs = [
        jax.ShapeDtypeStruct(state.shape, bf16),
        jax.ShapeDtypeStruct((total, depth), bf16),
        jax.ShapeDtypeStruct((depth, total), bf16),
        jax.ShapeDtypeStruct((total, LANES), f32),
        jax.ShapeDtypeStruct((total, units), bf16),
        jax.ShapeDtypeStruct((total, units), bf16),
    ]
    return call(forward_kernel, outs, 4 * total * depth * units, state, w_up, down_t)


def backward(grad, normed, factor, slope, w_down, up_t):
    total, units = slope.shape
    depth = normed.shape[1]
    outs = [
        jax.ShapeDtypeStruct((depth, total), jnp.bfloat16),
        jax.ShapeDtypeStruct((total, units), jnp.bfloat16),
    ]
    scratch = [pltpu.VMEM(grad.shape, jnp.bfloat16)]
    return call(
        backward_kernel, outs, 4 * total * depth * units, grad, normed, factor, slope, w_down, up_t,
        scratch=scratch,
    )


def gradient_blocks(left, right, bit, order, span_x, span_y):
    rows, columns = left.shape[0] // span_x, right.shape[1] // span_y
    places = []
    for at_x in range(span_x):
        line = []
        for group in range(span_y // 2):
            place = 0
            for axis, step in order:
                at = at_x if axis == "gx" else 2 * group
                place = 2 * place + (at >> step & 1)
            line.append(place)
        places.append(line)
    out = jax.ShapeDtypeStruct((span_x * span_y // 2, rows, columns), jnp.bfloat16)
    flops = left.shape[0] * left.shape[1] * right.shape[1]
    (blocks,) = call(
        functools.partial(blocks_kernel, places), [out], flops,
        bit.reshape(1).astype(jnp.int32), left, right, scalars=1,
    )
    return blocks


def pick(block, at):
    return lax.dynamic_index_in_dim(block, at, 0, keepdims=False).astype(jnp.float32)


def swap(block, axis, bit):
    pairs = [(source, source ^ (1 << bit)) for source in range(lax.axis_size(axis))]
    return lax.ppermute(block, axis, pairs)


def finish_sum(kept, taken, order):
    for axis, bit in order:
        mine = lax.axis_index(axis) // (1 << bit) % 2
        kept = kept.reshape((2, -1) + kept.shape[1:])
        taken = taken.reshape(kept.shape)
        give = (pick(kept, 1 - mine) + pick(taken, 1 - mine)).astype(jnp.bfloat16)
        kept = (pick(kept, mine) + pick(taken, mine)).astype(jnp.bfloat16)
        taken = swap(give, axis, bit)
    return (kept.astype(jnp.float32) + taken.astype(jnp.float32))[0]


def scatter_narrow(left, right, order, span_x, span_y):
    total = jnp.dot(left, right, preferred_element_type=jnp.float32).astype(jnp.bfloat16)
    rows, columns = left.shape[0] // span_x, right.shape[1] // span_y
    count_x, count_y = span_x.bit_length() - 1, span_y.bit_length() - 1
    dims = [("gx", bit) for bit in range(count_x)][::-1] + ["rows"]
    dims += [("gy", bit) for bit in range(count_y)][::-1] + ["columns"]
    blocks = total.reshape((2,) * count_x + (rows,) + (2,) * count_y + (columns,))
    blocks = blocks.transpose([dims.index(item) for item in list(order) + ["rows", "columns"]])
    blocks = blocks.reshape(-1, rows, columns)
    return finish_sum(blocks, jnp.zeros_like(blocks), order)


def local(signal, w_up, w_down, cotangent):
    span_x = lax.axis_size("gx")
    span_y = lax.axis_size("gy")
    groups = section_groups(span_x, span_y)
    rows, width = signal.shape
    state = exchange(signal.reshape(MEMBERS, rows // MEMBERS, width), groups)
    grad = exchange(cotangent.reshape(MEMBERS, rows // MEMBERS, width), groups)
    down_t, up_t = w_down.T, w_up.T
    state, normed, normed_t, factor, hidden, slope = forward(state, w_up, down_t)
    mixed_out = exchange(state, groups).reshape(rows, width)
    grad_t, d_pre = backward(grad, normed, factor, slope, w_down, up_t)

    rest_y = [("gy", bit) for bit in range(1, span_y.bit_length() - 1)]
    rest_x = [("gx", bit) for bit in range(1, span_x.bit_length() - 1)]
    core, across = ("gy", 0), ("gx", 0)
    order_down = [across] + rest_y + rest_x
    order_up = rest_y + [across] + rest_x
    if w_up.shape[1] // span_y % LANES:
        grad_down = scatter_narrow(grad_t, hidden, [core] + order_down, span_x, span_y)
        grad_up = scatter_narrow(normed_t, d_pre, [core] + order_up, span_x, span_y)
        return (mixed_out, grad_up, grad_down)

    mine = lax.axis_index("gy") % 2
    give_down = gradient_blocks(grad_t, hidden, 1 - mine, order_down, span_x, span_y)
    give_up = gradient_blocks(normed_t, d_pre, 1 - mine, order_up, span_x, span_y)
    take_down, take_up = swap(give_down, *core), swap(give_up, *core)
    keep_down = gradient_blocks(grad_t, hidden, mine, order_down, span_x, span_y)
    keep_up = gradient_blocks(normed_t, d_pre, mine, order_up, span_x, span_y)
    grad_down = finish_sum(keep_down, take_down, order_down)
    grad_up = finish_sum(keep_up, take_up, order_up)
    return (mixed_out, grad_up, grad_down)


def solution(mesh):
    return jax.shard_map(
        local,
        mesh=mesh,
        in_specs=(P(("gx", "gy"), None), P(), P(), P(("gx", "gy"), None)),
        out_specs=(P(("gx", "gy"), None), P("gx", "gy"), P("gx", "gy")),
        check_vma=False,
    )
```

```python
import functools
import math

import jax
import jax.numpy as jnp
from jax import lax
from jax.experimental import pallas as pl
from jax.experimental.pallas import tpu as pltpu
from jax.sharding import PartitionSpec as P

MEMBERS = 16
MASKS = (8, 4, 2, 1)
LANES = 128
CHUNK = 256
VMEM_BYTES = 16 * 1024 * 1024


def section_groups(span_x, span_y):
    bits_x = [span_x.bit_length() - 2, 0]
    bits_y = [span_y.bit_length() - 2, 0]
    mask_x = sum(1 << bit for bit in bits_x)
    mask_y = sum(1 << bit for bit in bits_y)
    groups = []
    for base_x in range(span_x):
        for base_y in range(span_y):
            if base_x & mask_x or base_y & mask_y:
                continue
            group = []
            for member in range(MEMBERS):
                at_x, at_y = base_x, base_y
                at_x |= (member >> 3 & 1) << bits_x[0] | (member >> 2 & 1) << bits_x[1]
                at_y |= (member >> 1 & 1) << bits_y[0] | (member & 1) << bits_y[1]
                group.append(at_x * span_y + at_y)
            groups.append(group)
    return groups


def exchange(block, groups):
    return lax.all_to_all(
        block, ("gx", "gy"), split_axis=0, concat_axis=0, axis_index_groups=groups, tiled=True
    )


def contract_last(left, right):
    return lax.dot_general(
        left, right, (((1,), (1,)), ((), ())), preferred_element_type=jnp.float32
    )


def low_members(mask):
    return [member for member in range(MEMBERS) if not member & mask]


def read_pair(ref, mask, first, rows):
    at = pl.ds(first, rows)
    low = jnp.concatenate([ref[member, at] for member in low_members(mask)], 0)
    high = jnp.concatenate([ref[member | mask, at] for member in low_members(mask)], 0)
    return jnp.concatenate([low, high], 1).astype(jnp.float32)


def write_pair(ref, mask, pair):
    rows, width = ref.shape[1:]
    for place, member in enumerate(low_members(mask)):
        part = pair[place * rows : (place + 1) * rows]
        ref[member] = part[:, :width]
        ref[member | mask] = part[:, width:]


def forward_kernel(
    both_ref, up_ref, down_ref, out_ref, normed_ref, normed_t_ref, factor_ref, hidden_ref, slope_ref
):
    rows = out_ref.shape[1]
    pairs = MEMBERS // 2 * rows
    hidden_units = up_ref.shape[1]
    for section, mask in enumerate(MASKS):
        at = pl.ds(section * pairs, pairs)
        pair = read_pair(both_ref if section == 0 else out_ref, mask, 0, rows)
        centre = jnp.mean(pair, axis=-1, keepdims=True)
        shifted = pair - centre
        spread = jnp.mean(shifted * shifted, axis=-1, keepdims=True)
        factor = lax.rsqrt(spread + 1e-05)
        normed = (shifted * factor).astype(jnp.bfloat16)
        normed_ref[at, :] = normed
        factor_ref[at, :] = jnp.broadcast_to(factor, (pairs, LANES))
        for start in range(0, hidden_units, CHUNK):
            units = pl.ds(start, CHUNK)
            pre = jnp.dot(normed, up_ref[:, units], preferred_element_type=jnp.float32)
            share = 0.5 * (1.0 + lax.erf(pre * (1.0 / math.sqrt(2.0))))
            hidden = (pre * share).astype(jnp.bfloat16)
            hidden_ref[at, units] = hidden
            bell = jnp.exp(-0.5 * pre * pre) * (1.0 / math.sqrt(2.0 * math.pi))
            slope_ref[at, units] = (share + pre * bell).astype(jnp.bfloat16)
        mixed = pair + contract_last(hidden_ref[at, :], down_ref[...])
        write_pair(out_ref, mask, mixed.astype(jnp.bfloat16))
        normed_t_ref[:, at] = normed.T


def backward_kernel(
    both_ref, normed_ref, factor_ref, slope_ref, down_ref, up_ref, grad_t_ref, d_pre_ref, work_ref
):
    rows = work_ref.shape[1]
    pairs = MEMBERS // 2 * rows
    hidden_units = down_ref.shape[1]
    last = len(MASKS) - 1
    for section in range(last, -1, -1):
        mask = MASKS[section]
        at = pl.ds(section * pairs, pairs)
        if section == last:
            pair_grad = read_pair(both_ref, mask, rows, rows)
        else:
            pair_grad = read_pair(work_ref, mask, 0, rows)
        pair_bf = pair_grad.astype(jnp.bfloat16)
        for start in range(0, hidden_units, CHUNK):
            units = pl.ds(start, CHUNK)
            d_hidden = jnp.dot(pair_bf, down_ref[:, units], preferred_element_type=jnp.float32)
            d_pre = (d_hidden * slope_ref[at, units].astype(jnp.float32)).astype(jnp.bfloat16)
            d_pre_ref[at, units] = d_pre
        if section > 0:
            d_norm = contract_last(d_pre_ref[at, :], up_ref[...])
            normed = normed_ref[at, :].astype(jnp.float32)
            d_pair = factor_ref[at, :][:, :1] * (
                d_norm
                - jnp.mean(d_norm, axis=-1, keepdims=True)
                - normed * jnp.mean(d_norm * normed, axis=-1, keepdims=True)
            )
            write_pair(work_ref, mask, (pair_grad + d_pair).astype(jnp.bfloat16))
        grad_t_ref[:, at] = pair_bf.T


def blocks_kernel(places, bit_ref, left_ref, right_ref, out_ref):
    rows, columns = out_ref.shape[1:]
    pieces = []
    for group in range(len(places[0])):
        base = (2 * group + bit_ref[0]) * columns
        for inner in range(0, columns, LANES):
            pieces.append((group, inner, pl.multiple_of(base + inner, LANES)))
    for first in range(0, len(pieces), 2):
        some = pieces[first : first + 2]
        right = jnp.concatenate([right_ref[:, pl.ds(start, LANES)] for _, _, start in some], 1)
        total = jnp.dot(left_ref[...], right, preferred_element_type=jnp.float32)
        total = total.astype(jnp.bfloat16)
        for which, (group, inner, _) in enumerate(some):
            for block in range(len(places)):
                out_ref[places[block][group], :, inner : inner + LANES] = total[
                    block * rows : (block + 1) * rows, which * LANES : (which + 1) * LANES
                ]


def call(kernel, outs, flops, *args, scalars=0, scratch=()):
    size = sum(math.prod(item.shape) * item.dtype.itemsize for item in list(args) + list(outs))
    whole = pl.BlockSpec(memory_space=pltpu.VMEM)
    return pl.pallas_call(
        kernel,
        out_shape=list(outs),
        in_specs=[pl.BlockSpec(memory_space=pltpu.SMEM)] * scalars + [whole] * (len(args) - scalars),
        out_specs=[whole] * len(outs),
        scratch_shapes=list(scratch),
        compiler_params=pltpu.CompilerParams(vmem_limit_bytes=VMEM_BYTES),
        cost_estimate=pl.CostEstimate(flops=flops, bytes_accessed=size, transcendentals=0),
    )(*args)


def forward(both, w_up, w_down):
    rows, width = both.shape[1] // 2, both.shape[2]
    total = len(MASKS) * (MEMBERS // 2) * rows
    depth, units = w_up.shape
    bf16, f32 = jnp.bfloat16, jnp.float32
    outs = [
        jax.ShapeDtypeStruct((MEMBERS, rows, width), bf16),
        jax.ShapeDtypeStruct((total, depth), bf16),
        jax.ShapeDtypeStruct((depth, total), bf16),
        jax.ShapeDtypeStruct((total, LANES), f32),
        jax.ShapeDtypeStruct((total, units), bf16),
        jax.ShapeDtypeStruct((total, units), bf16),
    ]
    return call(forward_kernel, outs, 4 * total * depth * units, both, w_up, w_down)


def backward(both, normed, factor, slope, w_down, w_up):
    total, units = slope.shape
    depth = normed.shape[1]
    outs = [
        jax.ShapeDtypeStruct((depth, total), jnp.bfloat16),
        jax.ShapeDtypeStruct((total, units), jnp.bfloat16),
    ]
    scratch = [pltpu.VMEM((MEMBERS, both.shape[1] // 2, both.shape[2]), jnp.bfloat16)]
    return call(
        backward_kernel, outs, 4 * total * depth * units, both, normed, factor, slope, w_down, w_up,
        scratch=scratch,
    )


def gradient_blocks(left, right, bit, order, span_x, span_y):
    rows, columns = left.shape[0] // span_x, right.shape[1] // span_y
    places = []
    for at_x in range(span_x):
        line = []
        for group in range(span_y // 2):
            place = 0
            for axis, step in order:
                at = at_x if axis == "gx" else 2 * group
                place = 2 * place + (at >> step & 1)
            line.append(place)
        places.append(line)
    out = jax.ShapeDtypeStruct((span_x * span_y // 2, rows, columns), jnp.bfloat16)
    flops = left.shape[0] * left.shape[1] * right.shape[1]
    (blocks,) = call(
        functools.partial(blocks_kernel, places), [out], flops,
        bit.reshape(1).astype(jnp.int32), left, right, scalars=1,
    )
    return blocks


def pick(block, at):
    return lax.dynamic_index_in_dim(block, at, 0, keepdims=False).astype(jnp.float32)


def swap(block, axis, bit):
    pairs = [(source, source ^ (1 << bit)) for source in range(lax.axis_size(axis))]
    return lax.ppermute(block, axis, pairs)


def finish_sum(kept, taken, order):
    for axis, bit in order:
        mine = lax.axis_index(axis) // (1 << bit) % 2
        kept = kept.reshape((2, -1) + kept.shape[1:])
        taken = taken.reshape(kept.shape)
        give = (pick(kept, 1 - mine) + pick(taken, 1 - mine)).astype(jnp.bfloat16)
        kept = (pick(kept, mine) + pick(taken, mine)).astype(jnp.bfloat16)
        taken = swap(give, axis, bit)
    return (kept.astype(jnp.float32) + taken.astype(jnp.float32))[0]


def scatter_narrow(left, right, order, span_x, span_y):
    total = jnp.dot(left, right, preferred_element_type=jnp.float32).astype(jnp.bfloat16)
    rows, columns = left.shape[0] // span_x, right.shape[1] // span_y
    count_x, count_y = span_x.bit_length() - 1, span_y.bit_length() - 1
    dims = [("gx", bit) for bit in range(count_x)][::-1] + ["rows"]
    dims += [("gy", bit) for bit in range(count_y)][::-1] + ["columns"]
    blocks = total.reshape((2,) * count_x + (rows,) + (2,) * count_y + (columns,))
    blocks = blocks.transpose([dims.index(item) for item in list(order) + ["rows", "columns"]])
    blocks = blocks.reshape(-1, rows, columns)
    return finish_sum(blocks, jnp.zeros_like(blocks), order)


def local(signal, w_up, w_down, cotangent):
    span_x = lax.axis_size("gx")
    span_y = lax.axis_size("gy")
    groups = section_groups(span_x, span_y)
    rows, width = signal.shape
    parts = (MEMBERS, rows // MEMBERS, width)
    both = jnp.concatenate([signal.reshape(parts), cotangent.reshape(parts)], 1)
    both = exchange(both, groups)
    state, normed, normed_t, factor, hidden, slope = forward(both, w_up, w_down)
    mixed_out = exchange(state, groups).reshape(rows, width)
    grad_t, d_pre = backward(both, normed, factor, slope, w_down, w_up)

    rest_y = [("gy", bit) for bit in range(1, span_y.bit_length() - 1)]
    rest_x = [("gx", bit) for bit in range(1, span_x.bit_length() - 1)]
    core, across = ("gy", 0), ("gx", 0)
    order_down = [across] + rest_y + rest_x[::-1]
    order_up = rest_y + [across] + rest_x
    if w_up.shape[1] // span_y % LANES:
        grad_down = scatter_narrow(grad_t, hidden, [core] + order_down, span_x, span_y)
        grad_up = scatter_narrow(normed_t, d_pre, [core] + order_up, span_x, span_y)
        return (mixed_out, grad_up, grad_down)

    mine = lax.axis_index("gy") % 2
    give_down = gradient_blocks(grad_t, hidden, 1 - mine, order_down, span_x, span_y)
    give_up = gradient_blocks(normed_t, d_pre, 1 - mine, order_up, span_x, span_y)
    take_down, take_up = swap(give_down, *core), swap(give_up, *core)
    keep_down = gradient_blocks(grad_t, hidden, mine, order_down, span_x, span_y)
    keep_up = gradient_blocks(normed_t, d_pre, mine, order_up, span_x, span_y)
    grad_down = finish_sum(keep_down, take_down, order_down)
    grad_up = finish_sum(keep_up, take_up, order_up)
    return (mixed_out, grad_up, grad_down)


def solution(mesh):
    return jax.shard_map(
        local,
        mesh=mesh,
        in_specs=(P(("gx", "gy"), None), P(), P(), P(("gx", "gy"), None)),
        out_specs=(P(("gx", "gy"), None), P("gx", "gy"), P("gx", "gy")),
        check_vma=False,
    )
```

```python
import functools
import math

import jax
import jax.numpy as jnp
from jax import lax
from jax.experimental import pallas as pl
from jax.experimental.pallas import tpu as pltpu
from jax.sharding import PartitionSpec as P

MEMBERS = 16
MASKS = (8, 4, 2, 1)
LANES = 128
CHUNK = 256
SECTIONS_BYTES = 20 * 1024 * 1024
KEEP_BYTES = 4 * 1024 * 1024


def section_groups(span_x, span_y):
    bits_x = [span_x.bit_length() - 2, 0]
    bits_y = [span_y.bit_length() - 2, 0]
    mask_x = sum(1 << bit for bit in bits_x)
    mask_y = sum(1 << bit for bit in bits_y)
    groups = []
    for base_x in range(span_x):
        for base_y in range(span_y):
            if base_x & mask_x or base_y & mask_y:
                continue
            group = []
            for member in range(MEMBERS):
                at_x, at_y = base_x, base_y
                at_x |= (member >> 3 & 1) << bits_x[0] | (member >> 2 & 1) << bits_x[1]
                at_y |= (member >> 1 & 1) << bits_y[0] | (member & 1) << bits_y[1]
                group.append(at_x * span_y + at_y)
            groups.append(group)
    return groups


def exchange(block, groups):
    return lax.all_to_all(
        block, ("gx", "gy"), split_axis=0, concat_axis=0, axis_index_groups=groups, tiled=True
    )


def contract_last(left, right):
    return lax.dot_general(
        left, right, (((1,), (1,)), ((), ())), preferred_element_type=jnp.float32
    )


def low_members(mask):
    return [member for member in range(MEMBERS) if not member & mask]


def read_pair(ref, mask, first, rows):
    at = pl.ds(first, rows)
    low = jnp.concatenate([ref[member, at] for member in low_members(mask)], 0)
    high = jnp.concatenate([ref[member | mask, at] for member in low_members(mask)], 0)
    return jnp.concatenate([low, high], 1).astype(jnp.float32)


def write_pair(ref, mask, pair, spots=range(MEMBERS), swapped=0):
    rows, width = ref.shape[1:]
    for place, member in enumerate(low_members(mask)):
        part = pair[place * rows : (place + 1) * rows]
        ref[spots[member] ^ swapped] = part[:, :width]
        ref[spots[member | mask] ^ swapped] = part[:, width:]


def write_blocks(places, bit, left_ref, right_ref, out_ref):
    rows, columns = out_ref.shape[1:]
    pieces = []
    for group in range(len(places[0])):
        base = (2 * group + bit) * columns
        for inner in range(0, columns, LANES):
            pieces.append((group, inner, pl.multiple_of(base + inner, LANES)))
    for first in range(0, len(pieces), 2):
        some = pieces[first : first + 2]
        right = jnp.concatenate([right_ref[:, pl.ds(start, LANES)] for _, _, start in some], 1)
        total = jnp.dot(left_ref[...], right, preferred_element_type=jnp.float32)
        total = total.astype(jnp.bfloat16)
        for which, (group, inner, _) in enumerate(some):
            for block in range(len(places)):
                out_ref[places[block][group], :, inner : inner + LANES] = total[
                    block * rows : (block + 1) * rows, which * LANES : (which + 1) * LANES
                ]


def sections_kernel(
    spots, places_down, places_up, place_ref, both_ref, up_hbm, down_hbm,
    out_ref, hidden_ref, d_pre_ref, normed_t_ref, grad_t_ref, *rest
):
    blocks, (up_ref, down_ref, normed_ref, factor_ref, slope_ref, work_ref, arrived) = rest[:-7], rest[-7:]
    fetch_up = pltpu.make_async_copy(up_hbm, up_ref, arrived.at[0])
    fetch_down = pltpu.make_async_copy(down_hbm, down_ref, arrived.at[1])
    fetch_up.start()
    fetch_down.start()
    rows = work_ref.shape[1]
    pairs = MEMBERS // 2 * rows
    hidden_units = up_ref.shape[1]
    last = len(MASKS) - 1

    for section, mask in enumerate(MASKS):
        at = pl.ds(section * pairs, pairs)
        pair = read_pair(both_ref if section == 0 else work_ref, mask, 0, rows)
        centre = jnp.mean(pair, axis=-1, keepdims=True)
        shifted = pair - centre
        spread = jnp.mean(shifted * shifted, axis=-1, keepdims=True)
        factor = lax.rsqrt(spread + 1e-05)
        normed = (shifted * factor).astype(jnp.bfloat16)
        normed_ref[at, :] = normed
        factor_ref[at, :] = jnp.broadcast_to(factor, (pairs, LANES))
        if section == 0:
            fetch_up.wait()
        for start in range(0, hidden_units, CHUNK):
            units = pl.ds(start, CHUNK)
            pre = jnp.dot(normed, up_ref[:, units], preferred_element_type=jnp.float32)
            share = 0.5 * (1.0 + lax.erf(pre * (1.0 / math.sqrt(2.0))))
            hidden_ref[at, units] = (pre * share).astype(jnp.bfloat16)
            bell = jnp.exp(-0.5 * pre * pre) * (1.0 / math.sqrt(2.0 * math.pi))
            slope_ref[at, units] = (share + pre * bell).astype(jnp.bfloat16)
        if section == 0:
            fetch_down.wait()
        mixed = (pair + contract_last(hidden_ref[at, :], down_ref[...])).astype(jnp.bfloat16)
        if section < last:
            write_pair(work_ref, mask, mixed)
        else:
            write_pair(out_ref, mask, mixed, spots, place_ref[2])
        normed_t_ref[:, at] = normed.T

    for section in range(last, -1, -1):
        mask = MASKS[section]
        at = pl.ds(section * pairs, pairs)
        if section == last:
            pair_grad = read_pair(both_ref, mask, rows, rows)
        else:
            pair_grad = read_pair(work_ref, mask, 0, rows)
        pair_bf = pair_grad.astype(jnp.bfloat16)
        for start in range(0, hidden_units, CHUNK):
            units = pl.ds(start, CHUNK)
            d_hidden = jnp.dot(pair_bf, down_ref[:, units], preferred_element_type=jnp.float32)
            d_pre_ref[at, units] = (d_hidden * slope_ref[at, units].astype(jnp.float32)).astype(jnp.bfloat16)
        if section > 0:
            d_norm = contract_last(d_pre_ref[at, :], up_ref[...])
            normed = normed_ref[at, :].astype(jnp.float32)
            d_pair = factor_ref[at, :][:, :1] * (
                d_norm
                - jnp.mean(d_norm, axis=-1, keepdims=True)
                - normed * jnp.mean(d_norm * normed, axis=-1, keepdims=True)
            )
            write_pair(work_ref, mask, (pair_grad + d_pair).astype(jnp.bfloat16))
        grad_t_ref[:, at] = pair_bf.T

    if blocks:
        write_blocks(places_down, place_ref[1], grad_t_ref, hidden_ref, blocks[0])
        write_blocks(places_up, place_ref[1], normed_t_ref, d_pre_ref, blocks[1])


def keep_kernel(
    places_down, places_up, place_ref, hidden_ref, d_pre_ref, normed_t_ref, grad_t_ref, down_ref, up_ref
):
    write_blocks(places_down, 1 - place_ref[1], grad_t_ref, hidden_ref, down_ref)
    write_blocks(places_up, 1 - place_ref[1], normed_t_ref, d_pre_ref, up_ref)


def join_kernel(first_ref, second_ref, out_ref, done):
    rows = first_ref.shape[1]
    copies = [
        pltpu.make_async_copy(ref, out_ref.at[:, pl.ds(place * rows, rows)], done.at[place])
        for place, ref in enumerate((first_ref, second_ref))
    ]
    for copy in copies:
        copy.start()
    for copy in copies:
        copy.wait()


def settle_kernel(sources, place_ref, blocks_ref, out_ref, done):
    rows = blocks_ref.shape[1]
    copies = []
    for index, source in enumerate(sources):
        first = pl.multiple_of((place_ref[0] ^ source) * rows, rows)
        copies.append(pltpu.make_async_copy(blocks_ref.at[index], out_ref.at[pl.ds(first, rows)], done.at[index]))
    for copy in copies:
        copy.start()
    for copy in copies:
        copy.wait()


def spec(space):
    return pl.BlockSpec(memory_space=space)


def join(first, second):
    members, rows, width = first.shape
    out = jax.ShapeDtypeStruct((members, 2 * rows, width), first.dtype)
    return pl.pallas_call(
        join_kernel,
        out_shape=out,
        in_specs=[spec(pltpu.HBM)] * 2,
        out_specs=spec(pltpu.HBM),
        scratch_shapes=[pltpu.SemaphoreType.DMA((2,))],
        cost_estimate=pl.CostEstimate(flops=0, bytes_accessed=4 * out.size, transcendentals=0),
    )(first, second)


def block_places(order, span_x, span_y):
    places = []
    for at_x in range(span_x):
        line = []
        for group in range(span_y // 2):
            place = 0
            for axis, step in order:
                at = at_x if axis == "gx" else 2 * group
                place = 2 * place + (at >> step & 1)
            line.append(place)
        places.append(line)
    return places


def sections(place, both, w_up, w_down, spots, places, block):
    rows, width = both.shape[1] // 2, both.shape[2]
    total = len(MASKS) * (MEMBERS // 2) * rows
    depth, units = w_up.shape
    bf16 = jnp.bfloat16
    outs = [
        jax.ShapeDtypeStruct((MEMBERS, rows, width), bf16),
        jax.ShapeDtypeStruct((total, units), bf16),
        jax.ShapeDtypeStruct((total, units), bf16),
        jax.ShapeDtypeStruct((depth, total), bf16),
        jax.ShapeDtypeStruct((depth, total), bf16),
    ]
    outs += [block] * 2 if block else []
    return pl.pallas_call(
        functools.partial(sections_kernel, spots, *places),
        out_shape=outs,
        in_specs=[spec(pltpu.SMEM), spec(pltpu.VMEM), spec(pltpu.HBM), spec(pltpu.HBM)],
        out_specs=[spec(pltpu.VMEM)] * len(outs),
        scratch_shapes=[
            pltpu.VMEM(w_up.shape, bf16),
            pltpu.VMEM(w_down.shape, bf16),
            pltpu.VMEM((total, depth), bf16),
            pltpu.VMEM((total, LANES), jnp.float32),
            pltpu.VMEM((total, units), bf16),
            pltpu.VMEM((MEMBERS, rows, width), bf16),
            pltpu.SemaphoreType.DMA((2,)),
        ],
        compiler_params=pltpu.CompilerParams(vmem_limit_bytes=SECTIONS_BYTES),
        cost_estimate=pl.CostEstimate(
            flops=10 * total * depth * units, bytes_accessed=16 * total * units, transcendentals=0
        ),
    )(place, both, w_up, w_down)


def keep_blocks(place, hidden, d_pre, normed_t, grad_t, places, block):
    total, units = hidden.shape
    depth = normed_t.shape[0]
    return pl.pallas_call(
        functools.partial(keep_kernel, *places),
        out_shape=[block] * 2,
        in_specs=[spec(pltpu.SMEM)] + [spec(pltpu.VMEM)] * 4,
        out_specs=[spec(pltpu.VMEM)] * 2,
        compiler_params=pltpu.CompilerParams(vmem_limit_bytes=KEEP_BYTES),
        cost_estimate=pl.CostEstimate(
            flops=2 * total * depth * units, bytes_accessed=8 * total * units, transcendentals=0
        ),
    )(place, hidden, d_pre, normed_t, grad_t)


def pick(block, at):
    return lax.dynamic_index_in_dim(block, at, 0, keepdims=False).astype(jnp.float32)


def swap(block, axis, bit):
    pairs = [(source, source ^ (1 << bit)) for source in range(lax.axis_size(axis))]
    return lax.ppermute(block, axis, pairs)


def halve(kept, taken, step):
    axis, bit = step
    mine = lax.axis_index(axis) // (1 << bit) % 2
    kept = kept.reshape((2, -1) + kept.shape[1:])
    taken = taken.reshape(kept.shape)
    give = (pick(kept, 1 - mine) + pick(taken, 1 - mine)).astype(jnp.bfloat16)
    keep = (pick(kept, mine) + pick(taken, mine)).astype(jnp.bfloat16)
    return keep, give


def finish_sum(kept, taken, order, beside=None):
    for phase, step in enumerate(order):
        kept, give = halve(kept, taken, step)
        if beside:
            give = beside(phase, give)
        taken = swap(give, *step)
    return (kept.astype(jnp.float32) + taken.astype(jnp.float32))[0]


def scatter_narrow(left, right, order, span_x, span_y):
    total = jnp.dot(left, right, preferred_element_type=jnp.float32).astype(jnp.bfloat16)
    rows, columns = left.shape[0] // span_x, right.shape[1] // span_y
    count_x, count_y = span_x.bit_length() - 1, span_y.bit_length() - 1
    dims = [("gx", bit) for bit in range(count_x)][::-1] + ["rows"]
    dims += [("gy", bit) for bit in range(count_y)][::-1] + ["columns"]
    blocks = total.reshape((2,) * count_x + (rows,) + (2,) * count_y + (columns,))
    blocks = blocks.transpose([dims.index(item) for item in list(order) + ["rows", "columns"]])
    blocks = blocks.reshape(-1, rows, columns)
    return finish_sum(blocks, jnp.zeros_like(blocks), order)


class Homeward:
    def __init__(self, state, steps):
        self.held = state[None]
        self.steps = list(steps)
        self.order = []

    def advance(self, other):
        if not self.steps:
            return other
        axis, bit, weight = self.steps.pop(0)
        self.order.append(weight)
        half = self.held.shape[1] // 2
        kept, given = self.held[:, :half], self.held[:, half:]
        given, other = lax.optimization_barrier((given, other))
        self.held = jnp.concatenate([kept, swap(given, axis, bit)], 0)
        return other

    def settle(self, place):
        blocks = self.held[:, 0]
        members, rows, width = blocks.shape
        sources = [sum(w for at, w in enumerate(self.order) if index >> at & 1) for index in range(members)]
        return pl.pallas_call(
            functools.partial(settle_kernel, sources),
            out_shape=jax.ShapeDtypeStruct((members * rows, width), blocks.dtype),
            in_specs=[spec(pltpu.SMEM), spec(pltpu.VMEM)],
            out_specs=spec(pltpu.HBM),
            scratch_shapes=[pltpu.SemaphoreType.DMA((members,))],
            cost_estimate=pl.CostEstimate(flops=0, bytes_accessed=4 * blocks.size, transcendentals=0),
        )(place, blocks)


def local(signal, w_up, w_down, cotangent):
    span_x = lax.axis_size("gx")
    span_y = lax.axis_size("gy")
    groups = section_groups(span_x, span_y)
    rows, width = signal.shape
    depth, units = w_up.shape
    steps = [("gx", span_x.bit_length() - 2), ("gx", 0), ("gy", span_y.bit_length() - 2), ("gy", 0)]
    bits = [lax.axis_index(axis) // (1 << bit) % 2 for axis, bit in steps]
    member = sum(bit * mask for bit, mask in zip(bits, MASKS))
    homeward = [0, 3, 2, 1]
    spots = [sum((m // MASKS[at] & 1) * mask for at, mask in zip(homeward, MASKS)) for m in range(MEMBERS)]
    spot = sum(bits[at] * mask for at, mask in zip(homeward, MASKS))
    place = jnp.stack([member, 1 - bits[3], spot]).astype(jnp.int32)

    rest_y = [("gy", bit) for bit in range(1, span_y.bit_length() - 1)]
    rest_x = [("gx", bit) for bit in range(1, span_x.bit_length() - 1)]
    core, across = ("gy", 0), ("gx", 0)
    order_down = [across] + rest_y + rest_x[::-1]
    order_up = rest_y + [across] + rest_x
    places = [block_places(order, span_x, span_y) for order in (order_down, order_up)]
    block = None
    if units // span_y % LANES == 0:
        block = jax.ShapeDtypeStruct(
            (span_x * span_y // 2, depth // span_x, units // span_y), jnp.bfloat16
        )

    parts = (MEMBERS, rows // MEMBERS, width)
    both = exchange(join(signal.reshape(parts), cotangent.reshape(parts)), groups)
    state, hidden, d_pre, normed_t, grad_t, *given = sections(
        place, both, w_up, w_down, spots, places, block
    )
    home = Homeward(state, [steps[at] + (MASKS[at],) for at in homeward])
    if not given:
        while home.steps:
            home.advance(place)
        mixed_out = home.settle(place)
        grad_down = scatter_narrow(grad_t, hidden, [core] + order_down, span_x, span_y)
        grad_up = scatter_narrow(normed_t, d_pre, [core] + order_up, span_x, span_y)
        return (mixed_out, grad_up, grad_down)
    given[0] = home.advance(given[0])
    take_down, take_up = [swap(part, *core) for part in given]
    keep_down, keep_up = keep_blocks(place, hidden, d_pre, normed_t, grad_t, places, block)
    grad_up = finish_sum(keep_up, take_up, order_up)
    beside = lambda phase, give: home.advance(give) if phase > 0 else give
    grad_down = finish_sum(keep_down, take_down, order_down, beside)
    while home.steps:
        home.advance(place)
    return (home.settle(place), grad_up, grad_down)


def solution(mesh):
    return jax.shard_map(
        local,
        mesh=mesh,
        in_specs=(P(("gx", "gy"), None), P(), P(), P(("gx", "gy"), None)),
        out_specs=(P(("gx", "gy"), None), P("gx", "gy"), P("gx", "gy")),
        check_vma=False,
    )
```

```python
import functools
import math

import jax
import jax.numpy as jnp
from jax import lax
from jax.experimental import pallas as pl
from jax.experimental.pallas import tpu as pltpu
from jax.sharding import PartitionSpec as P

MEMBERS = 16
MASKS = (8, 4, 2, 1)
LANES = 128
CHUNK = 256
SECTIONS_BYTES = 20 * 1024 * 1024
KEEP_BYTES = 4 * 1024 * 1024


def section_groups(span_x, span_y):
    bits_x = [span_x.bit_length() - 2, 0]
    bits_y = [span_y.bit_length() - 2, 0]
    mask_x = sum(1 << bit for bit in bits_x)
    mask_y = sum(1 << bit for bit in bits_y)
    groups = []
    for base_x in range(span_x):
        for base_y in range(span_y):
            if base_x & mask_x or base_y & mask_y:
                continue
            group = []
            for member in range(MEMBERS):
                at_x, at_y = base_x, base_y
                at_x |= (member >> 3 & 1) << bits_x[0] | (member >> 2 & 1) << bits_x[1]
                at_y |= (member >> 1 & 1) << bits_y[0] | (member & 1) << bits_y[1]
                group.append(at_x * span_y + at_y)
            groups.append(group)
    return groups


def exchange(block, groups):
    return lax.all_to_all(
        block, ("gx", "gy"), split_axis=0, concat_axis=0, axis_index_groups=groups, tiled=True
    )


def contract_last(left, right):
    return lax.dot_general(
        left, right, (((1,), (1,)), ((), ())), preferred_element_type=jnp.float32
    )


def low_members(mask):
    return [member for member in range(MEMBERS) if not member & mask]


def read_pair(ref, mask, first, rows):
    at = pl.ds(first, rows)
    low = jnp.concatenate([ref[member, at] for member in low_members(mask)], 0)
    high = jnp.concatenate([ref[member | mask, at] for member in low_members(mask)], 0)
    return jnp.concatenate([low, high], 1).astype(jnp.float32)


def write_pair(ref, mask, pair, spots=range(MEMBERS), swapped=0):
    rows, width = ref.shape[1:]
    for place, member in enumerate(low_members(mask)):
        part = pair[place * rows : (place + 1) * rows]
        ref[spots[member] ^ swapped] = part[:, :width]
        ref[spots[member | mask] ^ swapped] = part[:, width:]


def write_blocks(places, bit, left_ref, right_ref, out_ref):
    rows, columns = out_ref.shape[1:]
    pieces = []
    for group in range(len(places[0])):
        base = (2 * group + bit) * columns
        for inner in range(0, columns, LANES):
            pieces.append((group, inner, pl.multiple_of(base + inner, LANES)))
    for first in range(0, len(pieces), 2):
        some = pieces[first : first + 2]
        right = jnp.concatenate([right_ref[:, pl.ds(start, LANES)] for _, _, start in some], 1)
        total = jnp.dot(left_ref[...], right, preferred_element_type=jnp.float32)
        total = total.astype(jnp.bfloat16)
        for which, (group, inner, _) in enumerate(some):
            for block in range(len(places)):
                out_ref[places[block][group], :, inner : inner + LANES] = total[
                    block * rows : (block + 1) * rows, which * LANES : (which + 1) * LANES
                ]


def sections_kernel(
    spots, places_down, places_up, place_ref, both_hbm, up_hbm, down_hbm,
    out_ref, hidden_ref, d_pre_ref, normed_t_ref, grad_t_ref, *rest
):
    blocks = rest[:-8]
    both_ref, up_ref, down_ref, normed_ref, factor_ref, slope_ref, work_ref, arrived = rest[-8:]
    fetch_both = pltpu.make_async_copy(both_hbm, both_ref, arrived.at[0])
    fetch_up = pltpu.make_async_copy(up_hbm, up_ref, arrived.at[1])
    fetch_down = pltpu.make_async_copy(down_hbm, down_ref, arrived.at[2])
    fetch_both.start()
    fetch_up.start()
    fetch_down.start()
    fetch_both.wait()
    rows = work_ref.shape[1]
    pairs = MEMBERS // 2 * rows
    hidden_units = up_ref.shape[1]
    last = len(MASKS) - 1

    for section, mask in enumerate(MASKS):
        at = pl.ds(section * pairs, pairs)
        pair = read_pair(both_ref if section == 0 else work_ref, mask, 0, rows)
        centre = jnp.mean(pair, axis=-1, keepdims=True)
        shifted = pair - centre
        spread = jnp.mean(shifted * shifted, axis=-1, keepdims=True)
        factor = lax.rsqrt(spread + 1e-05)
        normed = (shifted * factor).astype(jnp.bfloat16)
        normed_ref[at, :] = normed
        factor_ref[at, :] = jnp.broadcast_to(factor, (pairs, LANES))
        if section == 0:
            fetch_up.wait()
        for start in range(0, hidden_units, CHUNK):
            units = pl.ds(start, CHUNK)
            pre = jnp.dot(normed, up_ref[:, units], preferred_element_type=jnp.float32)
            share = 0.5 * (1.0 + lax.erf(pre * (1.0 / math.sqrt(2.0))))
            hidden_ref[at, units] = (pre * share).astype(jnp.bfloat16)
            bell = jnp.exp(-0.5 * pre * pre) * (1.0 / math.sqrt(2.0 * math.pi))
            slope_ref[at, units] = (share + pre * bell).astype(jnp.bfloat16)
        if section == 0:
            fetch_down.wait()
        mixed = (pair + contract_last(hidden_ref[at, :], down_ref[...])).astype(jnp.bfloat16)
        if section < last:
            write_pair(work_ref, mask, mixed)
        else:
            write_pair(out_ref, mask, mixed, spots, place_ref[2])
        normed_t_ref[:, at] = normed.T

    for section in range(last, -1, -1):
        mask = MASKS[section]
        at = pl.ds(section * pairs, pairs)
        if section == last:
            pair_grad = read_pair(both_ref, mask, rows, rows)
        else:
            pair_grad = read_pair(work_ref, mask, 0, rows)
        pair_bf = pair_grad.astype(jnp.bfloat16)
        for start in range(0, hidden_units, CHUNK):
            units = pl.ds(start, CHUNK)
            d_hidden = jnp.dot(pair_bf, down_ref[:, units], preferred_element_type=jnp.float32)
            d_pre_ref[at, units] = (d_hidden * slope_ref[at, units].astype(jnp.float32)).astype(jnp.bfloat16)
        if section > 0:
            d_norm = contract_last(d_pre_ref[at, :], up_ref[...])
            normed = normed_ref[at, :].astype(jnp.float32)
            d_pair = factor_ref[at, :][:, :1] * (
                d_norm
                - jnp.mean(d_norm, axis=-1, keepdims=True)
                - normed * jnp.mean(d_norm * normed, axis=-1, keepdims=True)
            )
            write_pair(work_ref, mask, (pair_grad + d_pair).astype(jnp.bfloat16))
        grad_t_ref[:, at] = pair_bf.T

    if blocks:
        write_blocks(places_down, place_ref[1], grad_t_ref, hidden_ref, blocks[0])
        write_blocks(places_up, place_ref[1], normed_t_ref, d_pre_ref, blocks[1])


def keep_kernel(
    places_down, places_up, place_ref, hidden_ref, d_pre_ref, normed_t_ref, grad_t_ref, down_ref, up_ref
):
    write_blocks(places_down, 1 - place_ref[1], grad_t_ref, hidden_ref, down_ref)
    write_blocks(places_up, 1 - place_ref[1], normed_t_ref, d_pre_ref, up_ref)


def settle_kernel(sources, place_ref, blocks_ref, out_ref, done):
    rows = blocks_ref.shape[1]
    copies = []
    for index, source in enumerate(sources):
        first = pl.multiple_of((place_ref[0] ^ source) * rows, rows)
        copies.append(pltpu.make_async_copy(blocks_ref.at[index], out_ref.at[pl.ds(first, rows)], done.at[index]))
    for copy in copies:
        copy.start()
    for copy in copies:
        copy.wait()


def spec(space):
    return pl.BlockSpec(memory_space=space)


def block_places(order, span_x, span_y):
    places = []
    for at_x in range(span_x):
        line = []
        for group in range(span_y // 2):
            place = 0
            for axis, step in order:
                at = at_x if axis == "gx" else 2 * group
                place = 2 * place + (at >> step & 1)
            line.append(place)
        places.append(line)
    return places


def sections(place, both, w_up, w_down, spots, places, block):
    rows, width = both.shape[1] // 2, both.shape[2]
    total = len(MASKS) * (MEMBERS // 2) * rows
    depth, units = w_up.shape
    bf16 = jnp.bfloat16
    outs = [
        pltpu.VMEM((MEMBERS, rows, width), bf16),
        pltpu.VMEM((total, units), bf16),
        pltpu.VMEM((total, units), bf16),
        pltpu.VMEM((depth, total), bf16),
        pltpu.VMEM((depth, total), bf16),
    ]
    outs += [block] * 2 if block else []
    return pl.pallas_call(
        functools.partial(sections_kernel, spots, *places),
        out_shape=outs,
        in_specs=[spec(pltpu.SMEM)] + [spec(pltpu.HBM)] * 3,
        out_specs=[spec(pltpu.VMEM)] * len(outs),
        scratch_shapes=[
            pltpu.VMEM(both.shape, bf16),
            pltpu.VMEM(w_up.shape, bf16),
            pltpu.VMEM(w_down.shape, bf16),
            pltpu.VMEM((total, depth), bf16),
            pltpu.VMEM((total, LANES), jnp.float32),
            pltpu.VMEM((total, units), bf16),
            pltpu.VMEM((MEMBERS, rows, width), bf16),
            pltpu.SemaphoreType.DMA((3,)),
        ],
        compiler_params=pltpu.CompilerParams(vmem_limit_bytes=SECTIONS_BYTES),
        cost_estimate=pl.CostEstimate(
            flops=10 * total * depth * units, bytes_accessed=16 * total * units, transcendentals=0
        ),
    )(place, *[pltpu.with_memory_space_constraint(item, pltpu.HBM) for item in (both, w_up, w_down)])


def keep_blocks(place, hidden, d_pre, normed_t, grad_t, places, block):
    total, units = hidden.shape
    depth = normed_t.shape[0]
    return pl.pallas_call(
        functools.partial(keep_kernel, *places),
        out_shape=[block] * 2,
        in_specs=[spec(pltpu.SMEM)] + [spec(pltpu.VMEM)] * 4,
        out_specs=[spec(pltpu.VMEM)] * 2,
        compiler_params=pltpu.CompilerParams(vmem_limit_bytes=KEEP_BYTES),
        cost_estimate=pl.CostEstimate(
            flops=2 * total * depth * units, bytes_accessed=8 * total * units, transcendentals=0
        ),
    )(place, *[pltpu.with_memory_space_constraint(item, pltpu.VMEM) for item in (hidden, d_pre, normed_t, grad_t)])


def pick(block, at):
    return lax.dynamic_index_in_dim(block, at, 0, keepdims=False).astype(jnp.float32)


def swap(block, axis, bit):
    pairs = [(source, source ^ (1 << bit)) for source in range(lax.axis_size(axis))]
    return lax.ppermute(block, axis, pairs)


def halve(kept, taken, step):
    axis, bit = step
    mine = lax.axis_index(axis) // (1 << bit) % 2
    kept = kept.reshape((2, -1) + kept.shape[1:])
    taken = taken.reshape(kept.shape)
    give = (pick(kept, 1 - mine) + pick(taken, 1 - mine)).astype(jnp.bfloat16)
    keep = (pick(kept, mine) + pick(taken, mine)).astype(jnp.bfloat16)
    return keep, give


def finish_sum(kept, taken, order, beside=None):
    for phase, step in enumerate(order):
        kept, give = halve(kept, taken, step)
        if beside:
            give = beside(phase, give)
        taken = swap(give, *step)
    return (kept.astype(jnp.float32) + taken.astype(jnp.float32))[0]


def scatter_narrow(left, right, order, span_x, span_y):
    total = jnp.dot(left, right, preferred_element_type=jnp.float32).astype(jnp.bfloat16)
    rows, columns = left.shape[0] // span_x, right.shape[1] // span_y
    count_x, count_y = span_x.bit_length() - 1, span_y.bit_length() - 1
    dims = [("gx", bit) for bit in range(count_x)][::-1] + ["rows"]
    dims += [("gy", bit) for bit in range(count_y)][::-1] + ["columns"]
    blocks = total.reshape((2,) * count_x + (rows,) + (2,) * count_y + (columns,))
    blocks = blocks.transpose([dims.index(item) for item in list(order) + ["rows", "columns"]])
    blocks = blocks.reshape(-1, rows, columns)
    return finish_sum(blocks, jnp.zeros_like(blocks), order)


class Homeward:
    def __init__(self, state, steps):
        self.held = state[None]
        self.steps = list(steps)
        self.order = []

    def advance(self, other):
        if not self.steps:
            return other
        axis, bit, weight = self.steps.pop(0)
        self.order.append(weight)
        half = self.held.shape[1] // 2
        kept, given = self.held[:, :half], self.held[:, half:]
        given, other = lax.optimization_barrier((given, other))
        self.held = jnp.concatenate([kept, swap(given, axis, bit)], 0)
        return other

    def settle(self, place):
        blocks = self.held[:, 0]
        members, rows, width = blocks.shape
        sources = [sum(w for at, w in enumerate(self.order) if index >> at & 1) for index in range(members)]
        return pl.pallas_call(
            functools.partial(settle_kernel, sources),
            out_shape=jax.ShapeDtypeStruct((members * rows, width), blocks.dtype),
            in_specs=[spec(pltpu.SMEM), spec(pltpu.VMEM)],
            out_specs=spec(pltpu.HBM),
            scratch_shapes=[pltpu.SemaphoreType.DMA((members,))],
            cost_estimate=pl.CostEstimate(flops=0, bytes_accessed=4 * blocks.size, transcendentals=0),
        )(place, blocks)


def local(signal, w_up, w_down, cotangent):
    span_x = lax.axis_size("gx")
    span_y = lax.axis_size("gy")
    groups = section_groups(span_x, span_y)
    rows, width = signal.shape
    depth, units = w_up.shape
    steps = [("gx", span_x.bit_length() - 2), ("gx", 0), ("gy", span_y.bit_length() - 2), ("gy", 0)]
    bits = [lax.axis_index(axis) // (1 << bit) % 2 for axis, bit in steps]
    member = sum(bit * mask for bit, mask in zip(bits, MASKS))
    homeward = [2, 0, 3, 1]
    spots = [sum((m // MASKS[at] & 1) * mask for at, mask in zip(homeward, MASKS)) for m in range(MEMBERS)]
    spot = sum(bits[at] * mask for at, mask in zip(homeward, MASKS))
    place = jnp.stack([member, 1 - bits[3], spot]).astype(jnp.int32)

    rest_y = [("gy", bit) for bit in range(1, span_y.bit_length() - 1)]
    rest_x = [("gx", bit) for bit in range(1, span_x.bit_length() - 1)]
    core, across = ("gy", 0), ("gx", 0)
    order_down = [across] + rest_y + rest_x[::-1]
    order_up = rest_y + [across] + rest_x
    places = [block_places(order, span_x, span_y) for order in (order_down, order_up)]
    block = None
    if units // span_y % LANES == 0:
        block = pltpu.VMEM((span_x * span_y // 2, depth // span_x, units // span_y), jnp.bfloat16)

    parts = (MEMBERS, rows // MEMBERS, width)
    both = exchange(jnp.concatenate([signal.reshape(parts), cotangent.reshape(parts)], 1), groups)
    state, hidden, d_pre, normed_t, grad_t, *given = sections(
        place, both, w_up, w_down, spots, places, block
    )
    home = Homeward(state, [steps[at] + (MASKS[at],) for at in homeward])
    if not given:
        while home.steps:
            home.advance(place)
        mixed_out = home.settle(place)
        grad_down = scatter_narrow(grad_t, hidden, [core] + order_down, span_x, span_y)
        grad_up = scatter_narrow(normed_t, d_pre, [core] + order_up, span_x, span_y)
        return (mixed_out, grad_up, grad_down)
    given[0] = home.advance(given[0])
    take_down, take_up = [swap(part, *core) for part in given]
    keep_down, keep_up = keep_blocks(place, hidden, d_pre, normed_t, grad_t, places, block)
    grad_up = finish_sum(keep_up, take_up, order_up)
    beside = lambda phase, give: home.advance(give)
    grad_down = finish_sum(keep_down, take_down, order_down, beside)
    while home.steps:
        home.advance(place)
    return (home.settle(place), grad_up, grad_down)


def solution(mesh):
    return jax.shard_map(
        local,
        mesh=mesh,
        in_specs=(P(("gx", "gy"), None), P(), P(), P(("gx", "gy"), None)),
        out_specs=(P(("gx", "gy"), None), P("gx", "gy"), P("gx", "gy")),
        check_vma=False,
    )
```

```python
import functools
import math

import jax
import jax.numpy as jnp
from jax import lax
from jax.experimental import pallas as pl
from jax.experimental.pallas import tpu as pltpu
from jax.sharding import PartitionSpec as P

MEMBERS = 16
MASKS = (8, 4, 2, 1)
LANES = 128
CHUNK = 256
SECTIONS_BYTES = 20 * 1024 * 1024
KEEP_BYTES = 4 * 1024 * 1024


def section_groups(span_x, span_y):
    bits_x = [span_x.bit_length() - 2, 0]
    bits_y = [span_y.bit_length() - 2, 0]
    mask_x = sum(1 << bit for bit in bits_x)
    mask_y = sum(1 << bit for bit in bits_y)
    groups = []
    for base_x in range(span_x):
        for base_y in range(span_y):
            if base_x & mask_x or base_y & mask_y:
                continue
            group = []
            for member in range(MEMBERS):
                at_x, at_y = base_x, base_y
                at_x |= (member >> 3 & 1) << bits_x[0] | (member >> 2 & 1) << bits_x[1]
                at_y |= (member >> 1 & 1) << bits_y[0] | (member & 1) << bits_y[1]
                group.append(at_x * span_y + at_y)
            groups.append(group)
    return groups


def exchange(block, groups):
    return lax.all_to_all(
        block, ("gx", "gy"), split_axis=0, concat_axis=0, axis_index_groups=groups, tiled=True
    )


def contract_last(left, right):
    return lax.dot_general(
        left, right, (((1,), (1,)), ((), ())), preferred_element_type=jnp.float32
    )


def low_members(mask):
    return [member for member in range(MEMBERS) if not member & mask]


def read_pair(ref, mask, first, rows):
    at = pl.ds(first, rows)
    low = jnp.concatenate([ref[member, at] for member in low_members(mask)], 0)
    high = jnp.concatenate([ref[member | mask, at] for member in low_members(mask)], 0)
    return jnp.concatenate([low, high], 1).astype(jnp.float32)


def write_pair(ref, mask, pair, spots=range(MEMBERS), swapped=0):
    rows, width = ref.shape[1:]
    for place, member in enumerate(low_members(mask)):
        part = pair[place * rows : (place + 1) * rows]
        ref[spots[member] ^ swapped] = part[:, :width]
        ref[spots[member | mask] ^ swapped] = part[:, width:]


def write_blocks(places, bit, left_ref, right_ref, out_ref):
    rows, columns = out_ref.shape[1:]
    pieces = []
    for group in range(len(places[0])):
        base = (2 * group + bit) * columns
        for inner in range(0, columns, LANES):
            pieces.append((group, inner, pl.multiple_of(base + inner, LANES)))
    for first in range(0, len(pieces), 2):
        some = pieces[first : first + 2]
        right = jnp.concatenate([right_ref[:, pl.ds(start, LANES)] for _, _, start in some], 1)
        total = jnp.dot(left_ref[...], right, preferred_element_type=jnp.float32)
        total = total.astype(jnp.bfloat16)
        for which, (group, inner, _) in enumerate(some):
            for block in range(len(places)):
                out_ref[places[block][group], :, inner : inner + LANES] = total[
                    block * rows : (block + 1) * rows, which * LANES : (which + 1) * LANES
                ]


def sections_kernel(
    spots, places_down, places_up, place_ref, both_hbm, up_hbm, down_hbm,
    out_ref, hidden_ref, d_pre_ref, normed_t_ref, grad_t_ref, *rest
):
    blocks = rest[:-8]
    both_ref, up_ref, down_ref, normed_ref, factor_ref, slope_ref, work_ref, arrived = rest[-8:]
    fetch_both = pltpu.make_async_copy(both_hbm, both_ref, arrived.at[0])
    fetch_up = pltpu.make_async_copy(up_hbm, up_ref, arrived.at[1])
    fetch_down = pltpu.make_async_copy(down_hbm, down_ref, arrived.at[2])
    fetch_both.start()
    fetch_up.start()
    fetch_down.start()
    fetch_both.wait()
    rows = work_ref.shape[1]
    pairs = MEMBERS // 2 * rows
    hidden_units = up_ref.shape[1]
    last = len(MASKS) - 1

    for section, mask in enumerate(MASKS):
        at = pl.ds(section * pairs, pairs)
        pair = read_pair(both_ref if section == 0 else work_ref, mask, 0, rows)
        centre = jnp.mean(pair, axis=-1, keepdims=True)
        shifted = pair - centre
        spread = jnp.mean(shifted * shifted, axis=-1, keepdims=True)
        factor = lax.rsqrt(spread + 1e-05)
        normed = (shifted * factor).astype(jnp.bfloat16)
        normed_ref[at, :] = normed
        factor_ref[at, :] = jnp.broadcast_to(factor, (pairs, LANES))
        if section == 0:
            fetch_up.wait()
        for start in range(0, hidden_units, CHUNK):
            units = pl.ds(start, CHUNK)
            pre = jnp.dot(normed, up_ref[:, units], preferred_element_type=jnp.float32)
            share = 0.5 * (1.0 + lax.erf(pre * (1.0 / math.sqrt(2.0))))
            hidden_ref[at, units] = (pre * share).astype(jnp.bfloat16)
            bell = jnp.exp(-0.5 * pre * pre) * (1.0 / math.sqrt(2.0 * math.pi))
            slope_ref[at, units] = (share + pre * bell).astype(jnp.bfloat16)
        if section == 0:
            fetch_down.wait()
        mixed = (pair + contract_last(hidden_ref[at, :], down_ref[...])).astype(jnp.bfloat16)
        if section < last:
            write_pair(work_ref, mask, mixed)
        else:
            write_pair(out_ref, mask, mixed, spots, place_ref[2])
        normed_t_ref[:, at] = normed.T

    for section in range(last, -1, -1):
        mask = MASKS[section]
        at = pl.ds(section * pairs, pairs)
        if section == last:
            pair_grad = read_pair(both_ref, mask, rows, rows)
        else:
            pair_grad = read_pair(work_ref, mask, 0, rows)
        pair_bf = pair_grad.astype(jnp.bfloat16)
        for start in range(0, hidden_units, CHUNK):
            units = pl.ds(start, CHUNK)
            d_hidden = jnp.dot(pair_bf, down_ref[:, units], preferred_element_type=jnp.float32)
            d_pre_ref[at, units] = (d_hidden * slope_ref[at, units].astype(jnp.float32)).astype(jnp.bfloat16)
        if section > 0:
            d_norm = contract_last(d_pre_ref[at, :], up_ref[...])
            normed = normed_ref[at, :].astype(jnp.float32)
            d_pair = factor_ref[at, :][:, :1] * (
                d_norm
                - jnp.mean(d_norm, axis=-1, keepdims=True)
                - normed * jnp.mean(d_norm * normed, axis=-1, keepdims=True)
            )
            write_pair(work_ref, mask, (pair_grad + d_pair).astype(jnp.bfloat16))
        grad_t_ref[:, at] = pair_bf.T

    if blocks:
        write_blocks(places_down, place_ref[1], grad_t_ref, hidden_ref, blocks[0])
        write_blocks(places_up, place_ref[1], normed_t_ref, d_pre_ref, blocks[1])


def keep_kernel(
    places_down, places_up, place_ref, hidden_ref, d_pre_ref, normed_t_ref, grad_t_ref, down_ref, up_ref
):
    write_blocks(places_down, 1 - place_ref[1], grad_t_ref, hidden_ref, down_ref)
    write_blocks(places_up, 1 - place_ref[1], normed_t_ref, d_pre_ref, up_ref)


def settle_kernel(sources, place_ref, blocks_ref, out_ref, done):
    rows = blocks_ref.shape[1]
    copies = []
    for index, source in enumerate(sources):
        first = pl.multiple_of((place_ref[0] ^ source) * rows, rows)
        copies.append(pltpu.make_async_copy(blocks_ref.at[index], out_ref.at[pl.ds(first, rows)], done.at[index]))
    for copy in copies:
        copy.start()
    for copy in copies:
        copy.wait()


def spec(space):
    return pl.BlockSpec(memory_space=space)


def block_places(order, span_x, span_y):
    places = []
    for at_x in range(span_x):
        line = []
        for group in range(span_y // 2):
            place = 0
            for axis, step in order:
                at = at_x if axis == "gx" else 2 * group
                place = 2 * place + (at >> step & 1)
            line.append(place)
        places.append(line)
    return places


def sections(place, both, w_up, w_down, spots, places, block):
    rows, width = both.shape[1] // 2, both.shape[2]
    total = len(MASKS) * (MEMBERS // 2) * rows
    depth, units = w_up.shape
    bf16 = jnp.bfloat16
    outs = [
        pltpu.VMEM((MEMBERS, rows, width), bf16),
        pltpu.VMEM((total, units), bf16),
        pltpu.VMEM((total, units), bf16),
        pltpu.VMEM((depth, total), bf16),
        pltpu.VMEM((depth, total), bf16),
    ]
    outs += [block] * 2 if block else []
    return pl.pallas_call(
        functools.partial(sections_kernel, spots, *places),
        out_shape=outs,
        in_specs=[spec(pltpu.SMEM)] + [spec(pltpu.HBM)] * 3,
        out_specs=[spec(pltpu.VMEM)] * len(outs),
        scratch_shapes=[
            pltpu.VMEM(both.shape, bf16),
            pltpu.VMEM(w_up.shape, bf16),
            pltpu.VMEM(w_down.shape, bf16),
            pltpu.VMEM((total, depth), bf16),
            pltpu.VMEM((total, LANES), jnp.float32),
            pltpu.VMEM((total, units), bf16),
            pltpu.VMEM((MEMBERS, rows, width), bf16),
            pltpu.SemaphoreType.DMA((3,)),
        ],
        compiler_params=pltpu.CompilerParams(vmem_limit_bytes=SECTIONS_BYTES),
        cost_estimate=pl.CostEstimate(
            flops=10 * total * depth * units, bytes_accessed=16 * total * units, transcendentals=0
        ),
    )(place, *[pltpu.with_memory_space_constraint(item, pltpu.HBM) for item in (both, w_up, w_down)])


def keep_blocks(place, hidden, d_pre, normed_t, grad_t, places, block):
    total, units = hidden.shape
    depth = normed_t.shape[0]
    return pl.pallas_call(
        functools.partial(keep_kernel, *places),
        out_shape=[block] * 2,
        in_specs=[spec(pltpu.SMEM)] + [spec(pltpu.VMEM)] * 4,
        out_specs=[spec(pltpu.VMEM)] * 2,
        compiler_params=pltpu.CompilerParams(vmem_limit_bytes=KEEP_BYTES),
        cost_estimate=pl.CostEstimate(
            flops=2 * total * depth * units, bytes_accessed=8 * total * units, transcendentals=0
        ),
    )(place, *[pltpu.with_memory_space_constraint(item, pltpu.VMEM) for item in (hidden, d_pre, normed_t, grad_t)])


def halve_kernel(slot, place_ref, kept_ref, taken_ref, keep_ref, give_ref):
    mine = place_ref[slot]
    for out_ref, half in ((give_ref, 1 - mine), (keep_ref, mine)):
        total = kept_ref[half].astype(jnp.float32) + taken_ref[half].astype(jnp.float32)
        out_ref[...] = total.astype(out_ref.dtype)


def swap(block, axis, bit):
    pairs = [(source, source ^ (1 << bit)) for source in range(lax.axis_size(axis))]
    return lax.ppermute(block, axis, pairs)


def halve(place, slot, kept, taken):
    shape = (2, kept.shape[0] // 2) + kept.shape[1:]
    kept, taken = kept.reshape(shape), taken.reshape(shape)
    return pl.pallas_call(
        functools.partial(halve_kernel, slot),
        out_shape=[pltpu.VMEM(shape[1:], kept.dtype)] * 2,
        in_specs=[spec(pltpu.SMEM)] + [spec(pltpu.VMEM)] * 2,
        out_specs=[spec(pltpu.VMEM)] * 2,
        compiler_params=pltpu.CompilerParams(vmem_limit_bytes=KEEP_BYTES),
        cost_estimate=pl.CostEstimate(flops=kept.size, bytes_accessed=6 * kept.size, transcendentals=0),
    )(place, *[pltpu.with_memory_space_constraint(item, pltpu.VMEM) for item in (kept, taken)])


def finish_sum(place, slots, kept, taken, order, beside=None):
    for phase, step in enumerate(order):
        kept, give = halve(place, slots[step], kept, taken)
        if beside:
            give = beside(phase, give)
        taken = swap(give, *step)
    return (kept.astype(jnp.float32) + taken.astype(jnp.float32))[0]


def scatter_narrow(place, slots, left, right, order, span_x, span_y):
    total = jnp.dot(left, right, preferred_element_type=jnp.float32).astype(jnp.bfloat16)
    rows, columns = left.shape[0] // span_x, right.shape[1] // span_y
    count_x, count_y = span_x.bit_length() - 1, span_y.bit_length() - 1
    dims = [("gx", bit) for bit in range(count_x)][::-1] + ["rows"]
    dims += [("gy", bit) for bit in range(count_y)][::-1] + ["columns"]
    blocks = total.reshape((2,) * count_x + (rows,) + (2,) * count_y + (columns,))
    blocks = blocks.transpose([dims.index(item) for item in list(order) + ["rows", "columns"]])
    blocks = blocks.reshape(-1, rows, columns)
    return finish_sum(place, slots, blocks, jnp.zeros_like(blocks), order)


class Homeward:
    def __init__(self, state, steps):
        self.held = state[None]
        self.steps = list(steps)
        self.order = []

    def advance(self, other):
        if not self.steps:
            return other
        axis, bit, weight = self.steps.pop(0)
        self.order.append(weight)
        half = self.held.shape[1] // 2
        kept, given = self.held[:, :half], self.held[:, half:]
        given, other = lax.optimization_barrier((given, other))
        self.held = jnp.concatenate([kept, swap(given, axis, bit)], 0)
        return other

    def settle(self, place):
        blocks = self.held[:, 0]
        members, rows, width = blocks.shape
        sources = [sum(w for at, w in enumerate(self.order) if index >> at & 1) for index in range(members)]
        return pl.pallas_call(
            functools.partial(settle_kernel, sources),
            out_shape=jax.ShapeDtypeStruct((members * rows, width), blocks.dtype),
            in_specs=[spec(pltpu.SMEM), spec(pltpu.VMEM)],
            out_specs=spec(pltpu.HBM),
            scratch_shapes=[pltpu.SemaphoreType.DMA((members,))],
            cost_estimate=pl.CostEstimate(flops=0, bytes_accessed=4 * blocks.size, transcendentals=0),
        )(place, blocks)


def local(signal, w_up, w_down, cotangent):
    span_x = lax.axis_size("gx")
    span_y = lax.axis_size("gy")
    groups = section_groups(span_x, span_y)
    rows, width = signal.shape
    depth, units = w_up.shape
    steps = [("gx", span_x.bit_length() - 2), ("gx", 0), ("gy", span_y.bit_length() - 2), ("gy", 0)]
    bits = [lax.axis_index(axis) // (1 << bit) % 2 for axis, bit in steps]
    member = sum(bit * mask for bit, mask in zip(bits, MASKS))
    homeward = [2, 0, 1, 3]
    spots = [sum((m // MASKS[at] & 1) * mask for at, mask in zip(homeward, MASKS)) for m in range(MEMBERS)]
    spot = sum(bits[at] * mask for at, mask in zip(homeward, MASKS))

    rest_y = [("gy", bit) for bit in range(1, span_y.bit_length() - 1)]
    rest_x = [("gx", bit) for bit in range(1, span_x.bit_length() - 1)]
    core, across = ("gy", 0), ("gx", 0)
    order_down = [across] + rest_y + rest_x[::-1]
    order_up = rest_y + [across] + rest_x
    slots = {step: 3 + at for at, step in enumerate([core] + order_up)}
    owns = [lax.axis_index(axis) // (1 << bit) % 2 for axis, bit in slots]
    place = jnp.stack([member, 1 - bits[3], spot] + owns).astype(jnp.int32)
    places = [block_places(order, span_x, span_y) for order in (order_down, order_up)]
    block = None
    if units // span_y % LANES == 0:
        block = pltpu.VMEM((span_x * span_y // 2, depth // span_x, units // span_y), jnp.bfloat16)

    parts = (MEMBERS, rows // MEMBERS, width)
    both = exchange(jnp.concatenate([signal.reshape(parts), cotangent.reshape(parts)], 1), groups)
    state, hidden, d_pre, normed_t, grad_t, *given = sections(
        place, both, w_up, w_down, spots, places, block
    )
    home = Homeward(state, [steps[at] + (MASKS[at],) for at in homeward])
    if not given:
        while home.steps:
            home.advance(place)
        mixed_out = home.settle(place)
        grad_down = scatter_narrow(place, slots, grad_t, hidden, [core] + order_down, span_x, span_y)
        grad_up = scatter_narrow(place, slots, normed_t, d_pre, [core] + order_up, span_x, span_y)
        return (mixed_out, grad_up, grad_down)
    given[0] = home.advance(given[0])
    take_down, take_up = [swap(part, *core) for part in given]
    keep_down, keep_up = keep_blocks(place, hidden, d_pre, normed_t, grad_t, places, block)
    grad_up = finish_sum(place, slots, keep_up, take_up, order_up)
    beside = lambda phase, give: give if phase == 1 else home.advance(give)
    grad_down = finish_sum(place, slots, keep_down, take_down, order_down, beside)
    while home.steps:
        home.advance(place)
    return (home.settle(place), grad_up, grad_down)


def solution(mesh):
    return jax.shard_map(
        local,
        mesh=mesh,
        in_specs=(P(("gx", "gy"), None), P(), P(), P(("gx", "gy"), None)),
        out_specs=(P(("gx", "gy"), None), P("gx", "gy"), P("gx", "gy")),
        check_vma=False,
    )
```

```python
import functools
import math

import jax
import jax.numpy as jnp
from jax import lax
from jax.experimental import pallas as pl
from jax.experimental.pallas import tpu as pltpu
from jax.sharding import PartitionSpec as P

MEMBERS = 16
MASKS = (8, 4, 2, 1)
LANES = 128
CHUNK = 256
SECTIONS_BYTES = 8 * 1024 * 1024
KEEP_BYTES = 4 * 1024 * 1024


def section_groups(span_x, span_y):
    bits_x = [span_x.bit_length() - 2, 0]
    bits_y = [span_y.bit_length() - 2, 0]
    mask_x = sum(1 << bit for bit in bits_x)
    mask_y = sum(1 << bit for bit in bits_y)
    groups = []
    for base_x in range(span_x):
        for base_y in range(span_y):
            if base_x & mask_x or base_y & mask_y:
                continue
            group = []
            for member in range(MEMBERS):
                at_x, at_y = base_x, base_y
                at_x |= (member >> 3 & 1) << bits_x[0] | (member >> 2 & 1) << bits_x[1]
                at_y |= (member >> 1 & 1) << bits_y[0] | (member & 1) << bits_y[1]
                group.append(at_x * span_y + at_y)
            groups.append(group)
    return groups


def exchange(block, groups):
    return lax.all_to_all(
        block, ("gx", "gy"), split_axis=0, concat_axis=0, axis_index_groups=groups, tiled=True
    )


def contract_last(left, right):
    return lax.dot_general(
        left, right, (((1,), (1,)), ((), ())), preferred_element_type=jnp.float32
    )


def low_members(mask):
    return [member for member in range(MEMBERS) if not member & mask]


def read_pair(ref, mask, spots=range(MEMBERS), swapped=0):
    low = jnp.concatenate([ref[spots[member] ^ swapped] for member in low_members(mask)], 0)
    high = jnp.concatenate([ref[spots[member | mask] ^ swapped] for member in low_members(mask)], 0)
    return jnp.concatenate([low, high], 1).astype(jnp.float32)


def write_pair(ref, mask, pair, spots=range(MEMBERS), swapped=0):
    rows, width = ref.shape[1:]
    for place, member in enumerate(low_members(mask)):
        part = pair[place * rows : (place + 1) * rows]
        ref[spots[member] ^ swapped] = part[:, :width]
        ref[spots[member | mask] ^ swapped] = part[:, width:]


def write_blocks(places, bit, left_ref, right_ref, out_ref):
    rows, columns = out_ref.shape[1:]
    pieces = []
    for group in range(len(places[0])):
        base = (2 * group + bit) * columns
        for inner in range(0, columns, LANES):
            pieces.append((group, inner, pl.multiple_of(base + inner, LANES)))
    for first in range(0, len(pieces), 2):
        some = pieces[first : first + 2]
        right = jnp.concatenate([right_ref[:, pl.ds(start, LANES)] for _, _, start in some], 1)
        total = jnp.dot(left_ref[...], right, preferred_element_type=jnp.float32)
        total = total.astype(jnp.bfloat16)
        for which, (group, inner, _) in enumerate(some):
            for block in range(len(places)):
                out_ref[places[block][group], :, inner : inner + LANES] = total[
                    block * rows : (block + 1) * rows, which * LANES : (which + 1) * LANES
                ]


def forward_kernel(
    spots, place_ref, state_ref, up_hbm, down_hbm,
    out_ref, hidden_ref, slope_ref, normed_ref, normed_t_ref, factor_ref, up_ref, down_ref, work_ref, arrived
):
    fetch_up = pltpu.make_async_copy(up_hbm, up_ref, arrived.at[0])
    fetch_down = pltpu.make_async_copy(down_hbm, down_ref, arrived.at[1])
    fetch_up.start()
    fetch_down.start()
    pairs = MEMBERS // 2 * work_ref.shape[1]
    hidden_units = up_ref.shape[1]
    last = len(MASKS) - 1
    for section, mask in enumerate(MASKS):
        at = pl.ds(section * pairs, pairs)
        pair = read_pair(state_ref if section == 0 else work_ref, mask)
        centre = jnp.mean(pair, axis=-1, keepdims=True)
        shifted = pair - centre
        spread = jnp.mean(shifted * shifted, axis=-1, keepdims=True)
        factor = lax.rsqrt(spread + 1e-05)
        normed = (shifted * factor).astype(jnp.bfloat16)
        normed_ref[at, :] = normed
        factor_ref[at, :] = jnp.broadcast_to(factor, (pairs, LANES))
        if section == 0:
            fetch_up.wait()
        for start in range(0, hidden_units, CHUNK):
            units = pl.ds(start, CHUNK)
            pre = jnp.dot(normed, up_ref[:, units], preferred_element_type=jnp.float32)
            share = 0.5 * (1.0 + lax.erf(pre * (1.0 / math.sqrt(2.0))))
            hidden_ref[at, units] = (pre * share).astype(jnp.bfloat16)
            bell = jnp.exp(-0.5 * pre * pre) * (1.0 / math.sqrt(2.0 * math.pi))
            slope_ref[at, units] = (share + pre * bell).astype(jnp.bfloat16)
        if section == 0:
            fetch_down.wait()
        mixed = (pair + contract_last(hidden_ref[at, :], down_ref[...])).astype(jnp.bfloat16)
        if section < last:
            write_pair(work_ref, mask, mixed)
        else:
            write_pair(out_ref, mask, mixed, spots, place_ref[2])
        normed_t_ref[:, at] = normed.T


def backward_kernel(
    places_down, places_up, place_ref, grad_ref, hidden_ref, slope_ref, normed_ref, normed_t_ref, factor_ref,
    up_ref, down_ref, d_pre_ref, grad_t_ref, *rest
):
    blocks, work_ref = rest[:-1], rest[-1]
    pairs = MEMBERS // 2 * work_ref.shape[1]
    hidden_units = up_ref.shape[1]
    last = len(MASKS) - 1
    for section in range(last, -1, -1):
        mask = MASKS[section]
        at = pl.ds(section * pairs, pairs)
        if section == last:
            pair_grad = read_pair(grad_ref, mask, swapped=place_ref[0])
        else:
            pair_grad = read_pair(work_ref, mask)
        pair_bf = pair_grad.astype(jnp.bfloat16)
        for start in range(0, hidden_units, CHUNK):
            units = pl.ds(start, CHUNK)
            d_hidden = jnp.dot(pair_bf, down_ref[:, units], preferred_element_type=jnp.float32)
            d_pre_ref[at, units] = (d_hidden * slope_ref[at, units].astype(jnp.float32)).astype(jnp.bfloat16)
        if section > 0:
            d_norm = contract_last(d_pre_ref[at, :], up_ref[...])
            normed = normed_ref[at, :].astype(jnp.float32)
            d_pair = factor_ref[at, :][:, :1] * (
                d_norm
                - jnp.mean(d_norm, axis=-1, keepdims=True)
                - normed * jnp.mean(d_norm * normed, axis=-1, keepdims=True)
            )
            write_pair(work_ref, mask, (pair_grad + d_pair).astype(jnp.bfloat16))
        grad_t_ref[:, at] = pair_bf.T

    if blocks:
        write_blocks(places_down, place_ref[1], grad_t_ref, hidden_ref, blocks[0])
        write_blocks(places_up, place_ref[1], normed_t_ref, d_pre_ref, blocks[1])


def keep_kernel(
    places_down, places_up, place_ref, hidden_ref, d_pre_ref, normed_t_ref, grad_t_ref, down_ref, up_ref
):
    write_blocks(places_down, 1 - place_ref[1], grad_t_ref, hidden_ref, down_ref)
    write_blocks(places_up, 1 - place_ref[1], normed_t_ref, d_pre_ref, up_ref)


def arrange_kernel(spots, place_ref, block_ref, out_ref):
    rows = out_ref.shape[1]
    for member, spot in enumerate(spots):
        out_ref[spot ^ place_ref[3]] = block_ref[member * rows : (member + 1) * rows]


def settle_kernel(sources, place_ref, kept_ref, taken_ref, out_ref, done):
    half, rows = kept_ref.shape[:2]
    copies = []
    for index, source in enumerate(sources):
        block = kept_ref.at[index] if index < half else taken_ref.at[index - half]
        first = pl.multiple_of((place_ref[0] ^ source) * rows, rows)
        copies.append(pltpu.make_async_copy(block, out_ref.at[pl.ds(first, rows)], done.at[index]))
    for copy in copies:
        copy.start()
    for copy in copies:
        copy.wait()


def spec(space):
    return pl.BlockSpec(memory_space=space)


def block_places(order, span_x, span_y):
    places = []
    for at_x in range(span_x):
        line = []
        for group in range(span_y // 2):
            place = 0
            for axis, step in order:
                at = at_x if axis == "gx" else 2 * group
                place = 2 * place + (at >> step & 1)
            line.append(place)
        places.append(line)
    return places


def in_vmem(*items):
    return [pltpu.with_memory_space_constraint(item, pltpu.VMEM) for item in items]


def forward(place, state, w_up, w_down, spots):
    members, rows, width = state.shape
    total = len(MASKS) * (members // 2) * rows
    depth, units = w_up.shape
    bf16 = jnp.bfloat16
    outs = [
        pltpu.VMEM(state.shape, bf16),
        pltpu.VMEM((total, units), bf16),
        pltpu.VMEM((total, units), bf16),
        pltpu.VMEM((total, depth), bf16),
        pltpu.VMEM((depth, total), bf16),
        pltpu.VMEM((total, LANES), jnp.float32),
        pltpu.VMEM(w_up.shape, bf16),
        pltpu.VMEM(w_down.shape, bf16),
    ]
    return pl.pallas_call(
        functools.partial(forward_kernel, spots),
        out_shape=outs,
        in_specs=[spec(pltpu.SMEM), spec(pltpu.VMEM)] + [spec(pltpu.HBM)] * 2,
        out_specs=[spec(pltpu.VMEM)] * len(outs),
        scratch_shapes=[pltpu.VMEM(state.shape, bf16), pltpu.SemaphoreType.DMA((2,))],
        compiler_params=pltpu.CompilerParams(vmem_limit_bytes=SECTIONS_BYTES),
        cost_estimate=pl.CostEstimate(
            flops=10 * total * depth * units, bytes_accessed=16 * total * units, transcendentals=0
        ),
    )(place, state, *[pltpu.with_memory_space_constraint(item, pltpu.HBM) for item in (w_up, w_down)])


def backward(place, grad, kept, places, block):
    total, units = kept[0].shape
    depth = kept[2].shape[1]
    bf16 = jnp.bfloat16
    outs = [pltpu.VMEM((total, units), bf16), pltpu.VMEM((depth, total), bf16)]
    outs += [block] * 2 if block else []
    return pl.pallas_call(
        functools.partial(backward_kernel, *places),
        out_shape=outs,
        in_specs=[spec(pltpu.SMEM)] + [spec(pltpu.VMEM)] * (1 + len(kept)),
        out_specs=[spec(pltpu.VMEM)] * len(outs),
        scratch_shapes=[pltpu.VMEM(grad.shape, bf16)],
        compiler_params=pltpu.CompilerParams(vmem_limit_bytes=SECTIONS_BYTES),
        cost_estimate=pl.CostEstimate(
            flops=10 * total * depth * units, bytes_accessed=16 * total * units, transcendentals=0
        ),
    )(place, grad, *in_vmem(*kept))


def arrange(place, block, spots):
    rows, width = block.shape
    return pl.pallas_call(
        functools.partial(arrange_kernel, spots),
        out_shape=jax.ShapeDtypeStruct((MEMBERS, rows // MEMBERS, width), block.dtype),
        in_specs=[spec(pltpu.SMEM), spec(pltpu.VMEM)],
        out_specs=spec(pltpu.VMEM),
        compiler_params=pltpu.CompilerParams(vmem_limit_bytes=KEEP_BYTES),
        cost_estimate=pl.CostEstimate(flops=0, bytes_accessed=4 * block.size, transcendentals=0),
    )(place, block)


def keep_blocks(place, hidden, d_pre, normed_t, grad_t, places, block):
    total, units = hidden.shape
    depth = normed_t.shape[0]
    return pl.pallas_call(
        functools.partial(keep_kernel, *places),
        out_shape=[block] * 2,
        in_specs=[spec(pltpu.SMEM)] + [spec(pltpu.VMEM)] * 4,
        out_specs=[spec(pltpu.VMEM)] * 2,
        compiler_params=pltpu.CompilerParams(vmem_limit_bytes=KEEP_BYTES),
        cost_estimate=pl.CostEstimate(
            flops=2 * total * depth * units, bytes_accessed=8 * total * units, transcendentals=0
        ),
    )(place, *in_vmem(hidden, d_pre, normed_t, grad_t))


def swap(block, axis, bit):
    pairs = [(source, source ^ (1 << bit)) for source in range(lax.axis_size(axis))]
    return lax.ppermute(block, axis, pairs)


def pick(block, at):
    size = (1,) + block.shape[1:]
    start = (at,) + (0,) * (block.ndim - 1)
    return lax.dynamic_slice(block, start, size, allow_negative_indices=False)[0].astype(jnp.float32)


def finish_sum(halves, kept, taken, order, beside=None):
    for phase, step in enumerate(order):
        mine, other = halves[step]
        shape = (2, kept.shape[0] // 2) + kept.shape[1:]
        kept, taken = kept.reshape(shape), taken.reshape(shape)
        give = (pick(kept, other) + pick(taken, other)).astype(jnp.bfloat16)
        kept = (pick(kept, mine) + pick(taken, mine)).astype(jnp.bfloat16)
        if beside:
            give = beside(phase, give)
        taken = swap(give, *step)
    return (kept.astype(jnp.float32) + taken.astype(jnp.float32))[0]


def scatter_narrow(halves, left, right, order, span_x, span_y):
    total = jnp.dot(left, right, preferred_element_type=jnp.float32).astype(jnp.bfloat16)
    rows, columns = left.shape[0] // span_x, right.shape[1] // span_y
    count_x, count_y = span_x.bit_length() - 1, span_y.bit_length() - 1
    dims = [("gx", bit) for bit in range(count_x)][::-1] + ["rows"]
    dims += [("gy", bit) for bit in range(count_y)][::-1] + ["columns"]
    blocks = total.reshape((2,) * count_x + (rows,) + (2,) * count_y + (columns,))
    blocks = blocks.transpose([dims.index(item) for item in list(order) + ["rows", "columns"]])
    blocks = blocks.reshape(-1, rows, columns)
    return finish_sum(halves, blocks, jnp.zeros_like(blocks), order)


class Journey:
    def __init__(self, blocks, steps):
        self.parts = [blocks[None]]
        self.steps = list(steps)
        self.sources = [0]

    def advance(self, other):
        if not self.steps:
            return other
        axis, bit, weight = self.steps.pop(0)
        held = jnp.concatenate(self.parts, 0)
        half = held.shape[1] // 2
        kept, given = held[:, :half], held[:, half:]
        given, other = lax.optimization_barrier((given, other))
        self.parts = [kept, swap(given, axis, bit)]
        self.sources += [source | weight for source in self.sources]
        return other

    def arrived(self):
        return [part[:, 0] for part in self.parts]


def settle(place, journey):
    kept, taken = journey.arrived()
    half, rows, width = kept.shape
    return pl.pallas_call(
        functools.partial(settle_kernel, journey.sources),
        out_shape=jax.ShapeDtypeStruct((2 * half * rows, width), kept.dtype),
        in_specs=[spec(pltpu.SMEM)] + [spec(pltpu.VMEM)] * 2,
        out_specs=spec(pltpu.HBM),
        scratch_shapes=[pltpu.SemaphoreType.DMA((2 * half,))],
        cost_estimate=pl.CostEstimate(flops=0, bytes_accessed=8 * kept.size, transcendentals=0),
    )(place, kept, taken)


def spots_of(order):
    return [sum((m // MASKS[at] & 1) * mask for at, mask in zip(order, MASKS)) for m in range(MEMBERS)]


def local(signal, w_up, w_down, cotangent):
    span_x = lax.axis_size("gx")
    span_y = lax.axis_size("gy")
    groups = section_groups(span_x, span_y)
    rows, width = signal.shape
    depth, units = w_up.shape
    steps = [("gx", span_x.bit_length() - 2), ("gx", 0), ("gy", span_y.bit_length() - 2), ("gy", 0)]
    bits = [lax.axis_index(axis) // (1 << bit) % 2 for axis, bit in steps]
    member = sum(bit * mask for bit, mask in zip(bits, MASKS))
    rest_y = [("gy", bit) for bit in range(1, span_y.bit_length() - 1)]
    rest_x = [("gx", bit) for bit in range(1, span_x.bit_length() - 1)]
    core, across = ("gy", 0), ("gx", 0)
    order_down = [across] + rest_y + rest_x[::-1]
    order_up = rest_y + [across] + rest_x
    inbound, homeward = [3, 2, 1, 0], [0, 2, 3, 1]
    spot_in, spot_home = [sum(bits[at] * mask for at, mask in zip(o, MASKS)) for o in (inbound, homeward)]
    owns = [lax.axis_index(axis) // (1 << bit) % 2 for axis, bit in [core] + order_up]
    place = jnp.stack([member, 1 - bits[3], spot_home, spot_in]).astype(jnp.int32)
    place, owns, others = lax.optimization_barrier((place, owns, [1 - own for own in owns]))
    halves = {step: (own, other) for step, own, other in zip([core] + order_up, owns, others)}
    places = [block_places(order, span_x, span_y) for order in (order_down, order_up)]
    block = None
    if units // span_y % LANES == 0:
        block = pltpu.VMEM((span_x * span_y // 2, depth // span_x, units // span_y), jnp.bfloat16)

    state = exchange(signal.reshape(MEMBERS, rows // MEMBERS, width), groups)
    coming = Journey(arrange(place, cotangent, spots_of(inbound)), [steps[at] + (MASKS[at],) for at in inbound])
    for _ in range(3):
        place = coming.advance(place)
    state = coming.advance(state)
    state, *kept = forward(place, state, w_up, w_down, spots_of(homeward))
    going = Journey(state, [steps[at] + (MASKS[at],) for at in homeward])
    going.advance(place)
    grad = jnp.concatenate(coming.arrived(), 0)
    d_pre, grad_t, *given = backward(place, grad, kept, places, block)
    hidden, normed_t = kept[0], kept[3]
    if not given:
        while going.steps:
            going.advance(place)
        mixed_out = settle(place, going)
        grad_down = scatter_narrow(halves, grad_t, hidden, [core] + order_down, span_x, span_y)
        grad_up = scatter_narrow(halves, normed_t, d_pre, [core] + order_up, span_x, span_y)
        return (mixed_out, grad_up, grad_down)
    given[0] = going.advance(given[0])
    take_down, take_up = [swap(part, *core) for part in given]
    keep_down, keep_up = keep_blocks(place, hidden, d_pre, normed_t, grad_t, places, block)
    grad_up = finish_sum(halves, keep_up, take_up, order_up)
    beside = lambda phase, give: going.advance(give) if phase in (0, 2) else give
    grad_down = finish_sum(halves, keep_down, take_down, order_down, beside)
    while going.steps:
        going.advance(place)
    return (settle(place, going), grad_up, grad_down)


def solution(mesh):
    return jax.shard_map(
        local,
        mesh=mesh,
        in_specs=(P(("gx", "gy"), None), P(), P(), P(("gx", "gy"), None)),
        out_specs=(P(("gx", "gy"), None), P("gx", "gy"), P("gx", "gy")),
        check_vma=False,
    )
```

```python
import functools
import math

import jax
import jax.numpy as jnp
from jax import lax
from jax.experimental import pallas as pl
from jax.experimental.pallas import tpu as pltpu
from jax.sharding import PartitionSpec as P

MEMBERS = 16
MASKS = (8, 4, 2, 1)
LANES = 128
CHUNK = 256
SECTIONS_BYTES = 8 * 1024 * 1024
KEEP_BYTES = 4 * 1024 * 1024


def section_groups(span_x, span_y):
    bits_x = [span_x.bit_length() - 2, 0]
    bits_y = [span_y.bit_length() - 2, 0]
    mask_x = sum(1 << bit for bit in bits_x)
    mask_y = sum(1 << bit for bit in bits_y)
    groups = []
    for base_x in range(span_x):
        for base_y in range(span_y):
            if base_x & mask_x or base_y & mask_y:
                continue
            group = []
            for member in range(MEMBERS):
                at_x, at_y = base_x, base_y
                at_x |= (member >> 3 & 1) << bits_x[0] | (member >> 2 & 1) << bits_x[1]
                at_y |= (member >> 1 & 1) << bits_y[0] | (member & 1) << bits_y[1]
                group.append(at_x * span_y + at_y)
            groups.append(group)
    return groups


def exchange(block, groups):
    return lax.all_to_all(
        block, ("gx", "gy"), split_axis=0, concat_axis=0, axis_index_groups=groups, tiled=True
    )


def contract_last(left, right):
    return lax.dot_general(
        left, right, (((1,), (1,)), ((), ())), preferred_element_type=jnp.float32
    )


def low_members(mask):
    return [member for member in range(MEMBERS) if not member & mask]


def read_pair(ref, mask, spots=range(MEMBERS), swapped=0):
    low = jnp.concatenate([ref[spots[member] ^ swapped] for member in low_members(mask)], 0)
    high = jnp.concatenate([ref[spots[member | mask] ^ swapped] for member in low_members(mask)], 0)
    return jnp.concatenate([low, high], 1).astype(jnp.float32)


def write_pair(ref, mask, pair, spots=range(MEMBERS), swapped=0):
    rows, width = ref.shape[1:]
    for place, member in enumerate(low_members(mask)):
        part = pair[place * rows : (place + 1) * rows]
        ref[spots[member] ^ swapped] = part[:, :width]
        ref[spots[member | mask] ^ swapped] = part[:, width:]


def write_blocks(places, bit, products, out_ref):
    rows, columns = out_ref.shape[1:]
    pieces = []
    for group in range(len(places[0])):
        base = (2 * group + bit) * columns
        for inner in range(0, columns, LANES):
            pieces.append((group, inner, pl.multiple_of(base + inner, LANES)))
    for first in range(0, len(pieces), 2):
        some = pieces[first : first + 2]
        total = 0.0
        for left_ref, right_ref in products:
            right = jnp.concatenate([right_ref[:, pl.ds(start, LANES)] for _, _, start in some], 1)
            total += jnp.dot(left_ref[...], right, preferred_element_type=jnp.float32)
        total = total.astype(jnp.bfloat16)
        for which, (group, inner, _) in enumerate(some):
            for block in range(len(places)):
                out_ref[places[block][group], :, inner : inner + LANES] = total[
                    block * rows : (block + 1) * rows, which * LANES : (which + 1) * LANES
                ]


def forward_kernel(
    spots, place_ref, state_ref, up_hbm, down_hbm,
    out_ref, hidden_ref, slope_ref, normed_ref, normed_t_ref, factor_ref, up_ref, down_ref, work_ref, arrived
):
    pairs = MEMBERS // 2 * work_ref.shape[1]
    hidden_units = up_ref.shape[1]
    starts = range(0, hidden_units, CHUNK)
    fetches = []
    for which, (source, target) in enumerate(((up_hbm, up_ref), (down_hbm, down_ref))):
        for place, start in enumerate(starts):
            units = pl.ds(start, CHUNK)
            copy = pltpu.make_async_copy(source.at[:, units], target.at[:, units], arrived.at[which, place])
            copy.start()
            fetches.append(copy)
    last = len(MASKS) - 1
    for section, mask in enumerate(MASKS):
        at = pl.ds(section * pairs, pairs)
        pair = read_pair(state_ref if section == 0 else work_ref, mask)
        centre = jnp.mean(pair, axis=-1, keepdims=True)
        shifted = pair - centre
        spread = jnp.mean(shifted * shifted, axis=-1, keepdims=True)
        factor = lax.rsqrt(spread + 1e-05)
        normed = (shifted * factor).astype(jnp.bfloat16)
        normed_ref[at, :] = normed
        factor_ref[at, :] = jnp.broadcast_to(factor, (pairs, LANES))
        for place, start in enumerate(starts):
            units = pl.ds(start, CHUNK)
            if section == 0:
                fetches[place].wait()
            pre = jnp.dot(normed, up_ref[:, units], preferred_element_type=jnp.float32)
            share = 0.5 * (1.0 + lax.erf(pre * (1.0 / math.sqrt(2.0))))
            hidden_ref[at, units] = (pre * share).astype(jnp.bfloat16)
            bell = jnp.exp(-0.5 * pre * pre) * (1.0 / math.sqrt(2.0 * math.pi))
            slope_ref[at, units] = (share + pre * bell).astype(jnp.bfloat16)
        if section == 0:
            for copy in fetches[len(starts) :]:
                copy.wait()
        mixed = (pair + contract_last(hidden_ref[at, :], down_ref[...])).astype(jnp.bfloat16)
        if section < last:
            write_pair(work_ref, mask, mixed)
        else:
            write_pair(out_ref, mask, mixed, spots, place_ref[2])
        normed_t_ref[:, at] = normed.T


def backward_kernel(
    places, place_ref, grad_ref, hidden_ref, slope_ref, normed_ref, factor_ref, up_ref, down_ref,
    d_pre_ref, grad_t_ref, last_ref, *rest
):
    blocks, work_ref = rest[:-1], rest[-1]
    pairs = MEMBERS // 2 * work_ref.shape[1]
    for section in range(len(MASKS) - 1, 0, -1):
        mask = MASKS[section]
        at = pl.ds(section * pairs, pairs)
        later = pl.ds((section - 1) * pairs, pairs)
        if section == len(MASKS) - 1:
            pair_grad = read_pair(grad_ref, mask, swapped=place_ref[0])
        else:
            pair_grad = read_pair(work_ref, mask)
        pair_bf = pair_grad.astype(jnp.bfloat16)
        for start in range(0, up_ref.shape[1], CHUNK):
            units = pl.ds(start, CHUNK)
            d_hidden = jnp.dot(pair_bf, down_ref[:, units], preferred_element_type=jnp.float32)
            d_pre_ref[later, units] = (d_hidden * slope_ref[at, units].astype(jnp.float32)).astype(jnp.bfloat16)
        d_norm = contract_last(d_pre_ref[later, :], up_ref[...])
        normed = normed_ref[at, :].astype(jnp.float32)
        d_pair = factor_ref[at, :][:, :1] * (
            d_norm
            - jnp.mean(d_norm, axis=-1, keepdims=True)
            - normed * jnp.mean(d_norm * normed, axis=-1, keepdims=True)
        )
        write_pair(work_ref, mask, (pair_grad + d_pair).astype(jnp.bfloat16))
        grad_t_ref[:, at] = pair_bf.T
    pair_bf = read_pair(work_ref, MASKS[0]).astype(jnp.bfloat16)
    last_ref[...] = pair_bf
    grad_t_ref[:, pl.ds(0, pairs)] = pair_bf.T
    if blocks:
        write_blocks(places, place_ref[1], [(grad_t_ref, hidden_ref)], blocks[0])


def first_section(normed_t_ref, later_ref, first_ref):
    pairs = first_ref.shape[0]
    return [
        (normed_t_ref.at[:, pl.ds(pairs, later_ref.shape[0])], later_ref),
        (normed_t_ref.at[:, pl.ds(0, pairs)], first_ref),
    ]


def last_kernel(places, place_ref, last_ref, slope_ref, down_ref, normed_t_ref, later_ref, d_pre_ref, *blocks):
    pairs = last_ref.shape[0]
    for start in range(0, down_ref.shape[1], CHUNK):
        units = pl.ds(start, CHUNK)
        d_hidden = jnp.dot(last_ref[...], down_ref[:, units], preferred_element_type=jnp.float32)
        slope = slope_ref[pl.ds(0, pairs), units].astype(jnp.float32)
        d_pre_ref[:, units] = (d_hidden * slope).astype(jnp.bfloat16)
    if blocks:
        write_blocks(places, place_ref[1], first_section(normed_t_ref, later_ref, d_pre_ref), blocks[0])


def keep_down_kernel(places, place_ref, grad_t_ref, hidden_ref, out_ref):
    write_blocks(places, 1 - place_ref[1], [(grad_t_ref, hidden_ref)], out_ref)


def keep_up_kernel(places, place_ref, normed_t_ref, later_ref, first_ref, out_ref):
    write_blocks(places, 1 - place_ref[1], first_section(normed_t_ref, later_ref, first_ref), out_ref)


def arrange_kernel(spots, place_ref, block_ref, out_ref):
    rows = out_ref.shape[1]
    for member, spot in enumerate(spots):
        out_ref[spot ^ place_ref[3]] = block_ref[member * rows : (member + 1) * rows]


def settle_kernel(sources, place_ref, kept_ref, taken_ref, out_ref, done):
    half, rows = kept_ref.shape[:2]
    copies = []
    for index, source in enumerate(sources):
        block = kept_ref.at[index] if index < half else taken_ref.at[index - half]
        first = pl.multiple_of((place_ref[0] ^ source) * rows, rows)
        copies.append(pltpu.make_async_copy(block, out_ref.at[pl.ds(first, rows)], done.at[index]))
    for copy in copies:
        copy.start()
    for copy in copies:
        copy.wait()


def spec(space):
    return pl.BlockSpec(memory_space=space)


def block_places(order, span_x, span_y):
    places = []
    for at_x in range(span_x):
        line = []
        for group in range(span_y // 2):
            place = 0
            for axis, step in order:
                at = at_x if axis == "gx" else 2 * group
                place = 2 * place + (at >> step & 1)
            line.append(place)
        places.append(line)
    return places


def in_vmem(*items):
    return [pltpu.with_memory_space_constraint(item, pltpu.VMEM) for item in items]


def forward(place, state, w_up, w_down, spots):
    members, rows, width = state.shape
    total = len(MASKS) * (members // 2) * rows
    depth, units = w_up.shape
    bf16 = jnp.bfloat16
    outs = [
        pltpu.VMEM(state.shape, bf16),
        pltpu.VMEM((total, units), bf16),
        pltpu.VMEM((total, units), bf16),
        pltpu.VMEM((total, depth), bf16),
        pltpu.VMEM((depth, total), bf16),
        pltpu.VMEM((total, LANES), jnp.float32),
        pltpu.VMEM(w_up.shape, bf16),
        pltpu.VMEM(w_down.shape, bf16),
    ]
    return pl.pallas_call(
        functools.partial(forward_kernel, spots),
        out_shape=outs,
        in_specs=[spec(pltpu.SMEM), spec(pltpu.VMEM)] + [spec(pltpu.HBM)] * 2,
        out_specs=[spec(pltpu.VMEM)] * len(outs),
        scratch_shapes=[pltpu.VMEM(state.shape, bf16), pltpu.SemaphoreType.DMA((2, units // CHUNK))],
        compiler_params=pltpu.CompilerParams(vmem_limit_bytes=SECTIONS_BYTES),
        cost_estimate=pl.CostEstimate(
            flops=10 * total * depth * units, bytes_accessed=16 * total * units, transcendentals=0
        ),
    )(place, state, *[pltpu.with_memory_space_constraint(item, pltpu.HBM) for item in (w_up, w_down)])


def call(kernel, outs, flops, place, *args, scratch=()):
    size = sum(2 * math.prod(item.shape) for item in list(args) + list(outs))
    return pl.pallas_call(
        kernel,
        out_shape=list(outs),
        in_specs=[spec(pltpu.SMEM)] + [spec(pltpu.VMEM)] * len(args),
        out_specs=[spec(pltpu.VMEM)] * len(outs),
        scratch_shapes=list(scratch),
        compiler_params=pltpu.CompilerParams(vmem_limit_bytes=SECTIONS_BYTES),
        cost_estimate=pl.CostEstimate(flops=flops, bytes_accessed=size, transcendentals=0),
    )(place, *in_vmem(*args))


def arrange(place, block, spots):
    rows, width = block.shape
    return pl.pallas_call(
        functools.partial(arrange_kernel, spots),
        out_shape=jax.ShapeDtypeStruct((MEMBERS, rows // MEMBERS, width), block.dtype),
        in_specs=[spec(pltpu.SMEM), spec(pltpu.VMEM)],
        out_specs=spec(pltpu.VMEM),
        compiler_params=pltpu.CompilerParams(vmem_limit_bytes=KEEP_BYTES),
        cost_estimate=pl.CostEstimate(flops=0, bytes_accessed=4 * block.size, transcendentals=0),
    )(place, block)


def swap(block, axis, bit):
    pairs = [(source, source ^ (1 << bit)) for source in range(lax.axis_size(axis))]
    return lax.ppermute(block, axis, pairs)


def pick(block, at):
    size = (1,) + block.shape[1:]
    start = (at,) + (0,) * (block.ndim - 1)
    return lax.dynamic_slice(block, start, size, allow_negative_indices=False)[0].astype(jnp.float32)


def finish_sum(halves, kept, taken, order, beside=None):
    for phase, step in enumerate(order):
        mine, other = halves[step]
        shape = (2, kept.shape[0] // 2) + kept.shape[1:]
        kept, taken = kept.reshape(shape), taken.reshape(shape)
        give = (pick(kept, other) + pick(taken, other)).astype(jnp.bfloat16)
        kept = (pick(kept, mine) + pick(taken, mine)).astype(jnp.bfloat16)
        if beside:
            give = beside(phase, give)
        taken = swap(give, *step)
    return (kept.astype(jnp.float32) + taken.astype(jnp.float32))[0]


def scatter_narrow(halves, left, right, order, span_x, span_y):
    total = jnp.dot(left, right, preferred_element_type=jnp.float32).astype(jnp.bfloat16)
    rows, columns = left.shape[0] // span_x, right.shape[1] // span_y
    count_x, count_y = span_x.bit_length() - 1, span_y.bit_length() - 1
    dims = [("gx", bit) for bit in range(count_x)][::-1] + ["rows"]
    dims += [("gy", bit) for bit in range(count_y)][::-1] + ["columns"]
    blocks = total.reshape((2,) * count_x + (rows,) + (2,) * count_y + (columns,))
    blocks = blocks.transpose([dims.index(item) for item in list(order) + ["rows", "columns"]])
    blocks = blocks.reshape(-1, rows, columns)
    return finish_sum(halves, blocks, jnp.zeros_like(blocks), order)


class Journey:
    def __init__(self, blocks, steps):
        self.parts = [blocks[None]]
        self.steps = list(steps)
        self.sources = [0]

    def advance(self, other):
        if not self.steps:
            return other
        axis, bit, weight = self.steps.pop(0)
        held = jnp.concatenate(self.parts, 0)
        half = held.shape[1] // 2
        kept, given = held[:, :half], held[:, half:]
        given, other = lax.optimization_barrier((given, other))
        self.parts = [kept, swap(given, axis, bit)]
        self.sources += [source | weight for source in self.sources]
        return other

    def arrived(self):
        return [part[:, 0] for part in self.parts]


def settle(place, journey):
    kept, taken = journey.arrived()
    half, rows, width = kept.shape
    return pl.pallas_call(
        functools.partial(settle_kernel, journey.sources),
        out_shape=jax.ShapeDtypeStruct((2 * half * rows, width), kept.dtype),
        in_specs=[spec(pltpu.SMEM)] + [spec(pltpu.VMEM)] * 2,
        out_specs=spec(pltpu.HBM),
        scratch_shapes=[pltpu.SemaphoreType.DMA((2 * half,))],
        cost_estimate=pl.CostEstimate(flops=0, bytes_accessed=8 * kept.size, transcendentals=0),
    )(place, kept, taken)


def spots_of(order):
    return [sum((m // MASKS[at] & 1) * mask for at, mask in zip(order, MASKS)) for m in range(MEMBERS)]


def local(signal, w_up, w_down, cotangent):
    span_x = lax.axis_size("gx")
    span_y = lax.axis_size("gy")
    groups = section_groups(span_x, span_y)
    rows, width = signal.shape
    depth, units = w_up.shape
    steps = [("gx", span_x.bit_length() - 2), ("gx", 0), ("gy", span_y.bit_length() - 2), ("gy", 0)]
    bits = [lax.axis_index(axis) // (1 << bit) % 2 for axis, bit in steps]
    member = sum(bit * mask for bit, mask in zip(bits, MASKS))
    rest_y = [("gy", bit) for bit in range(1, span_y.bit_length() - 1)]
    rest_x = [("gx", bit) for bit in range(1, span_x.bit_length() - 1)]
    core, across = ("gy", 0), ("gx", 0)
    order_down = [across] + rest_y + rest_x[::-1]
    order_up = rest_y + [across] + rest_x
    inbound, homeward = [3, 2, 1, 0], [0, 2, 3, 1]
    spot_in, spot_home = [sum(bits[at] * mask for at, mask in zip(o, MASKS)) for o in (inbound, homeward)]
    owns = [lax.axis_index(axis) // (1 << bit) % 2 for axis, bit in [core] + order_up]
    place = jnp.stack([member, 1 - bits[3], spot_home, spot_in]).astype(jnp.int32)
    place, owns, others = lax.optimization_barrier((place, owns, [1 - own for own in owns]))
    halves = {step: (own, other) for step, own, other in zip([core] + order_up, owns, others)}
    places = [block_places(order, span_x, span_y) for order in (order_down, order_up)]
    block = None
    if units // span_y % LANES == 0:
        block = pltpu.VMEM((span_x * span_y // 2, depth // span_x, units // span_y), jnp.bfloat16)

    state = exchange(signal.reshape(MEMBERS, rows // MEMBERS, width), groups)
    coming = Journey(arrange(place, cotangent, spots_of(inbound)), [steps[at] + (MASKS[at],) for at in inbound])
    for _ in range(3):
        place = coming.advance(place)
    state = coming.advance(state)
    state, *kept = forward(place, state, w_up, w_down, spots_of(homeward))
    going = Journey(state, [steps[at] + (MASKS[at],) for at in homeward])
    going.advance(place)
    grad = jnp.concatenate(coming.arrived(), 0)
    hidden, slope, normed, normed_t, factor, up, down = kept
    total, pairs, bf16 = hidden.shape[0], hidden.shape[0] // len(MASKS), jnp.bfloat16
    matmul = 2 * depth * units
    blocks = [block] if block else []
    later, grad_t, last, *given_down = call(
        functools.partial(backward_kernel, places[0]),
        [pltpu.VMEM((total - pairs, units), bf16), pltpu.VMEM((depth, total), bf16), pltpu.VMEM((pairs, depth), bf16)]
        + blocks,
        3 * matmul * total,
        place, grad, hidden, slope, normed, factor, up, down,
        scratch=[pltpu.VMEM(state.shape, bf16)],
    )
    take_down = swap(given_down[0], *core) if blocks else None
    first, *given_up = call(
        functools.partial(last_kernel, places[1]),
        [pltpu.VMEM((pairs, units), bf16)] + blocks,
        matmul * (total // 2 + pairs),
        place, last, slope, down, normed_t, later,
    )
    if not block:
        while going.steps:
            going.advance(place)
        mixed_out = settle(place, going)
        d_pre = jnp.concatenate([first, later], 0)
        grad_down = scatter_narrow(halves, grad_t, hidden, [core] + order_down, span_x, span_y)
        grad_up = scatter_narrow(halves, normed_t, d_pre, [core] + order_up, span_x, span_y)
        return (mixed_out, grad_up, grad_down)
    take_up = swap(going.advance(given_up[0]), *core)
    (keep_down,) = call(
        functools.partial(keep_down_kernel, places[0]), blocks, matmul * total // 2, place, grad_t, hidden
    )
    (keep_up,) = call(
        functools.partial(keep_up_kernel, places[1]), blocks, matmul * total // 2, place, normed_t, later, first
    )
    grad_up = finish_sum(halves, keep_up, take_up, order_up)
    beside = lambda phase, give: going.advance(give) if phase in (1, 2) else give
    grad_down = finish_sum(halves, keep_down, take_down, order_down, beside)
    while going.steps:
        going.advance(place)
    return (settle(place, going), grad_up, grad_down)


def solution(mesh):
    return jax.shard_map(
        local,
        mesh=mesh,
        in_specs=(P(("gx", "gy"), None), P(), P(), P(("gx", "gy"), None)),
        out_specs=(P(("gx", "gy"), None), P("gx", "gy"), P("gx", "gy")),
        check_vma=False,
    )
```

```python
import functools
import math

import jax
import jax.numpy as jnp
from jax import lax
from jax.experimental import pallas as pl
from jax.experimental.pallas import tpu as pltpu
from jax.sharding import PartitionSpec as P

MEMBERS = 16
MASKS = (8, 4, 2, 1)
LANES = 128
CHUNK = 256
SECTIONS_BYTES = 8 * 1024 * 1024
KEEP_BYTES = 4 * 1024 * 1024


def contract_last(left, right):
    return lax.dot_general(
        left, right, (((1,), (1,)), ((), ())), preferred_element_type=jnp.float32
    )


def low_members(mask):
    return [member for member in range(MEMBERS) if not member & mask]


def join_pair(rows_of, mask):
    low = jnp.concatenate([rows_of(member) for member in low_members(mask)], 0)
    high = jnp.concatenate([rows_of(member | mask) for member in low_members(mask)], 0)
    return jnp.concatenate([low, high], 1).astype(jnp.float32)


def read_pair(ref, mask):
    return join_pair(lambda member: ref[member], mask)


def read_landed(refs, landings, spots, mask):
    return join_pair(
        lambda member: jnp.concatenate(
            [ref[landing[member] ^ spot] for ref, landing, spot in zip(refs, landings, spots)], 0
        ),
        mask,
    )


def write_pair(ref, mask, pair):
    rows, width = ref.shape[1:]
    for place, member in enumerate(low_members(mask)):
        part = pair[place * rows : (place + 1) * rows]
        ref[member] = part[:, :width]
        ref[member | mask] = part[:, width:]


def write_blocks(places, bit, products, out_ref):
    rows, columns = out_ref.shape[1:]
    pieces = []
    for group in range(len(places[0])):
        base = (2 * group + bit) * columns
        for inner in range(0, columns, LANES):
            pieces.append((group, inner, pl.multiple_of(base + inner, LANES)))
    for first in range(0, len(pieces), 2):
        some = pieces[first : first + 2]
        total = 0.0
        for left_ref, right_ref in products:
            right = jnp.concatenate([right_ref[:, pl.ds(start, LANES)] for _, _, start in some], 1)
            total += jnp.dot(left_ref[...], right, preferred_element_type=jnp.float32)
        total = total.astype(jnp.bfloat16)
        for which, (group, inner, _) in enumerate(some):
            for block in range(len(places)):
                out_ref[places[block][group], :, inner : inner + LANES] = total[
                    block * rows : (block + 1) * rows, which * LANES : (which + 1) * LANES
                ]


def load_kernel(place_ref, up_hbm, down_hbm, up_ref, down_ref, arrived):
    copies = [
        pltpu.make_async_copy(up_hbm, up_ref, arrived.at[0]),
        pltpu.make_async_copy(down_hbm, down_ref, arrived.at[1]),
    ]
    for copy in copies:
        copy.start()
    for copy in copies:
        copy.wait()


def forward_kernel(
    landings, place_ref, first_ref, second_ref, up_ref, down_ref,
    out_ref, hidden_ref, slope_ref, normed_ref, normed_t_ref, factor_ref, work_ref
):
    pairs = MEMBERS // 2 * work_ref.shape[1]
    last = len(MASKS) - 1
    for section, mask in enumerate(MASKS):
        at = pl.ds(section * pairs, pairs)
        if section == 0:
            pair = read_landed((first_ref, second_ref), landings, (place_ref[2], place_ref[3]), mask)
        else:
            pair = read_pair(work_ref, mask)
        centre = jnp.mean(pair, axis=-1, keepdims=True)
        shifted = pair - centre
        spread = jnp.mean(shifted * shifted, axis=-1, keepdims=True)
        factor = lax.rsqrt(spread + 1e-05)
        normed = (shifted * factor).astype(jnp.bfloat16)
        normed_ref[at, :] = normed
        factor_ref[at, :] = jnp.broadcast_to(factor, (pairs, LANES))
        for start in range(0, up_ref.shape[1], CHUNK):
            units = pl.ds(start, CHUNK)
            pre = jnp.dot(normed, up_ref[:, units], preferred_element_type=jnp.float32)
            share = 0.5 * (1.0 + lax.erf(pre * (1.0 / math.sqrt(2.0))))
            hidden_ref[at, units] = (pre * share).astype(jnp.bfloat16)
            bell = jnp.exp(-0.5 * pre * pre) * (1.0 / math.sqrt(2.0 * math.pi))
            slope_ref[at, units] = (share + pre * bell).astype(jnp.bfloat16)
        mixed = (pair + contract_last(hidden_ref[at, :], down_ref[...])).astype(jnp.bfloat16)
        write_pair(work_ref if section < last else out_ref, mask, mixed)
        normed_t_ref[:, at] = normed.T


def backward_kernel(
    places, place_ref, grad_ref, hidden_ref, slope_ref, normed_ref, factor_ref, up_ref, down_ref,
    d_pre_ref, grad_t_ref, last_ref, *rest
):
    blocks, work_ref = rest[:-1], rest[-1]
    pairs = MEMBERS // 2 * work_ref.shape[1]
    for section in range(len(MASKS) - 1, 0, -1):
        mask = MASKS[section]
        at = pl.ds(section * pairs, pairs)
        later = pl.ds((section - 1) * pairs, pairs)
        if section == len(MASKS) - 1:
            pair_grad = read_landed((grad_ref,), (range(MEMBERS),), (place_ref[0],), mask)
        else:
            pair_grad = read_pair(work_ref, mask)
        pair_bf = pair_grad.astype(jnp.bfloat16)
        for start in range(0, up_ref.shape[1], CHUNK):
            units = pl.ds(start, CHUNK)
            d_hidden = jnp.dot(pair_bf, down_ref[:, units], preferred_element_type=jnp.float32)
            d_pre_ref[later, units] = (d_hidden * slope_ref[at, units].astype(jnp.float32)).astype(jnp.bfloat16)
        d_norm = contract_last(d_pre_ref[later, :], up_ref[...])
        normed = normed_ref[at, :].astype(jnp.float32)
        d_pair = factor_ref[at, :][:, :1] * (
            d_norm
            - jnp.mean(d_norm, axis=-1, keepdims=True)
            - normed * jnp.mean(d_norm * normed, axis=-1, keepdims=True)
        )
        write_pair(work_ref, mask, (pair_grad + d_pair).astype(jnp.bfloat16))
        grad_t_ref[:, at] = pair_bf.T
    pair_bf = read_pair(work_ref, MASKS[0]).astype(jnp.bfloat16)
    last_ref[...] = pair_bf
    grad_t_ref[:, pl.ds(0, pairs)] = pair_bf.T
    if blocks:
        write_blocks(places, place_ref[1], [(grad_t_ref, hidden_ref)], blocks[0])


def first_section(normed_t_ref, later_ref, first_ref):
    pairs = first_ref.shape[0]
    return [
        (normed_t_ref.at[:, pl.ds(pairs, later_ref.shape[0])], later_ref),
        (normed_t_ref.at[:, pl.ds(0, pairs)], first_ref),
    ]


def last_kernel(places, place_ref, last_ref, slope_ref, down_ref, normed_t_ref, later_ref, d_pre_ref, *blocks):
    pairs = last_ref.shape[0]
    for start in range(0, down_ref.shape[1], CHUNK):
        units = pl.ds(start, CHUNK)
        d_hidden = jnp.dot(last_ref[...], down_ref[:, units], preferred_element_type=jnp.float32)
        slope = slope_ref[pl.ds(0, pairs), units].astype(jnp.float32)
        d_pre_ref[:, units] = (d_hidden * slope).astype(jnp.bfloat16)
    if blocks:
        write_blocks(places, place_ref[1], first_section(normed_t_ref, later_ref, d_pre_ref), blocks[0])


def keep_down_kernel(places, place_ref, grad_t_ref, hidden_ref, out_ref):
    write_blocks(places, 1 - place_ref[1], [(grad_t_ref, hidden_ref)], out_ref)


def keep_up_kernel(places, place_ref, normed_t_ref, later_ref, first_ref, out_ref):
    write_blocks(places, 1 - place_ref[1], first_section(normed_t_ref, later_ref, first_ref), out_ref)


def settle_kernel(sources, place_ref, kept_ref, taken_ref, out_ref, done):
    half, rows = kept_ref.shape[:2]
    copies = []
    for index, source in enumerate(sources):
        block = kept_ref.at[index] if index < half else taken_ref.at[index - half]
        first = pl.multiple_of((place_ref[0] ^ source) * rows, rows)
        copies.append(pltpu.make_async_copy(block, out_ref.at[pl.ds(first, rows)], done.at[index]))
    for copy in copies:
        copy.start()
    for copy in copies:
        copy.wait()


def spec(space):
    return pl.BlockSpec(memory_space=space)


def block_places(order, span_x, span_y):
    places = []
    for at_x in range(span_x):
        line = []
        for group in range(span_y // 2):
            place = 0
            for axis, step in order:
                at = at_x if axis == "gx" else 2 * group
                place = 2 * place + (at >> step & 1)
            line.append(place)
        places.append(line)
    return places


def in_vmem(*items):
    return [pltpu.with_memory_space_constraint(item, pltpu.VMEM) for item in items]


def load(place, *weights):
    return pl.pallas_call(
        load_kernel,
        out_shape=[pltpu.VMEM(item.shape, item.dtype) for item in weights],
        in_specs=[spec(pltpu.SMEM)] + [spec(pltpu.HBM)] * 2,
        out_specs=[spec(pltpu.VMEM)] * 2,
        scratch_shapes=[pltpu.SemaphoreType.DMA((2,))],
        compiler_params=pltpu.CompilerParams(vmem_limit_bytes=KEEP_BYTES),
        cost_estimate=pl.CostEstimate(flops=0, bytes_accessed=8 * weights[0].size, transcendentals=0),
    )(place, *[pltpu.with_memory_space_constraint(item, pltpu.HBM) for item in weights])


def call(kernel, outs, flops, place, *args, scratch=()):
    size = sum(2 * math.prod(item.shape) for item in list(args) + list(outs))
    return pl.pallas_call(
        kernel,
        out_shape=list(outs),
        in_specs=[spec(pltpu.SMEM)] + [spec(pltpu.VMEM)] * len(args),
        out_specs=[spec(pltpu.VMEM)] * len(outs),
        scratch_shapes=list(scratch),
        compiler_params=pltpu.CompilerParams(vmem_limit_bytes=SECTIONS_BYTES),
        cost_estimate=pl.CostEstimate(flops=flops, bytes_accessed=size, transcendentals=0),
    )(place, *in_vmem(*args))


def swap(block, axis, bit):
    pairs = [(source, source ^ (1 << bit)) for source in range(lax.axis_size(axis))]
    return lax.ppermute(block, axis, pairs)


def pick(block, at):
    return slice_at(block, 0, at).astype(jnp.float32)


def halve(halves, step, kept, taken):
    mine, other = halves[step]
    shape = (2, kept.shape[0] // 2) + kept.shape[1:]
    kept, taken = kept.reshape(shape), taken.reshape(shape)
    give = (pick(kept, other) + pick(taken, other)).astype(jnp.bfloat16)
    keep = (pick(kept, mine) + pick(taken, mine)).astype(jnp.bfloat16)
    return keep, give


def last_sum(kept, taken):
    return (kept.astype(jnp.float32) + taken.astype(jnp.float32))[0]


def finish_sum(halves, kept, taken, order):
    for step in order:
        kept, give = halve(halves, step, kept, taken)
        taken = swap(give, *step)
    return last_sum(kept, taken)


def scatter_narrow(halves, left, right, order, span_x, span_y):
    total = jnp.dot(left, right, preferred_element_type=jnp.float32).astype(jnp.bfloat16)
    rows, columns = left.shape[0] // span_x, right.shape[1] // span_y
    count_x, count_y = span_x.bit_length() - 1, span_y.bit_length() - 1
    dims = [("gx", bit) for bit in range(count_x)][::-1] + ["rows"]
    dims += [("gy", bit) for bit in range(count_y)][::-1] + ["columns"]
    blocks = total.reshape((2,) * count_x + (rows,) + (2,) * count_y + (columns,))
    blocks = blocks.transpose([dims.index(item) for item in list(order) + ["rows", "columns"]])
    blocks = blocks.reshape(-1, rows, columns)
    return finish_sum(halves, blocks, jnp.zeros_like(blocks), order)


class Journey:
    def __init__(self, held, bits=(0, 1, 2, 3), sources=(0,)):
        self.held = held
        self.bits = list(bits)
        self.sources = list(sources)
        self.parts = None

    def split(self):
        half = self.held.shape[-2] // 2
        return [Journey(part, self.bits, self.sources) for part in (self.held[..., :half, :], self.held[..., half:, :])]

    def hop(self, at, steps, halves, after=None):
        dim = self.bits.index(at)
        mine, other = halves[steps[at]]
        kept, given = [slice_at(self.held, dim, part) for part in (mine, other)]
        if after is not None:
            given, after = lax.optimization_barrier((given, after))
        self.parts = [kept, swap(given, *steps[at])]
        self.held = jnp.concatenate(self.parts, -3)
        self.bits.remove(at)
        self.sources += [source | MASKS[at] for source in self.sources]
        return after

    def landing(self):
        return [self.sources.index(member) for member in range(MEMBERS)]


def landing_of(order):
    return [sum(bool(member & MASKS[at]) << k for k, at in enumerate(order)) for member in range(MEMBERS)]


def slice_at(block, dim, at):
    start = [0] * block.ndim
    start[dim] = at
    size = list(block.shape)
    size[dim] = 1
    part = lax.dynamic_slice(block, start, size, allow_negative_indices=False)
    return lax.squeeze(part, (dim,))


def settle(place, journey):
    kept, taken = journey.parts
    half, rows, width = kept.shape
    return pl.pallas_call(
        functools.partial(settle_kernel, journey.sources),
        out_shape=jax.ShapeDtypeStruct((2 * half * rows, width), kept.dtype),
        in_specs=[spec(pltpu.SMEM)] + [spec(pltpu.VMEM)] * 2,
        out_specs=spec(pltpu.HBM),
        scratch_shapes=[pltpu.SemaphoreType.DMA((2 * half,))],
        cost_estimate=pl.CostEstimate(flops=0, bytes_accessed=8 * kept.size, transcendentals=0),
    )(place, kept, taken)


def local(signal, w_up, w_down, cotangent):
    span_x = lax.axis_size("gx")
    span_y = lax.axis_size("gy")
    rows, width = signal.shape
    depth, units = w_up.shape
    steps = [("gx", span_x.bit_length() - 2), ("gx", 0), ("gy", span_y.bit_length() - 2), ("gy", 0)]
    z, y, x, core = range(4)
    rest_y = [("gy", bit) for bit in range(1, span_y.bit_length() - 1)]
    rest_x = [("gx", bit) for bit in range(1, span_x.bit_length() - 1)]
    order_down = [steps[y]] + rest_y + rest_x[::-1]
    order_up = rest_y + [steps[y]] + rest_x
    orders = ((z, x, y, core), (z, y, x, core))
    landings = [landing_of(order) for order in orders]

    owns = [lax.axis_index(axis) // (1 << bit) % 2 for axis, bit in [steps[core]] + order_up]
    own = dict(zip([steps[core]] + order_up, owns))
    member = sum(own[step] * mask for step, mask in zip(steps, MASKS))
    spots = [sum(own[steps[at]] << k for k, at in enumerate(order)) for order in orders]
    place = jnp.stack([member, 1 - own[steps[core]]] + spots).astype(jnp.int32)
    place, owns, others = lax.optimization_barrier((place, owns, [1 - item for item in owns]))
    halves = {step: pair for step, pair in zip([steps[core]] + order_up, zip(owns, others))}
    places = [block_places(order, span_x, span_y) for order in (order_down, order_up)]
    block = None
    if units // span_y % LANES == 0:
        block = pltpu.VMEM((span_x * span_y // 2, depth // span_x, units // span_y), jnp.bfloat16)
    blocks = [block] if block else []

    parts = (2, 2, 2, 2, 1, rows // MEMBERS, width)
    whole, coming = Journey(signal.reshape(parts)), Journey(cotangent.reshape(parts))
    whole.hop(z, steps, halves)
    coming.hop(core, steps, halves)
    coming.hop(x, steps, halves)
    coming.hop(y, steps, halves)
    first, second = whole.split()
    first.hop(x, steps, halves)
    second.hop(y, steps, halves)
    first.hop(y, steps, halves)
    second.hop(x, steps, halves)
    first.hop(core, steps, halves)
    second.hop(core, steps, halves)
    first.held = coming.hop(z, steps, halves, first.held)
    up, down = load(place, w_up, w_down)

    total = len(MASKS) * (MEMBERS // 2) * (rows // MEMBERS)
    pairs, bf16 = total // len(MASKS), jnp.bfloat16
    matmul = 2 * depth * units
    state_type = (MEMBERS, rows // MEMBERS, width)
    state, hidden, slope, normed, normed_t, factor = call(
        functools.partial(forward_kernel, landings),
        [
            pltpu.VMEM(state_type, bf16),
            pltpu.VMEM((total, units), bf16),
            pltpu.VMEM((total, units), bf16),
            pltpu.VMEM((total, depth), bf16),
            pltpu.VMEM((depth, total), bf16),
            pltpu.VMEM((total, LANES), jnp.float32),
        ],
        4 * matmul * total,
        place, first.held, second.held, up, down,
        scratch=[pltpu.VMEM(state_type, bf16)],
    )
    going = Journey(state.reshape(parts))
    coming.held = going.hop(z, steps, halves, coming.held)
    later, grad_t, last, *given_down = call(
        functools.partial(backward_kernel, places[0]),
        [pltpu.VMEM((total - pairs, units), bf16), pltpu.VMEM((depth, total), bf16), pltpu.VMEM((pairs, depth), bf16)]
        + blocks,
        3 * matmul * total,
        place, coming.held, hidden, slope, normed, factor, up, down,
        scratch=[pltpu.VMEM(state_type, bf16)],
    )
    take_down = swap(given_down[0], *steps[core]) if blocks else None
    early, *given_up = call(
        functools.partial(last_kernel, places[1]),
        [pltpu.VMEM((pairs, units), bf16)] + blocks,
        matmul * (total // 2 + pairs),
        place, last, slope, down, normed_t, later,
    )
    if not block:
        for at in (x, core, y):
            going.hop(at, steps, halves)
        mixed_out = settle(place, going)
        d_pre = jnp.concatenate([early, later], 0)
        grad_down = scatter_narrow(halves, grad_t, hidden, [steps[core]] + order_down, span_x, span_y)
        grad_up = scatter_narrow(halves, normed_t, d_pre, [steps[core]] + order_up, span_x, span_y)
        return (mixed_out, grad_up, grad_down)
    take_up = swap(going.hop(x, steps, halves, given_up[0]), *steps[core])
    (keep_down,) = call(
        functools.partial(keep_down_kernel, places[0]), blocks, matmul * total // 2, place, grad_t, hidden
    )

    barrier = lax.optimization_barrier
    give_up = None
    for phase, (step_down, step_up) in enumerate(zip(order_down, order_up)):
        if phase > 0:
            keep_down, give_up = barrier((keep_down, give_up))
        keep_down, give_down = halve(halves, step_down, keep_down, take_down)
        if phase == 2:
            give_down = going.hop(y, steps, halves, give_down)
        take_down = swap(give_down, *step_down)
        if phase == 0:
            after, give_down = barrier((place, give_down))
            (keep_up,) = call(
                functools.partial(keep_up_kernel, places[1]), blocks, matmul * total // 2,
                after, normed_t, later, early,
            )
        else:
            keep_up, give_down = barrier((keep_up, give_down))
        keep_up, give_up = halve(halves, step_up, keep_up, take_up)
        if phase == 0:
            give_up = going.hop(core, steps, halves, give_up)
        take_up = swap(give_up, *step_up)
    return (settle(place, going), last_sum(keep_up, take_up), last_sum(keep_down, take_down))


def solution(mesh):
    return jax.shard_map(
        local,
        mesh=mesh,
        in_specs=(P(("gx", "gy"), None), P(), P(), P(("gx", "gy"), None)),
        out_specs=(P(("gx", "gy"), None), P("gx", "gy"), P("gx", "gy")),
        check_vma=False,
    )
```

```python
import functools
import math

import jax
import jax.numpy as jnp
from jax import lax
from jax.experimental import pallas as pl
from jax.experimental.pallas import tpu as pltpu
from jax.sharding import PartitionSpec as P

MEMBERS = 16
MASKS = (8, 4, 2, 1)
LANES = 128
CHUNK = 256
SECTIONS_BYTES = 8 * 1024 * 1024
KEEP_BYTES = 4 * 1024 * 1024


def section_groups(span_x, span_y):
    bits_x = [span_x.bit_length() - 2, 0]
    bits_y = [span_y.bit_length() - 2, 0]
    mask_x = sum(1 << bit for bit in bits_x)
    mask_y = sum(1 << bit for bit in bits_y)
    groups = []
    for base_x in range(span_x):
        for base_y in range(span_y):
            if base_x & mask_x or base_y & mask_y:
                continue
            group = []
            for member in range(MEMBERS):
                at_x, at_y = base_x, base_y
                at_x |= (member >> 3 & 1) << bits_x[0] | (member >> 2 & 1) << bits_x[1]
                at_y |= (member >> 1 & 1) << bits_y[0] | (member & 1) << bits_y[1]
                group.append(at_x * span_y + at_y)
            groups.append(group)
    return groups


def exchange(block, groups):
    return lax.all_to_all(
        block, ("gx", "gy"), split_axis=0, concat_axis=0, axis_index_groups=groups, tiled=True
    )


def contract_last(left, right):
    return lax.dot_general(
        left, right, (((1,), (1,)), ((), ())), preferred_element_type=jnp.float32
    )


def low_members(mask):
    return [member for member in range(MEMBERS) if not member & mask]


def read_pair(ref, mask, swapped=0):
    low = jnp.concatenate([ref[member ^ swapped] for member in low_members(mask)], 0)
    high = jnp.concatenate([ref[(member | mask) ^ swapped] for member in low_members(mask)], 0)
    return jnp.concatenate([low, high], 1).astype(jnp.float32)


def write_pair(ref, mask, pair):
    rows, width = ref.shape[1:]
    for place, member in enumerate(low_members(mask)):
        part = pair[place * rows : (place + 1) * rows]
        ref[member] = part[:, :width]
        ref[member | mask] = part[:, width:]


def write_blocks(places, bit, left_ref, right_ref, out_ref):
    rows, columns = out_ref.shape[1:]
    pieces = []
    for group in range(len(places[0])):
        base = (2 * group + bit) * columns
        for inner in range(0, columns, LANES):
            pieces.append((group, inner, pl.multiple_of(base + inner, LANES)))
    for first in range(0, len(pieces), 2):
        some = pieces[first : first + 2]
        right = jnp.concatenate([right_ref[:, pl.ds(start, LANES)] for _, _, start in some], 1)
        total = jnp.dot(left_ref[...], right, preferred_element_type=jnp.float32)
        total = total.astype(jnp.bfloat16)
        for which, (group, inner, _) in enumerate(some):
            for block in range(len(places)):
                out_ref[places[block][group], :, inner : inner + LANES] = total[
                    block * rows : (block + 1) * rows, which * LANES : (which + 1) * LANES
                ]


def load_kernel(place_ref, source, target, arrived):
    copy = pltpu.make_async_copy(source, target, arrived)
    copy.start()
    copy.wait()


def forward_kernel(
    state_ref, up_ref, down_hbm,
    out_ref, hidden_ref, slope_ref, normed_ref, normed_t_ref, factor_ref, down_ref, work_ref, arrived
):
    fetch_down = pltpu.make_async_copy(down_hbm, down_ref, arrived)
    fetch_down.start()
    pairs = MEMBERS // 2 * work_ref.shape[1]
    hidden_units = up_ref.shape[1]
    last = len(MASKS) - 1
    for section, mask in enumerate(MASKS):
        at = pl.ds(section * pairs, pairs)
        pair = read_pair(state_ref if section == 0 else work_ref, mask)
        centre = jnp.mean(pair, axis=-1, keepdims=True)
        shifted = pair - centre
        spread = jnp.mean(shifted * shifted, axis=-1, keepdims=True)
        factor = lax.rsqrt(spread + 1e-05)
        normed = (shifted * factor).astype(jnp.bfloat16)
        normed_ref[at, :] = normed
        factor_ref[at, :] = jnp.broadcast_to(factor, (pairs, LANES))
        for start in range(0, hidden_units, CHUNK):
            units = pl.ds(start, CHUNK)
            pre = jnp.dot(normed, up_ref[:, units], preferred_element_type=jnp.float32)
            share = 0.5 * (1.0 + lax.erf(pre * (1.0 / math.sqrt(2.0))))
            hidden_ref[at, units] = (pre * share).astype(jnp.bfloat16)
            bell = jnp.exp(-0.5 * pre * pre) * (1.0 / math.sqrt(2.0 * math.pi))
            slope_ref[at, units] = (share + pre * bell).astype(jnp.bfloat16)
        if section == 0:
            fetch_down.wait()
        mixed = (pair + contract_last(hidden_ref[at, :], down_ref[...])).astype(jnp.bfloat16)
        write_pair(work_ref if section < last else out_ref, mask, mixed)
        normed_t_ref[:, at] = normed.T


def backward_kernel(
    places_down, places_up, place_ref, grad_ref, hidden_ref, slope_ref, normed_ref, normed_t_ref, factor_ref,
    up_ref, down_ref, d_pre_ref, grad_t_ref, *rest
):
    blocks, work_ref = rest[:-1], rest[-1]
    pairs = MEMBERS // 2 * work_ref.shape[1]
    hidden_units = up_ref.shape[1]
    last = len(MASKS) - 1
    for section in range(last, -1, -1):
        mask = MASKS[section]
        at = pl.ds(section * pairs, pairs)
        if section == last:
            pair_grad = read_pair(grad_ref, mask, swapped=place_ref[0])
        else:
            pair_grad = read_pair(work_ref, mask)
        pair_bf = pair_grad.astype(jnp.bfloat16)
        for start in range(0, hidden_units, CHUNK):
            units = pl.ds(start, CHUNK)
            d_hidden = jnp.dot(pair_bf, down_ref[:, units], preferred_element_type=jnp.float32)
            d_pre_ref[at, units] = (d_hidden * slope_ref[at, units].astype(jnp.float32)).astype(jnp.bfloat16)
        if section > 0:
            d_norm = contract_last(d_pre_ref[at, :], up_ref[...])
            normed = normed_ref[at, :].astype(jnp.float32)
            d_pair = factor_ref[at, :][:, :1] * (
                d_norm
                - jnp.mean(d_norm, axis=-1, keepdims=True)
                - normed * jnp.mean(d_norm * normed, axis=-1, keepdims=True)
            )
            write_pair(work_ref, mask, (pair_grad + d_pair).astype(jnp.bfloat16))
        grad_t_ref[:, at] = pair_bf.T

    if blocks:
        write_blocks(places_down, place_ref[1], grad_t_ref, hidden_ref, blocks[0])
        write_blocks(places_up, place_ref[1], normed_t_ref, d_pre_ref, blocks[1])


def keep_kernel(
    places_down, places_up, place_ref, hidden_ref, d_pre_ref, normed_t_ref, grad_t_ref, down_ref, up_ref
):
    write_blocks(places_down, 1 - place_ref[1], grad_t_ref, hidden_ref, down_ref)
    write_blocks(places_up, 1 - place_ref[1], normed_t_ref, d_pre_ref, up_ref)


def settle_kernel(sources, place_ref, *refs):
    parts, out_ref, done = refs[:-2], refs[-2], refs[-1]
    count, rows = parts[0].shape[:2]
    copies = []
    for index, source in enumerate(sources):
        block = parts[index // count].at[index % count]
        first = pl.multiple_of((place_ref[0] ^ source) * rows, rows)
        copies.append(pltpu.make_async_copy(block, out_ref.at[pl.ds(first, rows)], done.at[index]))
    for copy in copies:
        copy.start()
    for copy in copies:
        copy.wait()


def spec(space):
    return pl.BlockSpec(memory_space=space)


def block_places(order, span_x, span_y):
    places = []
    for at_x in range(span_x):
        line = []
        for group in range(span_y // 2):
            place = 0
            for axis, step in order:
                at = at_x if axis == "gx" else 2 * group
                place = 2 * place + (at >> step & 1)
            line.append(place)
        places.append(line)
    return places


def in_vmem(*items):
    return [pltpu.with_memory_space_constraint(item, pltpu.VMEM) for item in items]


def load(place, weight):
    return pl.pallas_call(
        load_kernel,
        out_shape=pltpu.VMEM(weight.shape, weight.dtype),
        in_specs=[spec(pltpu.SMEM), spec(pltpu.HBM)],
        out_specs=spec(pltpu.VMEM),
        scratch_shapes=[pltpu.SemaphoreType.DMA],
        compiler_params=pltpu.CompilerParams(vmem_limit_bytes=KEEP_BYTES),
        cost_estimate=pl.CostEstimate(flops=0, bytes_accessed=4 * weight.size, transcendentals=0),
    )(place, pltpu.with_memory_space_constraint(weight, pltpu.HBM))


def forward(state, up, w_down):
    members, rows, width = state.shape
    total = len(MASKS) * (members // 2) * rows
    depth, units = up.shape
    bf16 = jnp.bfloat16
    outs = [
        pltpu.VMEM(state.shape, bf16),
        pltpu.VMEM((total, units), bf16),
        pltpu.VMEM((total, units), bf16),
        pltpu.VMEM((total, depth), bf16),
        pltpu.VMEM((depth, total), bf16),
        pltpu.VMEM((total, LANES), jnp.float32),
        pltpu.VMEM(w_down.shape, bf16),
    ]
    return pl.pallas_call(
        forward_kernel,
        out_shape=outs,
        in_specs=[spec(pltpu.VMEM)] * 2 + [spec(pltpu.HBM)],
        out_specs=[spec(pltpu.VMEM)] * len(outs),
        scratch_shapes=[pltpu.VMEM(state.shape, bf16), pltpu.SemaphoreType.DMA],
        compiler_params=pltpu.CompilerParams(vmem_limit_bytes=SECTIONS_BYTES),
        cost_estimate=pl.CostEstimate(
            flops=10 * total * depth * units, bytes_accessed=16 * total * units, transcendentals=0
        ),
    )(state, *in_vmem(up), pltpu.with_memory_space_constraint(w_down, pltpu.HBM))


def backward(place, grad, kept, places, block):
    total, units = kept[0].shape
    depth = kept[2].shape[1]
    bf16 = jnp.bfloat16
    outs = [pltpu.VMEM((total, units), bf16), pltpu.VMEM((depth, total), bf16)]
    outs += [block] * 2 if block else []
    return pl.pallas_call(
        functools.partial(backward_kernel, *places),
        out_shape=outs,
        in_specs=[spec(pltpu.SMEM)] + [spec(pltpu.VMEM)] * (1 + len(kept)),
        out_specs=[spec(pltpu.VMEM)] * len(outs),
        scratch_shapes=[pltpu.VMEM(grad.shape, bf16)],
        compiler_params=pltpu.CompilerParams(vmem_limit_bytes=SECTIONS_BYTES),
        cost_estimate=pl.CostEstimate(
            flops=10 * total * depth * units, bytes_accessed=16 * total * units, transcendentals=0
        ),
    )(place, grad, *in_vmem(*kept))


def keep_blocks(place, hidden, d_pre, normed_t, grad_t, places, block):
    total, units = hidden.shape
    depth = normed_t.shape[0]
    return pl.pallas_call(
        functools.partial(keep_kernel, *places),
        out_shape=[block] * 2,
        in_specs=[spec(pltpu.SMEM)] + [spec(pltpu.VMEM)] * 4,
        out_specs=[spec(pltpu.VMEM)] * 2,
        compiler_params=pltpu.CompilerParams(vmem_limit_bytes=KEEP_BYTES),
        cost_estimate=pl.CostEstimate(
            flops=2 * total * depth * units, bytes_accessed=8 * total * units, transcendentals=0
        ),
    )(place, *in_vmem(hidden, d_pre, normed_t, grad_t))


def swap(block, axis, bit):
    pairs = [(source, source ^ (1 << bit)) for source in range(lax.axis_size(axis))]
    return lax.ppermute(block, axis, pairs)


def pick(block, at):
    return slice_at(block, 0, at).astype(jnp.float32)


def finish_sum(halves, kept, taken, order, beside=None):
    for phase, step in enumerate(order):
        mine, other = halves[step]
        shape = (2, kept.shape[0] // 2) + kept.shape[1:]
        kept, taken = kept.reshape(shape), taken.reshape(shape)
        give = (pick(kept, other) + pick(taken, other)).astype(jnp.bfloat16)
        kept = (pick(kept, mine) + pick(taken, mine)).astype(jnp.bfloat16)
        if beside:
            give = beside(phase, give)
        taken = swap(give, *step)
    return (kept.astype(jnp.float32) + taken.astype(jnp.float32))[0]


def scatter_narrow(halves, left, right, order, span_x, span_y):
    total = jnp.dot(left, right, preferred_element_type=jnp.float32).astype(jnp.bfloat16)
    rows, columns = left.shape[0] // span_x, right.shape[1] // span_y
    count_x, count_y = span_x.bit_length() - 1, span_y.bit_length() - 1
    dims = [("gx", bit) for bit in range(count_x)][::-1] + ["rows"]
    dims += [("gy", bit) for bit in range(count_y)][::-1] + ["columns"]
    blocks = total.reshape((2,) * count_x + (rows,) + (2,) * count_y + (columns,))
    blocks = blocks.transpose([dims.index(item) for item in list(order) + ["rows", "columns"]])
    blocks = blocks.reshape(-1, rows, columns)
    return finish_sum(halves, blocks, jnp.zeros_like(blocks), order)


class Journey:
    def __init__(self, held, bits=(0, 1, 2, 3), sources=(0,)):
        self.held = held
        self.bits = list(bits)
        self.sources = list(sources)
        self.parts = None

    def hop(self, at, steps, halves, after=None):
        dim = self.bits.index(at)
        mine, other = halves[steps[at]]
        kept, given = [slice_at(self.held, dim, part) for part in (mine, other)]
        if after is not None:
            given, after = lax.optimization_barrier((given, after))
        self.parts = [kept, swap(given, *steps[at])]
        self.held = jnp.concatenate(self.parts, -3)
        self.bits.remove(at)
        self.sources += [source | MASKS[at] for source in self.sources]
        return after

    def hop_both(self, at, also, steps, halves, after=None):
        dims = self.bits.index(at), self.bits.index(also)
        parts = []
        for theirs, beyond in ((0, 0), (1, 0), (0, 1), (1, 1)):
            part = slice_at(self.held, dims[0], halves[steps[at]][theirs], keep=True)
            part = slice_at(part, dims[1], halves[steps[also]][beyond], keep=True)
            parts.append(lax.squeeze(part, dims))
        if after is not None:
            parts, after = lax.optimization_barrier((parts, after))
        self.parts = [
            parts[0],
            swap(parts[1], *steps[at]),
            swap(parts[2], *steps[also]),
            swap_both(parts[3], steps[at], steps[also]),
        ]
        self.held = jnp.concatenate(self.parts, -3)
        for bit in (at, also):
            self.bits.remove(bit)
            self.sources += [source | MASKS[bit] for source in self.sources]
        return after


def slice_at(block, dim, at, keep=False):
    start = [0] * block.ndim
    start[dim] = at
    size = list(block.shape)
    size[dim] = 1
    part = lax.dynamic_slice(block, start, size, allow_negative_indices=False)
    return part if keep else lax.squeeze(part, (dim,))


def swap_both(block, step, also):
    span_x, span_y = lax.axis_size("gx"), lax.axis_size("gy")
    flips = {step[0]: 1 << step[1], also[0]: 1 << also[1]}
    pairs = []
    for at_x in range(span_x):
        for at_y in range(span_y):
            pairs.append((at_x * span_y + at_y, (at_x ^ flips["gx"]) * span_y + (at_y ^ flips["gy"])))
    return lax.ppermute(block, ("gx", "gy"), pairs)


def settle(place, journey):
    parts = journey.parts
    rows, width = parts[0].shape[-2:]
    return pl.pallas_call(
        functools.partial(settle_kernel, journey.sources),
        out_shape=jax.ShapeDtypeStruct((MEMBERS * rows, width), parts[0].dtype),
        in_specs=[spec(pltpu.SMEM)] + [spec(pltpu.VMEM)] * len(parts),
        out_specs=spec(pltpu.HBM),
        scratch_shapes=[pltpu.SemaphoreType.DMA((MEMBERS,))],
        cost_estimate=pl.CostEstimate(flops=0, bytes_accessed=4 * MEMBERS * rows * width, transcendentals=0),
    )(place, *parts)


def local(signal, w_up, w_down, cotangent):
    span_x = lax.axis_size("gx")
    span_y = lax.axis_size("gy")
    groups = section_groups(span_x, span_y)
    rows, width = signal.shape
    depth, units = w_up.shape
    steps = [("gx", span_x.bit_length() - 2), ("gx", 0), ("gy", span_y.bit_length() - 2), ("gy", 0)]
    z, y, x, core = range(4)
    rest_y = [("gy", bit) for bit in range(1, span_y.bit_length() - 1)]
    rest_x = [("gx", bit) for bit in range(1, span_x.bit_length() - 1)]
    order_down = [steps[y]] + rest_y + rest_x[::-1]
    order_up = rest_y + [steps[y]] + rest_x

    owns = [lax.axis_index(axis) // (1 << bit) % 2 for axis, bit in [steps[core]] + order_up]
    own = dict(zip([steps[core]] + order_up, owns))
    member = sum(own[step] * mask for step, mask in zip(steps, MASKS))
    place = jnp.stack([member, 1 - own[steps[core]]]).astype(jnp.int32)
    place, owns, others = lax.optimization_barrier((place, owns, [1 - item for item in owns]))
    halves = {step: pair for step, pair in zip([steps[core]] + order_up, zip(owns, others))}
    places = [block_places(order, span_x, span_y) for order in (order_down, order_up)]
    block = None
    if units // span_y % LANES == 0:
        block = pltpu.VMEM((span_x * span_y // 2, depth // span_x, units // span_y), jnp.bfloat16)

    parts = (2, 2, 2, 2, 1, rows // MEMBERS, width)
    state = exchange(signal.reshape(MEMBERS, rows // MEMBERS, width), groups)
    coming = Journey(cotangent.reshape(parts))
    coming.hop(core, steps, halves)
    coming.hop_both(x, y, steps, halves)
    up = load(place, w_up)
    state = coming.hop(z, steps, halves, state)
    state, *kept, down = forward(state, up, w_down)
    kept += [up, down]
    going = Journey(state.reshape(parts))
    grad = going.hop(z, steps, halves, coming.held)
    d_pre, grad_t, *given = backward(place, grad, kept, places, block)
    hidden, normed_t = kept[0], kept[3]
    if not given:
        going.hop(core, steps, halves)
        going.hop_both(x, y, steps, halves)
        mixed_out = settle(place, going)
        grad_down = scatter_narrow(halves, grad_t, hidden, [steps[core]] + order_down, span_x, span_y)
        grad_up = scatter_narrow(halves, normed_t, d_pre, [steps[core]] + order_up, span_x, span_y)
        return (mixed_out, grad_up, grad_down)
    take_down, take_up = [swap(part, *steps[core]) for part in given]
    keep_down, keep_up = keep_blocks(place, hidden, d_pre, normed_t, grad_t, places, block)

    def beside(phase, give):
        if phase == 0:
            return going.hop(core, steps, halves, give)
        if phase == 2:
            return going.hop_both(x, y, steps, halves, give)
        if phase == len(order_down) - 1:
            going.parts, give = lax.optimization_barrier((going.parts, give))
        return give

    grad_up = finish_sum(halves, keep_up, take_up, order_up)
    grad_down = finish_sum(halves, keep_down, take_down, order_down, beside)
    return (settle(place, going), grad_up, grad_down)


def solution(mesh):
    return jax.shard_map(
        local,
        mesh=mesh,
        in_specs=(P(("gx", "gy"), None), P(), P(), P(("gx", "gy"), None)),
        out_specs=(P(("gx", "gy"), None), P("gx", "gy"), P("gx", "gy")),
        check_vma=False,
    )
```

```python
import functools
import math

import jax
import jax.numpy as jnp
from jax import lax
from jax.experimental import pallas as pl
from jax.experimental.pallas import tpu as pltpu
from jax.sharding import PartitionSpec as P

MEMBERS = 16
MASKS = (8, 4, 2, 1)
LANES = 128
CHUNK = 256
SECTIONS_BYTES = 8 * 1024 * 1024
KEEP_BYTES = 4 * 1024 * 1024


def section_groups(span_x, span_y):
    bits_x = [span_x.bit_length() - 2, 0]
    bits_y = [span_y.bit_length() - 2, 0]
    mask_x = sum(1 << bit for bit in bits_x)
    mask_y = sum(1 << bit for bit in bits_y)
    groups = []
    for base_x in range(span_x):
        for base_y in range(span_y):
            if base_x & mask_x or base_y & mask_y:
                continue
            group = []
            for member in range(MEMBERS):
                at_x, at_y = base_x, base_y
                at_x |= (member >> 3 & 1) << bits_x[0] | (member >> 2 & 1) << bits_x[1]
                at_y |= (member >> 1 & 1) << bits_y[0] | (member & 1) << bits_y[1]
                group.append(at_x * span_y + at_y)
            groups.append(group)
    return groups


def exchange(block, groups):
    return lax.all_to_all(
        block, ("gx", "gy"), split_axis=0, concat_axis=0, axis_index_groups=groups, tiled=True
    )


def contract_last(left, right):
    return lax.dot_general(
        left, right, (((1,), (1,)), ((), ())), preferred_element_type=jnp.float32
    )


def low_members(mask):
    return [member for member in range(MEMBERS) if not member & mask]


def read_pair(ref, mask, swapped=0):
    low = jnp.concatenate([ref[member ^ swapped] for member in low_members(mask)], 0)
    high = jnp.concatenate([ref[(member | mask) ^ swapped] for member in low_members(mask)], 0)
    return jnp.concatenate([low, high], 1).astype(jnp.float32)


def write_pair(ref, mask, pair):
    rows, width = ref.shape[1:]
    for place, member in enumerate(low_members(mask)):
        part = pair[place * rows : (place + 1) * rows]
        ref[member] = part[:, :width]
        ref[member | mask] = part[:, width:]


def write_blocks(places, bit, left_ref, right_ref, out_ref):
    rows, columns = out_ref.shape[1:]
    pieces = []
    for group in range(len(places[0])):
        base = (2 * group + bit) * columns
        for inner in range(0, columns, LANES):
            pieces.append((group, inner, pl.multiple_of(base + inner, LANES)))
    for first in range(0, len(pieces), 2):
        some = pieces[first : first + 2]
        right = jnp.concatenate([right_ref[:, pl.ds(start, LANES)] for _, _, start in some], 1)
        total = jnp.dot(left_ref[...], right, preferred_element_type=jnp.float32)
        total = total.astype(jnp.bfloat16)
        for which, (group, inner, _) in enumerate(some):
            for block in range(len(places)):
                out_ref[places[block][group], :, inner : inner + LANES] = total[
                    block * rows : (block + 1) * rows, which * LANES : (which + 1) * LANES
                ]


def load_kernel(place_ref, source, target, arrived):
    copy = pltpu.make_async_copy(source, target, arrived)
    copy.start()
    copy.wait()


def forward_kernel(
    state_ref, up_ref, down_hbm,
    out_ref, hidden_ref, slope_ref, normed_ref, normed_t_ref, factor_ref, down_ref, work_ref, arrived
):
    fetch_down = pltpu.make_async_copy(down_hbm, down_ref, arrived)
    fetch_down.start()
    pairs = MEMBERS // 2 * work_ref.shape[1]
    hidden_units = up_ref.shape[1]
    last = len(MASKS) - 1
    for section, mask in enumerate(MASKS):
        at = pl.ds(section * pairs, pairs)
        pair = read_pair(state_ref if section == 0 else work_ref, mask)
        centre = jnp.mean(pair, axis=-1, keepdims=True)
        shifted = pair - centre
        spread = jnp.mean(shifted * shifted, axis=-1, keepdims=True)
        factor = lax.rsqrt(spread + 1e-05)
        normed = (shifted * factor).astype(jnp.bfloat16)
        normed_ref[at, :] = normed
        factor_ref[at, :] = jnp.broadcast_to(factor, (pairs, LANES))
        for start in range(0, hidden_units, CHUNK):
            units = pl.ds(start, CHUNK)
            pre = jnp.dot(normed, up_ref[:, units], preferred_element_type=jnp.float32)
            share = 0.5 * (1.0 + lax.erf(pre * (1.0 / math.sqrt(2.0))))
            hidden_ref[at, units] = (pre * share).astype(jnp.bfloat16)
            bell = jnp.exp(-0.5 * pre * pre) * (1.0 / math.sqrt(2.0 * math.pi))
            slope_ref[at, units] = (share + pre * bell).astype(jnp.bfloat16)
        if section == 0:
            fetch_down.wait()
        mixed = (pair + contract_last(hidden_ref[at, :], down_ref[...])).astype(jnp.bfloat16)
        write_pair(work_ref if section < last else out_ref, mask, mixed)
        normed_t_ref[:, at] = normed.T


def backward_kernel(
    places_down, places_up, place_ref, grad_ref, hidden_ref, slope_ref, normed_ref, normed_t_ref, factor_ref,
    up_ref, down_ref, d_pre_ref, grad_t_ref, *rest
):
    blocks, work_ref = rest[:-1], rest[-1]
    pairs = MEMBERS // 2 * work_ref.shape[1]
    hidden_units = up_ref.shape[1]
    last = len(MASKS) - 1
    for section in range(last, -1, -1):
        mask = MASKS[section]
        at = pl.ds(section * pairs, pairs)
        if section == last:
            pair_grad = read_pair(grad_ref, mask, swapped=place_ref[0])
        else:
            pair_grad = read_pair(work_ref, mask)
        pair_bf = pair_grad.astype(jnp.bfloat16)
        for start in range(0, hidden_units, CHUNK):
            units = pl.ds(start, CHUNK)
            d_hidden = jnp.dot(pair_bf, down_ref[:, units], preferred_element_type=jnp.float32)
            d_pre_ref[at, units] = (d_hidden * slope_ref[at, units].astype(jnp.float32)).astype(jnp.bfloat16)
        if section > 0:
            d_norm = contract_last(d_pre_ref[at, :], up_ref[...])
            normed = normed_ref[at, :].astype(jnp.float32)
            d_pair = factor_ref[at, :][:, :1] * (
                d_norm
                - jnp.mean(d_norm, axis=-1, keepdims=True)
                - normed * jnp.mean(d_norm * normed, axis=-1, keepdims=True)
            )
            write_pair(work_ref, mask, (pair_grad + d_pair).astype(jnp.bfloat16))
        grad_t_ref[:, at] = pair_bf.T

    if blocks:
        write_blocks(places_down, place_ref[1], grad_t_ref, hidden_ref, blocks[0])
        write_blocks(places_up, place_ref[1], normed_t_ref, d_pre_ref, blocks[1])


def keep_kernel(
    places_down, places_up, place_ref, hidden_ref, d_pre_ref, normed_t_ref, grad_t_ref, down_ref, up_ref
):
    write_blocks(places_down, 1 - place_ref[1], grad_t_ref, hidden_ref, down_ref)
    write_blocks(places_up, 1 - place_ref[1], normed_t_ref, d_pre_ref, up_ref)


def settle_kernel(sources, place_ref, *refs):
    parts, out_ref, done = refs[:-2], refs[-2], refs[-1]
    count, rows = parts[0].shape[:2]
    copies = []
    for index, source in enumerate(sources):
        block = parts[index // count].at[index % count]
        first = pl.multiple_of((place_ref[0] ^ source) * rows, rows)
        copies.append(pltpu.make_async_copy(block, out_ref.at[pl.ds(first, rows)], done.at[index]))
    for copy in copies:
        copy.start()
    for copy in copies:
        copy.wait()


def spec(space):
    return pl.BlockSpec(memory_space=space)


def block_places(order, span_x, span_y):
    places = []
    for at_x in range(span_x):
        line = []
        for group in range(span_y // 2):
            place = 0
            for axis, step in order:
                at = at_x if axis == "gx" else 2 * group
                place = 2 * place + (at >> step & 1)
            line.append(place)
        places.append(line)
    return places


def in_vmem(*items):
    return [pltpu.with_memory_space_constraint(item, pltpu.VMEM) for item in items]


def load(place, weight):
    return pl.pallas_call(
        load_kernel,
        out_shape=pltpu.VMEM(weight.shape, weight.dtype),
        in_specs=[spec(pltpu.SMEM), spec(pltpu.HBM)],
        out_specs=spec(pltpu.VMEM),
        scratch_shapes=[pltpu.SemaphoreType.DMA],
        compiler_params=pltpu.CompilerParams(vmem_limit_bytes=KEEP_BYTES),
        cost_estimate=pl.CostEstimate(flops=0, bytes_accessed=4 * weight.size, transcendentals=0),
    )(place, pltpu.with_memory_space_constraint(weight, pltpu.HBM))


def forward(state, up, w_down):
    members, rows, width = state.shape
    total = len(MASKS) * (members // 2) * rows
    depth, units = up.shape
    bf16 = jnp.bfloat16
    outs = [
        pltpu.VMEM(state.shape, bf16),
        pltpu.VMEM((total, units), bf16),
        pltpu.VMEM((total, units), bf16),
        pltpu.VMEM((total, depth), bf16),
        pltpu.VMEM((depth, total), bf16),
        pltpu.VMEM((total, LANES), jnp.float32),
        pltpu.VMEM(w_down.shape, bf16),
    ]
    return pl.pallas_call(
        forward_kernel,
        out_shape=outs,
        in_specs=[spec(pltpu.VMEM)] * 2 + [spec(pltpu.HBM)],
        out_specs=[spec(pltpu.VMEM)] * len(outs),
        scratch_shapes=[pltpu.VMEM(state.shape, bf16), pltpu.SemaphoreType.DMA],
        compiler_params=pltpu.CompilerParams(vmem_limit_bytes=SECTIONS_BYTES),
        cost_estimate=pl.CostEstimate(
            flops=10 * total * depth * units, bytes_accessed=16 * total * units, transcendentals=0
        ),
    )(state, *in_vmem(up), pltpu.with_memory_space_constraint(w_down, pltpu.HBM))


def backward(place, grad, kept, places, block):
    total, units = kept[0].shape
    depth = kept[2].shape[1]
    bf16 = jnp.bfloat16
    outs = [pltpu.VMEM((total, units), bf16), pltpu.VMEM((depth, total), bf16)]
    outs += [block] * 2 if block else []
    return pl.pallas_call(
        functools.partial(backward_kernel, *places),
        out_shape=outs,
        in_specs=[spec(pltpu.SMEM)] + [spec(pltpu.VMEM)] * (1 + len(kept)),
        out_specs=[spec(pltpu.VMEM)] * len(outs),
        scratch_shapes=[pltpu.VMEM(grad.shape, bf16)],
        compiler_params=pltpu.CompilerParams(vmem_limit_bytes=SECTIONS_BYTES),
        cost_estimate=pl.CostEstimate(
            flops=10 * total * depth * units, bytes_accessed=16 * total * units, transcendentals=0
        ),
    )(place, grad, *in_vmem(*kept))


def keep_blocks(place, hidden, d_pre, normed_t, grad_t, places, block):
    total, units = hidden.shape
    depth = normed_t.shape[0]
    return pl.pallas_call(
        functools.partial(keep_kernel, *places),
        out_shape=[block] * 2,
        in_specs=[spec(pltpu.SMEM)] + [spec(pltpu.VMEM)] * 4,
        out_specs=[spec(pltpu.VMEM)] * 2,
        compiler_params=pltpu.CompilerParams(vmem_limit_bytes=KEEP_BYTES),
        cost_estimate=pl.CostEstimate(
            flops=2 * total * depth * units, bytes_accessed=8 * total * units, transcendentals=0
        ),
    )(place, *in_vmem(hidden, d_pre, normed_t, grad_t))


def swap(block, axis, bit):
    pairs = [(source, source ^ (1 << bit)) for source in range(lax.axis_size(axis))]
    return lax.ppermute(block, axis, pairs)


def pick(block, at):
    return slice_at(block, 0, at).astype(jnp.float32)


def finish_sum(halves, kept, taken, order, beside=None):
    for phase, step in enumerate(order):
        mine, other = halves[step]
        shape = (2, kept.shape[0] // 2) + kept.shape[1:]
        kept, taken = kept.reshape(shape), taken.reshape(shape)
        give = (pick(kept, other) + pick(taken, other)).astype(jnp.bfloat16)
        kept = (pick(kept, mine) + pick(taken, mine)).astype(jnp.bfloat16)
        if beside:
            give = beside(phase, give)
        taken = swap(give, *step)
    return (kept.astype(jnp.float32) + taken.astype(jnp.float32))[0]


def scatter_narrow(halves, left, right, order, span_x, span_y):
    total = jnp.dot(left, right, preferred_element_type=jnp.float32).astype(jnp.bfloat16)
    rows, columns = left.shape[0] // span_x, right.shape[1] // span_y
    count_x, count_y = span_x.bit_length() - 1, span_y.bit_length() - 1
    dims = [("gx", bit) for bit in range(count_x)][::-1] + ["rows"]
    dims += [("gy", bit) for bit in range(count_y)][::-1] + ["columns"]
    blocks = total.reshape((2,) * count_x + (rows,) + (2,) * count_y + (columns,))
    blocks = blocks.transpose([dims.index(item) for item in list(order) + ["rows", "columns"]])
    blocks = blocks.reshape(-1, rows, columns)
    return finish_sum(halves, blocks, jnp.zeros_like(blocks), order)


class Journey:
    def __init__(self, held, bits=(0, 1, 2, 3), sources=(0,)):
        self.held = held
        self.bits = list(bits)
        self.sources = list(sources)
        self.parts = None

    def hop(self, at, steps, halves, after=None):
        dim = self.bits.index(at)
        mine, other = halves[steps[at]]
        kept, given = [slice_at(self.held, dim, part) for part in (mine, other)]
        if after is not None:
            given, after = lax.optimization_barrier((given, after))
        self.parts = [kept, swap(given, *steps[at])]
        self.held = jnp.concatenate(self.parts, -3)
        self.bits.remove(at)
        self.sources += [source | MASKS[at] for source in self.sources]
        return after

    def hop_both(self, at, also, steps, halves, after=None):
        dims = self.bits.index(at), self.bits.index(also)
        parts = []
        for theirs, beyond in ((0, 0), (1, 0), (0, 1), (1, 1)):
            part = slice_at(self.held, dims[0], halves[steps[at]][theirs], keep=True)
            part = slice_at(part, dims[1], halves[steps[also]][beyond], keep=True)
            parts.append(lax.squeeze(part, dims))
        if after is not None:
            parts, after = lax.optimization_barrier((parts, after))
        self.parts = [
            parts[0],
            swap(parts[1], *steps[at]),
            swap(parts[2], *steps[also]),
            swap_both(parts[3], steps[at], steps[also]),
        ]
        self.held = jnp.concatenate(self.parts, -3)
        for bit in (at, also):
            self.bits.remove(bit)
            self.sources += [source | MASKS[bit] for source in self.sources]
        return after


def slice_at(block, dim, at, keep=False):
    start = [0] * block.ndim
    start[dim] = at
    size = list(block.shape)
    size[dim] = 1
    part = lax.dynamic_slice(block, start, size, allow_negative_indices=False)
    return part if keep else lax.squeeze(part, (dim,))


def swap_both(block, step, also):
    span_x, span_y = lax.axis_size("gx"), lax.axis_size("gy")
    flips = {step[0]: 1 << step[1], also[0]: 1 << also[1]}
    pairs = []
    for at_x in range(span_x):
        for at_y in range(span_y):
            pairs.append((at_x * span_y + at_y, (at_x ^ flips["gx"]) * span_y + (at_y ^ flips["gy"])))
    return lax.ppermute(block, ("gx", "gy"), pairs)


def settle(place, journey):
    parts = journey.parts
    rows, width = parts[0].shape[-2:]
    return pl.pallas_call(
        functools.partial(settle_kernel, journey.sources),
        out_shape=jax.ShapeDtypeStruct((MEMBERS * rows, width), parts[0].dtype),
        in_specs=[spec(pltpu.SMEM)] + [spec(pltpu.VMEM)] * len(parts),
        out_specs=spec(pltpu.HBM),
        scratch_shapes=[pltpu.SemaphoreType.DMA((MEMBERS,))],
        cost_estimate=pl.CostEstimate(flops=0, bytes_accessed=4 * MEMBERS * rows * width, transcendentals=0),
    )(place, *parts)


def local(signal, w_up, w_down, cotangent):
    span_x = lax.axis_size("gx")
    span_y = lax.axis_size("gy")
    groups = section_groups(span_x, span_y)
    rows, width = signal.shape
    depth, units = w_up.shape
    steps = [("gx", span_x.bit_length() - 2), ("gx", 0), ("gy", span_y.bit_length() - 2), ("gy", 0)]
    z, y, x, core = range(4)
    rest_y = [("gy", bit) for bit in range(1, span_y.bit_length() - 1)]
    rest_x = [("gx", bit) for bit in range(1, span_x.bit_length() - 1)]
    order_down = [steps[y]] + rest_y + rest_x[::-1]
    order_up = rest_y + [steps[y]] + rest_x

    owns = [lax.axis_index(axis) // (1 << bit) % 2 for axis, bit in [steps[core]] + order_up]
    own = dict(zip([steps[core]] + order_up, owns))
    member = sum(own[step] * mask for step, mask in zip(steps, MASKS))
    place = jnp.stack([member, 1 - own[steps[core]]]).astype(jnp.int32)
    place, owns, others = lax.optimization_barrier((place, owns, [1 - item for item in owns]))
    halves = {step: pair for step, pair in zip([steps[core]] + order_up, zip(owns, others))}
    places = [block_places(order, span_x, span_y) for order in (order_down, order_up)]
    block = None
    if units // span_y % LANES == 0:
        block = pltpu.VMEM((span_x * span_y // 2, depth // span_x, units // span_y), jnp.bfloat16)

    parts = (2, 2, 2, 2, 1, rows // MEMBERS, width)
    state = exchange(signal.reshape(MEMBERS, rows // MEMBERS, width), groups)
    coming = Journey(cotangent.reshape(parts))
    coming.hop(core, steps, halves)
    coming.hop_both(x, y, steps, halves)
    up = load(place, w_up)
    state = coming.hop(z, steps, halves, state)
    state, *kept, down = forward(state, up, w_down)
    kept += [up, down]
    going = Journey(state.reshape(parts))
    grad = going.hop(z, steps, halves, coming.held)
    d_pre, grad_t, *given = backward(place, grad, kept, places, block)
    hidden, normed_t = kept[0], kept[3]
    if not given:
        going.hop(core, steps, halves)
        going.hop_both(x, y, steps, halves)
        mixed_out = settle(place, going)
        grad_down = scatter_narrow(halves, grad_t, hidden, [steps[core]] + order_down, span_x, span_y)
        grad_up = scatter_narrow(halves, normed_t, d_pre, [steps[core]] + order_up, span_x, span_y)
        return (mixed_out, grad_up, grad_down)
    take_down, take_up = [swap(part, *steps[core]) for part in given]
    keep_down, keep_up = keep_blocks(place, hidden, d_pre, normed_t, grad_t, places, block)

    def beside(phase, give):
        if phase == 1:
            return going.hop(core, steps, halves, give)
        if phase == 2:
            return going.hop_both(x, y, steps, halves, give)
        if phase == len(order_down) - 1:
            going.parts, give = lax.optimization_barrier((going.parts, give))
        return give

    grad_up = finish_sum(halves, keep_up, take_up, order_up)
    grad_down = finish_sum(halves, keep_down, take_down, order_down, beside)
    return (settle(place, going), grad_up, grad_down)


def solution(mesh):
    return jax.shard_map(
        local,
        mesh=mesh,
        in_specs=(P(("gx", "gy"), None), P(), P(), P(("gx", "gy"), None)),
        out_specs=(P(("gx", "gy"), None), P("gx", "gy"), P("gx", "gy")),
        check_vma=False,
    )
```

```python
import functools
import math

import jax
import jax.numpy as jnp
from jax import lax
from jax.experimental import pallas as pl
from jax.experimental.pallas import tpu as pltpu
from jax.sharding import PartitionSpec as P

MEMBERS = 16
MASKS = (8, 4, 2, 1)
LANES = 128
CHUNK = 256
SECTIONS_BYTES = 8 * 1024 * 1024
KEEP_BYTES = 4 * 1024 * 1024


def section_groups(span_x, span_y):
    bits_x = [span_x.bit_length() - 2, 0]
    bits_y = [span_y.bit_length() - 2, 0]
    mask_x = sum(1 << bit for bit in bits_x)
    mask_y = sum(1 << bit for bit in bits_y)
    groups = []
    for base_x in range(span_x):
        for base_y in range(span_y):
            if base_x & mask_x or base_y & mask_y:
                continue
            group = []
            for member in range(MEMBERS):
                at_x, at_y = base_x, base_y
                at_x |= (member >> 3 & 1) << bits_x[0] | (member >> 2 & 1) << bits_x[1]
                at_y |= (member >> 1 & 1) << bits_y[0] | (member & 1) << bits_y[1]
                group.append(at_x * span_y + at_y)
            groups.append(group)
    return groups


def exchange(block, groups):
    return lax.all_to_all(
        block, ("gx", "gy"), split_axis=0, concat_axis=0, axis_index_groups=groups, tiled=True
    )


def contract_last(left, right):
    return lax.dot_general(
        left, right, (((1,), (1,)), ((), ())), preferred_element_type=jnp.float32
    )


def low_members(mask):
    return [member for member in range(MEMBERS) if not member & mask]


def read_pair(ref, mask, swapped=0):
    low = jnp.concatenate([ref[member ^ swapped] for member in low_members(mask)], 0)
    high = jnp.concatenate([ref[(member | mask) ^ swapped] for member in low_members(mask)], 0)
    return jnp.concatenate([low, high], 1).astype(jnp.float32)


def write_pair(ref, mask, pair):
    rows, width = ref.shape[1:]
    for place, member in enumerate(low_members(mask)):
        part = pair[place * rows : (place + 1) * rows]
        ref[member] = part[:, :width]
        ref[member | mask] = part[:, width:]


def write_blocks(places, bit, left_ref, right_ref, out_ref):
    rows, columns = out_ref.shape[1:]
    pieces = []
    for group in range(len(places[0])):
        base = (2 * group + bit) * columns
        for inner in range(0, columns, LANES):
            pieces.append((group, inner, pl.multiple_of(base + inner, LANES)))
    for first in range(0, len(pieces), 2):
        some = pieces[first : first + 2]
        right = jnp.concatenate([right_ref[:, pl.ds(start, LANES)] for _, _, start in some], 1)
        total = jnp.dot(left_ref[...], right, preferred_element_type=jnp.float32)
        total = total.astype(jnp.bfloat16)
        for which, (group, inner, _) in enumerate(some):
            for block in range(len(places)):
                out_ref[places[block][group], :, inner : inner + LANES] = total[
                    block * rows : (block + 1) * rows, which * LANES : (which + 1) * LANES
                ]


def load_kernel(place_ref, source, target, arrived):
    copy = pltpu.make_async_copy(source, target, arrived)
    copy.start()
    copy.wait()


def forward_kernel(
    state_ref, up_ref, down_hbm,
    out_ref, hidden_ref, slope_ref, normed_ref, normed_t_ref, factor_ref, down_ref, work_ref, arrived
):
    fetch_down = pltpu.make_async_copy(down_hbm, down_ref, arrived)
    fetch_down.start()
    pairs = MEMBERS // 2 * work_ref.shape[1]
    hidden_units = up_ref.shape[1]
    last = len(MASKS) - 1
    for section, mask in enumerate(MASKS):
        at = pl.ds(section * pairs, pairs)
        pair = read_pair(state_ref if section == 0 else work_ref, mask)
        centre = jnp.mean(pair, axis=-1, keepdims=True)
        shifted = pair - centre
        spread = jnp.mean(shifted * shifted, axis=-1, keepdims=True)
        factor = lax.rsqrt(spread + 1e-05)
        normed = (shifted * factor).astype(jnp.bfloat16)
        normed_ref[at, :] = normed
        factor_ref[at, :] = jnp.broadcast_to(factor, (pairs, LANES))
        for start in range(0, hidden_units, CHUNK):
            units = pl.ds(start, CHUNK)
            pre = jnp.dot(normed, up_ref[:, units], preferred_element_type=jnp.float32)
            share = 0.5 * (1.0 + lax.erf(pre * (1.0 / math.sqrt(2.0))))
            hidden_ref[at, units] = (pre * share).astype(jnp.bfloat16)
            bell = jnp.exp(-0.5 * pre * pre) * (1.0 / math.sqrt(2.0 * math.pi))
            slope_ref[at, units] = (share + pre * bell).astype(jnp.bfloat16)
        if section == 0:
            fetch_down.wait()
        mixed = (pair + contract_last(hidden_ref[at, :], down_ref[...])).astype(jnp.bfloat16)
        write_pair(work_ref if section < last else out_ref, mask, mixed)
        normed_t_ref[:, at] = normed.T


def backward_kernel(
    places_down, places_up, place_ref, grad_ref, hidden_ref, slope_ref, normed_ref, normed_t_ref, factor_ref,
    up_ref, down_ref, d_pre_ref, grad_t_ref, *rest
):
    blocks, work_ref = rest[:-1], rest[-1]
    pairs = MEMBERS // 2 * work_ref.shape[1]
    hidden_units = up_ref.shape[1]
    last = len(MASKS) - 1
    for section in range(last, -1, -1):
        mask = MASKS[section]
        at = pl.ds(section * pairs, pairs)
        if section == last:
            pair_grad = read_pair(grad_ref, mask, swapped=place_ref[0])
        else:
            pair_grad = read_pair(work_ref, mask)
        pair_bf = pair_grad.astype(jnp.bfloat16)
        for start in range(0, hidden_units, CHUNK):
            units = pl.ds(start, CHUNK)
            d_hidden = jnp.dot(pair_bf, down_ref[:, units], preferred_element_type=jnp.float32)
            d_pre_ref[at, units] = (d_hidden * slope_ref[at, units].astype(jnp.float32)).astype(jnp.bfloat16)
        if section > 0:
            d_norm = contract_last(d_pre_ref[at, :], up_ref[...])
            normed = normed_ref[at, :].astype(jnp.float32)
            d_pair = factor_ref[at, :][:, :1] * (
                d_norm
                - jnp.mean(d_norm, axis=-1, keepdims=True)
                - normed * jnp.mean(d_norm * normed, axis=-1, keepdims=True)
            )
            write_pair(work_ref, mask, (pair_grad + d_pair).astype(jnp.bfloat16))
        grad_t_ref[:, at] = pair_bf.T

    if blocks:
        write_blocks(places_down, place_ref[1], grad_t_ref, hidden_ref, blocks[0])
        write_blocks(places_up, place_ref[1], normed_t_ref, d_pre_ref, blocks[1])


def keep_kernel(
    places_down, places_up, place_ref, hidden_ref, d_pre_ref, normed_t_ref, grad_t_ref, down_ref, up_ref
):
    write_blocks(places_down, 1 - place_ref[1], grad_t_ref, hidden_ref, down_ref)
    write_blocks(places_up, 1 - place_ref[1], normed_t_ref, d_pre_ref, up_ref)


def settle_kernel(sources, place_ref, *refs):
    parts, out_ref, done = refs[:-2], refs[-2], refs[-1]
    count, rows = parts[0].shape[:2]
    copies = []
    for index, source in enumerate(sources):
        block = parts[index // count].at[index % count]
        first = pl.multiple_of((place_ref[0] ^ source) * rows, rows)
        copies.append(pltpu.make_async_copy(block, out_ref.at[pl.ds(first, rows)], done.at[index]))
    for copy in copies:
        copy.start()
    for copy in copies:
        copy.wait()


def spec(space):
    return pl.BlockSpec(memory_space=space)


def block_places(order, span_x, span_y):
    places = []
    for at_x in range(span_x):
        line = []
        for group in range(span_y // 2):
            place = 0
            for axis, step in order:
                at = at_x if axis == "gx" else 2 * group
                place = 2 * place + (at >> step & 1)
            line.append(place)
        places.append(line)
    return places


def in_vmem(*items):
    return [pltpu.with_memory_space_constraint(item, pltpu.VMEM) for item in items]


def load(place, weight):
    return pl.pallas_call(
        load_kernel,
        out_shape=pltpu.VMEM(weight.shape, weight.dtype),
        in_specs=[spec(pltpu.SMEM), spec(pltpu.HBM)],
        out_specs=spec(pltpu.VMEM),
        scratch_shapes=[pltpu.SemaphoreType.DMA],
        compiler_params=pltpu.CompilerParams(vmem_limit_bytes=KEEP_BYTES),
        cost_estimate=pl.CostEstimate(flops=0, bytes_accessed=4 * weight.size, transcendentals=0),
    )(place, pltpu.with_memory_space_constraint(weight, pltpu.HBM))


def forward(state, up, w_down):
    members, rows, width = state.shape
    total = len(MASKS) * (members // 2) * rows
    depth, units = up.shape
    bf16 = jnp.bfloat16
    outs = [
        pltpu.VMEM(state.shape, bf16),
        pltpu.VMEM((total, units), bf16),
        pltpu.VMEM((total, units), bf16),
        pltpu.VMEM((total, depth), bf16),
        pltpu.VMEM((depth, total), bf16),
        pltpu.VMEM((total, LANES), jnp.float32),
        pltpu.VMEM(w_down.shape, bf16),
    ]
    return pl.pallas_call(
        forward_kernel,
        out_shape=outs,
        in_specs=[spec(pltpu.VMEM)] * 2 + [spec(pltpu.HBM)],
        out_specs=[spec(pltpu.VMEM)] * len(outs),
        scratch_shapes=[pltpu.VMEM(state.shape, bf16), pltpu.SemaphoreType.DMA],
        compiler_params=pltpu.CompilerParams(vmem_limit_bytes=SECTIONS_BYTES),
        cost_estimate=pl.CostEstimate(
            flops=10 * total * depth * units, bytes_accessed=16 * total * units, transcendentals=0
        ),
    )(state, *in_vmem(up), pltpu.with_memory_space_constraint(w_down, pltpu.HBM))


def backward(place, grad, kept, places, block):
    total, units = kept[0].shape
    depth = kept[2].shape[1]
    bf16 = jnp.bfloat16
    outs = [pltpu.VMEM((total, units), bf16), pltpu.VMEM((depth, total), bf16)]
    outs += [block] * 2 if block else []
    return pl.pallas_call(
        functools.partial(backward_kernel, *places),
        out_shape=outs,
        in_specs=[spec(pltpu.SMEM)] + [spec(pltpu.VMEM)] * (1 + len(kept)),
        out_specs=[spec(pltpu.VMEM)] * len(outs),
        scratch_shapes=[pltpu.VMEM(grad.shape, bf16)],
        compiler_params=pltpu.CompilerParams(vmem_limit_bytes=SECTIONS_BYTES),
        cost_estimate=pl.CostEstimate(
            flops=10 * total * depth * units, bytes_accessed=16 * total * units, transcendentals=0
        ),
    )(place, grad, *in_vmem(*kept))


def keep_blocks(place, hidden, d_pre, normed_t, grad_t, places, block):
    total, units = hidden.shape
    depth = normed_t.shape[0]
    return pl.pallas_call(
        functools.partial(keep_kernel, *places),
        out_shape=[block] * 2,
        in_specs=[spec(pltpu.SMEM)] + [spec(pltpu.VMEM)] * 4,
        out_specs=[spec(pltpu.VMEM)] * 2,
        compiler_params=pltpu.CompilerParams(vmem_limit_bytes=KEEP_BYTES),
        cost_estimate=pl.CostEstimate(
            flops=2 * total * depth * units, bytes_accessed=8 * total * units, transcendentals=0
        ),
    )(place, *in_vmem(hidden, d_pre, normed_t, grad_t))


def swap(block, axis, bit):
    pairs = [(source, source ^ (1 << bit)) for source in range(lax.axis_size(axis))]
    return lax.ppermute(block, axis, pairs)


def pick(block, at):
    return slice_at(block, 0, at).astype(jnp.float32)


def finish_sum(halves, kept, taken, order, beside=None):
    for phase, step in enumerate(order):
        mine, other = halves[step]
        shape = (2, kept.shape[0] // 2) + kept.shape[1:]
        kept, taken = kept.reshape(shape), taken.reshape(shape)
        give = (pick(kept, other) + pick(taken, other)).astype(jnp.bfloat16)
        kept = (pick(kept, mine) + pick(taken, mine)).astype(jnp.bfloat16)
        if beside:
            give = beside(phase, give)
        taken = swap(give, *step)
    return (kept.astype(jnp.float32) + taken.astype(jnp.float32))[0]


def scatter_narrow(halves, left, right, order, span_x, span_y):
    total = jnp.dot(left, right, preferred_element_type=jnp.float32).astype(jnp.bfloat16)
    rows, columns = left.shape[0] // span_x, right.shape[1] // span_y
    count_x, count_y = span_x.bit_length() - 1, span_y.bit_length() - 1
    dims = [("gx", bit) for bit in range(count_x)][::-1] + ["rows"]
    dims += [("gy", bit) for bit in range(count_y)][::-1] + ["columns"]
    blocks = total.reshape((2,) * count_x + (rows,) + (2,) * count_y + (columns,))
    blocks = blocks.transpose([dims.index(item) for item in list(order) + ["rows", "columns"]])
    blocks = blocks.reshape(-1, rows, columns)
    return finish_sum(halves, blocks, jnp.zeros_like(blocks), order)


class Journey:
    def __init__(self, held, bits=(0, 1, 2, 3), sources=(0,)):
        self.held = held
        self.bits = list(bits)
        self.sources = list(sources)
        self.parts = None

    def hop(self, at, steps, halves, after=None):
        dim = self.bits.index(at)
        mine, other = halves[steps[at]]
        kept, given = [slice_at(self.held, dim, part) for part in (mine, other)]
        if after is not None:
            given, after = lax.optimization_barrier((given, after))
        self.parts = [kept, swap(given, *steps[at])]
        self.held = jnp.concatenate(self.parts, -3)
        self.bits.remove(at)
        self.sources += [source | MASKS[at] for source in self.sources]
        return after

    def hop_both(self, at, also, steps, halves, after=None):
        dims = self.bits.index(at), self.bits.index(also)
        parts = []
        for theirs, beyond in ((0, 0), (1, 0), (0, 1), (1, 1)):
            part = slice_at(self.held, dims[0], halves[steps[at]][theirs], keep=True)
            part = slice_at(part, dims[1], halves[steps[also]][beyond], keep=True)
            parts.append(lax.squeeze(part, dims))
        if after is not None:
            parts, after = lax.optimization_barrier((parts, after))
        self.parts = [
            parts[0],
            swap(parts[1], *steps[at]),
            swap(parts[2], *steps[also]),
            swap_both(parts[3], steps[at], steps[also]),
        ]
        self.held = jnp.concatenate(self.parts, -3)
        for bit in (at, also):
            self.bits.remove(bit)
            self.sources += [source | MASKS[bit] for source in self.sources]
        return after


def slice_at(block, dim, at, keep=False):
    start = [0] * block.ndim
    start[dim] = at
    size = list(block.shape)
    size[dim] = 1
    part = lax.dynamic_slice(block, start, size, allow_negative_indices=False)
    return part if keep else lax.squeeze(part, (dim,))


def swap_both(block, step, also):
    span_x, span_y = lax.axis_size("gx"), lax.axis_size("gy")
    flips = {step[0]: 1 << step[1], also[0]: 1 << also[1]}
    pairs = []
    for at_x in range(span_x):
        for at_y in range(span_y):
            pairs.append((at_x * span_y + at_y, (at_x ^ flips["gx"]) * span_y + (at_y ^ flips["gy"])))
    return lax.ppermute(block, ("gx", "gy"), pairs)


def settle(place, journey):
    parts = journey.parts
    rows, width = parts[0].shape[-2:]
    return pl.pallas_call(
        functools.partial(settle_kernel, journey.sources),
        out_shape=jax.ShapeDtypeStruct((MEMBERS * rows, width), parts[0].dtype),
        in_specs=[spec(pltpu.SMEM)] + [spec(pltpu.VMEM)] * len(parts),
        out_specs=spec(pltpu.HBM),
        scratch_shapes=[pltpu.SemaphoreType.DMA((MEMBERS,))],
        cost_estimate=pl.CostEstimate(flops=0, bytes_accessed=4 * MEMBERS * rows * width, transcendentals=0),
    )(place, *parts)


def local(signal, w_up, w_down, cotangent):
    span_x = lax.axis_size("gx")
    span_y = lax.axis_size("gy")
    groups = section_groups(span_x, span_y)
    rows, width = signal.shape
    depth, units = w_up.shape
    steps = [("gx", span_x.bit_length() - 2), ("gx", 0), ("gy", span_y.bit_length() - 2), ("gy", 0)]
    z, y, x, core = range(4)
    rest_y = [("gy", bit) for bit in range(1, span_y.bit_length() - 1)]
    rest_x = [("gx", bit) for bit in range(1, span_x.bit_length() - 1)]
    order_down = [steps[y]] + rest_y + rest_x
    order_up = rest_y + [steps[y]] + rest_x[::-1]

    owns = [lax.axis_index(axis) // (1 << bit) % 2 for axis, bit in [steps[core]] + order_up]
    own = dict(zip([steps[core]] + order_up, owns))
    member = sum(own[step] * mask for step, mask in zip(steps, MASKS))
    place = jnp.stack([member, 1 - own[steps[core]]]).astype(jnp.int32)
    place, owns, others = lax.optimization_barrier((place, owns, [1 - item for item in owns]))
    halves = {step: pair for step, pair in zip([steps[core]] + order_up, zip(owns, others))}
    places = [block_places(order, span_x, span_y) for order in (order_down, order_up)]
    block = None
    if units // span_y % LANES == 0:
        block = pltpu.VMEM((span_x * span_y // 2, depth // span_x, units // span_y), jnp.bfloat16)

    parts = (2, 2, 2, 2, 1, rows // MEMBERS, width)
    state = exchange(signal.reshape(MEMBERS, rows // MEMBERS, width), groups)
    coming = Journey(cotangent.reshape(parts))
    coming.hop(core, steps, halves)
    coming.hop_both(x, y, steps, halves)
    up = load(place, w_up)
    state = coming.hop(z, steps, halves, state)
    state, *kept, down = forward(state, up, w_down)
    kept += [up, down]
    going = Journey(state.reshape(parts))
    grad = going.hop(z, steps, halves, coming.held)
    d_pre, grad_t, *given = backward(place, grad, kept, places, block)
    hidden, normed_t = kept[0], kept[3]
    if not given:
        going.hop(core, steps, halves)
        going.hop_both(x, y, steps, halves)
        mixed_out = settle(place, going)
        grad_down = scatter_narrow(halves, grad_t, hidden, [steps[core]] + order_down, span_x, span_y)
        grad_up = scatter_narrow(halves, normed_t, d_pre, [steps[core]] + order_up, span_x, span_y)
        return (mixed_out, grad_up, grad_down)
    take_down, take_up = [swap(part, *steps[core]) for part in given]
    after = going.hop(core, steps, halves, place)
    keep_down, keep_up = keep_blocks(after, hidden, d_pre, normed_t, grad_t, places, block)

    def beside(phase, give):
        if phase == 2:
            return going.hop_both(x, y, steps, halves, give)
        if phase == len(order_down) - 1:
            going.parts, give = lax.optimization_barrier((going.parts, give))
        return give

    grad_up = finish_sum(halves, keep_up, take_up, order_up)
    grad_down = finish_sum(halves, keep_down, take_down, order_down, beside)
    return (settle(place, going), grad_up, grad_down)


def solution(mesh):
    return jax.shard_map(
        local,
        mesh=mesh,
        in_specs=(P(("gx", "gy"), None), P(), P(), P(("gx", "gy"), None)),
        out_specs=(P(("gx", "gy"), None), P("gx", "gy"), P("gx", "gy")),
        check_vma=False,
    )
```

```python
import functools
import math

import jax
import jax.numpy as jnp
from jax import lax
from jax.experimental import pallas as pl
from jax.experimental.pallas import tpu as pltpu
from jax.sharding import PartitionSpec as P

MEMBERS = 16
MASKS = (8, 4, 2, 1)
LANES = 128
CHUNK = 256
SECTIONS_BYTES = 8 * 1024 * 1024
KEEP_BYTES = 4 * 1024 * 1024


def section_groups(span_x, span_y):
    bits_x = [span_x.bit_length() - 2, 0]
    bits_y = [span_y.bit_length() - 2, 0]
    mask_x = sum(1 << bit for bit in bits_x)
    mask_y = sum(1 << bit for bit in bits_y)
    groups = []
    for base_x in range(span_x):
        for base_y in range(span_y):
            if base_x & mask_x or base_y & mask_y:
                continue
            group = []
            for member in range(MEMBERS):
                at_x, at_y = base_x, base_y
                at_x |= (member >> 3 & 1) << bits_x[0] | (member >> 2 & 1) << bits_x[1]
                at_y |= (member >> 1 & 1) << bits_y[0] | (member & 1) << bits_y[1]
                group.append(at_x * span_y + at_y)
            groups.append(group)
    return groups


def exchange(block, groups):
    return lax.all_to_all(
        block, ("gx", "gy"), split_axis=0, concat_axis=0, axis_index_groups=groups, tiled=True
    )


def contract_last(left, right):
    return lax.dot_general(
        left, right, (((1,), (1,)), ((), ())), preferred_element_type=jnp.float32
    )


def low_members(mask):
    return [member for member in range(MEMBERS) if not member & mask]


def read_pair(ref, mask, swapped=0):
    low = jnp.concatenate([ref[member ^ swapped] for member in low_members(mask)], 0)
    high = jnp.concatenate([ref[(member | mask) ^ swapped] for member in low_members(mask)], 0)
    return jnp.concatenate([low, high], 1).astype(jnp.float32)


def write_pair(ref, mask, pair):
    rows, width = ref.shape[1:]
    for place, member in enumerate(low_members(mask)):
        part = pair[place * rows : (place + 1) * rows]
        ref[member] = part[:, :width]
        ref[member | mask] = part[:, width:]


def write_blocks(places, bit, left_ref, right_ref, out_ref):
    rows, columns = out_ref.shape[1:]
    pieces = []
    for group in range(len(places[0])):
        base = (2 * group + bit) * columns
        for inner in range(0, columns, LANES):
            pieces.append((group, inner, pl.multiple_of(base + inner, LANES)))
    for first in range(0, len(pieces), 2):
        some = pieces[first : first + 2]
        right = jnp.concatenate([right_ref[:, pl.ds(start, LANES)] for _, _, start in some], 1)
        total = jnp.dot(left_ref[...], right, preferred_element_type=jnp.float32)
        total = total.astype(jnp.bfloat16)
        for which, (group, inner, _) in enumerate(some):
            for block in range(len(places)):
                out_ref[places[block][group], :, inner : inner + LANES] = total[
                    block * rows : (block + 1) * rows, which * LANES : (which + 1) * LANES
                ]


def load_kernel(place_ref, source, target, arrived):
    copy = pltpu.make_async_copy(source, target, arrived)
    copy.start()
    copy.wait()


def forward_kernel(
    state_ref, up_ref, down_hbm,
    out_ref, hidden_ref, slope_ref, normed_ref, normed_t_ref, factor_ref, down_ref, work_ref, arrived
):
    fetch_down = pltpu.make_async_copy(down_hbm, down_ref, arrived)
    fetch_down.start()
    pairs = MEMBERS // 2 * work_ref.shape[1]
    hidden_units = up_ref.shape[1]
    last = len(MASKS) - 1
    for section, mask in enumerate(MASKS):
        at = pl.ds(section * pairs, pairs)
        pair = read_pair(state_ref if section == 0 else work_ref, mask)
        centre = jnp.mean(pair, axis=-1, keepdims=True)
        shifted = pair - centre
        spread = jnp.mean(shifted * shifted, axis=-1, keepdims=True)
        factor = lax.rsqrt(spread + 1e-05)
        normed = (shifted * factor).astype(jnp.bfloat16)
        normed_ref[at, :] = normed
        factor_ref[at, :] = jnp.broadcast_to(factor, (pairs, LANES))
        for start in range(0, hidden_units, CHUNK):
            units = pl.ds(start, CHUNK)
            pre = jnp.dot(normed, up_ref[:, units], preferred_element_type=jnp.float32)
            share = 0.5 * (1.0 + lax.erf(pre * (1.0 / math.sqrt(2.0))))
            hidden_ref[at, units] = (pre * share).astype(jnp.bfloat16)
            bell = jnp.exp(-0.5 * pre * pre) * (1.0 / math.sqrt(2.0 * math.pi))
            slope_ref[at, units] = (share + pre * bell).astype(jnp.bfloat16)
        if section == 0:
            fetch_down.wait()
        mixed = (pair + contract_last(hidden_ref[at, :], down_ref[...])).astype(jnp.bfloat16)
        write_pair(work_ref if section < last else out_ref, mask, mixed)
        normed_t_ref[:, at] = normed.T


def backward_kernel(
    places_down, places_up, place_ref, grad_ref, hidden_ref, slope_ref, normed_ref, normed_t_ref, factor_ref,
    up_ref, down_ref, d_pre_ref, grad_t_ref, *rest
):
    blocks, work_ref = rest[:-1], rest[-1]
    pairs = MEMBERS // 2 * work_ref.shape[1]
    hidden_units = up_ref.shape[1]
    last = len(MASKS) - 1
    for section in range(last, -1, -1):
        mask = MASKS[section]
        at = pl.ds(section * pairs, pairs)
        if section == last:
            pair_grad = read_pair(grad_ref, mask, swapped=place_ref[0])
        else:
            pair_grad = read_pair(work_ref, mask)
        pair_bf = pair_grad.astype(jnp.bfloat16)
        for start in range(0, hidden_units, CHUNK):
            units = pl.ds(start, CHUNK)
            d_hidden = jnp.dot(pair_bf, down_ref[:, units], preferred_element_type=jnp.float32)
            d_pre_ref[at, units] = (d_hidden * slope_ref[at, units].astype(jnp.float32)).astype(jnp.bfloat16)
        if section > 0:
            d_norm = contract_last(d_pre_ref[at, :], up_ref[...])
            normed = normed_ref[at, :].astype(jnp.float32)
            d_pair = factor_ref[at, :][:, :1] * (
                d_norm
                - jnp.mean(d_norm, axis=-1, keepdims=True)
                - normed * jnp.mean(d_norm * normed, axis=-1, keepdims=True)
            )
            write_pair(work_ref, mask, (pair_grad + d_pair).astype(jnp.bfloat16))
        grad_t_ref[:, at] = pair_bf.T

    if blocks:
        write_blocks(places_down, place_ref[1], grad_t_ref, hidden_ref, blocks[0])
        write_blocks(places_up, place_ref[1], normed_t_ref, d_pre_ref, blocks[1])


def keep_kernel(
    places_down, places_up, place_ref, hidden_ref, d_pre_ref, normed_t_ref, grad_t_ref, down_ref, up_ref
):
    write_blocks(places_down, 1 - place_ref[1], grad_t_ref, hidden_ref, down_ref)
    write_blocks(places_up, 1 - place_ref[1], normed_t_ref, d_pre_ref, up_ref)


def settle_kernel(sources, place_ref, *refs):
    parts, out_ref, done = refs[:-2], refs[-2], refs[-1]
    count, rows = parts[0].shape[:2]
    copies = []
    for index, source in enumerate(sources):
        block = parts[index // count].at[index % count]
        first = pl.multiple_of((place_ref[0] ^ source) * rows, rows)
        copies.append(pltpu.make_async_copy(block, out_ref.at[pl.ds(first, rows)], done.at[index]))
    for copy in copies:
        copy.start()
    for copy in copies:
        copy.wait()


def spec(space):
    return pl.BlockSpec(memory_space=space)


def block_places(order, span_x, span_y):
    places = []
    for at_x in range(span_x):
        line = []
        for group in range(span_y // 2):
            place = 0
            for axis, step in order:
                at = at_x if axis == "gx" else 2 * group
                place = 2 * place + (at >> step & 1)
            line.append(place)
        places.append(line)
    return places


def in_vmem(*items):
    return [pltpu.with_memory_space_constraint(item, pltpu.VMEM) for item in items]


def load(place, weight):
    return pl.pallas_call(
        load_kernel,
        out_shape=pltpu.VMEM(weight.shape, weight.dtype),
        in_specs=[spec(pltpu.SMEM), spec(pltpu.HBM)],
        out_specs=spec(pltpu.VMEM),
        scratch_shapes=[pltpu.SemaphoreType.DMA],
        compiler_params=pltpu.CompilerParams(vmem_limit_bytes=KEEP_BYTES),
        cost_estimate=pl.CostEstimate(flops=0, bytes_accessed=4 * weight.size, transcendentals=0),
    )(place, pltpu.with_memory_space_constraint(weight, pltpu.HBM))


def forward(state, up, w_down):
    members, rows, width = state.shape
    total = len(MASKS) * (members // 2) * rows
    depth, units = up.shape
    bf16 = jnp.bfloat16
    outs = [
        pltpu.VMEM(state.shape, bf16),
        pltpu.VMEM((total, units), bf16),
        pltpu.VMEM((total, units), bf16),
        pltpu.VMEM((total, depth), bf16),
        pltpu.VMEM((depth, total), bf16),
        pltpu.VMEM((total, LANES), jnp.float32),
        pltpu.VMEM(w_down.shape, bf16),
    ]
    return pl.pallas_call(
        forward_kernel,
        out_shape=outs,
        in_specs=[spec(pltpu.VMEM)] * 2 + [spec(pltpu.HBM)],
        out_specs=[spec(pltpu.VMEM)] * len(outs),
        scratch_shapes=[pltpu.VMEM(state.shape, bf16), pltpu.SemaphoreType.DMA],
        compiler_params=pltpu.CompilerParams(vmem_limit_bytes=SECTIONS_BYTES),
        cost_estimate=pl.CostEstimate(
            flops=10 * total * depth * units, bytes_accessed=16 * total * units, transcendentals=0
        ),
    )(state, *in_vmem(up), pltpu.with_memory_space_constraint(w_down, pltpu.HBM))


def backward(place, grad, kept, places, block):
    total, units = kept[0].shape
    depth = kept[2].shape[1]
    bf16 = jnp.bfloat16
    outs = [pltpu.VMEM((total, units), bf16), pltpu.VMEM((depth, total), bf16)]
    outs += [block] * 2 if block else []
    return pl.pallas_call(
        functools.partial(backward_kernel, *places),
        out_shape=outs,
        in_specs=[spec(pltpu.SMEM)] + [spec(pltpu.VMEM)] * (1 + len(kept)),
        out_specs=[spec(pltpu.VMEM)] * len(outs),
        scratch_shapes=[pltpu.VMEM(grad.shape, bf16)],
        compiler_params=pltpu.CompilerParams(vmem_limit_bytes=SECTIONS_BYTES),
        cost_estimate=pl.CostEstimate(
            flops=10 * total * depth * units, bytes_accessed=16 * total * units, transcendentals=0
        ),
    )(place, grad, *in_vmem(*kept))


def keep_blocks(place, hidden, d_pre, normed_t, grad_t, places, block):
    total, units = hidden.shape
    depth = normed_t.shape[0]
    return pl.pallas_call(
        functools.partial(keep_kernel, *places),
        out_shape=[block] * 2,
        in_specs=[spec(pltpu.SMEM)] + [spec(pltpu.VMEM)] * 4,
        out_specs=[spec(pltpu.VMEM)] * 2,
        compiler_params=pltpu.CompilerParams(vmem_limit_bytes=KEEP_BYTES),
        cost_estimate=pl.CostEstimate(
            flops=2 * total * depth * units, bytes_accessed=8 * total * units, transcendentals=0
        ),
    )(place, *in_vmem(hidden, d_pre, normed_t, grad_t))


def swap(block, axis, bit):
    pairs = [(source, source ^ (1 << bit)) for source in range(lax.axis_size(axis))]
    return lax.ppermute(block, axis, pairs)


def pick(block, at):
    return slice_at(block, 0, at).astype(jnp.float32)


def finish_sum(halves, kept, taken, order, beside=None):
    for phase, step in enumerate(order):
        mine, other = halves[step]
        shape = (2, kept.shape[0] // 2) + kept.shape[1:]
        kept, taken = kept.reshape(shape), taken.reshape(shape)
        give = (pick(kept, other) + pick(taken, other)).astype(jnp.bfloat16)
        kept = (pick(kept, mine) + pick(taken, mine)).astype(jnp.bfloat16)
        if beside:
            give = beside(phase, give)
        taken = swap(give, *step)
    return (kept.astype(jnp.float32) + taken.astype(jnp.float32))[0]


def scatter_narrow(halves, left, right, order, span_x, span_y):
    total = jnp.dot(left, right, preferred_element_type=jnp.float32).astype(jnp.bfloat16)
    rows, columns = left.shape[0] // span_x, right.shape[1] // span_y
    count_x, count_y = span_x.bit_length() - 1, span_y.bit_length() - 1
    dims = [("gx", bit) for bit in range(count_x)][::-1] + ["rows"]
    dims += [("gy", bit) for bit in range(count_y)][::-1] + ["columns"]
    blocks = total.reshape((2,) * count_x + (rows,) + (2,) * count_y + (columns,))
    blocks = blocks.transpose([dims.index(item) for item in list(order) + ["rows", "columns"]])
    blocks = blocks.reshape(-1, rows, columns)
    return finish_sum(halves, blocks, jnp.zeros_like(blocks), order)


class Journey:
    def __init__(self, held, bits=(0, 1, 2, 3), sources=(0,)):
        self.held = held
        self.bits = list(bits)
        self.sources = list(sources)
        self.parts = None

    def hop(self, at, steps, halves, after=None):
        dim = self.bits.index(at)
        mine, other = halves[steps[at]]
        kept, given = [slice_at(self.held, dim, part) for part in (mine, other)]
        if after is not None:
            given, after = lax.optimization_barrier((given, after))
        self.parts = [kept, swap(given, *steps[at])]
        self.held = jnp.concatenate(self.parts, -3)
        self.bits.remove(at)
        self.sources += [source | MASKS[at] for source in self.sources]
        return after

    def hop_both(self, at, also, steps, halves, after=None):
        dims = self.bits.index(at), self.bits.index(also)
        parts = []
        for theirs, beyond in ((0, 0), (1, 0), (0, 1), (1, 1)):
            part = slice_at(self.held, dims[0], halves[steps[at]][theirs], keep=True)
            part = slice_at(part, dims[1], halves[steps[also]][beyond], keep=True)
            parts.append(lax.squeeze(part, dims))
        if after is not None:
            parts, after = lax.optimization_barrier((parts, after))
        self.parts = [
            parts[0],
            swap(parts[1], *steps[at]),
            swap(parts[2], *steps[also]),
            swap_both(parts[3], steps[at], steps[also]),
        ]
        self.held = jnp.concatenate(self.parts, -3)
        for bit in (at, also):
            self.bits.remove(bit)
            self.sources += [source | MASKS[bit] for source in self.sources]
        return after


def slice_at(block, dim, at, keep=False):
    start = [0] * block.ndim
    start[dim] = at
    size = list(block.shape)
    size[dim] = 1
    part = lax.dynamic_slice(block, start, size, allow_negative_indices=False)
    return part if keep else lax.squeeze(part, (dim,))


def swap_both(block, step, also):
    span_x, span_y = lax.axis_size("gx"), lax.axis_size("gy")
    flips = {step[0]: 1 << step[1], also[0]: 1 << also[1]}
    pairs = []
    for at_x in range(span_x):
        for at_y in range(span_y):
            pairs.append((at_x * span_y + at_y, (at_x ^ flips["gx"]) * span_y + (at_y ^ flips["gy"])))
    return lax.ppermute(block, ("gx", "gy"), pairs)


def settle(place, journey):
    parts = journey.parts
    rows, width = parts[0].shape[-2:]
    return pl.pallas_call(
        functools.partial(settle_kernel, journey.sources),
        out_shape=jax.ShapeDtypeStruct((MEMBERS * rows, width), parts[0].dtype),
        in_specs=[spec(pltpu.SMEM)] + [spec(pltpu.VMEM)] * len(parts),
        out_specs=spec(pltpu.HBM),
        scratch_shapes=[pltpu.SemaphoreType.DMA((MEMBERS,))],
        cost_estimate=pl.CostEstimate(flops=0, bytes_accessed=4 * MEMBERS * rows * width, transcendentals=0),
    )(place, *parts)


def local(signal, w_up, w_down, cotangent):
    span_x = lax.axis_size("gx")
    span_y = lax.axis_size("gy")
    groups = section_groups(span_x, span_y)
    rows, width = signal.shape
    depth, units = w_up.shape
    steps = [("gx", span_x.bit_length() - 2), ("gx", 0), ("gy", span_y.bit_length() - 2), ("gy", 0)]
    z, y, x, core = range(4)
    rest_y = [("gy", bit) for bit in range(1, span_y.bit_length() - 1)]
    rest_x = [("gx", bit) for bit in range(1, span_x.bit_length() - 1)]
    order_down = [steps[y]] + rest_y + rest_x
    order_up = rest_y + [steps[y]] + rest_x[::-1]

    owns = [lax.axis_index(axis) // (1 << bit) % 2 for axis, bit in [steps[core]] + order_up]
    own = dict(zip([steps[core]] + order_up, owns))
    member = sum(own[step] * mask for step, mask in zip(steps, MASKS))
    place = jnp.stack([member, 1 - own[steps[core]]]).astype(jnp.int32)
    place, owns, others = lax.optimization_barrier((place, owns, [1 - item for item in owns]))
    halves = {step: pair for step, pair in zip([steps[core]] + order_up, zip(owns, others))}
    places = [block_places(order, span_x, span_y) for order in (order_down, order_up)]
    block = None
    if units // span_y % LANES == 0:
        block = pltpu.VMEM((span_x * span_y // 2, depth // span_x, units // span_y), jnp.bfloat16)

    parts = (2, 2, 2, 2, 1, rows // MEMBERS, width)
    state = exchange(signal.reshape(MEMBERS, rows // MEMBERS, width), groups)
    coming = Journey(cotangent.reshape(parts))
    coming.hop(core, steps, halves)
    coming.hop_both(x, y, steps, halves)
    up = load(place, w_up)
    state = coming.hop(z, steps, halves, state)
    state, *kept, down = forward(state, up, w_down)
    kept += [up, down]
    going = Journey(state.reshape(parts))
    grad = going.hop(z, steps, halves, coming.held)
    d_pre, grad_t, *given = backward(place, grad, kept, places, block)
    hidden, normed_t = kept[0], kept[3]
    if not given:
        going.hop(core, steps, halves)
        going.hop_both(x, y, steps, halves)
        mixed_out = settle(place, going)
        grad_down = scatter_narrow(halves, grad_t, hidden, [steps[core]] + order_down, span_x, span_y)
        grad_up = scatter_narrow(halves, normed_t, d_pre, [steps[core]] + order_up, span_x, span_y)
        return (mixed_out, grad_up, grad_down)
    given[0] = going.hop(core, steps, halves, given[0])
    take_down, take_up = [swap(part, *steps[core]) for part in given]
    keep_down, keep_up = keep_blocks(place, hidden, d_pre, normed_t, grad_t, places, block)

    def beside(phase, give):
        if phase == 2:
            return going.hop_both(x, y, steps, halves, give)
        if phase == len(order_down) - 1:
            going.parts, give = lax.optimization_barrier((going.parts, give))
        return give

    grad_up = finish_sum(halves, keep_up, take_up, order_up)
    grad_down = finish_sum(halves, keep_down, take_down, order_down, beside)
    return (settle(place, going), grad_up, grad_down)


def solution(mesh):
    return jax.shard_map(
        local,
        mesh=mesh,
        in_specs=(P(("gx", "gy"), None), P(), P(), P(("gx", "gy"), None)),
        out_specs=(P(("gx", "gy"), None), P("gx", "gy"), P("gx", "gy")),
        check_vma=False,
    )
```

```python
import functools
import math

import jax
import jax.numpy as jnp
from jax import lax
from jax.experimental import pallas as pl
from jax.experimental.pallas import tpu as pltpu
from jax.sharding import PartitionSpec as P

MEMBERS = 16
MASKS = (8, 4, 2, 1)
LANES = 128
CHUNK = 256
SECTIONS_BYTES = 8 * 1024 * 1024
KEEP_BYTES = 4 * 1024 * 1024


def section_groups(span_x, span_y):
    bits_x = [span_x.bit_length() - 2, 0]
    bits_y = [span_y.bit_length() - 2, 0]
    mask_x = sum(1 << bit for bit in bits_x)
    mask_y = sum(1 << bit for bit in bits_y)
    groups = []
    for base_x in range(span_x):
        for base_y in range(span_y):
            if base_x & mask_x or base_y & mask_y:
                continue
            group = []
            for member in range(MEMBERS):
                at_x, at_y = base_x, base_y
                at_x |= (member >> 3 & 1) << bits_x[0] | (member >> 2 & 1) << bits_x[1]
                at_y |= (member >> 1 & 1) << bits_y[0] | (member & 1) << bits_y[1]
                group.append(at_x * span_y + at_y)
            groups.append(group)
    return groups


def exchange(block, groups):
    return lax.all_to_all(
        block, ("gx", "gy"), split_axis=0, concat_axis=0, axis_index_groups=groups, tiled=True
    )


def contract_last(left, right):
    return lax.dot_general(
        left, right, (((1,), (1,)), ((), ())), preferred_element_type=jnp.float32
    )


def low_members(mask):
    return [member for member in range(MEMBERS) if not member & mask]


def read_pair(ref, mask, swapped=0):
    low = jnp.concatenate([ref[member ^ swapped] for member in low_members(mask)], 0)
    high = jnp.concatenate([ref[(member | mask) ^ swapped] for member in low_members(mask)], 0)
    return jnp.concatenate([low, high], 1).astype(jnp.float32)


def write_pair(ref, mask, pair):
    rows, width = ref.shape[1:]
    for place, member in enumerate(low_members(mask)):
        part = pair[place * rows : (place + 1) * rows]
        ref[member] = part[:, :width]
        ref[member | mask] = part[:, width:]


def write_blocks(places, bit, left_ref, right_ref, out_ref):
    rows, columns = out_ref.shape[1:]
    pieces = []
    for group in range(len(places[0])):
        base = (2 * group + bit) * columns
        for inner in range(0, columns, LANES):
            pieces.append((group, inner, pl.multiple_of(base + inner, LANES)))
    for first in range(0, len(pieces), 2):
        some = pieces[first : first + 2]
        right = jnp.concatenate([right_ref[:, pl.ds(start, LANES)] for _, _, start in some], 1)
        total = jnp.dot(left_ref[...], right, preferred_element_type=jnp.float32)
        total = total.astype(jnp.bfloat16)
        for which, (group, inner, _) in enumerate(some):
            for block in range(len(places)):
                out_ref[places[block][group], :, inner : inner + LANES] = total[
                    block * rows : (block + 1) * rows, which * LANES : (which + 1) * LANES
                ]


def load_kernel(place_ref, source, target, arrived):
    copy = pltpu.make_async_copy(source, target, arrived)
    copy.start()
    copy.wait()


def forward_kernel(
    state_ref, up_ref, down_hbm,
    out_ref, hidden_ref, slope_ref, normed_ref, normed_t_ref, factor_ref, down_ref, work_ref, arrived
):
    fetch_down = pltpu.make_async_copy(down_hbm, down_ref, arrived)
    fetch_down.start()
    pairs = MEMBERS // 2 * work_ref.shape[1]
    hidden_units = up_ref.shape[1]
    last = len(MASKS) - 1
    for section, mask in enumerate(MASKS):
        at = pl.ds(section * pairs, pairs)
        pair = read_pair(state_ref if section == 0 else work_ref, mask)
        centre = jnp.mean(pair, axis=-1, keepdims=True)
        shifted = pair - centre
        spread = jnp.mean(shifted * shifted, axis=-1, keepdims=True)
        factor = lax.rsqrt(spread + 1e-05)
        normed = (shifted * factor).astype(jnp.bfloat16)
        normed_ref[at, :] = normed
        factor_ref[at, :] = jnp.broadcast_to(factor, (pairs, LANES))
        for start in range(0, hidden_units, CHUNK):
            units = pl.ds(start, CHUNK)
            pre = jnp.dot(normed, up_ref[:, units], preferred_element_type=jnp.float32)
            share = 0.5 * (1.0 + lax.erf(pre * (1.0 / math.sqrt(2.0))))
            hidden_ref[at, units] = (pre * share).astype(jnp.bfloat16)
            bell = jnp.exp(-0.5 * pre * pre) * (1.0 / math.sqrt(2.0 * math.pi))
            slope_ref[at, units] = (share + pre * bell).astype(jnp.bfloat16)
        if section == 0:
            fetch_down.wait()
        mixed = (pair + contract_last(hidden_ref[at, :], down_ref[...])).astype(jnp.bfloat16)
        write_pair(work_ref if section < last else out_ref, mask, mixed)
        normed_t_ref[:, at] = normed.T


def backward_kernel(
    places_down, places_up, place_ref, grad_ref, hidden_ref, slope_ref, normed_ref, normed_t_ref, factor_ref,
    up_ref, down_ref, d_pre_ref, grad_t_ref, *rest
):
    blocks, work_ref = rest[:-1], rest[-1]
    pairs = MEMBERS // 2 * work_ref.shape[1]
    hidden_units = up_ref.shape[1]
    last = len(MASKS) - 1
    for section in range(last, -1, -1):
        mask = MASKS[section]
        at = pl.ds(section * pairs, pairs)
        if section == last:
            pair_grad = read_pair(grad_ref, mask, swapped=place_ref[0])
        else:
            pair_grad = read_pair(work_ref, mask)
        pair_bf = pair_grad.astype(jnp.bfloat16)
        for start in range(0, hidden_units, CHUNK):
            units = pl.ds(start, CHUNK)
            d_hidden = jnp.dot(pair_bf, down_ref[:, units], preferred_element_type=jnp.float32)
            d_pre_ref[at, units] = (d_hidden * slope_ref[at, units].astype(jnp.float32)).astype(jnp.bfloat16)
        if section > 0:
            d_norm = contract_last(d_pre_ref[at, :], up_ref[...])
            normed = normed_ref[at, :].astype(jnp.float32)
            d_pair = factor_ref[at, :][:, :1] * (
                d_norm
                - jnp.mean(d_norm, axis=-1, keepdims=True)
                - normed * jnp.mean(d_norm * normed, axis=-1, keepdims=True)
            )
            write_pair(work_ref, mask, (pair_grad + d_pair).astype(jnp.bfloat16))
        grad_t_ref[:, at] = pair_bf.T

    if blocks:
        write_blocks(places_down, place_ref[1], grad_t_ref, hidden_ref, blocks[0])
        write_blocks(places_up, place_ref[1], normed_t_ref, d_pre_ref, blocks[1])


def keep_kernel(
    places_down, places_up, place_ref, hidden_ref, d_pre_ref, normed_t_ref, grad_t_ref, down_ref, up_ref
):
    write_blocks(places_down, 1 - place_ref[1], grad_t_ref, hidden_ref, down_ref)
    write_blocks(places_up, 1 - place_ref[1], normed_t_ref, d_pre_ref, up_ref)


def settle_kernel(sources, place_ref, *refs):
    parts, out_ref, done = refs[:-2], refs[-2], refs[-1]
    count, rows = parts[0].shape[:2]
    copies = []
    for index, source in enumerate(sources):
        block = parts[index // count].at[index % count]
        first = pl.multiple_of((place_ref[0] ^ source) * rows, rows)
        copies.append(pltpu.make_async_copy(block, out_ref.at[pl.ds(first, rows)], done.at[index]))
    for copy in copies:
        copy.start()
    for copy in copies:
        copy.wait()


def spec(space):
    return pl.BlockSpec(memory_space=space)


def block_places(order, span_x, span_y):
    places = []
    for at_x in range(span_x):
        line = []
        for group in range(span_y // 2):
            place = 0
            for axis, step in order:
                at = at_x if axis == "gx" else 2 * group
                place = 2 * place + (at >> step & 1)
            line.append(place)
        places.append(line)
    return places


def in_vmem(*items):
    return [pltpu.with_memory_space_constraint(item, pltpu.VMEM) for item in items]


def load(place, weight):
    return pl.pallas_call(
        load_kernel,
        out_shape=pltpu.VMEM(weight.shape, weight.dtype),
        in_specs=[spec(pltpu.SMEM), spec(pltpu.HBM)],
        out_specs=spec(pltpu.VMEM),
        scratch_shapes=[pltpu.SemaphoreType.DMA],
        compiler_params=pltpu.CompilerParams(vmem_limit_bytes=KEEP_BYTES),
        cost_estimate=pl.CostEstimate(flops=0, bytes_accessed=4 * weight.size, transcendentals=0),
    )(place, pltpu.with_memory_space_constraint(weight, pltpu.HBM))


def forward(state, up, w_down):
    members, rows, width = state.shape
    total = len(MASKS) * (members // 2) * rows
    depth, units = up.shape
    bf16 = jnp.bfloat16
    outs = [
        pltpu.VMEM(state.shape, bf16),
        pltpu.VMEM((total, units), bf16),
        pltpu.VMEM((total, units), bf16),
        pltpu.VMEM((total, depth), bf16),
        pltpu.VMEM((depth, total), bf16),
        pltpu.VMEM((total, LANES), jnp.float32),
        pltpu.VMEM(w_down.shape, bf16),
    ]
    return pl.pallas_call(
        forward_kernel,
        out_shape=outs,
        in_specs=[spec(pltpu.VMEM)] * 2 + [spec(pltpu.HBM)],
        out_specs=[spec(pltpu.VMEM)] * len(outs),
        scratch_shapes=[pltpu.VMEM(state.shape, bf16), pltpu.SemaphoreType.DMA],
        compiler_params=pltpu.CompilerParams(vmem_limit_bytes=SECTIONS_BYTES),
        cost_estimate=pl.CostEstimate(
            flops=10 * total * depth * units, bytes_accessed=16 * total * units, transcendentals=0
        ),
    )(state, *in_vmem(up), pltpu.with_memory_space_constraint(w_down, pltpu.HBM))


def backward(place, grad, kept, places, block):
    total, units = kept[0].shape
    depth = kept[2].shape[1]
    bf16 = jnp.bfloat16
    outs = [pltpu.VMEM((total, units), bf16), pltpu.VMEM((depth, total), bf16)]
    outs += [block] * 2 if block else []
    return pl.pallas_call(
        functools.partial(backward_kernel, *places),
        out_shape=outs,
        in_specs=[spec(pltpu.SMEM)] + [spec(pltpu.VMEM)] * (1 + len(kept)),
        out_specs=[spec(pltpu.VMEM)] * len(outs),
        scratch_shapes=[pltpu.VMEM(grad.shape, bf16)],
        compiler_params=pltpu.CompilerParams(vmem_limit_bytes=SECTIONS_BYTES),
        cost_estimate=pl.CostEstimate(
            flops=10 * total * depth * units, bytes_accessed=16 * total * units, transcendentals=0
        ),
    )(place, grad, *in_vmem(*kept))


def keep_blocks(place, hidden, d_pre, normed_t, grad_t, places, block):
    total, units = hidden.shape
    depth = normed_t.shape[0]
    return pl.pallas_call(
        functools.partial(keep_kernel, *places),
        out_shape=[block] * 2,
        in_specs=[spec(pltpu.SMEM)] + [spec(pltpu.VMEM)] * 4,
        out_specs=[spec(pltpu.VMEM)] * 2,
        compiler_params=pltpu.CompilerParams(vmem_limit_bytes=KEEP_BYTES),
        cost_estimate=pl.CostEstimate(
            flops=2 * total * depth * units, bytes_accessed=8 * total * units, transcendentals=0
        ),
    )(place, *in_vmem(hidden, d_pre, normed_t, grad_t))


def swap(block, axis, bit):
    pairs = [(source, source ^ (1 << bit)) for source in range(lax.axis_size(axis))]
    return lax.ppermute(block, axis, pairs)


def pick(block, at):
    return slice_at(block, 0, at).astype(jnp.float32)


def finish_sum(halves, kept, taken, order, beside=None):
    for phase, step in enumerate(order):
        mine, other = halves[step]
        shape = (2, kept.shape[0] // 2) + kept.shape[1:]
        kept, taken = kept.reshape(shape), taken.reshape(shape)
        give = (pick(kept, other) + pick(taken, other)).astype(jnp.bfloat16)
        kept = (pick(kept, mine) + pick(taken, mine)).astype(jnp.bfloat16)
        if beside:
            give = beside(phase, give)
        taken = swap(give, *step)
    return (kept.astype(jnp.float32) + taken.astype(jnp.float32))[0]


def scatter_narrow(halves, left, right, order, span_x, span_y):
    total = jnp.dot(left, right, preferred_element_type=jnp.float32).astype(jnp.bfloat16)
    rows, columns = left.shape[0] // span_x, right.shape[1] // span_y
    count_x, count_y = span_x.bit_length() - 1, span_y.bit_length() - 1
    dims = [("gx", bit) for bit in range(count_x)][::-1] + ["rows"]
    dims += [("gy", bit) for bit in range(count_y)][::-1] + ["columns"]
    blocks = total.reshape((2,) * count_x + (rows,) + (2,) * count_y + (columns,))
    blocks = blocks.transpose([dims.index(item) for item in list(order) + ["rows", "columns"]])
    blocks = blocks.reshape(-1, rows, columns)
    return finish_sum(halves, blocks, jnp.zeros_like(blocks), order)


class Journey:
    def __init__(self, held, bits=(0, 1, 2, 3), sources=(0,)):
        self.held = held
        self.bits = list(bits)
        self.sources = list(sources)
        self.parts = None

    def hop(self, at, steps, halves, after=None):
        dim = self.bits.index(at)
        mine, other = halves[steps[at]]
        kept, given = [slice_at(self.held, dim, part) for part in (mine, other)]
        if after is not None:
            given, after = lax.optimization_barrier((given, after))
        self.parts = [kept, swap(given, *steps[at])]
        self.held = jnp.concatenate(self.parts, -3)
        self.bits.remove(at)
        self.sources += [source | MASKS[at] for source in self.sources]
        return after

    def hop_both(self, at, also, steps, halves, after=None):
        dims = self.bits.index(at), self.bits.index(also)
        parts = []
        for theirs, beyond in ((0, 0), (1, 0), (0, 1), (1, 1)):
            part = slice_at(self.held, dims[0], halves[steps[at]][theirs], keep=True)
            part = slice_at(part, dims[1], halves[steps[also]][beyond], keep=True)
            parts.append(lax.squeeze(part, dims))
        if after is not None:
            parts, after = lax.optimization_barrier((parts, after))
        self.parts = [
            parts[0],
            swap(parts[1], *steps[at]),
            swap(parts[2], *steps[also]),
            swap_both(parts[3], steps[at], steps[also]),
        ]
        self.held = jnp.concatenate(self.parts, -3)
        for bit in (at, also):
            self.bits.remove(bit)
            self.sources += [source | MASKS[bit] for source in self.sources]
        return after


def slice_at(block, dim, at, keep=False):
    start = [0] * block.ndim
    start[dim] = at
    size = list(block.shape)
    size[dim] = 1
    part = lax.dynamic_slice(block, start, size, allow_negative_indices=False)
    return part if keep else lax.squeeze(part, (dim,))


def swap_both(block, step, also):
    span_x, span_y = lax.axis_size("gx"), lax.axis_size("gy")
    flips = {step[0]: 1 << step[1], also[0]: 1 << also[1]}
    pairs = []
    for at_x in range(span_x):
        for at_y in range(span_y):
            pairs.append((at_x * span_y + at_y, (at_x ^ flips["gx"]) * span_y + (at_y ^ flips["gy"])))
    return lax.ppermute(block, ("gx", "gy"), pairs)


def settle(place, journey):
    parts = journey.parts
    rows, width = parts[0].shape[-2:]
    return pl.pallas_call(
        functools.partial(settle_kernel, journey.sources),
        out_shape=jax.ShapeDtypeStruct((MEMBERS * rows, width), parts[0].dtype),
        in_specs=[spec(pltpu.SMEM)] + [spec(pltpu.VMEM)] * len(parts),
        out_specs=spec(pltpu.HBM),
        scratch_shapes=[pltpu.SemaphoreType.DMA((MEMBERS,))],
        cost_estimate=pl.CostEstimate(flops=0, bytes_accessed=4 * MEMBERS * rows * width, transcendentals=0),
    )(place, *parts)


def local(signal, w_up, w_down, cotangent):
    span_x = lax.axis_size("gx")
    span_y = lax.axis_size("gy")
    groups = section_groups(span_x, span_y)
    rows, width = signal.shape
    depth, units = w_up.shape
    steps = [("gx", span_x.bit_length() - 2), ("gx", 0), ("gy", span_y.bit_length() - 2), ("gy", 0)]
    z, y, x, core = range(4)
    rest_y = [("gy", bit) for bit in range(1, span_y.bit_length() - 1)]
    rest_x = [("gx", bit) for bit in range(1, span_x.bit_length() - 1)]
    order_down = [steps[y]] + rest_y + rest_x
    order_up = rest_y + [steps[y]] + rest_x[::-1]

    owns = [lax.axis_index(axis) // (1 << bit) % 2 for axis, bit in [steps[core]] + order_up]
    own = dict(zip([steps[core]] + order_up, owns))
    member = sum(own[step] * mask for step, mask in zip(steps, MASKS))
    place = jnp.stack([member, 1 - own[steps[core]]]).astype(jnp.int32)
    place, owns, others = lax.optimization_barrier((place, owns, [1 - item for item in owns]))
    halves = {step: pair for step, pair in zip([steps[core]] + order_up, zip(owns, others))}
    places = [block_places(order, span_x, span_y) for order in (order_down, order_up)]
    block = None
    if units // span_y % LANES == 0:
        block = pltpu.VMEM((span_x * span_y // 2, depth // span_x, units // span_y), jnp.bfloat16)

    parts = (2, 2, 2, 2, 1, rows // MEMBERS, width)
    state = exchange(signal.reshape(MEMBERS, rows // MEMBERS, width), groups)
    coming = Journey(cotangent.reshape(parts))
    coming.hop(core, steps, halves)
    coming.hop_both(x, y, steps, halves)
    up = load(place, w_up)
    state = coming.hop(z, steps, halves, state)
    state, *kept, down = forward(state, up, w_down)
    kept += [up, down]
    going = Journey(state.reshape(parts))
    grad = going.hop(z, steps, halves, coming.held)
    d_pre, grad_t, *given = backward(place, grad, kept, places, block)
    hidden, normed_t = kept[0], kept[3]
    if not given:
        going.hop(core, steps, halves)
        going.hop_both(x, y, steps, halves)
        mixed_out = settle(place, going)
        grad_down = scatter_narrow(halves, grad_t, hidden, [steps[core]] + order_down, span_x, span_y)
        grad_up = scatter_narrow(halves, normed_t, d_pre, [steps[core]] + order_up, span_x, span_y)
        return (mixed_out, grad_up, grad_down)
    take_down, take_up = [swap(part, *steps[core]) for part in given]
    keep_down, keep_up = keep_blocks(place, hidden, d_pre, normed_t, grad_t, places, block)

    def beside(phase, give):
        if phase == 1:
            return going.hop(core, steps, halves, give)
        if phase == 2:
            return going.hop_both(x, y, steps, halves, give)
        if phase == len(order_down) - 1:
            going.parts, give = lax.optimization_barrier((going.parts, give))
        return give

    grad_up = finish_sum(halves, keep_up, take_up, order_up)
    grad_down = finish_sum(halves, keep_down, take_down, order_down, beside)
    return (settle(place, going), grad_up, grad_down)


def solution(mesh):
    return jax.shard_map(
        local,
        mesh=mesh,
        in_specs=(P(("gx", "gy"), None), P(), P(), P(("gx", "gy"), None)),
        out_specs=(P(("gx", "gy"), None), P("gx", "gy"), P("gx", "gy")),
        check_vma=False,
    )
```

```python
import functools
import math

import jax
import jax.numpy as jnp
from jax import lax
from jax.experimental import pallas as pl
from jax.experimental.pallas import tpu as pltpu
from jax.sharding import PartitionSpec as P

MEMBERS = 16
MASKS = (8, 4, 2, 1)
LANES = 128
CHUNK = 256
SECTIONS_BYTES = 8 * 1024 * 1024
KEEP_BYTES = 4 * 1024 * 1024


def section_groups(span_x, span_y):
    bits_x = [span_x.bit_length() - 2, 0]
    bits_y = [span_y.bit_length() - 2, 0]
    mask_x = sum(1 << bit for bit in bits_x)
    mask_y = sum(1 << bit for bit in bits_y)
    groups = []
    for base_x in range(span_x):
        for base_y in range(span_y):
            if base_x & mask_x or base_y & mask_y:
                continue
            group = []
            for member in range(MEMBERS):
                at_x, at_y = base_x, base_y
                at_x |= (member >> 3 & 1) << bits_x[0] | (member >> 2 & 1) << bits_x[1]
                at_y |= (member >> 1 & 1) << bits_y[0] | (member & 1) << bits_y[1]
                group.append(at_x * span_y + at_y)
            groups.append(group)
    return groups


def exchange(block, groups):
    return lax.all_to_all(
        block, ("gx", "gy"), split_axis=0, concat_axis=0, axis_index_groups=groups, tiled=True
    )


def contract_last(left, right):
    return lax.dot_general(
        left, right, (((1,), (1,)), ((), ())), preferred_element_type=jnp.float32
    )


def low_members(mask):
    return [member for member in range(MEMBERS) if not member & mask]


def read_pair(ref, mask, spots=range(MEMBERS), swapped=0):
    low = jnp.concatenate([ref[spots[member] ^ swapped] for member in low_members(mask)], 0)
    high = jnp.concatenate([ref[spots[member | mask] ^ swapped] for member in low_members(mask)], 0)
    return jnp.concatenate([low, high], 1).astype(jnp.float32)


def write_pair(ref, mask, pair):
    rows, width = ref.shape[1:]
    for place, member in enumerate(low_members(mask)):
        part = pair[place * rows : (place + 1) * rows]
        ref[member] = part[:, :width]
        ref[member | mask] = part[:, width:]


def write_blocks(places, bit, left_ref, right_ref, out_ref):
    rows, columns = out_ref.shape[1:]
    pieces = []
    for group in range(len(places[0])):
        base = (2 * group + bit) * columns
        for inner in range(0, columns, LANES):
            pieces.append((group, inner, pl.multiple_of(base + inner, LANES)))
    for first in range(0, len(pieces), 2):
        some = pieces[first : first + 2]
        right = jnp.concatenate([right_ref[:, pl.ds(start, LANES)] for _, _, start in some], 1)
        total = jnp.dot(left_ref[...], right, preferred_element_type=jnp.float32)
        total = total.astype(jnp.bfloat16)
        for which, (group, inner, _) in enumerate(some):
            for block in range(len(places)):
                out_ref[places[block][group], :, inner : inner + LANES] = total[
                    block * rows : (block + 1) * rows, which * LANES : (which + 1) * LANES
                ]


def load_kernel(place_ref, source, target, arrived):
    copy = pltpu.make_async_copy(source, target, arrived)
    copy.start()
    copy.wait()


def forward_kernel(
    state_ref, up_ref, down_hbm,
    out_ref, hidden_ref, slope_ref, normed_ref, normed_t_ref, factor_ref, down_ref, work_ref, arrived
):
    fetch_down = pltpu.make_async_copy(down_hbm, down_ref, arrived)
    fetch_down.start()
    pairs = MEMBERS // 2 * work_ref.shape[1]
    hidden_units = up_ref.shape[1]
    last = len(MASKS) - 1
    for section, mask in enumerate(MASKS):
        at = pl.ds(section * pairs, pairs)
        pair = read_pair(state_ref if section == 0 else work_ref, mask)
        centre = jnp.mean(pair, axis=-1, keepdims=True)
        shifted = pair - centre
        spread = jnp.mean(shifted * shifted, axis=-1, keepdims=True)
        factor = lax.rsqrt(spread + 1e-05)
        normed = (shifted * factor).astype(jnp.bfloat16)
        normed_ref[at, :] = normed
        factor_ref[at, :] = jnp.broadcast_to(factor, (pairs, LANES))
        for start in range(0, hidden_units, CHUNK):
            units = pl.ds(start, CHUNK)
            pre = jnp.dot(normed, up_ref[:, units], preferred_element_type=jnp.float32)
            share = 0.5 * (1.0 + lax.erf(pre * (1.0 / math.sqrt(2.0))))
            hidden_ref[at, units] = (pre * share).astype(jnp.bfloat16)
            bell = jnp.exp(-0.5 * pre * pre) * (1.0 / math.sqrt(2.0 * math.pi))
            slope_ref[at, units] = (share + pre * bell).astype(jnp.bfloat16)
        if section == 0:
            fetch_down.wait()
        mixed = (pair + contract_last(hidden_ref[at, :], down_ref[...])).astype(jnp.bfloat16)
        write_pair(work_ref if section < last else out_ref, mask, mixed)
        normed_t_ref[:, at] = normed.T


def backward_kernel(
    spots, places_down, places_up, place_ref, grad_ref, hidden_ref, slope_ref, normed_ref, normed_t_ref, factor_ref,
    up_ref, down_ref, d_pre_ref, grad_t_ref, *rest
):
    blocks, work_ref = rest[:-1], rest[-1]
    pairs = MEMBERS // 2 * work_ref.shape[1]
    hidden_units = up_ref.shape[1]
    last = len(MASKS) - 1
    for section in range(last, -1, -1):
        mask = MASKS[section]
        at = pl.ds(section * pairs, pairs)
        if section == last:
            pair_grad = read_pair(grad_ref, mask, spots, place_ref[2])
        else:
            pair_grad = read_pair(work_ref, mask)
        pair_bf = pair_grad.astype(jnp.bfloat16)
        for start in range(0, hidden_units, CHUNK):
            units = pl.ds(start, CHUNK)
            d_hidden = jnp.dot(pair_bf, down_ref[:, units], preferred_element_type=jnp.float32)
            d_pre_ref[at, units] = (d_hidden * slope_ref[at, units].astype(jnp.float32)).astype(jnp.bfloat16)
        if section > 0:
            d_norm = contract_last(d_pre_ref[at, :], up_ref[...])
            normed = normed_ref[at, :].astype(jnp.float32)
            d_pair = factor_ref[at, :][:, :1] * (
                d_norm
                - jnp.mean(d_norm, axis=-1, keepdims=True)
                - normed * jnp.mean(d_norm * normed, axis=-1, keepdims=True)
            )
            write_pair(work_ref, mask, (pair_grad + d_pair).astype(jnp.bfloat16))
        grad_t_ref[:, at] = pair_bf.T

    if blocks:
        write_blocks(places_down, place_ref[1], grad_t_ref, hidden_ref, blocks[0])
        write_blocks(places_up, place_ref[1], normed_t_ref, d_pre_ref, blocks[1])


def keep_kernel(
    places_down, places_up, place_ref, hidden_ref, d_pre_ref, normed_t_ref, grad_t_ref, down_ref, up_ref
):
    write_blocks(places_down, 1 - place_ref[1], grad_t_ref, hidden_ref, down_ref)
    write_blocks(places_up, 1 - place_ref[1], normed_t_ref, d_pre_ref, up_ref)


def settle_kernel(sources, place_ref, *refs):
    parts, out_ref, done = refs[:-2], refs[-2], refs[-1]
    count, rows = parts[0].shape[:2]
    copies = []
    for index, source in enumerate(sources):
        block = parts[index // count].at[index % count]
        first = pl.multiple_of((place_ref[0] ^ source) * rows, rows)
        copies.append(pltpu.make_async_copy(block, out_ref.at[pl.ds(first, rows)], done.at[index]))
    for copy in copies:
        copy.start()
    for copy in copies:
        copy.wait()


def spec(space):
    return pl.BlockSpec(memory_space=space)


def block_places(order, span_x, span_y):
    places = []
    for at_x in range(span_x):
        line = []
        for group in range(span_y // 2):
            place = 0
            for axis, step in order:
                at = at_x if axis == "gx" else 2 * group
                place = 2 * place + (at >> step & 1)
            line.append(place)
        places.append(line)
    return places


def in_vmem(*items):
    return [pltpu.with_memory_space_constraint(item, pltpu.VMEM) for item in items]


def load(place, weight):
    return pl.pallas_call(
        load_kernel,
        out_shape=pltpu.VMEM(weight.shape, weight.dtype),
        in_specs=[spec(pltpu.SMEM), spec(pltpu.HBM)],
        out_specs=spec(pltpu.VMEM),
        scratch_shapes=[pltpu.SemaphoreType.DMA],
        compiler_params=pltpu.CompilerParams(vmem_limit_bytes=KEEP_BYTES),
        cost_estimate=pl.CostEstimate(flops=0, bytes_accessed=4 * weight.size, transcendentals=0),
    )(place, pltpu.with_memory_space_constraint(weight, pltpu.HBM))


def forward(state, up, w_down):
    members, rows, width = state.shape
    total = len(MASKS) * (members // 2) * rows
    depth, units = up.shape
    bf16 = jnp.bfloat16
    outs = [
        pltpu.VMEM(state.shape, bf16),
        pltpu.VMEM((total, units), bf16),
        pltpu.VMEM((total, units), bf16),
        pltpu.VMEM((total, depth), bf16),
        pltpu.VMEM((depth, total), bf16),
        pltpu.VMEM((total, LANES), jnp.float32),
        pltpu.VMEM(w_down.shape, bf16),
    ]
    return pl.pallas_call(
        forward_kernel,
        out_shape=outs,
        in_specs=[spec(pltpu.VMEM)] * 2 + [spec(pltpu.HBM)],
        out_specs=[spec(pltpu.VMEM)] * len(outs),
        scratch_shapes=[pltpu.VMEM(state.shape, bf16), pltpu.SemaphoreType.DMA],
        compiler_params=pltpu.CompilerParams(vmem_limit_bytes=SECTIONS_BYTES),
        cost_estimate=pl.CostEstimate(
            flops=10 * total * depth * units, bytes_accessed=16 * total * units, transcendentals=0
        ),
    )(state, *in_vmem(up), pltpu.with_memory_space_constraint(w_down, pltpu.HBM))


def backward(place, grad, kept, spots, places, block):
    total, units = kept[0].shape
    depth = kept[2].shape[1]
    bf16 = jnp.bfloat16
    outs = [pltpu.VMEM((total, units), bf16), pltpu.VMEM((depth, total), bf16)]
    outs += [block] * 2 if block else []
    return pl.pallas_call(
        functools.partial(backward_kernel, spots, *places),
        out_shape=outs,
        in_specs=[spec(pltpu.SMEM)] + [spec(pltpu.VMEM)] * (1 + len(kept)),
        out_specs=[spec(pltpu.VMEM)] * len(outs),
        scratch_shapes=[pltpu.VMEM(grad.shape, bf16)],
        compiler_params=pltpu.CompilerParams(vmem_limit_bytes=SECTIONS_BYTES),
        cost_estimate=pl.CostEstimate(
            flops=10 * total * depth * units, bytes_accessed=16 * total * units, transcendentals=0
        ),
    )(place, grad, *in_vmem(*kept))


def keep_blocks(place, hidden, d_pre, normed_t, grad_t, places, block):
    total, units = hidden.shape
    depth = normed_t.shape[0]
    return pl.pallas_call(
        functools.partial(keep_kernel, *places),
        out_shape=[block] * 2,
        in_specs=[spec(pltpu.SMEM)] + [spec(pltpu.VMEM)] * 4,
        out_specs=[spec(pltpu.VMEM)] * 2,
        compiler_params=pltpu.CompilerParams(vmem_limit_bytes=KEEP_BYTES),
        cost_estimate=pl.CostEstimate(
            flops=2 * total * depth * units, bytes_accessed=8 * total * units, transcendentals=0
        ),
    )(place, *in_vmem(hidden, d_pre, normed_t, grad_t))


def swap(block, axis, bit):
    pairs = [(source, source ^ (1 << bit)) for source in range(lax.axis_size(axis))]
    return lax.ppermute(block, axis, pairs)


def pick(block, at):
    return slice_at(block, 0, at).astype(jnp.float32)


def finish_sum(halves, kept, taken, order, beside=None):
    for phase, step in enumerate(order):
        mine, other = halves[step]
        shape = (2, kept.shape[0] // 2) + kept.shape[1:]
        kept, taken = kept.reshape(shape), taken.reshape(shape)
        give = (pick(kept, other) + pick(taken, other)).astype(jnp.bfloat16)
        kept = (pick(kept, mine) + pick(taken, mine)).astype(jnp.bfloat16)
        if beside:
            give = beside(phase, give)
        taken = swap(give, *step)
    return (kept.astype(jnp.float32) + taken.astype(jnp.float32))[0]


def scatter_narrow(halves, left, right, order, span_x, span_y):
    total = jnp.dot(left, right, preferred_element_type=jnp.float32).astype(jnp.bfloat16)
    rows, columns = left.shape[0] // span_x, right.shape[1] // span_y
    count_x, count_y = span_x.bit_length() - 1, span_y.bit_length() - 1
    dims = [("gx", bit) for bit in range(count_x)][::-1] + ["rows"]
    dims += [("gy", bit) for bit in range(count_y)][::-1] + ["columns"]
    blocks = total.reshape((2,) * count_x + (rows,) + (2,) * count_y + (columns,))
    blocks = blocks.transpose([dims.index(item) for item in list(order) + ["rows", "columns"]])
    blocks = blocks.reshape(-1, rows, columns)
    return finish_sum(halves, blocks, jnp.zeros_like(blocks), order)


class Journey:
    def __init__(self, held, bits=(0, 1, 2, 3), sources=(0,)):
        self.held = held
        self.bits = list(bits)
        self.sources = list(sources)
        self.parts = None

    def hop(self, at, steps, halves, after=None):
        dim = self.bits.index(at)
        mine, other = halves[steps[at]]
        kept, given = [slice_at(self.held, dim, part) for part in (mine, other)]
        if after is not None:
            given, after = lax.optimization_barrier((given, after))
        self.parts = [kept, swap(given, *steps[at])]
        self.held = jnp.concatenate(self.parts, -3)
        self.bits.remove(at)
        self.sources += [source | MASKS[at] for source in self.sources]
        return after

    def hop_both(self, at, also, steps, halves, after=None):
        dims = self.bits.index(at), self.bits.index(also)
        parts = []
        for theirs, beyond in ((0, 0), (1, 0), (0, 1), (1, 1)):
            part = slice_at(self.held, dims[0], halves[steps[at]][theirs], keep=True)
            part = slice_at(part, dims[1], halves[steps[also]][beyond], keep=True)
            parts.append(lax.squeeze(part, dims))
        if after is not None:
            parts, after = lax.optimization_barrier((parts, after))
        self.parts = [
            parts[0],
            swap(parts[1], *steps[at]),
            swap(parts[2], *steps[also]),
            swap_both(parts[3], steps[at], steps[also]),
        ]
        self.held = jnp.concatenate(self.parts, -3)
        for bit in (at, also):
            self.bits.remove(bit)
            self.sources += [source | MASKS[bit] for source in self.sources]
        return after


def slice_at(block, dim, at, keep=False):
    start = [0] * block.ndim
    start[dim] = at
    size = list(block.shape)
    size[dim] = 1
    part = lax.dynamic_slice(block, start, size, allow_negative_indices=False)
    return part if keep else lax.squeeze(part, (dim,))


def swap_both(block, step, also):
    span_x, span_y = lax.axis_size("gx"), lax.axis_size("gy")
    flips = {step[0]: 1 << step[1], also[0]: 1 << also[1]}
    pairs = []
    for at_x in range(span_x):
        for at_y in range(span_y):
            pairs.append((at_x * span_y + at_y, (at_x ^ flips["gx"]) * span_y + (at_y ^ flips["gy"])))
    return lax.ppermute(block, ("gx", "gy"), pairs)


def settle(place, journey):
    parts = journey.parts
    rows, width = parts[0].shape[-2:]
    return pl.pallas_call(
        functools.partial(settle_kernel, journey.sources),
        out_shape=jax.ShapeDtypeStruct((MEMBERS * rows, width), parts[0].dtype),
        in_specs=[spec(pltpu.SMEM)] + [spec(pltpu.VMEM)] * len(parts),
        out_specs=spec(pltpu.HBM),
        scratch_shapes=[pltpu.SemaphoreType.DMA((MEMBERS,))],
        cost_estimate=pl.CostEstimate(flops=0, bytes_accessed=4 * MEMBERS * rows * width, transcendentals=0),
    )(place, *parts)


def local(signal, w_up, w_down, cotangent):
    span_x = lax.axis_size("gx")
    span_y = lax.axis_size("gy")
    groups = section_groups(span_x, span_y)
    rows, width = signal.shape
    depth, units = w_up.shape
    steps = [("gx", span_x.bit_length() - 2), ("gx", 0), ("gy", span_y.bit_length() - 2), ("gy", 0)]
    z, y, x, core = range(4)
    rest_y = [("gy", bit) for bit in range(1, span_y.bit_length() - 1)]
    rest_x = [("gx", bit) for bit in range(1, span_x.bit_length() - 1)]
    order_down = [steps[y]] + rest_y + rest_x
    order_up = rest_y + [steps[y]] + rest_x[::-1]

    owns = [lax.axis_index(axis) // (1 << bit) % 2 for axis, bit in [steps[core]] + order_up]
    own = dict(zip([steps[core]] + order_up, owns))
    member = sum(own[step] * mask for step, mask in zip(steps, MASKS))
    inbound = (z, core, x, y)
    spots = [sum(bool(m & MASKS[at]) << k for k, at in enumerate(inbound)) for m in range(MEMBERS)]
    spot = sum(own[steps[at]] << k for k, at in enumerate(inbound))
    place = jnp.stack([member, 1 - own[steps[core]], spot]).astype(jnp.int32)
    place, owns, others = lax.optimization_barrier((place, owns, [1 - item for item in owns]))
    halves = {step: pair for step, pair in zip([steps[core]] + order_up, zip(owns, others))}
    places = [block_places(order, span_x, span_y) for order in (order_down, order_up)]
    block = None
    if units // span_y % LANES == 0:
        block = pltpu.VMEM((span_x * span_y // 2, depth // span_x, units // span_y), jnp.bfloat16)

    parts = (2, 2, 2, 2, 1, rows // MEMBERS, width)
    state = exchange(signal.reshape(MEMBERS, rows // MEMBERS, width), groups)
    coming = Journey(cotangent.reshape(parts))
    coming.hop(z, steps, halves)
    coming.hop(core, steps, halves)
    coming.hop_both(x, y, steps, halves)
    up = load(place, w_up)
    coming.held, state = lax.optimization_barrier((coming.held, state))
    state, *kept, down = forward(state, up, w_down)
    kept += [up, down]
    going = Journey(state.reshape(parts))
    grad = going.hop(z, steps, halves, coming.held)
    d_pre, grad_t, *given = backward(place, grad, kept, spots, places, block)
    hidden, normed_t = kept[0], kept[3]
    if not given:
        going.hop(core, steps, halves)
        going.hop_both(x, y, steps, halves)
        mixed_out = settle(place, going)
        grad_down = scatter_narrow(halves, grad_t, hidden, [steps[core]] + order_down, span_x, span_y)
        grad_up = scatter_narrow(halves, normed_t, d_pre, [steps[core]] + order_up, span_x, span_y)
        return (mixed_out, grad_up, grad_down)
    take_down, take_up = [swap(part, *steps[core]) for part in given]
    keep_down, keep_up = keep_blocks(place, hidden, d_pre, normed_t, grad_t, places, block)

    def beside(phase, give):
        if phase == 1:
            return going.hop(core, steps, halves, give)
        if phase == 2:
            return going.hop_both(x, y, steps, halves, give)
        if phase == len(order_down) - 1:
            going.parts, give = lax.optimization_barrier((going.parts, give))
        return give

    grad_up = finish_sum(halves, keep_up, take_up, order_up)
    grad_down = finish_sum(halves, keep_down, take_down, order_down, beside)
    return (settle(place, going), grad_up, grad_down)


def solution(mesh):
    return jax.shard_map(
        local,
        mesh=mesh,
        in_specs=(P(("gx", "gy"), None), P(), P(), P(("gx", "gy"), None)),
        out_specs=(P(("gx", "gy"), None), P("gx", "gy"), P("gx", "gy")),
        check_vma=False,
    )
```

```python
import functools
import math

import jax
import jax.numpy as jnp
from jax import lax
from jax.experimental import pallas as pl
from jax.experimental.pallas import tpu as pltpu
from jax.sharding import PartitionSpec as P

MEMBERS = 16
MASKS = (8, 4, 2, 1)
LANES = 128
CHUNK = 256
SECTIONS_BYTES = 8 * 1024 * 1024
KEEP_BYTES = 4 * 1024 * 1024


def section_groups(span_x, span_y):
    bits_x = [span_x.bit_length() - 2, 0]
    bits_y = [span_y.bit_length() - 2, 0]
    mask_x = sum(1 << bit for bit in bits_x)
    mask_y = sum(1 << bit for bit in bits_y)
    groups = []
    for base_x in range(span_x):
        for base_y in range(span_y):
            if base_x & mask_x or base_y & mask_y:
                continue
            group = []
            for member in range(MEMBERS):
                at_x, at_y = base_x, base_y
                at_x |= (member >> 3 & 1) << bits_x[0] | (member >> 2 & 1) << bits_x[1]
                at_y |= (member >> 1 & 1) << bits_y[0] | (member & 1) << bits_y[1]
                group.append(at_x * span_y + at_y)
            groups.append(group)
    return groups


def exchange(block, groups):
    return lax.all_to_all(
        block, ("gx", "gy"), split_axis=0, concat_axis=0, axis_index_groups=groups, tiled=True
    )


def contract_last(left, right):
    return lax.dot_general(
        left, right, (((1,), (1,)), ((), ())), preferred_element_type=jnp.float32
    )


def low_members(mask):
    return [member for member in range(MEMBERS) if not member & mask]


def read_pair(ref, mask, swapped=0):
    low = jnp.concatenate([ref[member ^ swapped] for member in low_members(mask)], 0)
    high = jnp.concatenate([ref[(member | mask) ^ swapped] for member in low_members(mask)], 0)
    return jnp.concatenate([low, high], 1).astype(jnp.float32)


def write_pair(ref, mask, pair):
    rows, width = ref.shape[1:]
    for place, member in enumerate(low_members(mask)):
        part = pair[place * rows : (place + 1) * rows]
        ref[member] = part[:, :width]
        ref[member | mask] = part[:, width:]


def write_blocks(places, bit, left_ref, right_ref, out_ref):
    rows, columns = out_ref.shape[1:]
    pieces = []
    for group in range(len(places[0])):
        base = (2 * group + bit) * columns
        for inner in range(0, columns, LANES):
            pieces.append((group, inner, pl.multiple_of(base + inner, LANES)))
    for first in range(0, len(pieces), 2):
        some = pieces[first : first + 2]
        right = jnp.concatenate([right_ref[:, pl.ds(start, LANES)] for _, _, start in some], 1)
        total = jnp.dot(left_ref[...], right, preferred_element_type=jnp.float32)
        total = total.astype(jnp.bfloat16)
        for which, (group, inner, _) in enumerate(some):
            for block in range(len(places)):
                out_ref[places[block][group], :, inner : inner + LANES] = total[
                    block * rows : (block + 1) * rows, which * LANES : (which + 1) * LANES
                ]


def load_kernel(place_ref, source, target, arrived):
    copy = pltpu.make_async_copy(source, target, arrived)
    copy.start()
    copy.wait()


def forward_kernel(
    state_ref, up_ref, down_hbm,
    out_ref, hidden_ref, slope_ref, normed_ref, normed_t_ref, factor_ref, down_ref, work_ref, arrived
):
    fetch_down = pltpu.make_async_copy(down_hbm, down_ref, arrived)
    fetch_down.start()
    pairs = MEMBERS // 2 * work_ref.shape[1]
    hidden_units = up_ref.shape[1]
    last = len(MASKS) - 1
    for section, mask in enumerate(MASKS):
        at = pl.ds(section * pairs, pairs)
        pair = read_pair(state_ref if section == 0 else work_ref, mask)
        centre = jnp.mean(pair, axis=-1, keepdims=True)
        shifted = pair - centre
        spread = jnp.mean(shifted * shifted, axis=-1, keepdims=True)
        factor = lax.rsqrt(spread + 1e-05)
        normed = (shifted * factor).astype(jnp.bfloat16)
        normed_ref[at, :] = normed
        factor_ref[at, :] = jnp.broadcast_to(factor, (pairs, LANES))
        for start in range(0, hidden_units, CHUNK):
            units = pl.ds(start, CHUNK)
            pre = jnp.dot(normed, up_ref[:, units], preferred_element_type=jnp.float32)
            share = 0.5 * (1.0 + lax.erf(pre * (1.0 / math.sqrt(2.0))))
            hidden_ref[at, units] = (pre * share).astype(jnp.bfloat16)
            bell = jnp.exp(-0.5 * pre * pre) * (1.0 / math.sqrt(2.0 * math.pi))
            slope_ref[at, units] = (share + pre * bell).astype(jnp.bfloat16)
        if section == 0:
            fetch_down.wait()
        mixed = (pair + contract_last(hidden_ref[at, :], down_ref[...])).astype(jnp.bfloat16)
        write_pair(work_ref if section < last else out_ref, mask, mixed)
        normed_t_ref[:, at] = normed.T


def backward_kernel(
    places_down, places_up, place_ref, grad_ref, hidden_ref, slope_ref, normed_ref, normed_t_ref, factor_ref,
    up_ref, down_ref, d_pre_ref, grad_t_ref, *rest
):
    blocks, work_ref = rest[:-1], rest[-1]
    pairs = MEMBERS // 2 * work_ref.shape[1]
    hidden_units = up_ref.shape[1]
    last = len(MASKS) - 1
    for section in range(last, -1, -1):
        mask = MASKS[section]
        at = pl.ds(section * pairs, pairs)
        if section == last:
            pair_grad = read_pair(grad_ref, mask, swapped=place_ref[0])
        else:
            pair_grad = read_pair(work_ref, mask)
        pair_bf = pair_grad.astype(jnp.bfloat16)
        for start in range(0, hidden_units, 2 * CHUNK):
            units = pl.ds(start, 2 * CHUNK)
            d_hidden = jnp.dot(pair_bf, down_ref[:, units], preferred_element_type=jnp.float32)
            d_pre_ref[at, units] = (d_hidden * slope_ref[at, units].astype(jnp.float32)).astype(jnp.bfloat16)
        if section > 0:
            d_norm = contract_last(d_pre_ref[at, :], up_ref[...])
            normed = normed_ref[at, :].astype(jnp.float32)
            d_pair = factor_ref[at, :][:, :1] * (
                d_norm
                - jnp.mean(d_norm, axis=-1, keepdims=True)
                - normed * jnp.mean(d_norm * normed, axis=-1, keepdims=True)
            )
            write_pair(work_ref, mask, (pair_grad + d_pair).astype(jnp.bfloat16))
        grad_t_ref[:, at] = pair_bf.T

    if blocks:
        write_blocks(places_down, place_ref[1], grad_t_ref, hidden_ref, blocks[0])
        write_blocks(places_up, place_ref[1], normed_t_ref, d_pre_ref, blocks[1])


def keep_kernel(
    places_down, places_up, place_ref, hidden_ref, d_pre_ref, normed_t_ref, grad_t_ref, down_ref, up_ref
):
    write_blocks(places_down, 1 - place_ref[1], grad_t_ref, hidden_ref, down_ref)
    write_blocks(places_up, 1 - place_ref[1], normed_t_ref, d_pre_ref, up_ref)


def settle_kernel(sources, place_ref, *refs):
    parts, out_ref, done = refs[:-2], refs[-2], refs[-1]
    count, rows = parts[0].shape[:2]
    copies = []
    for index, source in enumerate(sources):
        block = parts[index // count].at[index % count]
        first = pl.multiple_of((place_ref[0] ^ source) * rows, rows)
        copies.append(pltpu.make_async_copy(block, out_ref.at[pl.ds(first, rows)], done.at[index]))
    for copy in copies:
        copy.start()
    for copy in copies:
        copy.wait()


def spec(space):
    return pl.BlockSpec(memory_space=space)


def block_places(order, span_x, span_y):
    places = []
    for at_x in range(span_x):
        line = []
        for group in range(span_y // 2):
            place = 0
            for axis, step in order:
                at = at_x if axis == "gx" else 2 * group
                place = 2 * place + (at >> step & 1)
            line.append(place)
        places.append(line)
    return places


def in_vmem(*items):
    return [pltpu.with_memory_space_constraint(item, pltpu.VMEM) for item in items]


def load(place, weight):
    return pl.pallas_call(
        load_kernel,
        out_shape=pltpu.VMEM(weight.shape, weight.dtype),
        in_specs=[spec(pltpu.SMEM), spec(pltpu.HBM)],
        out_specs=spec(pltpu.VMEM),
        scratch_shapes=[pltpu.SemaphoreType.DMA],
        compiler_params=pltpu.CompilerParams(vmem_limit_bytes=KEEP_BYTES),
        cost_estimate=pl.CostEstimate(flops=0, bytes_accessed=4 * weight.size, transcendentals=0),
    )(place, pltpu.with_memory_space_constraint(weight, pltpu.HBM))


def forward(state, up, w_down):
    members, rows, width = state.shape
    total = len(MASKS) * (members // 2) * rows
    depth, units = up.shape
    bf16 = jnp.bfloat16
    outs = [
        pltpu.VMEM(state.shape, bf16),
        pltpu.VMEM((total, units), bf16),
        pltpu.VMEM((total, units), bf16),
        pltpu.VMEM((total, depth), bf16),
        pltpu.VMEM((depth, total), bf16),
        pltpu.VMEM((total, LANES), jnp.float32),
        pltpu.VMEM(w_down.shape, bf16),
    ]
    return pl.pallas_call(
        forward_kernel,
        out_shape=outs,
        in_specs=[spec(pltpu.VMEM)] * 2 + [spec(pltpu.HBM)],
        out_specs=[spec(pltpu.VMEM)] * len(outs),
        scratch_shapes=[pltpu.VMEM(state.shape, bf16), pltpu.SemaphoreType.DMA],
        compiler_params=pltpu.CompilerParams(vmem_limit_bytes=SECTIONS_BYTES),
        cost_estimate=pl.CostEstimate(
            flops=10 * total * depth * units, bytes_accessed=16 * total * units, transcendentals=0
        ),
    )(state, *in_vmem(up), pltpu.with_memory_space_constraint(w_down, pltpu.HBM))


def backward(place, grad, kept, places, block):
    total, units = kept[0].shape
    depth = kept[2].shape[1]
    bf16 = jnp.bfloat16
    outs = [pltpu.VMEM((total, units), bf16), pltpu.VMEM((depth, total), bf16)]
    outs += [block] * 2 if block else []
    return pl.pallas_call(
        functools.partial(backward_kernel, *places),
        out_shape=outs,
        in_specs=[spec(pltpu.SMEM)] + [spec(pltpu.VMEM)] * (1 + len(kept)),
        out_specs=[spec(pltpu.VMEM)] * len(outs),
        scratch_shapes=[pltpu.VMEM(grad.shape, bf16)],
        compiler_params=pltpu.CompilerParams(vmem_limit_bytes=SECTIONS_BYTES),
        cost_estimate=pl.CostEstimate(
            flops=10 * total * depth * units, bytes_accessed=16 * total * units, transcendentals=0
        ),
    )(place, grad, *in_vmem(*kept))


def keep_blocks(place, hidden, d_pre, normed_t, grad_t, places, block):
    total, units = hidden.shape
    depth = normed_t.shape[0]
    return pl.pallas_call(
        functools.partial(keep_kernel, *places),
        out_shape=[block] * 2,
        in_specs=[spec(pltpu.SMEM)] + [spec(pltpu.VMEM)] * 4,
        out_specs=[spec(pltpu.VMEM)] * 2,
        compiler_params=pltpu.CompilerParams(vmem_limit_bytes=KEEP_BYTES),
        cost_estimate=pl.CostEstimate(
            flops=2 * total * depth * units, bytes_accessed=8 * total * units, transcendentals=0
        ),
    )(place, *in_vmem(hidden, d_pre, normed_t, grad_t))


def swap(block, axis, bit):
    pairs = [(source, source ^ (1 << bit)) for source in range(lax.axis_size(axis))]
    return lax.ppermute(block, axis, pairs)


def pick(block, at):
    return slice_at(block, 0, at).astype(jnp.float32)


def halve(halves, step, kept, taken):
    mine, other = halves[step]
    shape = (2, kept.shape[0] // 2) + kept.shape[1:]
    kept, taken = kept.reshape(shape), taken.reshape(shape)
    give = (pick(kept, other) + pick(taken, other)).astype(jnp.bfloat16)
    keep = (pick(kept, mine) + pick(taken, mine)).astype(jnp.bfloat16)
    return keep, give


def last_sum(kept, taken):
    return (kept.astype(jnp.float32) + taken.astype(jnp.float32))[0]


def finish_sum(halves, kept, taken, order):
    for step in order:
        kept, give = halve(halves, step, kept, taken)
        taken = swap(give, *step)
    return last_sum(kept, taken)


def scatter_narrow(halves, left, right, order, span_x, span_y):
    total = jnp.dot(left, right, preferred_element_type=jnp.float32).astype(jnp.bfloat16)
    rows, columns = left.shape[0] // span_x, right.shape[1] // span_y
    count_x, count_y = span_x.bit_length() - 1, span_y.bit_length() - 1
    dims = [("gx", bit) for bit in range(count_x)][::-1] + ["rows"]
    dims += [("gy", bit) for bit in range(count_y)][::-1] + ["columns"]
    blocks = total.reshape((2,) * count_x + (rows,) + (2,) * count_y + (columns,))
    blocks = blocks.transpose([dims.index(item) for item in list(order) + ["rows", "columns"]])
    blocks = blocks.reshape(-1, rows, columns)
    return finish_sum(halves, blocks, jnp.zeros_like(blocks), order)


class Journey:
    def __init__(self, held, bits=(0, 1, 2, 3), sources=(0,)):
        self.held = held
        self.bits = list(bits)
        self.sources = list(sources)
        self.parts = None

    def hop(self, at, steps, halves, after=None):
        dim = self.bits.index(at)
        mine, other = halves[steps[at]]
        kept, given = [slice_at(self.held, dim, part) for part in (mine, other)]
        if after is not None:
            given, after = lax.optimization_barrier((given, after))
        self.parts = [kept, swap(given, *steps[at])]
        self.held = jnp.concatenate(self.parts, -3)
        self.bits.remove(at)
        self.sources += [source | MASKS[at] for source in self.sources]
        return after

    def hop_both(self, at, also, steps, halves, after=None):
        dims = self.bits.index(at), self.bits.index(also)
        parts = []
        for theirs, beyond in ((0, 0), (1, 0), (0, 1), (1, 1)):
            part = slice_at(self.held, dims[0], halves[steps[at]][theirs], keep=True)
            part = slice_at(part, dims[1], halves[steps[also]][beyond], keep=True)
            parts.append(lax.squeeze(part, dims))
        if after is not None:
            parts, after = lax.optimization_barrier((parts, after))
        self.parts = [
            parts[0],
            swap(parts[1], *steps[at]),
            swap(parts[2], *steps[also]),
            swap_both(parts[3], steps[at], steps[also]),
        ]
        self.held = jnp.concatenate(self.parts, -3)
        for bit in (at, also):
            self.bits.remove(bit)
            self.sources += [source | MASKS[bit] for source in self.sources]
        return after


def slice_at(block, dim, at, keep=False):
    start = [0] * block.ndim
    start[dim] = at
    size = list(block.shape)
    size[dim] = 1
    part = lax.dynamic_slice(block, start, size, allow_negative_indices=False)
    return part if keep else lax.squeeze(part, (dim,))


def swap_both(block, step, also):
    span_x, span_y = lax.axis_size("gx"), lax.axis_size("gy")
    flips = {step[0]: 1 << step[1], also[0]: 1 << also[1]}
    pairs = []
    for at_x in range(span_x):
        for at_y in range(span_y):
            pairs.append((at_x * span_y + at_y, (at_x ^ flips["gx"]) * span_y + (at_y ^ flips["gy"])))
    return lax.ppermute(block, ("gx", "gy"), pairs)


def settle(place, journey):
    parts = journey.parts
    rows, width = parts[0].shape[-2:]
    return pl.pallas_call(
        functools.partial(settle_kernel, journey.sources),
        out_shape=jax.ShapeDtypeStruct((MEMBERS * rows, width), parts[0].dtype),
        in_specs=[spec(pltpu.SMEM)] + [spec(pltpu.VMEM)] * len(parts),
        out_specs=spec(pltpu.HBM),
        scratch_shapes=[pltpu.SemaphoreType.DMA((MEMBERS,))],
        cost_estimate=pl.CostEstimate(flops=0, bytes_accessed=4 * MEMBERS * rows * width, transcendentals=0),
    )(place, *parts)


def local(signal, w_up, w_down, cotangent):
    span_x = lax.axis_size("gx")
    span_y = lax.axis_size("gy")
    groups = section_groups(span_x, span_y)
    rows, width = signal.shape
    depth, units = w_up.shape
    steps = [("gx", span_x.bit_length() - 2), ("gx", 0), ("gy", span_y.bit_length() - 2), ("gy", 0)]
    z, y, x, core = range(4)
    rest_y = [("gy", bit) for bit in range(1, span_y.bit_length() - 1)]
    rest_x = [("gx", bit) for bit in range(1, span_x.bit_length() - 1)]
    order_down = [steps[y]] + rest_y + rest_x
    order_up = rest_y + [steps[y]] + rest_x[::-1]

    owns = [lax.axis_index(axis) // (1 << bit) % 2 for axis, bit in [steps[core]] + order_up]
    own = dict(zip([steps[core]] + order_up, owns))
    member = sum(own[step] * mask for step, mask in zip(steps, MASKS))
    place = jnp.stack([member, 1 - own[steps[core]]]).astype(jnp.int32)
    place, owns, others = lax.optimization_barrier((place, owns, [1 - item for item in owns]))
    halves = {step: pair for step, pair in zip([steps[core]] + order_up, zip(owns, others))}
    places = [block_places(order, span_x, span_y) for order in (order_down, order_up)]
    block = None
    if units // span_y % LANES == 0:
        block = pltpu.VMEM((span_x * span_y // 2, depth // span_x, units // span_y), jnp.bfloat16)

    parts = (2, 2, 2, 2, 1, rows // MEMBERS, width)
    state = exchange(signal.reshape(MEMBERS, rows // MEMBERS, width), groups)
    coming = Journey(cotangent.reshape(parts))
    coming.hop(core, steps, halves)
    coming.hop_both(x, y, steps, halves)
    up = load(place, w_up)
    state = coming.hop(z, steps, halves, state)
    state, *kept, down = forward(state, up, w_down)
    kept += [up, down]
    going = Journey(state.reshape(parts))
    grad = going.hop(z, steps, halves, coming.held)
    d_pre, grad_t, *given = backward(place, grad, kept, places, block)
    hidden, normed_t = kept[0], kept[3]
    if not given:
        going.hop(core, steps, halves)
        going.hop_both(x, y, steps, halves)
        mixed_out = settle(place, going)
        grad_down = scatter_narrow(halves, grad_t, hidden, [steps[core]] + order_down, span_x, span_y)
        grad_up = scatter_narrow(halves, normed_t, d_pre, [steps[core]] + order_up, span_x, span_y)
        return (mixed_out, grad_up, grad_down)
    take_down, take_up = [swap(part, *steps[core]) for part in given]
    keep_down, keep_up = keep_blocks(place, hidden, d_pre, normed_t, grad_t, places, block)

    barrier = lax.optimization_barrier
    for phase, (step_down, step_up) in enumerate(zip(order_down, order_up)):
        ending = phase == len(order_down) - 1
        if not ending:
            keep_up, give_up = halve(halves, step_up, keep_up, take_up)
            take_up = swap(give_up, *step_up)
        keep_down, give_down = halve(halves, step_down, keep_down, take_down)
        if phase == 1:
            give_down = going.hop(core, steps, halves, give_down)
        if phase == 2:
            give_down = going.hop_both(x, y, steps, halves, give_down)
        take_down = swap(give_down, *step_down)
        if ending:
            take_up, give_down = barrier((take_up, give_down))
            keep_up, give_up = halve(halves, step_up, keep_up, take_up)
            going.parts, give_up = barrier((going.parts, give_up))
            take_up = swap(give_up, *step_up)
    return (settle(place, going), last_sum(keep_up, take_up), last_sum(keep_down, take_down))


def solution(mesh):
    return jax.shard_map(
        local,
        mesh=mesh,
        in_specs=(P(("gx", "gy"), None), P(), P(), P(("gx", "gy"), None)),
        out_specs=(P(("gx", "gy"), None), P("gx", "gy"), P("gx", "gy")),
        check_vma=False,
    )
```

```python
import functools
import math

import jax
import jax.numpy as jnp
from jax import lax
from jax.experimental import pallas as pl
from jax.experimental.pallas import tpu as pltpu
from jax.sharding import PartitionSpec as P

MEMBERS = 16
MASKS = (8, 4, 2, 1)
LANES = 128
CHUNK = 256
SECTIONS_BYTES = 8 * 1024 * 1024
KEEP_BYTES = 4 * 1024 * 1024


def section_groups(span_x, span_y):
    bits_x = [span_x.bit_length() - 2, 0]
    bits_y = [span_y.bit_length() - 2, 0]
    mask_x = sum(1 << bit for bit in bits_x)
    mask_y = sum(1 << bit for bit in bits_y)
    groups = []
    for base_x in range(span_x):
        for base_y in range(span_y):
            if base_x & mask_x or base_y & mask_y:
                continue
            group = []
            for member in range(MEMBERS):
                at_x, at_y = base_x, base_y
                at_x |= (member >> 3 & 1) << bits_x[0] | (member >> 2 & 1) << bits_x[1]
                at_y |= (member >> 1 & 1) << bits_y[0] | (member & 1) << bits_y[1]
                group.append(at_x * span_y + at_y)
            groups.append(group)
    return groups


def exchange(block, groups):
    return lax.all_to_all(
        block, ("gx", "gy"), split_axis=0, concat_axis=0, axis_index_groups=groups, tiled=True
    )


def contract_last(left, right):
    return lax.dot_general(
        left, right, (((1,), (1,)), ((), ())), preferred_element_type=jnp.float32
    )


def low_members(mask):
    return [member for member in range(MEMBERS) if not member & mask]


def read_pair(ref, mask, swapped=0):
    low = jnp.concatenate([ref[member ^ swapped] for member in low_members(mask)], 0)
    high = jnp.concatenate([ref[(member | mask) ^ swapped] for member in low_members(mask)], 0)
    return jnp.concatenate([low, high], 1).astype(jnp.float32)


def write_pair(ref, mask, pair):
    rows, width = ref.shape[1:]
    for place, member in enumerate(low_members(mask)):
        part = pair[place * rows : (place + 1) * rows]
        ref[member] = part[:, :width]
        ref[member | mask] = part[:, width:]


def write_blocks(places, bit, left_ref, right_ref, out_ref):
    rows, columns = out_ref.shape[1:]
    pieces = []
    for group in range(len(places[0])):
        base = (2 * group + bit) * columns
        for inner in range(0, columns, LANES):
            pieces.append((group, inner, pl.multiple_of(base + inner, LANES)))
    for first in range(0, len(pieces), 2):
        some = pieces[first : first + 2]
        right = jnp.concatenate([right_ref[:, pl.ds(start, LANES)] for _, _, start in some], 1)
        total = jnp.dot(left_ref[...], right, preferred_element_type=jnp.float32)
        total = total.astype(jnp.bfloat16)
        for which, (group, inner, _) in enumerate(some):
            for block in range(len(places)):
                out_ref[places[block][group], :, inner : inner + LANES] = total[
                    block * rows : (block + 1) * rows, which * LANES : (which + 1) * LANES
                ]


def load_kernel(place_ref, source, target, arrived):
    copy = pltpu.make_async_copy(source, target, arrived)
    copy.start()
    copy.wait()


def forward_kernel(
    state_ref, up_ref, down_hbm,
    out_ref, hidden_ref, slope_ref, normed_ref, normed_t_ref, factor_ref, down_ref, work_ref, arrived
):
    fetch_down = pltpu.make_async_copy(down_hbm, down_ref, arrived)
    fetch_down.start()
    pairs = MEMBERS // 2 * work_ref.shape[1]
    hidden_units = up_ref.shape[1]
    last = len(MASKS) - 1
    for section, mask in enumerate(MASKS):
        at = pl.ds(section * pairs, pairs)
        pair = read_pair(state_ref if section == 0 else work_ref, mask)
        centre = jnp.mean(pair, axis=-1, keepdims=True)
        shifted = pair - centre
        spread = jnp.mean(shifted * shifted, axis=-1, keepdims=True)
        factor = lax.rsqrt(spread + 1e-05)
        normed = (shifted * factor).astype(jnp.bfloat16)
        normed_ref[at, :] = normed
        factor_ref[at, :] = jnp.broadcast_to(factor, (pairs, LANES))
        for start in range(0, hidden_units, CHUNK):
            units = pl.ds(start, CHUNK)
            pre = jnp.dot(normed, up_ref[:, units], preferred_element_type=jnp.float32)
            share = 0.5 * (1.0 + lax.erf(pre * (1.0 / math.sqrt(2.0))))
            hidden_ref[at, units] = (pre * share).astype(jnp.bfloat16)
            bell = jnp.exp(-0.5 * pre * pre) * (1.0 / math.sqrt(2.0 * math.pi))
            slope_ref[at, units] = (share + pre * bell).astype(jnp.bfloat16)
        if section == 0:
            fetch_down.wait()
        mixed = (pair + contract_last(hidden_ref[at, :], down_ref[...])).astype(jnp.bfloat16)
        write_pair(work_ref if section < last else out_ref, mask, mixed)
        normed_t_ref[:, at] = normed.T


def backward_kernel(
    places_down, places_up, place_ref, grad_ref, hidden_ref, slope_ref, normed_ref, normed_t_ref, factor_ref,
    up_ref, down_ref, d_pre_ref, grad_t_ref, *rest
):
    blocks, work_ref = rest[:-1], rest[-1]
    pairs = MEMBERS // 2 * work_ref.shape[1]
    hidden_units = up_ref.shape[1]
    last = len(MASKS) - 1
    for section in range(last, -1, -1):
        mask = MASKS[section]
        at = pl.ds(section * pairs, pairs)
        if section == last:
            pair_grad = read_pair(grad_ref, mask, swapped=place_ref[0])
        else:
            pair_grad = read_pair(work_ref, mask)
        pair_bf = pair_grad.astype(jnp.bfloat16)
        for start in range(0, hidden_units, CHUNK):
            units = pl.ds(start, CHUNK)
            d_hidden = jnp.dot(pair_bf, down_ref[:, units], preferred_element_type=jnp.float32)
            d_pre_ref[at, units] = (d_hidden * slope_ref[at, units].astype(jnp.float32)).astype(jnp.bfloat16)
        if section > 0:
            d_norm = contract_last(d_pre_ref[at, :], up_ref[...])
            normed = normed_ref[at, :].astype(jnp.float32)
            d_pair = factor_ref[at, :][:, :1] * (
                d_norm
                - jnp.mean(d_norm, axis=-1, keepdims=True)
                - normed * jnp.mean(d_norm * normed, axis=-1, keepdims=True)
            )
            write_pair(work_ref, mask, (pair_grad + d_pair).astype(jnp.bfloat16))
        grad_t_ref[:, at] = pair_bf.T

    if blocks:
        write_blocks(places_down, place_ref[1], grad_t_ref, hidden_ref, blocks[0])
        write_blocks(places_up, place_ref[1], normed_t_ref, d_pre_ref, blocks[1])


def keep_kernel(
    places_down, places_up, place_ref, hidden_ref, d_pre_ref, normed_t_ref, grad_t_ref, down_ref, up_ref
):
    write_blocks(places_down, 1 - place_ref[1], grad_t_ref, hidden_ref, down_ref)
    write_blocks(places_up, 1 - place_ref[1], normed_t_ref, d_pre_ref, up_ref)


def settle_kernel(sources, place_ref, *refs):
    parts, out_ref, done = refs[:-2], refs[-2], refs[-1]
    count, rows = parts[0].shape[:2]
    copies = []
    for index, source in enumerate(sources):
        block = parts[index // count].at[index % count]
        first = pl.multiple_of((place_ref[0] ^ source) * rows, rows)
        copies.append(pltpu.make_async_copy(block, out_ref.at[pl.ds(first, rows)], done.at[index]))
    for copy in copies:
        copy.start()
    for copy in copies:
        copy.wait()


def spec(space):
    return pl.BlockSpec(memory_space=space)


def block_places(order, span_x, span_y):
    places = []
    for at_x in range(span_x):
        line = []
        for group in range(span_y // 2):
            place = 0
            for axis, step in order:
                at = at_x if axis == "gx" else 2 * group
                place = 2 * place + (at >> step & 1)
            line.append(place)
        places.append(line)
    return places


def in_vmem(*items):
    return [pltpu.with_memory_space_constraint(item, pltpu.VMEM) for item in items]


def load(place, weight):
    return pl.pallas_call(
        load_kernel,
        out_shape=pltpu.VMEM(weight.shape, weight.dtype),
        in_specs=[spec(pltpu.SMEM), spec(pltpu.HBM)],
        out_specs=spec(pltpu.VMEM),
        scratch_shapes=[pltpu.SemaphoreType.DMA],
        compiler_params=pltpu.CompilerParams(vmem_limit_bytes=KEEP_BYTES),
        cost_estimate=pl.CostEstimate(flops=0, bytes_accessed=4 * weight.size, transcendentals=0),
    )(place, pltpu.with_memory_space_constraint(weight, pltpu.HBM))


def forward(state, up, w_down):
    members, rows, width = state.shape
    total = len(MASKS) * (members // 2) * rows
    depth, units = up.shape
    bf16 = jnp.bfloat16
    outs = [
        pltpu.VMEM(state.shape, bf16),
        pltpu.VMEM((total, units), bf16),
        pltpu.VMEM((total, units), bf16),
        pltpu.VMEM((total, depth), bf16),
        pltpu.VMEM((depth, total), bf16),
        pltpu.VMEM((total, LANES), jnp.float32),
        pltpu.VMEM(w_down.shape, bf16),
    ]
    return pl.pallas_call(
        forward_kernel,
        out_shape=outs,
        in_specs=[spec(pltpu.VMEM)] * 2 + [spec(pltpu.HBM)],
        out_specs=[spec(pltpu.VMEM)] * len(outs),
        scratch_shapes=[pltpu.VMEM(state.shape, bf16), pltpu.SemaphoreType.DMA],
        compiler_params=pltpu.CompilerParams(vmem_limit_bytes=SECTIONS_BYTES),
        cost_estimate=pl.CostEstimate(
            flops=10 * total * depth * units, bytes_accessed=16 * total * units, transcendentals=0
        ),
    )(state, *in_vmem(up), pltpu.with_memory_space_constraint(w_down, pltpu.HBM))


def backward(place, grad, kept, places, block):
    total, units = kept[0].shape
    depth = kept[2].shape[1]
    bf16 = jnp.bfloat16
    outs = [pltpu.VMEM((total, units), bf16), pltpu.VMEM((depth, total), bf16)]
    outs += [block] * 2 if block else []
    return pl.pallas_call(
        functools.partial(backward_kernel, *places),
        out_shape=outs,
        in_specs=[spec(pltpu.SMEM)] + [spec(pltpu.VMEM)] * (1 + len(kept)),
        out_specs=[spec(pltpu.VMEM)] * len(outs),
        scratch_shapes=[pltpu.VMEM(grad.shape, bf16)],
        compiler_params=pltpu.CompilerParams(vmem_limit_bytes=SECTIONS_BYTES),
        cost_estimate=pl.CostEstimate(
            flops=10 * total * depth * units, bytes_accessed=16 * total * units, transcendentals=0
        ),
    )(place, grad, *in_vmem(*kept))


def keep_blocks(place, hidden, d_pre, normed_t, grad_t, places, block):
    total, units = hidden.shape
    depth = normed_t.shape[0]
    return pl.pallas_call(
        functools.partial(keep_kernel, *places),
        out_shape=[block] * 2,
        in_specs=[spec(pltpu.SMEM)] + [spec(pltpu.VMEM)] * 4,
        out_specs=[spec(pltpu.VMEM)] * 2,
        compiler_params=pltpu.CompilerParams(vmem_limit_bytes=KEEP_BYTES),
        cost_estimate=pl.CostEstimate(
            flops=2 * total * depth * units, bytes_accessed=8 * total * units, transcendentals=0
        ),
    )(place, *in_vmem(hidden, d_pre, normed_t, grad_t))


def swap(block, axis, bit):
    pairs = [(source, source ^ (1 << bit)) for source in range(lax.axis_size(axis))]
    return lax.ppermute(block, axis, pairs)


def pick(block, at):
    return slice_at(block, 0, at).astype(jnp.float32)


def halve(halves, step, kept, taken):
    mine, other = halves[step]
    shape = (2, kept.shape[0] // 2) + kept.shape[1:]
    kept, taken = kept.reshape(shape), taken.reshape(shape)
    give = (pick(kept, other) + pick(taken, other)).astype(jnp.bfloat16)
    keep = (pick(kept, mine) + pick(taken, mine)).astype(jnp.bfloat16)
    return keep, give


def last_sum(kept, taken):
    return (kept.astype(jnp.float32) + taken.astype(jnp.float32))[0]


def finish_sum(halves, kept, taken, order):
    for step in order:
        kept, give = halve(halves, step, kept, taken)
        taken = swap(give, *step)
    return last_sum(kept, taken)


def scatter_narrow(halves, left, right, order, span_x, span_y):
    total = jnp.dot(left, right, preferred_element_type=jnp.float32).astype(jnp.bfloat16)
    rows, columns = left.shape[0] // span_x, right.shape[1] // span_y
    count_x, count_y = span_x.bit_length() - 1, span_y.bit_length() - 1
    dims = [("gx", bit) for bit in range(count_x)][::-1] + ["rows"]
    dims += [("gy", bit) for bit in range(count_y)][::-1] + ["columns"]
    blocks = total.reshape((2,) * count_x + (rows,) + (2,) * count_y + (columns,))
    blocks = blocks.transpose([dims.index(item) for item in list(order) + ["rows", "columns"]])
    blocks = blocks.reshape(-1, rows, columns)
    return finish_sum(halves, blocks, jnp.zeros_like(blocks), order)


class Journey:
    def __init__(self, held, bits=(0, 1, 2, 3), sources=(0,)):
        self.held = held
        self.bits = list(bits)
        self.sources = list(sources)
        self.parts = None

    def hop(self, at, steps, halves, after=None):
        dim = self.bits.index(at)
        mine, other = halves[steps[at]]
        kept, given = [slice_at(self.held, dim, part) for part in (mine, other)]
        if after is not None:
            given, after = lax.optimization_barrier((given, after))
        self.parts = [kept, swap(given, *steps[at])]
        self.held = jnp.concatenate(self.parts, -3)
        self.bits.remove(at)
        self.sources += [source | MASKS[at] for source in self.sources]
        return after

    def hop_both(self, at, also, steps, halves, after=None):
        dims = self.bits.index(at), self.bits.index(also)
        parts = []
        for theirs, beyond in ((0, 0), (1, 0), (0, 1), (1, 1)):
            part = slice_at(self.held, dims[0], halves[steps[at]][theirs], keep=True)
            part = slice_at(part, dims[1], halves[steps[also]][beyond], keep=True)
            parts.append(lax.squeeze(part, dims))
        if after is not None:
            parts, after = lax.optimization_barrier((parts, after))
        self.parts = [
            parts[0],
            swap(parts[1], *steps[at]),
            swap(parts[2], *steps[also]),
            swap_both(parts[3], steps[at], steps[also]),
        ]
        self.held = jnp.concatenate(self.parts, -3)
        for bit in (at, also):
            self.bits.remove(bit)
            self.sources += [source | MASKS[bit] for source in self.sources]
        return after


def slice_at(block, dim, at, keep=False):
    start = [0] * block.ndim
    start[dim] = at
    size = list(block.shape)
    size[dim] = 1
    part = lax.dynamic_slice(block, start, size, allow_negative_indices=False)
    return part if keep else lax.squeeze(part, (dim,))


def swap_both(block, step, also):
    span_x, span_y = lax.axis_size("gx"), lax.axis_size("gy")
    flips = {step[0]: 1 << step[1], also[0]: 1 << also[1]}
    pairs = []
    for at_x in range(span_x):
        for at_y in range(span_y):
            pairs.append((at_x * span_y + at_y, (at_x ^ flips["gx"]) * span_y + (at_y ^ flips["gy"])))
    return lax.ppermute(block, ("gx", "gy"), pairs)


def settle(place, journey):
    parts = journey.parts
    rows, width = parts[0].shape[-2:]
    return pl.pallas_call(
        functools.partial(settle_kernel, journey.sources),
        out_shape=jax.ShapeDtypeStruct((MEMBERS * rows, width), parts[0].dtype),
        in_specs=[spec(pltpu.SMEM)] + [spec(pltpu.VMEM)] * len(parts),
        out_specs=spec(pltpu.HBM),
        scratch_shapes=[pltpu.SemaphoreType.DMA((MEMBERS,))],
        cost_estimate=pl.CostEstimate(flops=0, bytes_accessed=4 * MEMBERS * rows * width, transcendentals=0),
    )(place, *parts)


def local(signal, w_up, w_down, cotangent):
    span_x = lax.axis_size("gx")
    span_y = lax.axis_size("gy")
    groups = section_groups(span_x, span_y)
    rows, width = signal.shape
    depth, units = w_up.shape
    steps = [("gx", span_x.bit_length() - 2), ("gx", 0), ("gy", span_y.bit_length() - 2), ("gy", 0)]
    z, y, x, core = range(4)
    rest_y = [("gy", bit) for bit in range(1, span_y.bit_length() - 1)]
    rest_x = [("gx", bit) for bit in range(1, span_x.bit_length() - 1)]
    order_down = [steps[y]] + rest_y + rest_x
    order_up = rest_y + [steps[y]] + rest_x[::-1]

    owns = [lax.axis_index(axis) // (1 << bit) % 2 for axis, bit in [steps[core]] + order_up]
    own = dict(zip([steps[core]] + order_up, owns))
    member = sum(own[step] * mask for step, mask in zip(steps, MASKS))
    place = jnp.stack([member, 1 - own[steps[core]]]).astype(jnp.int32)
    place, owns, others = lax.optimization_barrier((place, owns, [1 - item for item in owns]))
    halves = {step: pair for step, pair in zip([steps[core]] + order_up, zip(owns, others))}
    places = [block_places(order, span_x, span_y) for order in (order_down, order_up)]
    block = None
    if units // span_y % LANES == 0:
        block = pltpu.VMEM((span_x * span_y // 2, depth // span_x, units // span_y), jnp.bfloat16)

    parts = (2, 2, 2, 2, 1, rows // MEMBERS, width)
    state = exchange(signal.reshape(MEMBERS, rows // MEMBERS, width), groups)
    coming = Journey(cotangent.reshape(parts))
    coming.hop(core, steps, halves)
    coming.hop_both(x, y, steps, halves)
    up = load(place, w_up)
    state = coming.hop(z, steps, halves, state)
    state, *kept, down = forward(state, up, w_down)
    kept += [up, down]
    going = Journey(state.reshape(parts))
    grad = going.hop(z, steps, halves, coming.held)
    d_pre, grad_t, *given = backward(place, grad, kept, places, block)
    hidden, normed_t = kept[0], kept[3]
    if not given:
        going.hop(core, steps, halves)
        going.hop_both(x, y, steps, halves)
        mixed_out = settle(place, going)
        grad_down = scatter_narrow(halves, grad_t, hidden, [steps[core]] + order_down, span_x, span_y)
        grad_up = scatter_narrow(halves, normed_t, d_pre, [steps[core]] + order_up, span_x, span_y)
        return (mixed_out, grad_up, grad_down)
    take_down, take_up = [swap(part, *steps[core]) for part in given]
    keep_down, keep_up = keep_blocks(place, hidden, d_pre, normed_t, grad_t, places, block)

    for phase, (step_down, step_up) in enumerate(zip(order_down, order_up)):
        if phase == 2:
            keep_up = going.hop_both(x, y, steps, halves, keep_up)
        keep_up, give_up = halve(halves, step_up, keep_up, take_up)
        take_up = swap(give_up, *step_up)
        keep_down, give_down = halve(halves, step_down, keep_down, take_down)
        if phase == 1:
            give_down = going.hop(core, steps, halves, give_down)
        if phase == len(order_down) - 1:
            going.parts, give_down = lax.optimization_barrier((going.parts, give_down))
        take_down = swap(give_down, *step_down)
    return (settle(place, going), last_sum(keep_up, take_up), last_sum(keep_down, take_down))


def solution(mesh):
    return jax.shard_map(
        local,
        mesh=mesh,
        in_specs=(P(("gx", "gy"), None), P(), P(), P(("gx", "gy"), None)),
        out_specs=(P(("gx", "gy"), None), P("gx", "gy"), P("gx", "gy")),
        check_vma=False,
    )
```

```python
import functools
import math

import jax
import jax.numpy as jnp
from jax import lax
from jax.experimental import pallas as pl
from jax.experimental.pallas import tpu as pltpu
from jax.sharding import PartitionSpec as P

MEMBERS = 16
MASKS = (8, 4, 2, 1)
LANES = 128
CHUNK = 256
SECTIONS_BYTES = 8 * 1024 * 1024
KEEP_BYTES = 4 * 1024 * 1024


def section_groups(span_x, span_y):
    bits_x = [span_x.bit_length() - 2, 0]
    bits_y = [span_y.bit_length() - 2, 0]
    mask_x = sum(1 << bit for bit in bits_x)
    mask_y = sum(1 << bit for bit in bits_y)
    groups = []
    for base_x in range(span_x):
        for base_y in range(span_y):
            if base_x & mask_x or base_y & mask_y:
                continue
            group = []
            for member in range(MEMBERS):
                at_x, at_y = base_x, base_y
                at_x |= (member >> 3 & 1) << bits_x[0] | (member >> 2 & 1) << bits_x[1]
                at_y |= (member >> 1 & 1) << bits_y[0] | (member & 1) << bits_y[1]
                group.append(at_x * span_y + at_y)
            groups.append(group)
    return groups


def exchange(block, groups):
    return lax.all_to_all(
        block, ("gx", "gy"), split_axis=0, concat_axis=0, axis_index_groups=groups, tiled=True
    )


def contract_last(left, right):
    return lax.dot_general(
        left, right, (((1,), (1,)), ((), ())), preferred_element_type=jnp.float32
    )


def low_members(mask):
    return [member for member in range(MEMBERS) if not member & mask]


def read_pair(ref, mask, swapped=0):
    low = jnp.concatenate([ref[member ^ swapped] for member in low_members(mask)], 0)
    high = jnp.concatenate([ref[(member | mask) ^ swapped] for member in low_members(mask)], 0)
    return jnp.concatenate([low, high], 1).astype(jnp.float32)


def write_pair(ref, mask, pair):
    rows, width = ref.shape[1:]
    for place, member in enumerate(low_members(mask)):
        part = pair[place * rows : (place + 1) * rows]
        ref[member] = part[:, :width]
        ref[member | mask] = part[:, width:]


def write_blocks(places, bit, left_ref, right_ref, out_ref):
    rows, columns = out_ref.shape[1:]
    pieces = []
    for group in range(len(places[0])):
        base = (2 * group + bit) * columns
        for inner in range(0, columns, LANES):
            pieces.append((group, inner, pl.multiple_of(base + inner, LANES)))
    for first in range(0, len(pieces), 2):
        some = pieces[first : first + 2]
        right = jnp.concatenate([right_ref[:, pl.ds(start, LANES)] for _, _, start in some], 1)
        total = jnp.dot(left_ref[...], right, preferred_element_type=jnp.float32)
        total = total.astype(jnp.bfloat16)
        for which, (group, inner, _) in enumerate(some):
            for block in range(len(places)):
                out_ref[places[block][group], :, inner : inner + LANES] = total[
                    block * rows : (block + 1) * rows, which * LANES : (which + 1) * LANES
                ]


def load_kernel(place_ref, source, target, arrived):
    copy = pltpu.make_async_copy(source, target, arrived)
    copy.start()
    copy.wait()


def forward_kernel(
    state_ref, up_ref, down_hbm,
    out_ref, hidden_ref, slope_ref, normed_ref, normed_t_ref, factor_ref, up_t_ref, down_ref, work_ref, arrived
):
    fetch_down = pltpu.make_async_copy(down_hbm, down_ref, arrived)
    fetch_down.start()
    pairs = MEMBERS // 2 * work_ref.shape[1]
    hidden_units = up_ref.shape[1]
    last = len(MASKS) - 1
    for section, mask in enumerate(MASKS):
        at = pl.ds(section * pairs, pairs)
        pair = read_pair(state_ref if section == 0 else work_ref, mask)
        centre = jnp.mean(pair, axis=-1, keepdims=True)
        shifted = pair - centre
        spread = jnp.mean(shifted * shifted, axis=-1, keepdims=True)
        factor = lax.rsqrt(spread + 1e-05)
        normed = (shifted * factor).astype(jnp.bfloat16)
        normed_ref[at, :] = normed
        factor_ref[at, :] = jnp.broadcast_to(factor, (pairs, LANES))
        for start in range(0, hidden_units, CHUNK):
            units = pl.ds(start, CHUNK)
            pre = jnp.dot(normed, up_ref[:, units], preferred_element_type=jnp.float32)
            share = 0.5 * (1.0 + lax.erf(pre * (1.0 / math.sqrt(2.0))))
            hidden_ref[at, units] = (pre * share).astype(jnp.bfloat16)
            bell = jnp.exp(-0.5 * pre * pre) * (1.0 / math.sqrt(2.0 * math.pi))
            slope_ref[at, units] = (share + pre * bell).astype(jnp.bfloat16)
        if section == 0:
            fetch_down.wait()
        mixed = (pair + contract_last(hidden_ref[at, :], down_ref[...])).astype(jnp.bfloat16)
        write_pair(work_ref if section < last else out_ref, mask, mixed)
        normed_t_ref[:, at] = normed.T
        quarter = pl.ds(section * (hidden_units // len(MASKS)), hidden_units // len(MASKS))
        up_t_ref[quarter, :] = up_ref[:, quarter].T


def backward_kernel(
    places_down, places_up, place_ref, grad_ref, hidden_ref, slope_ref, normed_ref, normed_t_ref, factor_ref,
    up_t_ref, down_ref, d_pre_ref, grad_t_ref, *rest
):
    blocks, work_ref = rest[:-1], rest[-1]
    pairs = MEMBERS // 2 * work_ref.shape[1]
    hidden_units = down_ref.shape[1]
    last = len(MASKS) - 1
    for section in range(last, -1, -1):
        mask = MASKS[section]
        at = pl.ds(section * pairs, pairs)
        if section == last:
            pair_grad = read_pair(grad_ref, mask, swapped=place_ref[0])
        else:
            pair_grad = read_pair(work_ref, mask)
        pair_bf = pair_grad.astype(jnp.bfloat16)
        for start in range(0, hidden_units, CHUNK):
            units = pl.ds(start, CHUNK)
            d_hidden = jnp.dot(pair_bf, down_ref[:, units], preferred_element_type=jnp.float32)
            d_pre_ref[at, units] = (d_hidden * slope_ref[at, units].astype(jnp.float32)).astype(jnp.bfloat16)
        if section > 0:
            d_norm = jnp.dot(d_pre_ref[at, :], up_t_ref[...], preferred_element_type=jnp.float32)
            normed = normed_ref[at, :].astype(jnp.float32)
            d_pair = factor_ref[at, :][:, :1] * (
                d_norm
                - jnp.mean(d_norm, axis=-1, keepdims=True)
                - normed * jnp.mean(d_norm * normed, axis=-1, keepdims=True)
            )
            write_pair(work_ref, mask, (pair_grad + d_pair).astype(jnp.bfloat16))
        grad_t_ref[:, at] = pair_bf.T

    if blocks:
        write_blocks(places_down, place_ref[1], grad_t_ref, hidden_ref, blocks[0])
        write_blocks(places_up, place_ref[1], normed_t_ref, d_pre_ref, blocks[1])


def keep_kernel(
    places_down, places_up, place_ref, hidden_ref, d_pre_ref, normed_t_ref, grad_t_ref, down_ref, up_ref
):
    write_blocks(places_down, 1 - place_ref[1], grad_t_ref, hidden_ref, down_ref)
    write_blocks(places_up, 1 - place_ref[1], normed_t_ref, d_pre_ref, up_ref)


def settle_kernel(sources, place_ref, *refs):
    parts, out_ref, done = refs[:-2], refs[-2], refs[-1]
    count, rows = parts[0].shape[:2]
    copies = []
    for index, source in enumerate(sources):
        block = parts[index // count].at[index % count]
        first = pl.multiple_of((place_ref[0] ^ source) * rows, rows)
        copies.append(pltpu.make_async_copy(block, out_ref.at[pl.ds(first, rows)], done.at[index]))
    for copy in copies:
        copy.start()
    for copy in copies:
        copy.wait()


def spec(space):
    return pl.BlockSpec(memory_space=space)


def block_places(order, span_x, span_y):
    places = []
    for at_x in range(span_x):
        line = []
        for group in range(span_y // 2):
            place = 0
            for axis, step in order:
                at = at_x if axis == "gx" else 2 * group
                place = 2 * place + (at >> step & 1)
            line.append(place)
        places.append(line)
    return places


def in_vmem(*items):
    return [pltpu.with_memory_space_constraint(item, pltpu.VMEM) for item in items]


def load(place, weight):
    return pl.pallas_call(
        load_kernel,
        out_shape=pltpu.VMEM(weight.shape, weight.dtype),
        in_specs=[spec(pltpu.SMEM), spec(pltpu.HBM)],
        out_specs=spec(pltpu.VMEM),
        scratch_shapes=[pltpu.SemaphoreType.DMA],
        compiler_params=pltpu.CompilerParams(vmem_limit_bytes=KEEP_BYTES),
        cost_estimate=pl.CostEstimate(flops=0, bytes_accessed=4 * weight.size, transcendentals=0),
    )(place, pltpu.with_memory_space_constraint(weight, pltpu.HBM))


def forward(state, up, w_down):
    members, rows, width = state.shape
    total = len(MASKS) * (members // 2) * rows
    depth, units = up.shape
    bf16 = jnp.bfloat16
    outs = [
        pltpu.VMEM(state.shape, bf16),
        pltpu.VMEM((total, units), bf16),
        pltpu.VMEM((total, units), bf16),
        pltpu.VMEM((total, depth), bf16),
        pltpu.VMEM((depth, total), bf16),
        pltpu.VMEM((total, LANES), jnp.float32),
        pltpu.VMEM((units, depth), bf16),
        pltpu.VMEM(w_down.shape, bf16),
    ]
    return pl.pallas_call(
        forward_kernel,
        out_shape=outs,
        in_specs=[spec(pltpu.VMEM)] * 2 + [spec(pltpu.HBM)],
        out_specs=[spec(pltpu.VMEM)] * len(outs),
        scratch_shapes=[pltpu.VMEM(state.shape, bf16), pltpu.SemaphoreType.DMA],
        compiler_params=pltpu.CompilerParams(vmem_limit_bytes=SECTIONS_BYTES),
        cost_estimate=pl.CostEstimate(
            flops=10 * total * depth * units, bytes_accessed=16 * total * units, transcendentals=0
        ),
    )(state, *in_vmem(up), pltpu.with_memory_space_constraint(w_down, pltpu.HBM))


def backward(place, grad, kept, places, block):
    total, units = kept[0].shape
    depth = kept[2].shape[1]
    bf16 = jnp.bfloat16
    outs = [pltpu.VMEM((total, units), bf16), pltpu.VMEM((depth, total), bf16)]
    outs += [block] * 2 if block else []
    return pl.pallas_call(
        functools.partial(backward_kernel, *places),
        out_shape=outs,
        in_specs=[spec(pltpu.SMEM)] + [spec(pltpu.VMEM)] * (1 + len(kept)),
        out_specs=[spec(pltpu.VMEM)] * len(outs),
        scratch_shapes=[pltpu.VMEM(grad.shape, bf16)],
        compiler_params=pltpu.CompilerParams(vmem_limit_bytes=SECTIONS_BYTES),
        cost_estimate=pl.CostEstimate(
            flops=10 * total * depth * units, bytes_accessed=16 * total * units, transcendentals=0
        ),
    )(place, grad, *in_vmem(*kept))


def keep_blocks(place, hidden, d_pre, normed_t, grad_t, places, block):
    total, units = hidden.shape
    depth = normed_t.shape[0]
    return pl.pallas_call(
        functools.partial(keep_kernel, *places),
        out_shape=[block] * 2,
        in_specs=[spec(pltpu.SMEM)] + [spec(pltpu.VMEM)] * 4,
        out_specs=[spec(pltpu.VMEM)] * 2,
        compiler_params=pltpu.CompilerParams(vmem_limit_bytes=KEEP_BYTES),
        cost_estimate=pl.CostEstimate(
            flops=2 * total * depth * units, bytes_accessed=8 * total * units, transcendentals=0
        ),
    )(place, *in_vmem(hidden, d_pre, normed_t, grad_t))


def swap(block, axis, bit):
    pairs = [(source, source ^ (1 << bit)) for source in range(lax.axis_size(axis))]
    return lax.ppermute(block, axis, pairs)


def pick(block, at):
    return slice_at(block, 0, at).astype(jnp.float32)


def finish_sum(halves, kept, taken, order, beside=None):
    for phase, step in enumerate(order):
        mine, other = halves[step]
        shape = (2, kept.shape[0] // 2) + kept.shape[1:]
        kept, taken = kept.reshape(shape), taken.reshape(shape)
        give = (pick(kept, other) + pick(taken, other)).astype(jnp.bfloat16)
        kept = (pick(kept, mine) + pick(taken, mine)).astype(jnp.bfloat16)
        if beside:
            give = beside(phase, give)
        taken = swap(give, *step)
    return (kept.astype(jnp.float32) + taken.astype(jnp.float32))[0]


def scatter_narrow(halves, left, right, order, span_x, span_y):
    total = jnp.dot(left, right, preferred_element_type=jnp.float32).astype(jnp.bfloat16)
    rows, columns = left.shape[0] // span_x, right.shape[1] // span_y
    count_x, count_y = span_x.bit_length() - 1, span_y.bit_length() - 1
    dims = [("gx", bit) for bit in range(count_x)][::-1] + ["rows"]
    dims += [("gy", bit) for bit in range(count_y)][::-1] + ["columns"]
    blocks = total.reshape((2,) * count_x + (rows,) + (2,) * count_y + (columns,))
    blocks = blocks.transpose([dims.index(item) for item in list(order) + ["rows", "columns"]])
    blocks = blocks.reshape(-1, rows, columns)
    return finish_sum(halves, blocks, jnp.zeros_like(blocks), order)


class Journey:
    def __init__(self, held, bits=(0, 1, 2, 3), sources=(0,)):
        self.held = held
        self.bits = list(bits)
        self.sources = list(sources)
        self.parts = None

    def hop(self, at, steps, halves, after=None):
        dim = self.bits.index(at)
        mine, other = halves[steps[at]]
        kept, given = [slice_at(self.held, dim, part) for part in (mine, other)]
        if after is not None:
            given, after = lax.optimization_barrier((given, after))
        self.parts = [kept, swap(given, *steps[at])]
        self.held = jnp.concatenate(self.parts, -3)
        self.bits.remove(at)
        self.sources += [source | MASKS[at] for source in self.sources]
        return after

    def hop_both(self, at, also, steps, halves, after=None):
        dims = self.bits.index(at), self.bits.index(also)
        parts = []
        for theirs, beyond in ((0, 0), (1, 0), (0, 1), (1, 1)):
            part = slice_at(self.held, dims[0], halves[steps[at]][theirs], keep=True)
            part = slice_at(part, dims[1], halves[steps[also]][beyond], keep=True)
            parts.append(lax.squeeze(part, dims))
        if after is not None:
            parts, after = lax.optimization_barrier((parts, after))
        self.parts = [
            parts[0],
            swap(parts[1], *steps[at]),
            swap(parts[2], *steps[also]),
            swap_both(parts[3], steps[at], steps[also]),
        ]
        self.held = jnp.concatenate(self.parts, -3)
        for bit in (at, also):
            self.bits.remove(bit)
            self.sources += [source | MASKS[bit] for source in self.sources]
        return after


def slice_at(block, dim, at, keep=False):
    start = [0] * block.ndim
    start[dim] = at
    size = list(block.shape)
    size[dim] = 1
    part = lax.dynamic_slice(block, start, size, allow_negative_indices=False)
    return part if keep else lax.squeeze(part, (dim,))


def swap_both(block, step, also):
    span_x, span_y = lax.axis_size("gx"), lax.axis_size("gy")
    flips = {step[0]: 1 << step[1], also[0]: 1 << also[1]}
    pairs = []
    for at_x in range(span_x):
        for at_y in range(span_y):
            pairs.append((at_x * span_y + at_y, (at_x ^ flips["gx"]) * span_y + (at_y ^ flips["gy"])))
    return lax.ppermute(block, ("gx", "gy"), pairs)


def settle(place, journey):
    parts = journey.parts
    rows, width = parts[0].shape[-2:]
    return pl.pallas_call(
        functools.partial(settle_kernel, journey.sources),
        out_shape=jax.ShapeDtypeStruct((MEMBERS * rows, width), parts[0].dtype),
        in_specs=[spec(pltpu.SMEM)] + [spec(pltpu.VMEM)] * len(parts),
        out_specs=spec(pltpu.HBM),
        scratch_shapes=[pltpu.SemaphoreType.DMA((MEMBERS,))],
        cost_estimate=pl.CostEstimate(flops=0, bytes_accessed=4 * MEMBERS * rows * width, transcendentals=0),
    )(place, *parts)


def local(signal, w_up, w_down, cotangent):
    span_x = lax.axis_size("gx")
    span_y = lax.axis_size("gy")
    groups = section_groups(span_x, span_y)
    rows, width = signal.shape
    depth, units = w_up.shape
    steps = [("gx", span_x.bit_length() - 2), ("gx", 0), ("gy", span_y.bit_length() - 2), ("gy", 0)]
    z, y, x, core = range(4)
    rest_y = [("gy", bit) for bit in range(1, span_y.bit_length() - 1)]
    rest_x = [("gx", bit) for bit in range(1, span_x.bit_length() - 1)]
    order_down = [steps[y]] + rest_y + rest_x[::-1]
    order_up = rest_y + [steps[y]] + rest_x

    owns = [lax.axis_index(axis) // (1 << bit) % 2 for axis, bit in [steps[core]] + order_up]
    own = dict(zip([steps[core]] + order_up, owns))
    member = sum(own[step] * mask for step, mask in zip(steps, MASKS))
    place = jnp.stack([member, 1 - own[steps[core]]]).astype(jnp.int32)
    place, owns, others = lax.optimization_barrier((place, owns, [1 - item for item in owns]))
    halves = {step: pair for step, pair in zip([steps[core]] + order_up, zip(owns, others))}
    places = [block_places(order, span_x, span_y) for order in (order_down, order_up)]
    block = None
    if units // span_y % LANES == 0:
        block = pltpu.VMEM((span_x * span_y // 2, depth // span_x, units // span_y), jnp.bfloat16)

    parts = (2, 2, 2, 2, 1, rows // MEMBERS, width)
    state = exchange(signal.reshape(MEMBERS, rows // MEMBERS, width), groups)
    coming = Journey(cotangent.reshape(parts))
    coming.hop(core, steps, halves)
    coming.hop_both(x, y, steps, halves)
    up = load(place, w_up)
    state = coming.hop(z, steps, halves, state)
    state, *kept = forward(state, up, w_down)
    going = Journey(state.reshape(parts))
    grad = going.hop(z, steps, halves, coming.held)
    d_pre, grad_t, *given = backward(place, grad, kept, places, block)
    hidden, normed_t = kept[0], kept[3]
    if not given:
        going.hop(core, steps, halves)
        going.hop_both(x, y, steps, halves)
        mixed_out = settle(place, going)
        grad_down = scatter_narrow(halves, grad_t, hidden, [steps[core]] + order_down, span_x, span_y)
        grad_up = scatter_narrow(halves, normed_t, d_pre, [steps[core]] + order_up, span_x, span_y)
        return (mixed_out, grad_up, grad_down)
    take_down, take_up = [swap(part, *steps[core]) for part in given]
    keep_down, keep_up = keep_blocks(place, hidden, d_pre, normed_t, grad_t, places, block)

    def beside(phase, give):
        if phase == 1:
            return going.hop(core, steps, halves, give)
        if phase == 2:
            return going.hop_both(x, y, steps, halves, give)
        if phase == len(order_down) - 1:
            going.parts, give = lax.optimization_barrier((going.parts, give))
        return give

    grad_up = finish_sum(halves, keep_up, take_up, order_up)
    grad_down = finish_sum(halves, keep_down, take_down, order_down, beside)
    return (settle(place, going), grad_up, grad_down)


def solution(mesh):
    return jax.shard_map(
        local,
        mesh=mesh,
        in_specs=(P(("gx", "gy"), None), P(), P(), P(("gx", "gy"), None)),
        out_specs=(P(("gx", "gy"), None), P("gx", "gy"), P("gx", "gy")),
        check_vma=False,
    )
```

```python
import functools
import math

import jax
import jax.numpy as jnp
from jax import lax
from jax.experimental import pallas as pl
from jax.experimental.pallas import tpu as pltpu
from jax.sharding import PartitionSpec as P

MEMBERS = 16
MASKS = (8, 4, 2, 1)
LANES = 128
CHUNK = 256
SECTIONS_BYTES = 8 * 1024 * 1024
KEEP_BYTES = 4 * 1024 * 1024


def section_groups(span_x, span_y):
    bits_x = [span_x.bit_length() - 2, 0]
    bits_y = [span_y.bit_length() - 2, 0]
    mask_x = sum(1 << bit for bit in bits_x)
    mask_y = sum(1 << bit for bit in bits_y)
    groups = []
    for base_x in range(span_x):
        for base_y in range(span_y):
            if base_x & mask_x or base_y & mask_y:
                continue
            group = []
            for member in range(MEMBERS):
                at_x, at_y = base_x, base_y
                at_x |= (member >> 3 & 1) << bits_x[0] | (member >> 2 & 1) << bits_x[1]
                at_y |= (member >> 1 & 1) << bits_y[0] | (member & 1) << bits_y[1]
                group.append(at_x * span_y + at_y)
            groups.append(group)
    return groups


def exchange(block, groups):
    return lax.all_to_all(
        block, ("gx", "gy"), split_axis=0, concat_axis=0, axis_index_groups=groups, tiled=True
    )


def contract_last(left, right):
    return lax.dot_general(
        left, right, (((1,), (1,)), ((), ())), preferred_element_type=jnp.float32
    )


def low_members(mask):
    return [member for member in range(MEMBERS) if not member & mask]


def read_pair(ref, mask, swapped=0):
    low = jnp.concatenate([ref[member ^ swapped] for member in low_members(mask)], 0)
    high = jnp.concatenate([ref[(member | mask) ^ swapped] for member in low_members(mask)], 0)
    return jnp.concatenate([low, high], 1).astype(jnp.float32)


def write_pair(ref, mask, pair):
    rows, width = ref.shape[1:]
    for place, member in enumerate(low_members(mask)):
        part = pair[place * rows : (place + 1) * rows]
        ref[member] = part[:, :width]
        ref[member | mask] = part[:, width:]


def write_blocks(places, bit, left_ref, right_ref, out_ref):
    rows, columns = out_ref.shape[1:]
    pieces = []
    for group in range(len(places[0])):
        base = (2 * group + bit) * columns
        for inner in range(0, columns, LANES):
            pieces.append((group, inner, pl.multiple_of(base + inner, LANES)))
    for first in range(0, len(pieces), 2):
        some = pieces[first : first + 2]
        right = jnp.concatenate([right_ref[:, pl.ds(start, LANES)] for _, _, start in some], 1)
        total = jnp.dot(left_ref[...], right, preferred_element_type=jnp.float32)
        total = total.astype(jnp.bfloat16)
        for which, (group, inner, _) in enumerate(some):
            for block in range(len(places)):
                out_ref[places[block][group], :, inner : inner + LANES] = total[
                    block * rows : (block + 1) * rows, which * LANES : (which + 1) * LANES
                ]


def load_kernel(place_ref, source, target, arrived):
    copy = pltpu.make_async_copy(source, target, arrived)
    copy.start()
    copy.wait()


def forward_kernel(
    state_ref, up_ref, down_hbm,
    out_ref, hidden_ref, slope_ref, normed_ref, normed_t_ref, factor_ref, down_ref, work_ref, arrived
):
    fetch_down = pltpu.make_async_copy(down_hbm, down_ref, arrived)
    fetch_down.start()
    pairs = MEMBERS // 2 * work_ref.shape[1]
    hidden_units = up_ref.shape[1]
    last = len(MASKS) - 1
    for section, mask in enumerate(MASKS):
        at = pl.ds(section * pairs, pairs)
        pair = read_pair(state_ref if section == 0 else work_ref, mask)
        centre = jnp.mean(pair, axis=-1, keepdims=True)
        shifted = pair - centre
        spread = jnp.mean(shifted * shifted, axis=-1, keepdims=True)
        factor = lax.rsqrt(spread + 1e-05)
        normed = (shifted * factor).astype(jnp.bfloat16)
        normed_ref[at, :] = normed
        factor_ref[at, :] = jnp.broadcast_to(factor, (pairs, LANES))
        for start in range(0, hidden_units, CHUNK):
            units = pl.ds(start, CHUNK)
            pre = jnp.dot(normed, up_ref[:, units], preferred_element_type=jnp.float32)
            share = 0.5 * (1.0 + lax.erf(pre * (1.0 / math.sqrt(2.0))))
            hidden_ref[at, units] = (pre * share).astype(jnp.bfloat16)
            bell = jnp.exp(-0.5 * pre * pre) * (1.0 / math.sqrt(2.0 * math.pi))
            slope_ref[at, units] = (share + pre * bell).astype(jnp.bfloat16)
        if section == 0:
            fetch_down.wait()
        mixed = (pair + contract_last(hidden_ref[at, :], down_ref[...])).astype(jnp.bfloat16)
        write_pair(work_ref if section < last else out_ref, mask, mixed)
        normed_t_ref[:, at] = normed.T


def backward_kernel(
    places_down, places_up, place_ref, grad_ref, hidden_ref, slope_ref, normed_ref, normed_t_ref, factor_ref,
    up_ref, down_ref, d_pre_ref, grad_t_ref, *rest
):
    blocks, work_ref = rest[:-1], rest[-1]
    pairs = MEMBERS // 2 * work_ref.shape[1]
    hidden_units = up_ref.shape[1]
    last = len(MASKS) - 1
    for section in range(last, -1, -1):
        mask = MASKS[section]
        at = pl.ds(section * pairs, pairs)
        if section == last:
            pair_grad = read_pair(grad_ref, mask, swapped=place_ref[0])
        else:
            pair_grad = read_pair(work_ref, mask)
        pair_bf = pair_grad.astype(jnp.bfloat16)
        for start in range(0, hidden_units, CHUNK):
            units = pl.ds(start, CHUNK)
            d_hidden = jnp.dot(pair_bf, down_ref[:, units], preferred_element_type=jnp.float32)
            d_pre_ref[at, units] = (d_hidden * slope_ref[at, units].astype(jnp.float32)).astype(jnp.bfloat16)
        if section > 0:
            d_norm = contract_last(d_pre_ref[at, :], up_ref[...])
            normed = normed_ref[at, :].astype(jnp.float32)
            d_pair = factor_ref[at, :][:, :1] * (
                d_norm
                - jnp.mean(d_norm, axis=-1, keepdims=True)
                - normed * jnp.mean(d_norm * normed, axis=-1, keepdims=True)
            )
            write_pair(work_ref, mask, (pair_grad + d_pair).astype(jnp.bfloat16))
        grad_t_ref[:, at] = pair_bf.T

    if blocks:
        write_blocks(places_down, place_ref[1], grad_t_ref, hidden_ref, blocks[0])
        write_blocks(places_up, place_ref[1], normed_t_ref, d_pre_ref, blocks[1])


def keep_kernel(
    places_down, places_up, place_ref, hidden_ref, d_pre_ref, normed_t_ref, grad_t_ref, down_ref, up_ref
):
    write_blocks(places_down, 1 - place_ref[1], grad_t_ref, hidden_ref, down_ref)
    write_blocks(places_up, 1 - place_ref[1], normed_t_ref, d_pre_ref, up_ref)


def settle_kernel(sources, place_ref, *refs):
    parts, out_ref, done = refs[:-2], refs[-2], refs[-1]
    count, rows = parts[0].shape[:2]
    copies = []
    for index, source in enumerate(sources):
        block = parts[index // count].at[index % count]
        first = pl.multiple_of((place_ref[0] ^ source) * rows, rows)
        copies.append(pltpu.make_async_copy(block, out_ref.at[pl.ds(first, rows)], done.at[index]))
    for copy in copies:
        copy.start()
    for copy in copies:
        copy.wait()


def spec(space):
    return pl.BlockSpec(memory_space=space)


def block_places(order, span_x, span_y):
    places = []
    for at_x in range(span_x):
        line = []
        for group in range(span_y // 2):
            place = 0
            for axis, step in order:
                at = at_x if axis == "gx" else 2 * group
                place = 2 * place + (at >> step & 1)
            line.append(place)
        places.append(line)
    return places


def in_vmem(*items):
    return [pltpu.with_memory_space_constraint(item, pltpu.VMEM) for item in items]


def load(place, weight):
    return pl.pallas_call(
        load_kernel,
        out_shape=pltpu.VMEM(weight.shape, weight.dtype),
        in_specs=[spec(pltpu.SMEM), spec(pltpu.HBM)],
        out_specs=spec(pltpu.VMEM),
        scratch_shapes=[pltpu.SemaphoreType.DMA],
        compiler_params=pltpu.CompilerParams(vmem_limit_bytes=KEEP_BYTES),
        cost_estimate=pl.CostEstimate(flops=0, bytes_accessed=4 * weight.size, transcendentals=0),
    )(place, pltpu.with_memory_space_constraint(weight, pltpu.HBM))


def forward(state, up, w_down):
    members, rows, width = state.shape
    total = len(MASKS) * (members // 2) * rows
    depth, units = up.shape
    bf16 = jnp.bfloat16
    outs = [
        pltpu.VMEM(state.shape, bf16),
        pltpu.VMEM((total, units), bf16),
        pltpu.VMEM((total, units), bf16),
        pltpu.VMEM((total, depth), bf16),
        pltpu.VMEM((depth, total), bf16),
        pltpu.VMEM((total, LANES), jnp.float32),
        pltpu.VMEM(w_down.shape, bf16),
    ]
    return pl.pallas_call(
        forward_kernel,
        out_shape=outs,
        in_specs=[spec(pltpu.VMEM)] * 2 + [spec(pltpu.HBM)],
        out_specs=[spec(pltpu.VMEM)] * len(outs),
        scratch_shapes=[pltpu.VMEM(state.shape, bf16), pltpu.SemaphoreType.DMA],
        compiler_params=pltpu.CompilerParams(vmem_limit_bytes=SECTIONS_BYTES),
        cost_estimate=pl.CostEstimate(
            flops=10 * total * depth * units, bytes_accessed=16 * total * units, transcendentals=0
        ),
    )(state, *in_vmem(up), pltpu.with_memory_space_constraint(w_down, pltpu.HBM))


def backward(place, grad, kept, places, block):
    total, units = kept[0].shape
    depth = kept[2].shape[1]
    bf16 = jnp.bfloat16
    outs = [pltpu.VMEM((total, units), bf16), pltpu.VMEM((depth, total), bf16)]
    outs += [block] * 2 if block else []
    return pl.pallas_call(
        functools.partial(backward_kernel, *places),
        out_shape=outs,
        in_specs=[spec(pltpu.SMEM)] + [spec(pltpu.VMEM)] * (1 + len(kept)),
        out_specs=[spec(pltpu.VMEM)] * len(outs),
        scratch_shapes=[pltpu.VMEM(grad.shape, bf16)],
        compiler_params=pltpu.CompilerParams(vmem_limit_bytes=SECTIONS_BYTES),
        cost_estimate=pl.CostEstimate(
            flops=10 * total * depth * units, bytes_accessed=16 * total * units, transcendentals=0
        ),
    )(place, grad, *in_vmem(*kept))


def keep_blocks(place, hidden, d_pre, normed_t, grad_t, places, block):
    total, units = hidden.shape
    depth = normed_t.shape[0]
    return pl.pallas_call(
        functools.partial(keep_kernel, *places),
        out_shape=[block] * 2,
        in_specs=[spec(pltpu.SMEM)] + [spec(pltpu.VMEM)] * 4,
        out_specs=[spec(pltpu.VMEM)] * 2,
        compiler_params=pltpu.CompilerParams(vmem_limit_bytes=KEEP_BYTES),
        cost_estimate=pl.CostEstimate(flops=0, bytes_accessed=0, transcendentals=0),
    )(place, *in_vmem(hidden, d_pre, normed_t, grad_t))


def swap(block, axis, bit):
    pairs = [(source, source ^ (1 << bit)) for source in range(lax.axis_size(axis))]
    return lax.ppermute(block, axis, pairs)


def pick(block, at):
    return slice_at(block, 0, at).astype(jnp.float32)


def halve(halves, step, kept, taken):
    mine, other = halves[step]
    shape = (2, kept.shape[0] // 2) + kept.shape[1:]
    kept, taken = kept.reshape(shape), taken.reshape(shape)
    give = (pick(kept, other) + pick(taken, other)).astype(jnp.bfloat16)
    keep = (pick(kept, mine) + pick(taken, mine)).astype(jnp.bfloat16)
    return keep, give


def last_sum(kept, taken):
    return (kept.astype(jnp.float32) + taken.astype(jnp.float32))[0]


def finish_sum(halves, kept, taken, order):
    for step in order:
        kept, give = halve(halves, step, kept, taken)
        taken = swap(give, *step)
    return last_sum(kept, taken)


def scatter_narrow(halves, left, right, order, span_x, span_y):
    total = jnp.dot(left, right, preferred_element_type=jnp.float32).astype(jnp.bfloat16)
    rows, columns = left.shape[0] // span_x, right.shape[1] // span_y
    count_x, count_y = span_x.bit_length() - 1, span_y.bit_length() - 1
    dims = [("gx", bit) for bit in range(count_x)][::-1] + ["rows"]
    dims += [("gy", bit) for bit in range(count_y)][::-1] + ["columns"]
    blocks = total.reshape((2,) * count_x + (rows,) + (2,) * count_y + (columns,))
    blocks = blocks.transpose([dims.index(item) for item in list(order) + ["rows", "columns"]])
    blocks = blocks.reshape(-1, rows, columns)
    return finish_sum(halves, blocks, jnp.zeros_like(blocks), order)


class Journey:
    def __init__(self, held, bits=(0, 1, 2, 3), sources=(0,)):
        self.held = held
        self.bits = list(bits)
        self.sources = list(sources)
        self.parts = None

    def hop(self, at, steps, halves, after=None):
        dim = self.bits.index(at)
        mine, other = halves[steps[at]]
        kept, given = [slice_at(self.held, dim, part) for part in (mine, other)]
        if after is not None:
            given, after = lax.optimization_barrier((given, after))
        self.parts = [kept, swap(given, *steps[at])]
        self.held = jnp.concatenate(self.parts, -3)
        self.bits.remove(at)
        self.sources += [source | MASKS[at] for source in self.sources]
        return after

    def hop_both(self, at, also, steps, halves, after=None):
        dims = self.bits.index(at), self.bits.index(also)
        parts = []
        for theirs, beyond in ((0, 0), (1, 0), (0, 1), (1, 1)):
            part = slice_at(self.held, dims[0], halves[steps[at]][theirs], keep=True)
            part = slice_at(part, dims[1], halves[steps[also]][beyond], keep=True)
            parts.append(lax.squeeze(part, dims))
        if after is not None:
            parts, after = lax.optimization_barrier((parts, after))
        self.parts = [
            parts[0],
            swap(parts[1], *steps[at]),
            swap(parts[2], *steps[also]),
            swap_both(parts[3], steps[at], steps[also]),
        ]
        self.held = jnp.concatenate(self.parts, -3)
        for bit in (at, also):
            self.bits.remove(bit)
            self.sources += [source | MASKS[bit] for source in self.sources]
        return after


def slice_at(block, dim, at, keep=False):
    start = [0] * block.ndim
    start[dim] = at
    size = list(block.shape)
    size[dim] = 1
    part = lax.dynamic_slice(block, start, size, allow_negative_indices=False)
    return part if keep else lax.squeeze(part, (dim,))


def swap_both(block, step, also):
    span_x, span_y = lax.axis_size("gx"), lax.axis_size("gy")
    flips = {step[0]: 1 << step[1], also[0]: 1 << also[1]}
    pairs = []
    for at_x in range(span_x):
        for at_y in range(span_y):
            pairs.append((at_x * span_y + at_y, (at_x ^ flips["gx"]) * span_y + (at_y ^ flips["gy"])))
    return lax.ppermute(block, ("gx", "gy"), pairs)


def settle(place, journey):
    parts = journey.parts
    rows, width = parts[0].shape[-2:]
    return pl.pallas_call(
        functools.partial(settle_kernel, journey.sources),
        out_shape=jax.ShapeDtypeStruct((MEMBERS * rows, width), parts[0].dtype),
        in_specs=[spec(pltpu.SMEM)] + [spec(pltpu.VMEM)] * len(parts),
        out_specs=spec(pltpu.HBM),
        scratch_shapes=[pltpu.SemaphoreType.DMA((MEMBERS,))],
        cost_estimate=pl.CostEstimate(flops=0, bytes_accessed=0, transcendentals=0),
    )(place, *parts)


def local(signal, w_up, w_down, cotangent):
    span_x = lax.axis_size("gx")
    span_y = lax.axis_size("gy")
    groups = section_groups(span_x, span_y)
    rows, width = signal.shape
    depth, units = w_up.shape
    steps = [("gx", span_x.bit_length() - 2), ("gx", 0), ("gy", span_y.bit_length() - 2), ("gy", 0)]
    z, y, x, core = range(4)
    rest_y = [("gy", bit) for bit in range(1, span_y.bit_length() - 1)]
    rest_x = [("gx", bit) for bit in range(1, span_x.bit_length() - 1)]
    order_down = [steps[y]] + rest_y + rest_x
    order_up = rest_y + [steps[y]] + rest_x[::-1]

    owns = [lax.axis_index(axis) // (1 << bit) % 2 for axis, bit in [steps[core]] + order_up]
    own = dict(zip([steps[core]] + order_up, owns))
    member = sum(own[step] * mask for step, mask in zip(steps, MASKS))
    place = jnp.stack([member, 1 - own[steps[core]]]).astype(jnp.int32)
    place, owns, others = lax.optimization_barrier((place, owns, [1 - item for item in owns]))
    halves = {step: pair for step, pair in zip([steps[core]] + order_up, zip(owns, others))}
    places = [block_places(order, span_x, span_y) for order in (order_down, order_up)]
    block = None
    if units // span_y % LANES == 0:
        block = pltpu.VMEM((span_x * span_y // 2, depth // span_x, units // span_y), jnp.bfloat16)

    parts = (2, 2, 2, 2, 1, rows // MEMBERS, width)
    state = exchange(signal.reshape(MEMBERS, rows // MEMBERS, width), groups)
    coming = Journey(cotangent.reshape(parts))
    coming.hop(core, steps, halves)
    coming.hop_both(x, y, steps, halves)
    up = load(place, w_up)
    state = coming.hop(z, steps, halves, state)
    state, *kept, down = forward(state, up, w_down)
    kept += [up, down]
    going = Journey(state.reshape(parts))
    grad = going.hop(z, steps, halves, coming.held)
    d_pre, grad_t, *given = backward(place, grad, kept, places, block)
    hidden, normed_t = kept[0], kept[3]
    if not given:
        going.hop(core, steps, halves)
        going.hop_both(x, y, steps, halves)
        mixed_out = settle(place, going)
        grad_down = scatter_narrow(halves, grad_t, hidden, [steps[core]] + order_down, span_x, span_y)
        grad_up = scatter_narrow(halves, normed_t, d_pre, [steps[core]] + order_up, span_x, span_y)
        return (mixed_out, grad_up, grad_down)
    take_down, take_up = [swap(part, *steps[core]) for part in given]
    keep_down, keep_up = keep_blocks(place, hidden, d_pre, normed_t, grad_t, places, block)

    barrier = lax.optimization_barrier
    for phase, (step_down, step_up) in enumerate(zip(order_down, order_up)):
        ending = phase == len(order_down) - 1
        if not ending:
            keep_up, give_up = halve(halves, step_up, keep_up, take_up)
            take_up = swap(give_up, *step_up)
        keep_down, give_down = halve(halves, step_down, keep_down, take_down)
        if phase == 1:
            give_down = going.hop(core, steps, halves, give_down)
        if phase == 2:
            give_down = going.hop_both(x, y, steps, halves, give_down)
        take_down = swap(give_down, *step_down)
        if ending:
            take_up, give_down = barrier((take_up, give_down))
            keep_up, give_up = halve(halves, step_up, keep_up, take_up)
            going.parts, give_up = barrier((going.parts, give_up))
            take_up = swap(give_up, *step_up)
    return (settle(place, going), last_sum(keep_up, take_up), last_sum(keep_down, take_down))


def solution(mesh):
    return jax.shard_map(
        local,
        mesh=mesh,
        in_specs=(P(("gx", "gy"), None), P(), P(), P(("gx", "gy"), None)),
        out_specs=(P(("gx", "gy"), None), P("gx", "gy"), P("gx", "gy")),
        check_vma=False,
    )
```

```python
import functools
import math

import jax
import jax.numpy as jnp
from jax import lax
from jax.experimental import pallas as pl
from jax.experimental.pallas import tpu as pltpu
from jax.sharding import PartitionSpec as P

MEMBERS = 16
MASKS = (8, 4, 2, 1)
LANES = 128
CHUNK = 256
SECTIONS_BYTES = 8 * 1024 * 1024
KEEP_BYTES = 4 * 1024 * 1024


def section_groups(span_x, span_y):
    bits_x = [span_x.bit_length() - 2, 0]
    bits_y = [span_y.bit_length() - 2, 0]
    mask_x = sum(1 << bit for bit in bits_x)
    mask_y = sum(1 << bit for bit in bits_y)
    groups = []
    for base_x in range(span_x):
        for base_y in range(span_y):
            if base_x & mask_x or base_y & mask_y:
                continue
            group = []
            for member in range(MEMBERS):
                at_x, at_y = base_x, base_y
                at_x |= (member >> 3 & 1) << bits_x[0] | (member >> 2 & 1) << bits_x[1]
                at_y |= (member >> 1 & 1) << bits_y[0] | (member & 1) << bits_y[1]
                group.append(at_x * span_y + at_y)
            groups.append(group)
    return groups


def exchange(block, groups):
    return lax.all_to_all(
        block, ("gx", "gy"), split_axis=0, concat_axis=0, axis_index_groups=groups, tiled=True
    )


def contract_last(left, right):
    return lax.dot_general(
        left, right, (((1,), (1,)), ((), ())), preferred_element_type=jnp.float32
    )


def low_members(mask):
    return [member for member in range(MEMBERS) if not member & mask]


def read_pair(ref, mask, swapped=0):
    low = jnp.concatenate([ref[member ^ swapped] for member in low_members(mask)], 0)
    high = jnp.concatenate([ref[(member | mask) ^ swapped] for member in low_members(mask)], 0)
    return jnp.concatenate([low, high], 1).astype(jnp.float32)


def write_pair(ref, mask, pair):
    rows, width = ref.shape[1:]
    for place, member in enumerate(low_members(mask)):
        part = pair[place * rows : (place + 1) * rows]
        ref[member] = part[:, :width]
        ref[member | mask] = part[:, width:]


def write_blocks(places, bit, left_ref, right_ref, out_ref):
    rows, columns = out_ref.shape[1:]
    pieces = []
    for group in range(len(places[0])):
        base = (2 * group + bit) * columns
        for inner in range(0, columns, LANES):
            pieces.append((group, inner, pl.multiple_of(base + inner, LANES)))
    for first in range(0, len(pieces), 2):
        some = pieces[first : first + 2]
        right = jnp.concatenate([right_ref[:, pl.ds(start, LANES)] for _, _, start in some], 1)
        total = jnp.dot(left_ref[...], right, preferred_element_type=jnp.float32)
        total = total.astype(jnp.bfloat16)
        for which, (group, inner, _) in enumerate(some):
            for block in range(len(places)):
                out_ref[places[block][group], :, inner : inner + LANES] = total[
                    block * rows : (block + 1) * rows, which * LANES : (which + 1) * LANES
                ]


def load_kernel(place_ref, source, target, arrived):
    copy = pltpu.make_async_copy(source, target, arrived)
    copy.start()
    copy.wait()


def forward_kernel(
    state_ref, up_ref, down_hbm,
    out_ref, hidden_ref, slope_ref, normed_ref, normed_t_ref, factor_ref, up_t_ref, down_ref, work_ref, arrived
):
    fetch_down = pltpu.make_async_copy(down_hbm, down_ref, arrived)
    fetch_down.start()
    pairs = MEMBERS // 2 * work_ref.shape[1]
    hidden_units = up_ref.shape[1]
    last = len(MASKS) - 1
    for section, mask in enumerate(MASKS):
        at = pl.ds(section * pairs, pairs)
        pair = read_pair(state_ref if section == 0 else work_ref, mask)
        centre = jnp.mean(pair, axis=-1, keepdims=True)
        shifted = pair - centre
        spread = jnp.mean(shifted * shifted, axis=-1, keepdims=True)
        factor = lax.rsqrt(spread + 1e-05)
        normed = (shifted * factor).astype(jnp.bfloat16)
        normed_ref[at, :] = normed
        factor_ref[at, :] = jnp.broadcast_to(factor, (pairs, LANES))
        for start in range(0, hidden_units, CHUNK):
            units = pl.ds(start, CHUNK)
            pre = jnp.dot(normed, up_ref[:, units], preferred_element_type=jnp.float32)
            share = 0.5 * (1.0 + lax.erf(pre * (1.0 / math.sqrt(2.0))))
            hidden_ref[at, units] = (pre * share).astype(jnp.bfloat16)
            bell = jnp.exp(-0.5 * pre * pre) * (1.0 / math.sqrt(2.0 * math.pi))
            slope_ref[at, units] = (share + pre * bell).astype(jnp.bfloat16)
        if section == 0:
            fetch_down.wait()
        mixed = (pair + contract_last(hidden_ref[at, :], down_ref[...])).astype(jnp.bfloat16)
        write_pair(work_ref if section < last else out_ref, mask, mixed)
        normed_t_ref[:, at] = normed.T
        quarter = pl.ds(section * (hidden_units // len(MASKS)), hidden_units // len(MASKS))
        up_t_ref[quarter, :] = up_ref[:, quarter].T


def backward_kernel(
    places_down, places_up, place_ref, grad_ref, hidden_ref, slope_ref, normed_ref, normed_t_ref, factor_ref,
    up_t_ref, down_ref, d_pre_ref, grad_t_ref, *rest
):
    blocks, work_ref = rest[:-1], rest[-1]
    pairs = MEMBERS // 2 * work_ref.shape[1]
    hidden_units = down_ref.shape[1]
    last = len(MASKS) - 1
    for section in range(last, -1, -1):
        mask = MASKS[section]
        at = pl.ds(section * pairs, pairs)
        if section == last:
            pair_grad = read_pair(grad_ref, mask, swapped=place_ref[0])
        else:
            pair_grad = read_pair(work_ref, mask)
        pair_bf = pair_grad.astype(jnp.bfloat16)
        for start in range(0, hidden_units, CHUNK):
            units = pl.ds(start, CHUNK)
            d_hidden = jnp.dot(pair_bf, down_ref[:, units], preferred_element_type=jnp.float32)
            d_pre_ref[at, units] = (d_hidden * slope_ref[at, units].astype(jnp.float32)).astype(jnp.bfloat16)
        if section > 0:
            d_norm = jnp.dot(d_pre_ref[at, :], up_t_ref[...], preferred_element_type=jnp.float32)
            normed = normed_ref[at, :].astype(jnp.float32)
            d_pair = factor_ref[at, :][:, :1] * (
                d_norm
                - jnp.mean(d_norm, axis=-1, keepdims=True)
                - normed * jnp.mean(d_norm * normed, axis=-1, keepdims=True)
            )
            write_pair(work_ref, mask, (pair_grad + d_pair).astype(jnp.bfloat16))
        grad_t_ref[:, at] = pair_bf.T

    if blocks:
        write_blocks(places_down, place_ref[1], grad_t_ref, hidden_ref, blocks[0])
        write_blocks(places_up, place_ref[1], normed_t_ref, d_pre_ref, blocks[1])


def keep_kernel(
    places_down, places_up, place_ref, hidden_ref, d_pre_ref, normed_t_ref, grad_t_ref, down_ref, up_ref
):
    write_blocks(places_down, 1 - place_ref[1], grad_t_ref, hidden_ref, down_ref)
    write_blocks(places_up, 1 - place_ref[1], normed_t_ref, d_pre_ref, up_ref)


def settle_kernel(sources, place_ref, *refs):
    parts, out_ref, done = refs[:-2], refs[-2], refs[-1]
    count, rows = parts[0].shape[:2]
    copies = []
    for index, source in enumerate(sources):
        block = parts[index // count].at[index % count]
        first = pl.multiple_of((place_ref[0] ^ source) * rows, rows)
        copies.append(pltpu.make_async_copy(block, out_ref.at[pl.ds(first, rows)], done.at[index]))
    for copy in copies:
        copy.start()
    for copy in copies:
        copy.wait()


def spec(space):
    return pl.BlockSpec(memory_space=space)


def block_places(order, span_x, span_y):
    places = []
    for at_x in range(span_x):
        line = []
        for group in range(span_y // 2):
            place = 0
            for axis, step in order:
                at = at_x if axis == "gx" else 2 * group
                place = 2 * place + (at >> step & 1)
            line.append(place)
        places.append(line)
    return places


def in_vmem(*items):
    return [pltpu.with_memory_space_constraint(item, pltpu.VMEM) for item in items]


def load(place, weight):
    return pl.pallas_call(
        load_kernel,
        out_shape=pltpu.VMEM(weight.shape, weight.dtype),
        in_specs=[spec(pltpu.SMEM), spec(pltpu.HBM)],
        out_specs=spec(pltpu.VMEM),
        scratch_shapes=[pltpu.SemaphoreType.DMA],
        compiler_params=pltpu.CompilerParams(vmem_limit_bytes=KEEP_BYTES),
        cost_estimate=pl.CostEstimate(flops=0, bytes_accessed=4 * weight.size, transcendentals=0),
    )(place, pltpu.with_memory_space_constraint(weight, pltpu.HBM))


def forward(state, up, w_down):
    members, rows, width = state.shape
    total = len(MASKS) * (members // 2) * rows
    depth, units = up.shape
    bf16 = jnp.bfloat16
    outs = [
        pltpu.VMEM(state.shape, bf16),
        pltpu.VMEM((total, units), bf16),
        pltpu.VMEM((total, units), bf16),
        pltpu.VMEM((total, depth), bf16),
        pltpu.VMEM((depth, total), bf16),
        pltpu.VMEM((total, LANES), jnp.float32),
        pltpu.VMEM((units, depth), bf16),
        pltpu.VMEM(w_down.shape, bf16),
    ]
    return pl.pallas_call(
        forward_kernel,
        out_shape=outs,
        in_specs=[spec(pltpu.VMEM)] * 2 + [spec(pltpu.HBM)],
        out_specs=[spec(pltpu.VMEM)] * len(outs),
        scratch_shapes=[pltpu.VMEM(state.shape, bf16), pltpu.SemaphoreType.DMA],
        compiler_params=pltpu.CompilerParams(vmem_limit_bytes=SECTIONS_BYTES),
        cost_estimate=pl.CostEstimate(
            flops=10 * total * depth * units, bytes_accessed=16 * total * units, transcendentals=0
        ),
    )(state, *in_vmem(up), pltpu.with_memory_space_constraint(w_down, pltpu.HBM))


def backward(place, grad, kept, places, block):
    total, units = kept[0].shape
    depth = kept[2].shape[1]
    bf16 = jnp.bfloat16
    outs = [pltpu.VMEM((total, units), bf16), pltpu.VMEM((depth, total), bf16)]
    outs += [block] * 2 if block else []
    return pl.pallas_call(
        functools.partial(backward_kernel, *places),
        out_shape=outs,
        in_specs=[spec(pltpu.SMEM)] + [spec(pltpu.VMEM)] * (1 + len(kept)),
        out_specs=[spec(pltpu.VMEM)] * len(outs),
        scratch_shapes=[pltpu.VMEM(grad.shape, bf16)],
        compiler_params=pltpu.CompilerParams(vmem_limit_bytes=SECTIONS_BYTES),
        cost_estimate=pl.CostEstimate(
            flops=10 * total * depth * units, bytes_accessed=16 * total * units, transcendentals=0
        ),
    )(place, grad, *in_vmem(*kept))


def keep_blocks(place, hidden, d_pre, normed_t, grad_t, places, block):
    total, units = hidden.shape
    depth = normed_t.shape[0]
    return pl.pallas_call(
        functools.partial(keep_kernel, *places),
        out_shape=[block] * 2,
        in_specs=[spec(pltpu.SMEM)] + [spec(pltpu.VMEM)] * 4,
        out_specs=[spec(pltpu.VMEM)] * 2,
        compiler_params=pltpu.CompilerParams(vmem_limit_bytes=KEEP_BYTES),
        cost_estimate=pl.CostEstimate(
            flops=2 * total * depth * units, bytes_accessed=8 * total * units, transcendentals=0
        ),
    )(place, *in_vmem(hidden, d_pre, normed_t, grad_t))


def swap(block, axis, bit):
    pairs = [(source, source ^ (1 << bit)) for source in range(lax.axis_size(axis))]
    return lax.ppermute(block, axis, pairs)


def pick(block, at):
    return slice_at(block, 0, at).astype(jnp.float32)


def finish_sum(halves, kept, taken, order, beside=None):
    for phase, step in enumerate(order):
        mine, other = halves[step]
        shape = (2, kept.shape[0] // 2) + kept.shape[1:]
        kept, taken = kept.reshape(shape), taken.reshape(shape)
        give = (pick(kept, other) + pick(taken, other)).astype(jnp.bfloat16)
        kept = (pick(kept, mine) + pick(taken, mine)).astype(jnp.bfloat16)
        if beside:
            give = beside(phase, give)
        taken = swap(give, *step)
    return (kept.astype(jnp.float32) + taken.astype(jnp.float32))[0]


def scatter_narrow(halves, left, right, order, span_x, span_y):
    total = jnp.dot(left, right, preferred_element_type=jnp.float32).astype(jnp.bfloat16)
    rows, columns = left.shape[0] // span_x, right.shape[1] // span_y
    count_x, count_y = span_x.bit_length() - 1, span_y.bit_length() - 1
    dims = [("gx", bit) for bit in range(count_x)][::-1] + ["rows"]
    dims += [("gy", bit) for bit in range(count_y)][::-1] + ["columns"]
    blocks = total.reshape((2,) * count_x + (rows,) + (2,) * count_y + (columns,))
    blocks = blocks.transpose([dims.index(item) for item in list(order) + ["rows", "columns"]])
    blocks = blocks.reshape(-1, rows, columns)
    return finish_sum(halves, blocks, jnp.zeros_like(blocks), order)


class Journey:
    def __init__(self, held, bits=(0, 1, 2, 3), sources=(0,)):
        self.held = held
        self.bits = list(bits)
        self.sources = list(sources)
        self.parts = None

    def hop(self, at, steps, halves, after=None):
        dim = self.bits.index(at)
        mine, other = halves[steps[at]]
        kept, given = [slice_at(self.held, dim, part) for part in (mine, other)]
        if after is not None:
            given, after = lax.optimization_barrier((given, after))
        self.parts = [kept, swap(given, *steps[at])]
        self.held = jnp.concatenate(self.parts, -3)
        self.bits.remove(at)
        self.sources += [source | MASKS[at] for source in self.sources]
        return after

    def hop_both(self, at, also, steps, halves, after=None):
        dims = self.bits.index(at), self.bits.index(also)
        parts = []
        for theirs, beyond in ((0, 0), (1, 0), (0, 1), (1, 1)):
            part = slice_at(self.held, dims[0], halves[steps[at]][theirs], keep=True)
            part = slice_at(part, dims[1], halves[steps[also]][beyond], keep=True)
            parts.append(lax.squeeze(part, dims))
        if after is not None:
            parts, after = lax.optimization_barrier((parts, after))
        self.parts = [
            parts[0],
            swap(parts[1], *steps[at]),
            swap(parts[2], *steps[also]),
            swap_both(parts[3], steps[at], steps[also]),
        ]
        self.held = jnp.concatenate(self.parts, -3)
        for bit in (at, also):
            self.bits.remove(bit)
            self.sources += [source | MASKS[bit] for source in self.sources]
        return after


def slice_at(block, dim, at, keep=False):
    start = [0] * block.ndim
    start[dim] = at
    size = list(block.shape)
    size[dim] = 1
    part = lax.dynamic_slice(block, start, size, allow_negative_indices=False)
    return part if keep else lax.squeeze(part, (dim,))


def swap_both(block, step, also):
    span_x, span_y = lax.axis_size("gx"), lax.axis_size("gy")
    flips = {step[0]: 1 << step[1], also[0]: 1 << also[1]}
    pairs = []
    for at_x in range(span_x):
        for at_y in range(span_y):
            pairs.append((at_x * span_y + at_y, (at_x ^ flips["gx"]) * span_y + (at_y ^ flips["gy"])))
    return lax.ppermute(block, ("gx", "gy"), pairs)


def settle(place, journey):
    parts = journey.parts
    rows, width = parts[0].shape[-2:]
    return pl.pallas_call(
        functools.partial(settle_kernel, journey.sources),
        out_shape=jax.ShapeDtypeStruct((MEMBERS * rows, width), parts[0].dtype),
        in_specs=[spec(pltpu.SMEM)] + [spec(pltpu.VMEM)] * len(parts),
        out_specs=spec(pltpu.HBM),
        scratch_shapes=[pltpu.SemaphoreType.DMA((MEMBERS,))],
        cost_estimate=pl.CostEstimate(flops=0, bytes_accessed=4 * MEMBERS * rows * width, transcendentals=0),
    )(place, *parts)


def local(signal, w_up, w_down, cotangent):
    span_x = lax.axis_size("gx")
    span_y = lax.axis_size("gy")
    groups = section_groups(span_x, span_y)
    rows, width = signal.shape
    depth, units = w_up.shape
    steps = [("gx", span_x.bit_length() - 2), ("gx", 0), ("gy", span_y.bit_length() - 2), ("gy", 0)]
    z, y, x, core = range(4)
    rest_y = [("gy", bit) for bit in range(1, span_y.bit_length() - 1)]
    rest_x = [("gx", bit) for bit in range(1, span_x.bit_length() - 1)]
    order_down = [steps[y]] + rest_y + rest_x[::-1]
    order_up = rest_y + [steps[y]] + rest_x

    owns = [lax.axis_index(axis) // (1 << bit) % 2 for axis, bit in [steps[core]] + order_up]
    own = dict(zip([steps[core]] + order_up, owns))
    member = sum(own[step] * mask for step, mask in zip(steps, MASKS))
    place = jnp.stack([member, 1 - own[steps[core]]]).astype(jnp.int32)
    place, owns, others = lax.optimization_barrier((place, owns, [1 - item for item in owns]))
    halves = {step: pair for step, pair in zip([steps[core]] + order_up, zip(owns, others))}
    places = [block_places(order, span_x, span_y) for order in (order_down, order_up)]
    block = None
    if units // span_y % LANES == 0:
        block = pltpu.VMEM((span_x * span_y // 2, depth // span_x, units // span_y), jnp.bfloat16)

    parts = (2, 2, 2, 2, 1, rows // MEMBERS, width)
    state = exchange(signal.reshape(MEMBERS, rows // MEMBERS, width), groups)
    coming = Journey(cotangent.reshape(parts))
    coming.hop(core, steps, halves)
    coming.hop_both(x, y, steps, halves)
    up = load(place, w_up)
    state = coming.hop(z, steps, halves, state)
    state, *kept = forward(state, up, w_down)
    going = Journey(state.reshape(parts))
    grad = going.hop_both(x, y, steps, halves, coming.held)
    d_pre, grad_t, *given = backward(place, grad, kept, places, block)
    hidden, normed_t = kept[0], kept[3]
    if not given:
        going.hop(z, steps, halves)
        going.hop(core, steps, halves)
        mixed_out = settle(place, going)
        grad_down = scatter_narrow(halves, grad_t, hidden, [steps[core]] + order_down, span_x, span_y)
        grad_up = scatter_narrow(halves, normed_t, d_pre, [steps[core]] + order_up, span_x, span_y)
        return (mixed_out, grad_up, grad_down)
    given[0] = going.hop(z, steps, halves, given[0])
    take_down, take_up = [swap(part, *steps[core]) for part in given]
    keep_down, keep_up = keep_blocks(place, hidden, d_pre, normed_t, grad_t, places, block)

    def beside(phase, give):
        if phase == 1:
            return going.hop(core, steps, halves, give)
        if phase == 2:
            going.parts, give = lax.optimization_barrier((going.parts, give))
        return give

    grad_up = finish_sum(halves, keep_up, take_up, order_up)
    grad_down = finish_sum(halves, keep_down, take_down, order_down, beside)
    return (settle(place, going), grad_up, grad_down)


def solution(mesh):
    return jax.shard_map(
        local,
        mesh=mesh,
        in_specs=(P(("gx", "gy"), None), P(), P(), P(("gx", "gy"), None)),
        out_specs=(P(("gx", "gy"), None), P("gx", "gy"), P("gx", "gy")),
        check_vma=False,
    )
```

```python
import functools
import math

import jax
import jax.numpy as jnp
from jax import lax
from jax.experimental import pallas as pl
from jax.experimental.pallas import tpu as pltpu
from jax.sharding import PartitionSpec as P

MEMBERS = 16
MASKS = (8, 4, 2, 1)
LANES = 128
CHUNK = 256
SECTIONS_BYTES = 8 * 1024 * 1024
KEEP_BYTES = 4 * 1024 * 1024


def section_groups(span_x, span_y):
    bits_x = [span_x.bit_length() - 2, 0]
    bits_y = [span_y.bit_length() - 2, 0]
    mask_x = sum(1 << bit for bit in bits_x)
    mask_y = sum(1 << bit for bit in bits_y)
    groups = []
    for base_x in range(span_x):
        for base_y in range(span_y):
            if base_x & mask_x or base_y & mask_y:
                continue
            group = []
            for member in range(MEMBERS):
                at_x, at_y = base_x, base_y
                at_x |= (member >> 3 & 1) << bits_x[0] | (member >> 2 & 1) << bits_x[1]
                at_y |= (member >> 1 & 1) << bits_y[0] | (member & 1) << bits_y[1]
                group.append(at_x * span_y + at_y)
            groups.append(group)
    return groups


def exchange(block, groups):
    return lax.all_to_all(
        block, ("gx", "gy"), split_axis=0, concat_axis=0, axis_index_groups=groups, tiled=True
    )


def contract_last(left, right):
    return lax.dot_general(
        left, right, (((1,), (1,)), ((), ())), preferred_element_type=jnp.float32
    )


def low_members(mask):
    return [member for member in range(MEMBERS) if not member & mask]


def read_pair(ref, mask, swapped=0):
    low = jnp.concatenate([ref[member ^ swapped] for member in low_members(mask)], 0)
    high = jnp.concatenate([ref[(member | mask) ^ swapped] for member in low_members(mask)], 0)
    return jnp.concatenate([low, high], 1).astype(jnp.float32)


def write_pair(ref, mask, pair):
    rows, width = ref.shape[1:]
    for place, member in enumerate(low_members(mask)):
        part = pair[place * rows : (place + 1) * rows]
        ref[member] = part[:, :width]
        ref[member | mask] = part[:, width:]


def write_blocks(places, bit, left_ref, right_ref, out_ref):
    rows, columns = out_ref.shape[1:]
    pieces = []
    for group in range(len(places[0])):
        base = (2 * group + bit) * columns
        for inner in range(0, columns, LANES):
            pieces.append((group, inner, pl.multiple_of(base + inner, LANES)))
    for first in range(0, len(pieces), 2):
        some = pieces[first : first + 2]
        right = jnp.concatenate([right_ref[:, pl.ds(start, LANES)] for _, _, start in some], 1)
        total = jnp.dot(left_ref[...], right, preferred_element_type=jnp.float32)
        total = total.astype(jnp.bfloat16)
        for which, (group, inner, _) in enumerate(some):
            for block in range(len(places)):
                out_ref[places[block][group], :, inner : inner + LANES] = total[
                    block * rows : (block + 1) * rows, which * LANES : (which + 1) * LANES
                ]


def load_kernel(place_ref, source, target, arrived):
    copy = pltpu.make_async_copy(source, target, arrived)
    copy.start()
    copy.wait()


def forward_kernel(
    state_ref, up_ref, down_hbm,
    out_ref, hidden_ref, slope_ref, normed_ref, normed_t_ref, factor_ref, up_t_ref, down_ref, work_ref, arrived
):
    fetch_down = pltpu.make_async_copy(down_hbm, down_ref, arrived)
    fetch_down.start()
    pairs = MEMBERS // 2 * work_ref.shape[1]
    hidden_units = up_ref.shape[1]
    last = len(MASKS) - 1
    for section, mask in enumerate(MASKS):
        at = pl.ds(section * pairs, pairs)
        pair = read_pair(state_ref if section == 0 else work_ref, mask)
        centre = jnp.mean(pair, axis=-1, keepdims=True)
        shifted = pair - centre
        spread = jnp.mean(shifted * shifted, axis=-1, keepdims=True)
        factor = lax.rsqrt(spread + 1e-05)
        normed = (shifted * factor).astype(jnp.bfloat16)
        normed_ref[at, :] = normed
        factor_ref[at, :] = jnp.broadcast_to(factor, (pairs, LANES))
        for start in range(0, hidden_units, CHUNK):
            units = pl.ds(start, CHUNK)
            pre = jnp.dot(normed, up_ref[:, units], preferred_element_type=jnp.float32)
            share = 0.5 * (1.0 + lax.erf(pre * (1.0 / math.sqrt(2.0))))
            hidden_ref[at, units] = (pre * share).astype(jnp.bfloat16)
            bell = jnp.exp(-0.5 * pre * pre) * (1.0 / math.sqrt(2.0 * math.pi))
            slope_ref[at, units] = (share + pre * bell).astype(jnp.bfloat16)
        if section == 0:
            fetch_down.wait()
        mixed = (pair + contract_last(hidden_ref[at, :], down_ref[...])).astype(jnp.bfloat16)
        write_pair(work_ref if section < last else out_ref, mask, mixed)
        normed_t_ref[:, at] = normed.T
        quarter = pl.ds(section * (hidden_units // len(MASKS)), hidden_units // len(MASKS))
        up_t_ref[quarter, :] = up_ref[:, quarter].T


def backward_kernel(
    places_down, places_up, place_ref, grad_ref, hidden_ref, slope_ref, normed_ref, normed_t_ref, factor_ref,
    up_t_ref, down_ref, d_pre_ref, grad_t_ref, *rest
):
    blocks, work_ref = rest[:-1], rest[-1]
    pairs = MEMBERS // 2 * work_ref.shape[1]
    hidden_units = down_ref.shape[1]
    last = len(MASKS) - 1
    for section in range(last, -1, -1):
        mask = MASKS[section]
        at = pl.ds(section * pairs, pairs)
        if section == last:
            pair_grad = read_pair(grad_ref, mask, swapped=place_ref[0])
        else:
            pair_grad = read_pair(work_ref, mask)
        pair_bf = pair_grad.astype(jnp.bfloat16)
        for start in range(0, hidden_units, CHUNK):
            units = pl.ds(start, CHUNK)
            d_hidden = jnp.dot(pair_bf, down_ref[:, units], preferred_element_type=jnp.float32)
            d_pre_ref[at, units] = (d_hidden * slope_ref[at, units].astype(jnp.float32)).astype(jnp.bfloat16)
        if section > 0:
            d_norm = jnp.dot(d_pre_ref[at, :], up_t_ref[...], preferred_element_type=jnp.float32)
            normed = normed_ref[at, :].astype(jnp.float32)
            d_pair = factor_ref[at, :][:, :1] * (
                d_norm
                - jnp.mean(d_norm, axis=-1, keepdims=True)
                - normed * jnp.mean(d_norm * normed, axis=-1, keepdims=True)
            )
            write_pair(work_ref, mask, (pair_grad + d_pair).astype(jnp.bfloat16))
        grad_t_ref[:, at] = pair_bf.T

    if blocks:
        write_blocks(places_down, place_ref[1], grad_t_ref, hidden_ref, blocks[0])
        write_blocks(places_up, place_ref[1], normed_t_ref, d_pre_ref, blocks[1])


def keep_kernel(
    places_down, places_up, place_ref, hidden_ref, d_pre_ref, normed_t_ref, grad_t_ref, down_ref, up_ref
):
    write_blocks(places_down, 1 - place_ref[1], grad_t_ref, hidden_ref, down_ref)
    write_blocks(places_up, 1 - place_ref[1], normed_t_ref, d_pre_ref, up_ref)


def settle_kernel(sources, place_ref, *refs):
    parts, out_ref, done = refs[:-2], refs[-2], refs[-1]
    count, rows = parts[0].shape[:2]
    copies = []
    for index, source in enumerate(sources):
        block = parts[index // count].at[index % count]
        first = pl.multiple_of((place_ref[0] ^ source) * rows, rows)
        copies.append(pltpu.make_async_copy(block, out_ref.at[pl.ds(first, rows)], done.at[index]))
    for copy in copies:
        copy.start()
    for copy in copies:
        copy.wait()


def spec(space):
    return pl.BlockSpec(memory_space=space)


def block_places(order, span_x, span_y):
    places = []
    for at_x in range(span_x):
        line = []
        for group in range(span_y // 2):
            place = 0
            for axis, step in order:
                at = at_x if axis == "gx" else 2 * group
                place = 2 * place + (at >> step & 1)
            line.append(place)
        places.append(line)
    return places


def in_vmem(*items):
    return [pltpu.with_memory_space_constraint(item, pltpu.VMEM) for item in items]


def load(place, weight):
    return pl.pallas_call(
        load_kernel,
        out_shape=pltpu.VMEM(weight.shape, weight.dtype),
        in_specs=[spec(pltpu.SMEM), spec(pltpu.HBM)],
        out_specs=spec(pltpu.VMEM),
        scratch_shapes=[pltpu.SemaphoreType.DMA],
        compiler_params=pltpu.CompilerParams(vmem_limit_bytes=KEEP_BYTES),
        cost_estimate=pl.CostEstimate(flops=0, bytes_accessed=4 * weight.size, transcendentals=0),
    )(place, pltpu.with_memory_space_constraint(weight, pltpu.HBM))


def forward(state, up, w_down):
    members, rows, width = state.shape
    total = len(MASKS) * (members // 2) * rows
    depth, units = up.shape
    bf16 = jnp.bfloat16
    outs = [
        pltpu.VMEM(state.shape, bf16),
        pltpu.VMEM((total, units), bf16),
        pltpu.VMEM((total, units), bf16),
        pltpu.VMEM((total, depth), bf16),
        pltpu.VMEM((depth, total), bf16),
        pltpu.VMEM((total, LANES), jnp.float32),
        pltpu.VMEM((units, depth), bf16),
        pltpu.VMEM(w_down.shape, bf16),
    ]
    return pl.pallas_call(
        forward_kernel,
        out_shape=outs,
        in_specs=[spec(pltpu.VMEM)] * 2 + [spec(pltpu.HBM)],
        out_specs=[spec(pltpu.VMEM)] * len(outs),
        scratch_shapes=[pltpu.VMEM(state.shape, bf16), pltpu.SemaphoreType.DMA],
        compiler_params=pltpu.CompilerParams(vmem_limit_bytes=SECTIONS_BYTES),
        cost_estimate=pl.CostEstimate(
            flops=10 * total * depth * units, bytes_accessed=16 * total * units, transcendentals=0
        ),
    )(state, *in_vmem(up), pltpu.with_memory_space_constraint(w_down, pltpu.HBM))


def backward(place, grad, kept, places, block):
    total, units = kept[0].shape
    depth = kept[2].shape[1]
    bf16 = jnp.bfloat16
    outs = [pltpu.VMEM((total, units), bf16), pltpu.VMEM((depth, total), bf16)]
    outs += [block] * 2 if block else []
    return pl.pallas_call(
        functools.partial(backward_kernel, *places),
        out_shape=outs,
        in_specs=[spec(pltpu.SMEM)] + [spec(pltpu.VMEM)] * (1 + len(kept)),
        out_specs=[spec(pltpu.VMEM)] * len(outs),
        scratch_shapes=[pltpu.VMEM(grad.shape, bf16)],
        compiler_params=pltpu.CompilerParams(vmem_limit_bytes=SECTIONS_BYTES),
        cost_estimate=pl.CostEstimate(
            flops=10 * total * depth * units, bytes_accessed=16 * total * units, transcendentals=0
        ),
    )(place, grad, *in_vmem(*kept))


def keep_blocks(place, hidden, d_pre, normed_t, grad_t, places, block):
    total, units = hidden.shape
    depth = normed_t.shape[0]
    return pl.pallas_call(
        functools.partial(keep_kernel, *places),
        out_shape=[block] * 2,
        in_specs=[spec(pltpu.SMEM)] + [spec(pltpu.VMEM)] * 4,
        out_specs=[spec(pltpu.VMEM)] * 2,
        compiler_params=pltpu.CompilerParams(vmem_limit_bytes=KEEP_BYTES),
        cost_estimate=pl.CostEstimate(
            flops=2 * total * depth * units, bytes_accessed=8 * total * units, transcendentals=0
        ),
    )(place, *in_vmem(hidden, d_pre, normed_t, grad_t))


def swap(block, axis, bit):
    pairs = [(source, source ^ (1 << bit)) for source in range(lax.axis_size(axis))]
    return lax.ppermute(block, axis, pairs)


def pick(block, at):
    return slice_at(block, 0, at).astype(jnp.float32)


def finish_sum(halves, kept, taken, order, beside=None):
    for phase, step in enumerate(order):
        mine, other = halves[step]
        shape = (2, kept.shape[0] // 2) + kept.shape[1:]
        kept, taken = kept.reshape(shape), taken.reshape(shape)
        give = (pick(kept, other) + pick(taken, other)).astype(jnp.bfloat16)
        kept = (pick(kept, mine) + pick(taken, mine)).astype(jnp.bfloat16)
        if beside:
            give = beside(phase, give)
        taken = swap(give, *step)
    return (kept.astype(jnp.float32) + taken.astype(jnp.float32))[0]


def scatter_narrow(halves, left, right, order, span_x, span_y):
    total = jnp.dot(left, right, preferred_element_type=jnp.float32).astype(jnp.bfloat16)
    rows, columns = left.shape[0] // span_x, right.shape[1] // span_y
    count_x, count_y = span_x.bit_length() - 1, span_y.bit_length() - 1
    dims = [("gx", bit) for bit in range(count_x)][::-1] + ["rows"]
    dims += [("gy", bit) for bit in range(count_y)][::-1] + ["columns"]
    blocks = total.reshape((2,) * count_x + (rows,) + (2,) * count_y + (columns,))
    blocks = blocks.transpose([dims.index(item) for item in list(order) + ["rows", "columns"]])
    blocks = blocks.reshape(-1, rows, columns)
    return finish_sum(halves, blocks, jnp.zeros_like(blocks), order)


class Journey:
    def __init__(self, held, bits=(0, 1, 2, 3), sources=(0,)):
        self.held = held
        self.bits = list(bits)
        self.sources = list(sources)
        self.parts = None

    def hop(self, at, steps, halves, after=None):
        dim = self.bits.index(at)
        mine, other = halves[steps[at]]
        kept, given = [slice_at(self.held, dim, part) for part in (mine, other)]
        if after is not None:
            given, after = lax.optimization_barrier((given, after))
        self.parts = [kept, swap(given, *steps[at])]
        self.held = jnp.concatenate(self.parts, -3)
        self.bits.remove(at)
        self.sources += [source | MASKS[at] for source in self.sources]
        return after

    def hop_both(self, at, also, steps, halves, after=None):
        dims = self.bits.index(at), self.bits.index(also)
        parts = []
        for theirs, beyond in ((0, 0), (1, 0), (0, 1), (1, 1)):
            part = slice_at(self.held, dims[0], halves[steps[at]][theirs], keep=True)
            part = slice_at(part, dims[1], halves[steps[also]][beyond], keep=True)
            parts.append(lax.squeeze(part, dims))
        if after is not None:
            parts, after = lax.optimization_barrier((parts, after))
        self.parts = [
            parts[0],
            swap(parts[1], *steps[at]),
            swap(parts[2], *steps[also]),
            swap_both(parts[3], steps[at], steps[also]),
        ]
        self.held = jnp.concatenate(self.parts, -3)
        for bit in (at, also):
            self.bits.remove(bit)
            self.sources += [source | MASKS[bit] for source in self.sources]
        return after


def slice_at(block, dim, at, keep=False):
    start = [0] * block.ndim
    start[dim] = at
    size = list(block.shape)
    size[dim] = 1
    part = lax.dynamic_slice(block, start, size, allow_negative_indices=False)
    return part if keep else lax.squeeze(part, (dim,))


def swap_both(block, step, also):
    span_x, span_y = lax.axis_size("gx"), lax.axis_size("gy")
    flips = {step[0]: 1 << step[1], also[0]: 1 << also[1]}
    pairs = []
    for at_x in range(span_x):
        for at_y in range(span_y):
            pairs.append((at_x * span_y + at_y, (at_x ^ flips["gx"]) * span_y + (at_y ^ flips["gy"])))
    return lax.ppermute(block, ("gx", "gy"), pairs)


def settle(place, journey):
    parts = journey.parts
    rows, width = parts[0].shape[-2:]
    return pl.pallas_call(
        functools.partial(settle_kernel, journey.sources),
        out_shape=jax.ShapeDtypeStruct((MEMBERS * rows, width), parts[0].dtype),
        in_specs=[spec(pltpu.SMEM)] + [spec(pltpu.VMEM)] * len(parts),
        out_specs=spec(pltpu.HBM),
        scratch_shapes=[pltpu.SemaphoreType.DMA((MEMBERS,))],
        cost_estimate=pl.CostEstimate(flops=0, bytes_accessed=4 * MEMBERS * rows * width, transcendentals=0),
    )(place, *parts)


def local(signal, w_up, w_down, cotangent):
    span_x = lax.axis_size("gx")
    span_y = lax.axis_size("gy")
    groups = section_groups(span_x, span_y)
    rows, width = signal.shape
    depth, units = w_up.shape
    steps = [("gx", span_x.bit_length() - 2), ("gx", 0), ("gy", span_y.bit_length() - 2), ("gy", 0)]
    z, y, x, core = range(4)
    rest_y = [("gy", bit) for bit in range(1, span_y.bit_length() - 1)]
    rest_x = [("gx", bit) for bit in range(1, span_x.bit_length() - 1)]
    order_down = [steps[y]] + rest_y + rest_x[::-1]
    order_up = rest_y + [steps[y]] + rest_x

    owns = [lax.axis_index(axis) // (1 << bit) % 2 for axis, bit in [steps[core]] + order_up]
    own = dict(zip([steps[core]] + order_up, owns))
    member = sum(own[step] * mask for step, mask in zip(steps, MASKS))
    place = jnp.stack([member, 1 - own[steps[core]]]).astype(jnp.int32)
    place, owns, others = lax.optimization_barrier((place, owns, [1 - item for item in owns]))
    halves = {step: pair for step, pair in zip([steps[core]] + order_up, zip(owns, others))}
    places = [block_places(order, span_x, span_y) for order in (order_down, order_up)]
    block = None
    if units // span_y % LANES == 0:
        block = pltpu.VMEM((span_x * span_y // 2, depth // span_x, units // span_y), jnp.bfloat16)

    parts = (2, 2, 2, 2, 1, rows // MEMBERS, width)
    state = exchange(signal.reshape(MEMBERS, rows // MEMBERS, width), groups)
    coming = Journey(cotangent.reshape(parts))
    coming.hop(core, steps, halves)
    coming.hop_both(x, y, steps, halves)
    up = load(place, w_up)
    state = coming.hop(z, steps, halves, state)
    state, *kept = forward(state, up, w_down)
    going = Journey(state.reshape(parts))
    going.hop_both(x, y, steps, halves)
    d_pre, grad_t, *given = backward(place, coming.held, kept, places, block)
    hidden, normed_t = kept[0], kept[3]
    if not given:
        going.hop(z, steps, halves)
        going.hop(core, steps, halves)
        mixed_out = settle(place, going)
        grad_down = scatter_narrow(halves, grad_t, hidden, [steps[core]] + order_down, span_x, span_y)
        grad_up = scatter_narrow(halves, normed_t, d_pre, [steps[core]] + order_up, span_x, span_y)
        return (mixed_out, grad_up, grad_down)
    given[0] = going.hop(z, steps, halves, given[0])
    take_down, take_up = [swap(part, *steps[core]) for part in given]
    keep_down, keep_up = keep_blocks(place, hidden, d_pre, normed_t, grad_t, places, block)

    def beside(phase, give):
        if phase == 1:
            return going.hop(core, steps, halves, give)
        if phase == 2:
            going.parts, give = lax.optimization_barrier((going.parts, give))
        return give

    grad_up = finish_sum(halves, keep_up, take_up, order_up)
    grad_down = finish_sum(halves, keep_down, take_down, order_down, beside)
    return (settle(place, going), grad_up, grad_down)


def solution(mesh):
    return jax.shard_map(
        local,
        mesh=mesh,
        in_specs=(P(("gx", "gy"), None), P(), P(), P(("gx", "gy"), None)),
        out_specs=(P(("gx", "gy"), None), P("gx", "gy"), P("gx", "gy")),
        check_vma=False,
    )
```

```python
import functools
import math

import jax
import jax.numpy as jnp
from jax import lax
from jax.experimental import pallas as pl
from jax.experimental.pallas import tpu as pltpu
from jax.sharding import PartitionSpec as P

MEMBERS = 16
MASKS = (8, 4, 2, 1)
LANES = 128
CHUNK = 256
SECTIONS_BYTES = 8 * 1024 * 1024
KEEP_BYTES = 4 * 1024 * 1024


def section_groups(span_x, span_y):
    bits_x = [span_x.bit_length() - 2, 0]
    bits_y = [span_y.bit_length() - 2, 0]
    mask_x = sum(1 << bit for bit in bits_x)
    mask_y = sum(1 << bit for bit in bits_y)
    groups = []
    for base_x in range(span_x):
        for base_y in range(span_y):
            if base_x & mask_x or base_y & mask_y:
                continue
            group = []
            for member in range(MEMBERS):
                at_x, at_y = base_x, base_y
                at_x |= (member >> 3 & 1) << bits_x[0] | (member >> 2 & 1) << bits_x[1]
                at_y |= (member >> 1 & 1) << bits_y[0] | (member & 1) << bits_y[1]
                group.append(at_x * span_y + at_y)
            groups.append(group)
    return groups


def exchange(block, groups):
    return lax.all_to_all(
        block, ("gx", "gy"), split_axis=0, concat_axis=0, axis_index_groups=groups, tiled=True
    )


def contract_last(left, right):
    return lax.dot_general(
        left, right, (((1,), (1,)), ((), ())), preferred_element_type=jnp.float32
    )


def low_members(mask):
    return [member for member in range(MEMBERS) if not member & mask]


def read_pair(ref, mask, swapped=0):
    low = jnp.concatenate([ref[member ^ swapped] for member in low_members(mask)], 0)
    high = jnp.concatenate([ref[(member | mask) ^ swapped] for member in low_members(mask)], 0)
    return jnp.concatenate([low, high], 1).astype(jnp.float32)


def write_pair(ref, mask, pair):
    rows, width = ref.shape[1:]
    for place, member in enumerate(low_members(mask)):
        part = pair[place * rows : (place + 1) * rows]
        ref[member] = part[:, :width]
        ref[member | mask] = part[:, width:]


def write_blocks(places, bit, left_ref, right_ref, out_ref):
    rows, columns = out_ref.shape[1:]
    pieces = []
    for group in range(len(places[0])):
        base = (2 * group + bit) * columns
        for inner in range(0, columns, LANES):
            pieces.append((group, inner, pl.multiple_of(base + inner, LANES)))
    for first in range(0, len(pieces), 2):
        some = pieces[first : first + 2]
        right = jnp.concatenate([right_ref[:, pl.ds(start, LANES)] for _, _, start in some], 1)
        total = jnp.dot(left_ref[...], right, preferred_element_type=jnp.float32)
        total = total.astype(jnp.bfloat16)
        for which, (group, inner, _) in enumerate(some):
            for block in range(len(places)):
                out_ref[places[block][group], :, inner : inner + LANES] = total[
                    block * rows : (block + 1) * rows, which * LANES : (which + 1) * LANES
                ]


def load_kernel(place_ref, source, target, arrived):
    copy = pltpu.make_async_copy(source, target, arrived)
    copy.start()
    copy.wait()


def forward_kernel(
    state_ref, up_ref, down_hbm,
    out_ref, hidden_ref, slope_ref, normed_ref, normed_t_ref, factor_ref, up_t_ref, down_ref, work_ref, arrived
):
    fetch_down = pltpu.make_async_copy(down_hbm, down_ref, arrived)
    fetch_down.start()
    pairs = MEMBERS // 2 * work_ref.shape[1]
    hidden_units = up_ref.shape[1]
    last = len(MASKS) - 1
    for section, mask in enumerate(MASKS):
        at = pl.ds(section * pairs, pairs)
        pair = read_pair(state_ref if section == 0 else work_ref, mask)
        centre = jnp.mean(pair, axis=-1, keepdims=True)
        shifted = pair - centre
        spread = jnp.mean(shifted * shifted, axis=-1, keepdims=True)
        factor = lax.rsqrt(spread + 1e-05)
        normed = (shifted * factor).astype(jnp.bfloat16)
        normed_ref[at, :] = normed
        factor_ref[at, :] = jnp.broadcast_to(factor, (pairs, LANES))
        for start in range(0, hidden_units, CHUNK):
            units = pl.ds(start, CHUNK)
            pre = jnp.dot(normed, up_ref[:, units], preferred_element_type=jnp.float32)
            share = 0.5 * (1.0 + lax.erf(pre * (1.0 / math.sqrt(2.0))))
            hidden_ref[at, units] = (pre * share).astype(jnp.bfloat16)
            bell = jnp.exp(-0.5 * pre * pre) * (1.0 / math.sqrt(2.0 * math.pi))
            slope_ref[at, units] = (share + pre * bell).astype(jnp.bfloat16)
        if section == 0:
            fetch_down.wait()
        mixed = (pair + contract_last(hidden_ref[at, :], down_ref[...])).astype(jnp.bfloat16)
        write_pair(work_ref if section < last else out_ref, mask, mixed)
        normed_t_ref[:, at] = normed.T
        quarter = pl.ds(section * (hidden_units // len(MASKS)), hidden_units // len(MASKS))
        up_t_ref[quarter, :] = up_ref[:, quarter].T


def backward_kernel(
    places_down, places_up, place_ref, grad_ref, hidden_ref, slope_ref, normed_ref, normed_t_ref, factor_ref,
    up_t_ref, down_ref, d_pre_ref, grad_t_ref, *rest
):
    blocks, work_ref = rest[:-1], rest[-1]
    pairs = MEMBERS // 2 * work_ref.shape[1]
    hidden_units = down_ref.shape[1]
    last = len(MASKS) - 1
    for section in range(last, -1, -1):
        mask = MASKS[section]
        at = pl.ds(section * pairs, pairs)
        if section == last:
            pair_grad = read_pair(grad_ref, mask, swapped=place_ref[0])
        else:
            pair_grad = read_pair(work_ref, mask)
        pair_bf = pair_grad.astype(jnp.bfloat16)
        for start in range(0, hidden_units, CHUNK):
            units = pl.ds(start, CHUNK)
            d_hidden = jnp.dot(pair_bf, down_ref[:, units], preferred_element_type=jnp.float32)
            d_pre_ref[at, units] = (d_hidden * slope_ref[at, units].astype(jnp.float32)).astype(jnp.bfloat16)
        if section > 0:
            d_norm = jnp.dot(d_pre_ref[at, :], up_t_ref[...], preferred_element_type=jnp.float32)
            normed = normed_ref[at, :].astype(jnp.float32)
            d_pair = factor_ref[at, :][:, :1] * (
                d_norm
                - jnp.mean(d_norm, axis=-1, keepdims=True)
                - normed * jnp.mean(d_norm * normed, axis=-1, keepdims=True)
            )
            write_pair(work_ref, mask, (pair_grad + d_pair).astype(jnp.bfloat16))
        grad_t_ref[:, at] = pair_bf.T

    if blocks:
        write_blocks(places_down, place_ref[1], grad_t_ref, hidden_ref, blocks[0])
        write_blocks(places_up, place_ref[1], normed_t_ref, d_pre_ref, blocks[1])


def keep_kernel(
    places_down, places_up, place_ref, hidden_ref, d_pre_ref, normed_t_ref, grad_t_ref, down_ref, up_ref
):
    write_blocks(places_down, 1 - place_ref[1], grad_t_ref, hidden_ref, down_ref)
    write_blocks(places_up, 1 - place_ref[1], normed_t_ref, d_pre_ref, up_ref)


def settle_kernel(sources, place_ref, *refs):
    parts, out_ref, done = refs[:-2], refs[-2], refs[-1]
    count, rows = parts[0].shape[:2]
    copies = []
    for index, source in enumerate(sources):
        block = parts[index // count].at[index % count]
        first = pl.multiple_of((place_ref[0] ^ source) * rows, rows)
        copies.append(pltpu.make_async_copy(block, out_ref.at[pl.ds(first, rows)], done.at[index]))
    for copy in copies:
        copy.start()
    for copy in copies:
        copy.wait()


def spec(space):
    return pl.BlockSpec(memory_space=space)


def block_places(order, span_x, span_y):
    places = []
    for at_x in range(span_x):
        line = []
        for group in range(span_y // 2):
            place = 0
            for axis, step in order:
                at = at_x if axis == "gx" else 2 * group
                place = 2 * place + (at >> step & 1)
            line.append(place)
        places.append(line)
    return places


def in_vmem(*items):
    return [pltpu.with_memory_space_constraint(item, pltpu.VMEM) for item in items]


def load(place, weight):
    return pl.pallas_call(
        load_kernel,
        out_shape=pltpu.VMEM(weight.shape, weight.dtype),
        in_specs=[spec(pltpu.SMEM), spec(pltpu.HBM)],
        out_specs=spec(pltpu.VMEM),
        scratch_shapes=[pltpu.SemaphoreType.DMA],
        compiler_params=pltpu.CompilerParams(vmem_limit_bytes=KEEP_BYTES),
        cost_estimate=pl.CostEstimate(flops=0, bytes_accessed=4 * weight.size, transcendentals=0),
    )(place, pltpu.with_memory_space_constraint(weight, pltpu.HBM))


def forward(state, up, w_down):
    members, rows, width = state.shape
    total = len(MASKS) * (members // 2) * rows
    depth, units = up.shape
    bf16 = jnp.bfloat16
    outs = [
        pltpu.VMEM(state.shape, bf16),
        pltpu.VMEM((total, units), bf16),
        pltpu.VMEM((total, units), bf16),
        pltpu.VMEM((total, depth), bf16),
        pltpu.VMEM((depth, total), bf16),
        pltpu.VMEM((total, LANES), jnp.float32),
        pltpu.VMEM((units, depth), bf16),
        pltpu.VMEM(w_down.shape, bf16),
    ]
    return pl.pallas_call(
        forward_kernel,
        out_shape=outs,
        in_specs=[spec(pltpu.VMEM)] * 2 + [spec(pltpu.HBM)],
        out_specs=[spec(pltpu.VMEM)] * len(outs),
        scratch_shapes=[pltpu.VMEM(state.shape, bf16), pltpu.SemaphoreType.DMA],
        compiler_params=pltpu.CompilerParams(vmem_limit_bytes=SECTIONS_BYTES),
        cost_estimate=pl.CostEstimate(
            flops=10 * total * depth * units, bytes_accessed=16 * total * units, transcendentals=0
        ),
    )(state, *in_vmem(up), pltpu.with_memory_space_constraint(w_down, pltpu.HBM))


def backward(place, grad, kept, places, block):
    total, units = kept[0].shape
    depth = kept[2].shape[1]
    bf16 = jnp.bfloat16
    outs = [pltpu.VMEM((total, units), bf16), pltpu.VMEM((depth, total), bf16)]
    outs += [block] * 2 if block else []
    return pl.pallas_call(
        functools.partial(backward_kernel, *places),
        out_shape=outs,
        in_specs=[spec(pltpu.SMEM)] + [spec(pltpu.VMEM)] * (1 + len(kept)),
        out_specs=[spec(pltpu.VMEM)] * len(outs),
        scratch_shapes=[pltpu.VMEM(grad.shape, bf16)],
        compiler_params=pltpu.CompilerParams(vmem_limit_bytes=SECTIONS_BYTES),
        cost_estimate=pl.CostEstimate(
            flops=10 * total * depth * units, bytes_accessed=16 * total * units, transcendentals=0
        ),
    )(place, grad, *in_vmem(*kept))


def keep_blocks(place, hidden, d_pre, normed_t, grad_t, places, block):
    total, units = hidden.shape
    depth = normed_t.shape[0]
    return pl.pallas_call(
        functools.partial(keep_kernel, *places),
        out_shape=[block] * 2,
        in_specs=[spec(pltpu.SMEM)] + [spec(pltpu.VMEM)] * 4,
        out_specs=[spec(pltpu.VMEM)] * 2,
        compiler_params=pltpu.CompilerParams(vmem_limit_bytes=KEEP_BYTES),
        cost_estimate=pl.CostEstimate(
            flops=2 * total * depth * units, bytes_accessed=8 * total * units, transcendentals=0
        ),
    )(place, *in_vmem(hidden, d_pre, normed_t, grad_t))


def swap(block, axis, bit):
    pairs = [(source, source ^ (1 << bit)) for source in range(lax.axis_size(axis))]
    return lax.ppermute(block, axis, pairs)


def pick(block, at):
    return slice_at(block, 0, at).astype(jnp.float32)


def finish_sum(halves, kept, taken, order, beside=None):
    for phase, step in enumerate(order):
        mine, other = halves[step]
        shape = (2, kept.shape[0] // 2) + kept.shape[1:]
        kept, taken = kept.reshape(shape), taken.reshape(shape)
        give = (pick(kept, other) + pick(taken, other)).astype(jnp.bfloat16)
        kept = (pick(kept, mine) + pick(taken, mine)).astype(jnp.bfloat16)
        if beside:
            give = beside(phase, give)
        taken = swap(give, *step)
    return (kept.astype(jnp.float32) + taken.astype(jnp.float32))[0]


def scatter_narrow(halves, left, right, order, span_x, span_y):
    total = jnp.dot(left, right, preferred_element_type=jnp.float32).astype(jnp.bfloat16)
    rows, columns = left.shape[0] // span_x, right.shape[1] // span_y
    count_x, count_y = span_x.bit_length() - 1, span_y.bit_length() - 1
    dims = [("gx", bit) for bit in range(count_x)][::-1] + ["rows"]
    dims += [("gy", bit) for bit in range(count_y)][::-1] + ["columns"]
    blocks = total.reshape((2,) * count_x + (rows,) + (2,) * count_y + (columns,))
    blocks = blocks.transpose([dims.index(item) for item in list(order) + ["rows", "columns"]])
    blocks = blocks.reshape(-1, rows, columns)
    return finish_sum(halves, blocks, jnp.zeros_like(blocks), order)


class Journey:
    def __init__(self, held, bits=(0, 1, 2, 3), sources=(0,)):
        self.held = held
        self.bits = list(bits)
        self.sources = list(sources)
        self.parts = None

    def hop(self, at, steps, halves, after=None):
        dim = self.bits.index(at)
        mine, other = halves[steps[at]]
        kept, given = [slice_at(self.held, dim, part) for part in (mine, other)]
        if after is not None:
            given, after = lax.optimization_barrier((given, after))
        self.parts = [kept, swap(given, *steps[at])]
        self.held = jnp.concatenate(self.parts, -3)
        self.bits.remove(at)
        self.sources += [source | MASKS[at] for source in self.sources]
        return after

    def hop_both(self, at, also, steps, halves, after=None):
        dims = self.bits.index(at), self.bits.index(also)
        parts = []
        for theirs, beyond in ((0, 0), (1, 0), (0, 1), (1, 1)):
            part = slice_at(self.held, dims[0], halves[steps[at]][theirs], keep=True)
            part = slice_at(part, dims[1], halves[steps[also]][beyond], keep=True)
            parts.append(lax.squeeze(part, dims))
        if after is not None:
            parts, after = lax.optimization_barrier((parts, after))
        self.parts = [
            parts[0],
            swap(parts[1], *steps[at]),
            swap(parts[2], *steps[also]),
            swap_both(parts[3], steps[at], steps[also]),
        ]
        self.held = jnp.concatenate(self.parts, -3)
        for bit in (at, also):
            self.bits.remove(bit)
            self.sources += [source | MASKS[bit] for source in self.sources]
        return after


def slice_at(block, dim, at, keep=False):
    start = [0] * block.ndim
    start[dim] = at
    size = list(block.shape)
    size[dim] = 1
    part = lax.dynamic_slice(block, start, size, allow_negative_indices=False)
    return part if keep else lax.squeeze(part, (dim,))


def swap_both(block, step, also):
    span_x, span_y = lax.axis_size("gx"), lax.axis_size("gy")
    flips = {step[0]: 1 << step[1], also[0]: 1 << also[1]}
    pairs = []
    for at_x in range(span_x):
        for at_y in range(span_y):
            pairs.append((at_x * span_y + at_y, (at_x ^ flips["gx"]) * span_y + (at_y ^ flips["gy"])))
    return lax.ppermute(block, ("gx", "gy"), pairs)


def settle(place, journey):
    parts = journey.parts
    rows, width = parts[0].shape[-2:]
    return pl.pallas_call(
        functools.partial(settle_kernel, journey.sources),
        out_shape=jax.ShapeDtypeStruct((MEMBERS * rows, width), parts[0].dtype),
        in_specs=[spec(pltpu.SMEM)] + [spec(pltpu.VMEM)] * len(parts),
        out_specs=spec(pltpu.HBM),
        scratch_shapes=[pltpu.SemaphoreType.DMA((MEMBERS,))],
        cost_estimate=pl.CostEstimate(flops=0, bytes_accessed=4 * MEMBERS * rows * width, transcendentals=0),
    )(place, *parts)


def local(signal, w_up, w_down, cotangent):
    span_x = lax.axis_size("gx")
    span_y = lax.axis_size("gy")
    groups = section_groups(span_x, span_y)
    rows, width = signal.shape
    depth, units = w_up.shape
    steps = [("gx", span_x.bit_length() - 2), ("gx", 0), ("gy", span_y.bit_length() - 2), ("gy", 0)]
    z, y, x, core = range(4)
    rest_y = [("gy", bit) for bit in range(1, span_y.bit_length() - 1)]
    rest_x = [("gx", bit) for bit in range(1, span_x.bit_length() - 1)]
    order_down = [steps[y]] + rest_y + rest_x[::-1]
    order_up = rest_y + [steps[y]] + rest_x

    owns = [lax.axis_index(axis) // (1 << bit) % 2 for axis, bit in [steps[core]] + order_up]
    own = dict(zip([steps[core]] + order_up, owns))
    member = sum(own[step] * mask for step, mask in zip(steps, MASKS))
    place = jnp.stack([member, 1 - own[steps[core]]]).astype(jnp.int32)
    place, owns, others = lax.optimization_barrier((place, owns, [1 - item for item in owns]))
    halves = {step: pair for step, pair in zip([steps[core]] + order_up, zip(owns, others))}
    places = [block_places(order, span_x, span_y) for order in (order_down, order_up)]
    block = None
    if units // span_y % LANES == 0:
        block = pltpu.VMEM((span_x * span_y // 2, depth // span_x, units // span_y), jnp.bfloat16)

    parts = (2, 2, 2, 2, 1, rows // MEMBERS, width)
    state = exchange(signal.reshape(MEMBERS, rows // MEMBERS, width), groups)
    coming = Journey(cotangent.reshape(parts))
    coming.hop(core, steps, halves)
    coming.hop_both(x, y, steps, halves)
    up = load(place, w_up)
    state = coming.hop(z, steps, halves, state)
    state, *kept = forward(state, up, w_down)
    going = Journey(state.reshape(parts))
    d_pre, grad_t, *given = backward(place, coming.held, kept, places, block)
    hidden, normed_t = kept[0], kept[3]
    if not given:
        for at in (x, z, core, y):
            going.hop(at, steps, halves)
        mixed_out = settle(place, going)
        grad_down = scatter_narrow(halves, grad_t, hidden, [steps[core]] + order_down, span_x, span_y)
        grad_up = scatter_narrow(halves, normed_t, d_pre, [steps[core]] + order_up, span_x, span_y)
        return (mixed_out, grad_up, grad_down)
    given[1] = going.hop(x, steps, halves, given[1])
    take_down, take_up = [swap(part, *steps[core]) for part in given]
    keep_down, keep_up = keep_blocks(place, hidden, d_pre, normed_t, grad_t, places, block)

    def beside(phase, give):
        if phase < 3:
            return going.hop((z, core, y)[phase], steps, halves, give)
        going.parts, give = lax.optimization_barrier((going.parts, give))
        return give

    grad_up = finish_sum(halves, keep_up, take_up, order_up)
    grad_down = finish_sum(halves, keep_down, take_down, order_down, beside)
    return (settle(place, going), grad_up, grad_down)


def solution(mesh):
    return jax.shard_map(
        local,
        mesh=mesh,
        in_specs=(P(("gx", "gy"), None), P(), P(), P(("gx", "gy"), None)),
        out_specs=(P(("gx", "gy"), None), P("gx", "gy"), P("gx", "gy")),
        check_vma=False,
    )
```

```python
import functools
import math

import jax
import jax.numpy as jnp
from jax import lax
from jax.experimental import pallas as pl
from jax.experimental.pallas import tpu as pltpu
from jax.sharding import PartitionSpec as P

MEMBERS = 16
MASKS = (8, 4, 2, 1)
LANES = 128
CHUNK = 256
SECTIONS_BYTES = 8 * 1024 * 1024
KEEP_BYTES = 4 * 1024 * 1024


def section_groups(span_x, span_y):
    bits_x = [span_x.bit_length() - 2, 0]
    bits_y = [span_y.bit_length() - 2, 0]
    mask_x = sum(1 << bit for bit in bits_x)
    mask_y = sum(1 << bit for bit in bits_y)
    groups = []
    for base_x in range(span_x):
        for base_y in range(span_y):
            if base_x & mask_x or base_y & mask_y:
                continue
            group = []
            for member in range(MEMBERS):
                at_x, at_y = base_x, base_y
                at_x |= (member >> 3 & 1) << bits_x[0] | (member >> 2 & 1) << bits_x[1]
                at_y |= (member >> 1 & 1) << bits_y[0] | (member & 1) << bits_y[1]
                group.append(at_x * span_y + at_y)
            groups.append(group)
    return groups


def exchange(block, groups):
    return lax.all_to_all(
        block, ("gx", "gy"), split_axis=0, concat_axis=0, axis_index_groups=groups, tiled=True
    )


def contract_last(left, right):
    return lax.dot_general(
        left, right, (((1,), (1,)), ((), ())), preferred_element_type=jnp.float32
    )


def low_members(mask):
    return [member for member in range(MEMBERS) if not member & mask]


def read_pair(ref, mask, swapped=0):
    low = jnp.concatenate([ref[member ^ swapped] for member in low_members(mask)], 0)
    high = jnp.concatenate([ref[(member | mask) ^ swapped] for member in low_members(mask)], 0)
    return jnp.concatenate([low, high], 1).astype(jnp.float32)


def write_pair(ref, mask, pair):
    rows, width = ref.shape[1:]
    for place, member in enumerate(low_members(mask)):
        part = pair[place * rows : (place + 1) * rows]
        ref[member] = part[:, :width]
        ref[member | mask] = part[:, width:]


def write_blocks(places, bit, left_ref, right_ref, out_ref):
    rows, columns = out_ref.shape[1:]
    pieces = []
    for group in range(len(places[0])):
        base = (2 * group + bit) * columns
        for inner in range(0, columns, LANES):
            pieces.append((group, inner, pl.multiple_of(base + inner, LANES)))
    for first in range(0, len(pieces), 2):
        some = pieces[first : first + 2]
        right = jnp.concatenate([right_ref[:, pl.ds(start, LANES)] for _, _, start in some], 1)
        total = jnp.dot(left_ref[...], right, preferred_element_type=jnp.float32)
        total = total.astype(jnp.bfloat16)
        for which, (group, inner, _) in enumerate(some):
            for block in range(len(places)):
                out_ref[places[block][group], :, inner : inner + LANES] = total[
                    block * rows : (block + 1) * rows, which * LANES : (which + 1) * LANES
                ]


def load_kernel(place_ref, source, target, arrived):
    copy = pltpu.make_async_copy(source, target, arrived)
    copy.start()
    copy.wait()


def forward_kernel(
    state_ref, up_ref, down_hbm,
    out_ref, hidden_ref, slope_ref, normed_ref, normed_t_ref, factor_ref, up_t_ref, down_ref, work_ref, arrived
):
    fetch_down = pltpu.make_async_copy(down_hbm, down_ref, arrived)
    fetch_down.start()
    pairs = MEMBERS // 2 * work_ref.shape[1]
    hidden_units = up_ref.shape[1]
    last = len(MASKS) - 1
    for section, mask in enumerate(MASKS):
        at = pl.ds(section * pairs, pairs)
        pair = read_pair(state_ref if section == 0 else work_ref, mask)
        centre = jnp.mean(pair, axis=-1, keepdims=True)
        shifted = pair - centre
        spread = jnp.mean(shifted * shifted, axis=-1, keepdims=True)
        factor = lax.rsqrt(spread + 1e-05)
        normed = (shifted * factor).astype(jnp.bfloat16)
        normed_ref[at, :] = normed
        factor_ref[at, :] = jnp.broadcast_to(factor, (pairs, LANES))
        for start in range(0, hidden_units, CHUNK):
            units = pl.ds(start, CHUNK)
            pre = jnp.dot(normed, up_ref[:, units], preferred_element_type=jnp.float32)
            share = 0.5 * (1.0 + lax.erf(pre * (1.0 / math.sqrt(2.0))))
            hidden_ref[at, units] = (pre * share).astype(jnp.bfloat16)
            bell = jnp.exp(-0.5 * pre * pre) * (1.0 / math.sqrt(2.0 * math.pi))
            slope_ref[at, units] = (share + pre * bell).astype(jnp.bfloat16)
        if section == 0:
            fetch_down.wait()
        mixed = (pair + contract_last(hidden_ref[at, :], down_ref[...])).astype(jnp.bfloat16)
        write_pair(work_ref if section < last else out_ref, mask, mixed)
        normed_t_ref[:, at] = normed.T
        quarter = pl.ds(section * (hidden_units // len(MASKS)), hidden_units // len(MASKS))
        up_t_ref[quarter, :] = up_ref[:, quarter].T


def backward_kernel(
    places_down, places_up, place_ref, grad_ref, hidden_ref, slope_ref, normed_ref, normed_t_ref, factor_ref,
    up_t_ref, down_ref, d_pre_ref, grad_t_ref, *rest
):
    blocks, work_ref = rest[:-1], rest[-1]
    pairs = MEMBERS // 2 * work_ref.shape[1]
    hidden_units = down_ref.shape[1]
    last = len(MASKS) - 1
    for section in range(last, -1, -1):
        mask = MASKS[section]
        at = pl.ds(section * pairs, pairs)
        if section == last:
            pair_grad = read_pair(grad_ref, mask, swapped=place_ref[0])
        else:
            pair_grad = read_pair(work_ref, mask)
        pair_bf = pair_grad.astype(jnp.bfloat16)
        for start in range(0, hidden_units, CHUNK):
            units = pl.ds(start, CHUNK)
            d_hidden = jnp.dot(pair_bf, down_ref[:, units], preferred_element_type=jnp.float32)
            d_pre_ref[at, units] = (d_hidden * slope_ref[at, units].astype(jnp.float32)).astype(jnp.bfloat16)
        if section > 0:
            d_norm = jnp.dot(d_pre_ref[at, :], up_t_ref[...], preferred_element_type=jnp.float32)
            normed = normed_ref[at, :].astype(jnp.float32)
            d_pair = factor_ref[at, :][:, :1] * (
                d_norm
                - jnp.mean(d_norm, axis=-1, keepdims=True)
                - normed * jnp.mean(d_norm * normed, axis=-1, keepdims=True)
            )
            write_pair(work_ref, mask, (pair_grad + d_pair).astype(jnp.bfloat16))
        grad_t_ref[:, at] = pair_bf.T

    if blocks:
        write_blocks(places_down, place_ref[1], grad_t_ref, hidden_ref, blocks[0])
        write_blocks(places_up, place_ref[1], normed_t_ref, d_pre_ref, blocks[1])


def keep_kernel(
    places_down, places_up, place_ref, hidden_ref, d_pre_ref, normed_t_ref, grad_t_ref, down_ref, up_ref
):
    write_blocks(places_down, 1 - place_ref[1], grad_t_ref, hidden_ref, down_ref)
    write_blocks(places_up, 1 - place_ref[1], normed_t_ref, d_pre_ref, up_ref)


def settle_kernel(sources, place_ref, *refs):
    parts, out_ref, done = refs[:-2], refs[-2], refs[-1]
    count, rows = parts[0].shape[:2]
    copies = []
    for index, source in enumerate(sources):
        block = parts[index // count].at[index % count]
        first = pl.multiple_of((place_ref[0] ^ source) * rows, rows)
        copies.append(pltpu.make_async_copy(block, out_ref.at[pl.ds(first, rows)], done.at[index]))
    for copy in copies:
        copy.start()
    for copy in copies:
        copy.wait()


def spec(space):
    return pl.BlockSpec(memory_space=space)


def block_places(order, span_x, span_y):
    places = []
    for at_x in range(span_x):
        line = []
        for group in range(span_y // 2):
            place = 0
            for axis, step in order:
                at = at_x if axis == "gx" else 2 * group
                place = 2 * place + (at >> step & 1)
            line.append(place)
        places.append(line)
    return places


def in_vmem(*items):
    return [pltpu.with_memory_space_constraint(item, pltpu.VMEM) for item in items]


def load(place, weight):
    return pl.pallas_call(
        load_kernel,
        out_shape=pltpu.VMEM(weight.shape, weight.dtype),
        in_specs=[spec(pltpu.SMEM), spec(pltpu.HBM)],
        out_specs=spec(pltpu.VMEM),
        scratch_shapes=[pltpu.SemaphoreType.DMA],
        compiler_params=pltpu.CompilerParams(vmem_limit_bytes=KEEP_BYTES),
        cost_estimate=pl.CostEstimate(flops=0, bytes_accessed=4 * weight.size, transcendentals=0),
    )(place, pltpu.with_memory_space_constraint(weight, pltpu.HBM))


def forward(state, up, w_down):
    members, rows, width = state.shape
    total = len(MASKS) * (members // 2) * rows
    depth, units = up.shape
    bf16 = jnp.bfloat16
    outs = [
        pltpu.VMEM(state.shape, bf16),
        pltpu.VMEM((total, units), bf16),
        pltpu.VMEM((total, units), bf16),
        pltpu.VMEM((total, depth), bf16),
        pltpu.VMEM((depth, total), bf16),
        pltpu.VMEM((total, LANES), jnp.float32),
        pltpu.VMEM((units, depth), bf16),
        pltpu.VMEM(w_down.shape, bf16),
    ]
    return pl.pallas_call(
        forward_kernel,
        out_shape=outs,
        in_specs=[spec(pltpu.VMEM)] * 2 + [spec(pltpu.HBM)],
        out_specs=[spec(pltpu.VMEM)] * len(outs),
        scratch_shapes=[pltpu.VMEM(state.shape, bf16), pltpu.SemaphoreType.DMA],
        compiler_params=pltpu.CompilerParams(vmem_limit_bytes=SECTIONS_BYTES),
        cost_estimate=pl.CostEstimate(
            flops=10 * total * depth * units, bytes_accessed=16 * total * units, transcendentals=0
        ),
    )(state, *in_vmem(up), pltpu.with_memory_space_constraint(w_down, pltpu.HBM))


def backward(place, grad, kept, places, block):
    total, units = kept[0].shape
    depth = kept[2].shape[1]
    bf16 = jnp.bfloat16
    outs = [pltpu.VMEM((total, units), bf16), pltpu.VMEM((depth, total), bf16)]
    outs += [block] * 2 if block else []
    return pl.pallas_call(
        functools.partial(backward_kernel, *places),
        out_shape=outs,
        in_specs=[spec(pltpu.SMEM)] + [spec(pltpu.VMEM)] * (1 + len(kept)),
        out_specs=[spec(pltpu.VMEM)] * len(outs),
        scratch_shapes=[pltpu.VMEM(grad.shape, bf16)],
        compiler_params=pltpu.CompilerParams(vmem_limit_bytes=SECTIONS_BYTES),
        cost_estimate=pl.CostEstimate(
            flops=10 * total * depth * units, bytes_accessed=16 * total * units, transcendentals=0
        ),
    )(place, grad, *in_vmem(*kept))


def keep_blocks(place, hidden, d_pre, normed_t, grad_t, places, block):
    total, units = hidden.shape
    depth = normed_t.shape[0]
    return pl.pallas_call(
        functools.partial(keep_kernel, *places),
        out_shape=[block] * 2,
        in_specs=[spec(pltpu.SMEM)] + [spec(pltpu.VMEM)] * 4,
        out_specs=[spec(pltpu.VMEM)] * 2,
        compiler_params=pltpu.CompilerParams(vmem_limit_bytes=KEEP_BYTES),
        cost_estimate=pl.CostEstimate(
            flops=2 * total * depth * units, bytes_accessed=8 * total * units, transcendentals=0
        ),
    )(place, *in_vmem(hidden, d_pre, normed_t, grad_t))


def swap(block, axis, bit):
    pairs = [(source, source ^ (1 << bit)) for source in range(lax.axis_size(axis))]
    return lax.ppermute(block, axis, pairs)


def pick(block, at):
    return slice_at(block, 0, at).astype(jnp.float32)


def finish_sum(halves, kept, taken, order, beside=None):
    for phase, step in enumerate(order):
        mine, other = halves[step]
        shape = (2, kept.shape[0] // 2) + kept.shape[1:]
        kept, taken = kept.reshape(shape), taken.reshape(shape)
        give = (pick(kept, other) + pick(taken, other)).astype(jnp.bfloat16)
        kept = (pick(kept, mine) + pick(taken, mine)).astype(jnp.bfloat16)
        if beside:
            give = beside(phase, give)
        taken = swap(give, *step)
    return (kept.astype(jnp.float32) + taken.astype(jnp.float32))[0]


def scatter_narrow(halves, left, right, order, span_x, span_y):
    total = jnp.dot(left, right, preferred_element_type=jnp.float32).astype(jnp.bfloat16)
    rows, columns = left.shape[0] // span_x, right.shape[1] // span_y
    count_x, count_y = span_x.bit_length() - 1, span_y.bit_length() - 1
    dims = [("gx", bit) for bit in range(count_x)][::-1] + ["rows"]
    dims += [("gy", bit) for bit in range(count_y)][::-1] + ["columns"]
    blocks = total.reshape((2,) * count_x + (rows,) + (2,) * count_y + (columns,))
    blocks = blocks.transpose([dims.index(item) for item in list(order) + ["rows", "columns"]])
    blocks = blocks.reshape(-1, rows, columns)
    return finish_sum(halves, blocks, jnp.zeros_like(blocks), order)


class Journey:
    def __init__(self, held, bits=(0, 1, 2, 3), sources=(0,)):
        self.held = held
        self.bits = list(bits)
        self.sources = list(sources)
        self.parts = None

    def hop(self, at, steps, halves, after=None):
        dim = self.bits.index(at)
        mine, other = halves[steps[at]]
        kept, given = [slice_at(self.held, dim, part) for part in (mine, other)]
        if after is not None:
            given, after = lax.optimization_barrier((given, after))
        self.parts = [kept, swap(given, *steps[at])]
        self.held = jnp.concatenate(self.parts, -3)
        self.bits.remove(at)
        self.sources += [source | MASKS[at] for source in self.sources]
        return after

    def hop_both(self, at, also, steps, halves, after=None):
        dims = self.bits.index(at), self.bits.index(also)
        parts = []
        for theirs, beyond in ((0, 0), (1, 0), (0, 1), (1, 1)):
            part = slice_at(self.held, dims[0], halves[steps[at]][theirs], keep=True)
            part = slice_at(part, dims[1], halves[steps[also]][beyond], keep=True)
            parts.append(lax.squeeze(part, dims))
        if after is not None:
            parts, after = lax.optimization_barrier((parts, after))
        self.parts = [
            parts[0],
            swap(parts[1], *steps[at]),
            swap(parts[2], *steps[also]),
            swap_both(parts[3], steps[at], steps[also]),
        ]
        self.held = jnp.concatenate(self.parts, -3)
        for bit in (at, also):
            self.bits.remove(bit)
            self.sources += [source | MASKS[bit] for source in self.sources]
        return after


def slice_at(block, dim, at, keep=False):
    start = [0] * block.ndim
    start[dim] = at
    size = list(block.shape)
    size[dim] = 1
    part = lax.dynamic_slice(block, start, size, allow_negative_indices=False)
    return part if keep else lax.squeeze(part, (dim,))


def swap_both(block, step, also):
    span_x, span_y = lax.axis_size("gx"), lax.axis_size("gy")
    flips = {step[0]: 1 << step[1], also[0]: 1 << also[1]}
    pairs = []
    for at_x in range(span_x):
        for at_y in range(span_y):
            pairs.append((at_x * span_y + at_y, (at_x ^ flips["gx"]) * span_y + (at_y ^ flips["gy"])))
    return lax.ppermute(block, ("gx", "gy"), pairs)


def settle(place, journey):
    parts = journey.parts
    rows, width = parts[0].shape[-2:]
    return pl.pallas_call(
        functools.partial(settle_kernel, journey.sources),
        out_shape=jax.ShapeDtypeStruct((MEMBERS * rows, width), parts[0].dtype),
        in_specs=[spec(pltpu.SMEM)] + [spec(pltpu.VMEM)] * len(parts),
        out_specs=spec(pltpu.HBM),
        scratch_shapes=[pltpu.SemaphoreType.DMA((MEMBERS,))],
        cost_estimate=pl.CostEstimate(flops=0, bytes_accessed=4 * MEMBERS * rows * width, transcendentals=0),
    )(place, *parts)


def local(signal, w_up, w_down, cotangent):
    span_x = lax.axis_size("gx")
    span_y = lax.axis_size("gy")
    groups = section_groups(span_x, span_y)
    rows, width = signal.shape
    depth, units = w_up.shape
    steps = [("gx", span_x.bit_length() - 2), ("gx", 0), ("gy", span_y.bit_length() - 2), ("gy", 0)]
    z, y, x, core = range(4)
    rest_y = [("gy", bit) for bit in range(1, span_y.bit_length() - 1)]
    rest_x = [("gx", bit) for bit in range(1, span_x.bit_length() - 1)]
    order_down = [steps[y]] + rest_y + rest_x[::-1]
    order_up = rest_y + [steps[y]] + rest_x

    owns = [lax.axis_index(axis) // (1 << bit) % 2 for axis, bit in [steps[core]] + order_up]
    own = dict(zip([steps[core]] + order_up, owns))
    member = sum(own[step] * mask for step, mask in zip(steps, MASKS))
    place = jnp.stack([member, 1 - own[steps[core]]]).astype(jnp.int32)
    place, owns, others = lax.optimization_barrier((place, owns, [1 - item for item in owns]))
    halves = {step: pair for step, pair in zip([steps[core]] + order_up, zip(owns, others))}
    places = [block_places(order, span_x, span_y) for order in (order_down, order_up)]
    block = None
    if units // span_y % LANES == 0:
        block = pltpu.VMEM((span_x * span_y // 2, depth // span_x, units // span_y), jnp.bfloat16)

    parts = (2, 2, 2, 2, 1, rows // MEMBERS, width)
    state = exchange(signal.reshape(MEMBERS, rows // MEMBERS, width), groups)
    coming = Journey(cotangent.reshape(parts))
    coming.hop(core, steps, halves)
    coming.hop_both(x, y, steps, halves)
    up = load(place, w_up)
    state = coming.hop(z, steps, halves, state)
    state, *kept = forward(state, up, w_down)
    going = Journey(state.reshape(parts))
    kept[4] = going.hop_both(x, y, steps, halves, kept[4])
    d_pre, grad_t, *given = backward(place, coming.held, kept, places, block)
    hidden, normed_t = kept[0], kept[3]
    if not given:
        going.hop(z, steps, halves)
        going.hop(core, steps, halves)
        mixed_out = settle(place, going)
        grad_down = scatter_narrow(halves, grad_t, hidden, [steps[core]] + order_down, span_x, span_y)
        grad_up = scatter_narrow(halves, normed_t, d_pre, [steps[core]] + order_up, span_x, span_y)
        return (mixed_out, grad_up, grad_down)
    given[0] = going.hop(z, steps, halves, given[0])
    take_down, take_up = [swap(part, *steps[core]) for part in given]
    keep_down, keep_up = keep_blocks(place, hidden, d_pre, normed_t, grad_t, places, block)

    def beside(phase, give):
        if phase == 1:
            return going.hop(core, steps, halves, give)
        if phase == 2:
            going.parts, give = lax.optimization_barrier((going.parts, give))
        return give

    grad_up = finish_sum(halves, keep_up, take_up, order_up)
    grad_down = finish_sum(halves, keep_down, take_down, order_down, beside)
    return (settle(place, going), grad_up, grad_down)


def solution(mesh):
    return jax.shard_map(
        local,
        mesh=mesh,
        in_specs=(P(("gx", "gy"), None), P(), P(), P(("gx", "gy"), None)),
        out_specs=(P(("gx", "gy"), None), P("gx", "gy"), P("gx", "gy")),
        check_vma=False,
    )
```

```python
import functools
import math

import jax
import jax.numpy as jnp
from jax import lax
from jax.experimental import pallas as pl
from jax.experimental.pallas import tpu as pltpu
from jax.sharding import PartitionSpec as P

MEMBERS = 16
MASKS = (8, 4, 2, 1)
LANES = 128
CHUNK = 256
SECTIONS_BYTES = 8 * 1024 * 1024
KEEP_BYTES = 4 * 1024 * 1024


def section_groups(span_x, span_y):
    bits_x = [span_x.bit_length() - 2, 0]
    bits_y = [span_y.bit_length() - 2, 0]
    mask_x = sum(1 << bit for bit in bits_x)
    mask_y = sum(1 << bit for bit in bits_y)
    groups = []
    for base_x in range(span_x):
        for base_y in range(span_y):
            if base_x & mask_x or base_y & mask_y:
                continue
            group = []
            for member in range(MEMBERS):
                at_x, at_y = base_x, base_y
                at_x |= (member >> 3 & 1) << bits_x[0] | (member >> 2 & 1) << bits_x[1]
                at_y |= (member >> 1 & 1) << bits_y[0] | (member & 1) << bits_y[1]
                group.append(at_x * span_y + at_y)
            groups.append(group)
    return groups


def exchange(block, groups):
    return lax.all_to_all(
        block, ("gx", "gy"), split_axis=0, concat_axis=0, axis_index_groups=groups, tiled=True
    )


def contract_last(left, right):
    return lax.dot_general(
        left, right, (((1,), (1,)), ((), ())), preferred_element_type=jnp.float32
    )


def low_members(mask):
    return [member for member in range(MEMBERS) if not member & mask]


def read_pair(ref, mask, swapped=0):
    low = jnp.concatenate([ref[member ^ swapped] for member in low_members(mask)], 0)
    high = jnp.concatenate([ref[(member | mask) ^ swapped] for member in low_members(mask)], 0)
    return jnp.concatenate([low, high], 1).astype(jnp.float32)


def write_pair(ref, mask, pair):
    rows, width = ref.shape[1:]
    for place, member in enumerate(low_members(mask)):
        part = pair[place * rows : (place + 1) * rows]
        ref[member] = part[:, :width]
        ref[member | mask] = part[:, width:]


def write_blocks(places, bit, left_ref, right_ref, out_ref):
    rows, columns = out_ref.shape[1:]
    pieces = []
    for group in range(len(places[0])):
        base = (2 * group + bit) * columns
        for inner in range(0, columns, LANES):
            pieces.append((group, inner, pl.multiple_of(base + inner, LANES)))
    for first in range(0, len(pieces), 2):
        some = pieces[first : first + 2]
        right = jnp.concatenate([right_ref[:, pl.ds(start, LANES)] for _, _, start in some], 1)
        total = jnp.dot(left_ref[...], right, preferred_element_type=jnp.float32)
        total = total.astype(jnp.bfloat16)
        for which, (group, inner, _) in enumerate(some):
            for block in range(len(places)):
                out_ref[places[block][group], :, inner : inner + LANES] = total[
                    block * rows : (block + 1) * rows, which * LANES : (which + 1) * LANES
                ]


def load_kernel(place_ref, source, target, arrived):
    copy = pltpu.make_async_copy(source, target, arrived)
    copy.start()
    copy.wait()


def forward_kernel(
    state_ref, up_ref, down_hbm,
    out_ref, hidden_ref, slope_ref, normed_ref, normed_t_ref, factor_ref, up_t_ref, down_ref, work_ref, arrived
):
    fetch_down = pltpu.make_async_copy(down_hbm, down_ref, arrived)
    fetch_down.start()
    pairs = MEMBERS // 2 * work_ref.shape[1]
    hidden_units = up_ref.shape[1]
    last = len(MASKS) - 1
    for section, mask in enumerate(MASKS):
        at = pl.ds(section * pairs, pairs)
        pair = read_pair(state_ref if section == 0 else work_ref, mask)
        centre = jnp.mean(pair, axis=-1, keepdims=True)
        shifted = pair - centre
        spread = jnp.mean(shifted * shifted, axis=-1, keepdims=True)
        factor = lax.rsqrt(spread + 1e-05)
        normed = (shifted * factor).astype(jnp.bfloat16)
        normed_ref[at, :] = normed
        factor_ref[at, :] = jnp.broadcast_to(factor, (pairs, LANES))
        for start in range(0, hidden_units, CHUNK):
            units = pl.ds(start, CHUNK)
            pre = jnp.dot(normed, up_ref[:, units], preferred_element_type=jnp.float32)
            share = 0.5 * (1.0 + lax.erf(pre * (1.0 / math.sqrt(2.0))))
            hidden_ref[at, units] = (pre * share).astype(jnp.bfloat16)
            bell = jnp.exp(-0.5 * pre * pre) * (1.0 / math.sqrt(2.0 * math.pi))
            slope_ref[at, units] = (share + pre * bell).astype(jnp.bfloat16)
        if section == 0:
            fetch_down.wait()
        mixed = (pair + contract_last(hidden_ref[at, :], down_ref[...])).astype(jnp.bfloat16)
        write_pair(work_ref if section < last else out_ref, mask, mixed)
        normed_t_ref[:, at] = normed.T
        quarter = pl.ds(section * (hidden_units // len(MASKS)), hidden_units // len(MASKS))
        up_t_ref[quarter, :] = up_ref[:, quarter].T


def backward_kernel(
    places_down, places_up, place_ref, grad_ref, hidden_ref, slope_ref, normed_ref, normed_t_ref, factor_ref,
    up_t_ref, down_ref, d_pre_ref, grad_t_ref, *rest
):
    blocks, work_ref = rest[:-1], rest[-1]
    pairs = MEMBERS // 2 * work_ref.shape[1]
    hidden_units = down_ref.shape[1]
    last = len(MASKS) - 1
    for section in range(last, -1, -1):
        mask = MASKS[section]
        at = pl.ds(section * pairs, pairs)
        if section == last:
            pair_grad = read_pair(grad_ref, mask, swapped=place_ref[0])
        else:
            pair_grad = read_pair(work_ref, mask)
        pair_bf = pair_grad.astype(jnp.bfloat16)
        for start in range(0, hidden_units, CHUNK):
            units = pl.ds(start, CHUNK)
            d_hidden = jnp.dot(pair_bf, down_ref[:, units], preferred_element_type=jnp.float32)
            d_pre_ref[at, units] = (d_hidden * slope_ref[at, units].astype(jnp.float32)).astype(jnp.bfloat16)
        if section > 0:
            d_norm = jnp.dot(d_pre_ref[at, :], up_t_ref[...], preferred_element_type=jnp.float32)
            normed = normed_ref[at, :].astype(jnp.float32)
            d_pair = factor_ref[at, :][:, :1] * (
                d_norm
                - jnp.mean(d_norm, axis=-1, keepdims=True)
                - normed * jnp.mean(d_norm * normed, axis=-1, keepdims=True)
            )
            write_pair(work_ref, mask, (pair_grad + d_pair).astype(jnp.bfloat16))
        grad_t_ref[:, at] = pair_bf.T

    if blocks:
        write_blocks(places_down, place_ref[1], grad_t_ref, hidden_ref, blocks[0])
        write_blocks(places_up, place_ref[1], normed_t_ref, d_pre_ref, blocks[1])


def keep_kernel(places, place_ref, left_ref, right_ref, out_ref):
    write_blocks(places, 1 - place_ref[1], left_ref, right_ref, out_ref)


def settle_kernel(sources, place_ref, *refs):
    parts, out_ref, done = refs[:-2], refs[-2], refs[-1]
    count, rows = parts[0].shape[:2]
    copies = []
    for index, source in enumerate(sources):
        block = parts[index // count].at[index % count]
        first = pl.multiple_of((place_ref[0] ^ source) * rows, rows)
        copies.append(pltpu.make_async_copy(block, out_ref.at[pl.ds(first, rows)], done.at[index]))
    for copy in copies:
        copy.start()
    for copy in copies:
        copy.wait()


def spec(space):
    return pl.BlockSpec(memory_space=space)


def block_places(order, span_x, span_y):
    places = []
    for at_x in range(span_x):
        line = []
        for group in range(span_y // 2):
            place = 0
            for axis, step in order:
                at = at_x if axis == "gx" else 2 * group
                place = 2 * place + (at >> step & 1)
            line.append(place)
        places.append(line)
    return places


def in_vmem(*items):
    return [pltpu.with_memory_space_constraint(item, pltpu.VMEM) for item in items]


def load(place, weight):
    return pl.pallas_call(
        load_kernel,
        out_shape=pltpu.VMEM(weight.shape, weight.dtype),
        in_specs=[spec(pltpu.SMEM), spec(pltpu.HBM)],
        out_specs=spec(pltpu.VMEM),
        scratch_shapes=[pltpu.SemaphoreType.DMA],
        compiler_params=pltpu.CompilerParams(vmem_limit_bytes=KEEP_BYTES),
        cost_estimate=pl.CostEstimate(flops=0, bytes_accessed=4 * weight.size, transcendentals=0),
    )(place, pltpu.with_memory_space_constraint(weight, pltpu.HBM))


def forward(state, up, w_down):
    members, rows, width = state.shape
    total = len(MASKS) * (members // 2) * rows
    depth, units = up.shape
    bf16 = jnp.bfloat16
    outs = [
        pltpu.VMEM(state.shape, bf16),
        pltpu.VMEM((total, units), bf16),
        pltpu.VMEM((total, units), bf16),
        pltpu.VMEM((total, depth), bf16),
        pltpu.VMEM((depth, total), bf16),
        pltpu.VMEM((total, LANES), jnp.float32),
        pltpu.VMEM((units, depth), bf16),
        pltpu.VMEM(w_down.shape, bf16),
    ]
    return pl.pallas_call(
        forward_kernel,
        out_shape=outs,
        in_specs=[spec(pltpu.VMEM)] * 2 + [spec(pltpu.HBM)],
        out_specs=[spec(pltpu.VMEM)] * len(outs),
        scratch_shapes=[pltpu.VMEM(state.shape, bf16), pltpu.SemaphoreType.DMA],
        compiler_params=pltpu.CompilerParams(vmem_limit_bytes=SECTIONS_BYTES),
        cost_estimate=pl.CostEstimate(
            flops=10 * total * depth * units, bytes_accessed=16 * total * units, transcendentals=0
        ),
    )(state, *in_vmem(up), pltpu.with_memory_space_constraint(w_down, pltpu.HBM))


def backward(place, grad, kept, places, block):
    total, units = kept[0].shape
    depth = kept[2].shape[1]
    bf16 = jnp.bfloat16
    outs = [pltpu.VMEM((total, units), bf16), pltpu.VMEM((depth, total), bf16)]
    outs += [block] * 2 if block else []
    return pl.pallas_call(
        functools.partial(backward_kernel, *places),
        out_shape=outs,
        in_specs=[spec(pltpu.SMEM)] + [spec(pltpu.VMEM)] * (1 + len(kept)),
        out_specs=[spec(pltpu.VMEM)] * len(outs),
        scratch_shapes=[pltpu.VMEM(grad.shape, bf16)],
        compiler_params=pltpu.CompilerParams(vmem_limit_bytes=SECTIONS_BYTES),
        cost_estimate=pl.CostEstimate(
            flops=10 * total * depth * units, bytes_accessed=16 * total * units, transcendentals=0
        ),
    )(place, grad, *in_vmem(*kept))


def keep_blocks(place, left, right, places, block):
    total, units = right.shape
    return pl.pallas_call(
        functools.partial(keep_kernel, places),
        out_shape=block,
        in_specs=[spec(pltpu.SMEM)] + [spec(pltpu.VMEM)] * 2,
        out_specs=spec(pltpu.VMEM),
        compiler_params=pltpu.CompilerParams(vmem_limit_bytes=KEEP_BYTES),
        cost_estimate=pl.CostEstimate(
            flops=total * left.shape[0] * units, bytes_accessed=4 * total * units, transcendentals=0
        ),
    )(place, *in_vmem(left, right))


def swap(block, axis, bit):
    pairs = [(source, source ^ (1 << bit)) for source in range(lax.axis_size(axis))]
    return lax.ppermute(block, axis, pairs)


def pick(block, at):
    return slice_at(block, 0, at).astype(jnp.float32)


def finish_sum(halves, kept, taken, order, beside=None):
    for phase, step in enumerate(order):
        mine, other = halves[step]
        shape = (2, kept.shape[0] // 2) + kept.shape[1:]
        kept, taken = kept.reshape(shape), taken.reshape(shape)
        give = (pick(kept, other) + pick(taken, other)).astype(jnp.bfloat16)
        kept = (pick(kept, mine) + pick(taken, mine)).astype(jnp.bfloat16)
        if beside:
            give = beside(phase, give)
        taken = swap(give, *step)
    return (kept.astype(jnp.float32) + taken.astype(jnp.float32))[0]


def scatter_narrow(halves, left, right, order, span_x, span_y):
    total = jnp.dot(left, right, preferred_element_type=jnp.float32).astype(jnp.bfloat16)
    rows, columns = left.shape[0] // span_x, right.shape[1] // span_y
    count_x, count_y = span_x.bit_length() - 1, span_y.bit_length() - 1
    dims = [("gx", bit) for bit in range(count_x)][::-1] + ["rows"]
    dims += [("gy", bit) for bit in range(count_y)][::-1] + ["columns"]
    blocks = total.reshape((2,) * count_x + (rows,) + (2,) * count_y + (columns,))
    blocks = blocks.transpose([dims.index(item) for item in list(order) + ["rows", "columns"]])
    blocks = blocks.reshape(-1, rows, columns)
    return finish_sum(halves, blocks, jnp.zeros_like(blocks), order)


class Journey:
    def __init__(self, held, bits=(0, 1, 2, 3), sources=(0,)):
        self.held = held
        self.bits = list(bits)
        self.sources = list(sources)
        self.parts = None

    def hop(self, at, steps, halves, after=None):
        dim = self.bits.index(at)
        mine, other = halves[steps[at]]
        kept, given = [slice_at(self.held, dim, part) for part in (mine, other)]
        if after is not None:
            given, after = lax.optimization_barrier((given, after))
        self.parts = [kept, swap(given, *steps[at])]
        self.held = jnp.concatenate(self.parts, -3)
        self.bits.remove(at)
        self.sources += [source | MASKS[at] for source in self.sources]
        return after

    def hop_both(self, at, also, steps, halves, after=None):
        dims = self.bits.index(at), self.bits.index(also)
        parts = []
        for theirs, beyond in ((0, 0), (1, 0), (0, 1), (1, 1)):
            part = slice_at(self.held, dims[0], halves[steps[at]][theirs], keep=True)
            part = slice_at(part, dims[1], halves[steps[also]][beyond], keep=True)
            parts.append(lax.squeeze(part, dims))
        if after is not None:
            parts, after = lax.optimization_barrier((parts, after))
        self.parts = [
            parts[0],
            swap(parts[1], *steps[at]),
            swap(parts[2], *steps[also]),
            swap_both(parts[3], steps[at], steps[also]),
        ]
        self.held = jnp.concatenate(self.parts, -3)
        for bit in (at, also):
            self.bits.remove(bit)
            self.sources += [source | MASKS[bit] for source in self.sources]
        return after


def slice_at(block, dim, at, keep=False):
    start = [0] * block.ndim
    start[dim] = at
    size = list(block.shape)
    size[dim] = 1
    part = lax.dynamic_slice(block, start, size, allow_negative_indices=False)
    return part if keep else lax.squeeze(part, (dim,))


def swap_both(block, step, also):
    span_x, span_y = lax.axis_size("gx"), lax.axis_size("gy")
    flips = {step[0]: 1 << step[1], also[0]: 1 << also[1]}
    pairs = []
    for at_x in range(span_x):
        for at_y in range(span_y):
            pairs.append((at_x * span_y + at_y, (at_x ^ flips["gx"]) * span_y + (at_y ^ flips["gy"])))
    return lax.ppermute(block, ("gx", "gy"), pairs)


def settle(place, journey):
    parts = journey.parts
    rows, width = parts[0].shape[-2:]
    return pl.pallas_call(
        functools.partial(settle_kernel, journey.sources),
        out_shape=jax.ShapeDtypeStruct((MEMBERS * rows, width), parts[0].dtype),
        in_specs=[spec(pltpu.SMEM)] + [spec(pltpu.VMEM)] * len(parts),
        out_specs=spec(pltpu.HBM),
        scratch_shapes=[pltpu.SemaphoreType.DMA((MEMBERS,))],
        cost_estimate=pl.CostEstimate(flops=0, bytes_accessed=4 * MEMBERS * rows * width, transcendentals=0),
    )(place, *parts)


def local(signal, w_up, w_down, cotangent):
    span_x = lax.axis_size("gx")
    span_y = lax.axis_size("gy")
    groups = section_groups(span_x, span_y)
    rows, width = signal.shape
    depth, units = w_up.shape
    steps = [("gx", span_x.bit_length() - 2), ("gx", 0), ("gy", span_y.bit_length() - 2), ("gy", 0)]
    z, y, x, core = range(4)
    rest_y = [("gy", bit) for bit in range(1, span_y.bit_length() - 1)]
    rest_x = [("gx", bit) for bit in range(1, span_x.bit_length() - 1)]
    order_down = [steps[y]] + rest_y + rest_x[::-1]
    order_up = rest_y + [steps[y]] + rest_x

    owns = [lax.axis_index(axis) // (1 << bit) % 2 for axis, bit in [steps[core]] + order_up]
    own = dict(zip([steps[core]] + order_up, owns))
    member = sum(own[step] * mask for step, mask in zip(steps, MASKS))
    place = jnp.stack([member, 1 - own[steps[core]]]).astype(jnp.int32)
    place, owns, others = lax.optimization_barrier((place, owns, [1 - item for item in owns]))
    halves = {step: pair for step, pair in zip([steps[core]] + order_up, zip(owns, others))}
    places = [block_places(order, span_x, span_y) for order in (order_down, order_up)]
    block = None
    if units // span_y % LANES == 0:
        block = pltpu.VMEM((span_x * span_y // 2, depth // span_x, units // span_y), jnp.bfloat16)

    parts = (2, 2, 2, 2, 1, rows // MEMBERS, width)
    state = exchange(signal.reshape(MEMBERS, rows // MEMBERS, width), groups)
    coming = Journey(cotangent.reshape(parts))
    coming.hop(core, steps, halves)
    coming.hop_both(x, y, steps, halves)
    up = load(place, w_up)
    state = coming.hop(z, steps, halves, state)
    state, *kept = forward(state, up, w_down)
    going = Journey(state.reshape(parts))
    grad = going.hop(z, steps, halves, coming.held)
    d_pre, grad_t, *given = backward(place, grad, kept, places, block)
    hidden, normed_t = kept[0], kept[3]
    if not given:
        going.hop(core, steps, halves)
        going.hop_both(x, y, steps, halves)
        mixed_out = settle(place, going)
        grad_down = scatter_narrow(halves, grad_t, hidden, [steps[core]] + order_down, span_x, span_y)
        grad_up = scatter_narrow(halves, normed_t, d_pre, [steps[core]] + order_up, span_x, span_y)
        return (mixed_out, grad_up, grad_down)
    take_down, take_up = [swap(part, *steps[core]) for part in given]
    keep_up = keep_blocks(place, normed_t, d_pre, places[1], block)
    keep_down = keep_blocks(place, grad_t, hidden, places[0], block)

    def beside(phase, give):
        if phase == 1:
            return going.hop(core, steps, halves, give)
        if phase == 2:
            return going.hop_both(x, y, steps, halves, give)
        if phase == len(order_down) - 1:
            going.parts, give = lax.optimization_barrier((going.parts, give))
        return give

    grad_up = finish_sum(halves, keep_up, take_up, order_up)
    grad_down = finish_sum(halves, keep_down, take_down, order_down, beside)
    return (settle(place, going), grad_up, grad_down)


def solution(mesh):
    return jax.shard_map(
        local,
        mesh=mesh,
        in_specs=(P(("gx", "gy"), None), P(), P(), P(("gx", "gy"), None)),
        out_specs=(P(("gx", "gy"), None), P("gx", "gy"), P("gx", "gy")),
        check_vma=False,
    )
```
